32 devices in a mesh: seq: 32 (over z, y, x, core).
Axes of the slice: x: 2, y: 2, z: 4, core: 2. Of those that a mesh axis runs over, the one named last changes fastest.
Arguments:
- byte_acts: bfloat16 [16384, 1024], P('seq'), may hold values from -6 to 6
- resets: int32 [2048], P('seq'), may hold values from 0 to 1, as said below
- out_grad: bfloat16 [16384, 1024], P('seq'), may hold values from -6 to 6
- patch_weight: bfloat16 [8192, 1024], P('seq'), may hold values from -0.0625 to 0.0625
- patch_gain: bfloat16 [1024], P('seq'), may hold values from 0.5 to 1.5
- mixer_in: bfloat16 [1024, 4384], P('seq'), may hold values from -0.1875 to 0.1875
- conv_weight: bfloat16 [4, 2304], P(None, 'seq'), may hold values from -3 to 3
- conv_bias: bfloat16 [2304], P('seq'), may hold values from -3 to 3
- head_params: float32 [3, 32], replicated, may hold values from -10 to 2
- mixer_gain: bfloat16 [2048], P('seq'), may hold values from 0.5 to 1.5
- mixer_out: bfloat16 [2048, 1024], P('seq'), may hold values from -0.125 to 0.125
- unpatch_weight: bfloat16 [1024, 8192], P('seq'), may hold values from -0.1875 to 0.1875
- attn_gain: bfloat16 [1024], P('seq'), may hold values from 0.5 to 1.5
- qkv_weight: bfloat16 [1024, 3072], P('seq'), may hold values from -0.1875 to 0.1875
- attn_out: bfloat16 [1024, 1024], P('seq'), may hold values from -0.375 to 0.375
- ffn_gain: bfloat16 [1024], P('seq'), may hold values from 0.5 to 1.5
- gate_up: bfloat16 [1024, 8192], P('seq'), may hold values from -0.1875 to 0.1875
- down_weight: bfloat16 [4096, 1024], P('seq'), may hold values from -0.09375 to 0.09375
Outputs:
- layer_out: bfloat16 [16384, 1024], P('seq')
- input_grad: bfloat16 [16384, 1024], P('seq')
- grad_patch: float32 [8192, 1024], P('seq')
- grad_patch_gain: float32 [1024], P('seq')
- grad_mixer_in: float32 [1024, 4384], P('seq')
- grad_conv_weight: float32 [4, 2304], P(None, 'seq')
- grad_conv_bias: float32 [2304], P('seq')
- grad_head: float32 [3, 32], replicated
- grad_mixer_gain: float32 [2048], P('seq')
- grad_mixer_out: float32 [2048, 1024], P('seq')
- grad_unpatch: float32 [1024, 8192], P('seq')
- grad_attn_gain: float32 [1024], P('seq')
- grad_qkv: float32 [1024, 3072], P('seq')
- grad_attn_out: float32 [1024, 1024], P('seq')
- grad_ffn_gain: float32 [1024], P('seq')
- grad_gate_up: float32 [1024, 8192], P('seq')
- grad_down: float32 [4096, 1024], P('seq')
The draws below stay inside these ranges and needn't reach their ends.
Inputs may be any that keep to these rules, and one draw needn't show every extreme that they name: resets[0] = 1; one document begins within the first 64 patches and ends within the last 64; shorter documents lie before and after it.
All inputs are finite; a program needn't handle non-finite values.
Results may differ from the reference program's by a relative error of at most 0.035.
Values may be sent and summed in bfloat16 or wider, within the bound.
A program may use at most 640 MiB of HBM per device.

```python
import math
import jax
import jax.numpy as jnp
from jax import lax

D = 1024
PATCH = 8
MHEADS = 32
MHEAD_DIM = 64
DI = 2048
NSTATE = 128
CONV = 4
AHEADS = 16
AHEAD_DIM = 64
FF = 4096
PATCH_DEV = 64
CONV_CH = 2304
PROJ = 4384
PATCHES = 2048
BYTES = 16384


def draw_resets(key, part):
    key = jax.random.fold_in(key, 7)
    first_key, second_key, third_key = jax.random.split(key, 3)
    patch_total = PATCHES
    long_start = jax.random.randint(first_key, (), 1, PATCH_DEV)
    long_end = patch_total - jax.random.randint(second_key, (), 1, PATCH_DEV)
    position = jnp.arange(patch_total)
    scattered = (jax.random.randint(third_key, (patch_total,), 0, 8) == 0).astype(jnp.int32)
    starts = jnp.where((position < long_start) | (position >= long_end), scattered, 0)
    starts = jnp.where((position == 0) | (position == long_start) | (position == long_end), 1, starts)
    return starts.astype(jnp.int32)


def draw_head_params(key, part):
    key = jax.random.fold_in(key, 11)
    keys_all = jax.random.split(key, 5)
    step_bias = jax.random.uniform(keys_all[0], (MHEADS,), jnp.float32, -4.5, -2.0)
    log_rate = jax.random.uniform(keys_all[1], (MHEADS,), jnp.float32, -10.0, 1.0)
    skip_weight = jax.random.uniform(keys_all[4], (MHEADS,), jnp.float32, 0.5, 2.0)
    return jnp.stack([step_bias, log_rate, skip_weight]).astype(jnp.float32)


def block_scale(own_key, dims, cuts, low, top_value):
    def one(axis_at, blocks):
        steps = jax.random.uniform(jax.random.fold_in(jax.random.fold_in(own_key, 6), axis_at), (blocks,), jnp.float32, low / len(cuts), top_value / len(cuts))
        return jnp.repeat(jnp.exp(steps), dims[axis_at] // blocks).reshape((-1,) + (1,) * (len(dims) - axis_at - 1))

    gain = one(*cuts[0])
    for cut in cuts[1:]:
        gain = gain * one(*cut)
    return gain


def normal_values(own_key, shape, width, bound, cuts=(), kind=jnp.bfloat16):
    values = jax.random.normal(own_key, shape, jnp.float32) * width
    if len(cuts) > 0:
        values = block_scale(own_key, shape, cuts, -0.22, 0.18) * values
    return jnp.clip(values, min=-bound, max=bound).astype(kind)


def setup_inputs(seed: int = 0) -> dict:
    keys = jax.random.split(jax.random.key(seed), 19)
    return {
        "byte_acts": normal_values(keys[0], (BYTES, D), 1.0, 6.0, ((0, 32),)),
        "resets": draw_resets(jax.random.fold_in(keys[18], 71), 0),
        "out_grad": normal_values(keys[2], (BYTES, D), 1.0, 6.0, ((0, 32),)),
        "patch_weight": normal_values(keys[3], (PATCH * D, D), (PATCH * D) ** -0.5, 0.0625, ((0, 32),)),
        "patch_gain": jnp.clip(1.0 + 0.1 * jax.random.normal(keys[4], (D,), jnp.float32), 0.5, 1.5).astype(jnp.bfloat16),
        "mixer_in": normal_values(keys[5], (D, PROJ), D ** -0.5, 0.1875, ((0, 32),)),
        "conv_weight": normal_values(keys[6], (CONV, CONV_CH), CONV ** -0.5, 3.0, ((1, 32),)),
        "conv_bias": normal_values(keys[7], (CONV_CH,), 0.5, 3.0, ((0, 32),)),
        "head_params": draw_head_params(jax.random.fold_in(keys[18], 71), 0),
        "mixer_gain": jnp.clip(1.0 + 0.1 * jax.random.normal(keys[9], (DI,), jnp.float32), 0.5, 1.5).astype(jnp.bfloat16),
        "mixer_out": normal_values(keys[10], (DI, D), DI ** -0.5, 0.125, ((0, 32),)),
        "unpatch_weight": normal_values(keys[11], (D, PATCH * D), D ** -0.5, 0.1875, ((0, 32),)),
        "attn_gain": jnp.clip(1.0 + 0.1 * jax.random.normal(keys[12], (D,), jnp.float32), 0.5, 1.5).astype(jnp.bfloat16),
        "qkv_weight": normal_values(keys[13], (D, 3 * D), D ** -0.5, 0.1875, ((0, 32),)),
        "attn_out": normal_values(keys[14], (D, D), (D // 4) ** -0.5, 0.375, ((0, 32),)),
        "ffn_gain": jnp.clip(1.0 + 0.1 * jax.random.normal(keys[15], (D,), jnp.float32), 0.5, 1.5).astype(jnp.bfloat16),
        "gate_up": normal_values(keys[16], (D, 2 * FF), D ** -0.5, 0.1875, ((0, 32),)),
        "down_weight": normal_values(keys[17], (FF, D), FF ** -0.5, 0.09375, ((0, 32),)),
    }


EPS = 1e-05
HIGH = lax.Precision.HIGHEST

@jax.custom_vjp
def low(v):
    return lax.optimization_barrier(v.astype(jnp.bfloat16)).astype(jnp.float32)

@jax.custom_vjp
def low_back(v):
    return v

def low_keep(v):
    return (low(v), None)

def low_pass(kept, grad):
    return (grad,)

def back_keep(v):
    return (v, None)

def back_low(kept, grad):
    return (low(grad),)
low.defvjp(low_keep, low_pass)
low_back.defvjp(back_keep, back_low)

def product(matrix, second):
    return jnp.dot(matrix, second, precision=HIGH)

def rms_scale(values, gain_vec):
    return values * lax.rsqrt(lax.optimization_barrier(jnp.mean(values * values, axis=-1, keepdims=True)) + EPS) * gain_vec

def global_front(patches, patch_weight, patch_gain, mixer_in):
    embedded = low_back(product(patches, patch_weight))
    normed = low(rms_scale(embedded, patch_gain))
    projected = low_back(product(normed, mixer_in))
    gate_z = projected[:, :DI]
    conv_in = low(projected[:, DI:DI + CONV_CH])
    dt_raw = projected[:, DI + CONV_CH:]
    return (embedded, gate_z, conv_in, dt_raw)

def tap_masks(flags_ext, row_count):
    not_reset = 1.0 - flags_ext.astype(jnp.float32)
    validity = [jnp.ones((row_count,), jnp.float32)]
    for offset in range(1, CONV):
        validity.append(validity[-1] * not_reset[CONV - offset:CONV - offset + row_count])
    return validity

def conv_apply(conv_ext, conv_weight, conv_bias, validity, row_count):
    summed = conv_bias + conv_ext[CONV - 1:CONV - 1 + row_count] * conv_weight[0]
    for offset in range(1, CONV):
        summed = summed + validity[offset][:, None] * conv_ext[CONV - 1 - offset:CONV - 1 - offset + row_count] * conv_weight[offset]
    return jax.nn.silu(summed)

def block_parts(conv_out, dt_raw, head_params, starts):
    row_count = conv_out.shape[0]
    values = conv_out[:, :DI].reshape(row_count, MHEADS, MHEAD_DIM)
    key_rows = conv_out[:, DI:DI + NSTATE]
    queries = conv_out[:, DI + NSTATE:]
    step_size = jax.nn.softplus(dt_raw + head_params[0])
    cumlog = jnp.cumsum(-step_size * jnp.exp(head_params[1]), axis=0)
    segment = jnp.cumsum(starts, axis=0, dtype=jnp.int32)
    return (values, key_rows, queries, step_size, cumlog, segment)

def block_state(conv_out, dt_raw, head_params, starts):
    values, key_rows, queries, step_size, cumlog, segment = block_parts(conv_out, dt_raw, head_params, starts)
    same_doc = (segment == segment[-1]).astype(jnp.float32)
    weighting = jnp.exp(cumlog[-1][None, :] - cumlog) * same_doc[:, None] * step_size
    state_out = jnp.einsum('rh,rhp,rn->hpn', weighting, values, key_rows, precision=HIGH)
    decay_total = jnp.exp(cumlog[-1]) * (segment[-1] == 0).astype(jnp.float32)
    return (state_out, decay_total)

def block_output(conv_out, dt_raw, head_params, state_in, starts):
    values, key_rows, queries, step_size, cumlog, segment = block_parts(conv_out, dt_raw, head_params, starts)
    position = jnp.arange(conv_out.shape[0])
    causal = (position[:, None] >= position[None, :]) & (segment[:, None] == segment[None, :])
    log_gaps = jnp.where(causal[:, :, None], cumlog[:, None, :] - cumlog[None, :, :], 0.0)
    decays = jnp.exp(log_gaps) * causal[:, :, None].astype(jnp.float32)
    scores = jnp.dot(queries, key_rows.T, precision=HIGH)
    mixing = scores[:, :, None] * decays * step_size[None, :, :]
    within = jnp.einsum('tsh,shp->thp', mixing, values, precision=HIGH)
    inflow = jnp.exp(cumlog) * (segment == 0).astype(jnp.float32)[:, None]
    carried = jnp.einsum('tn,hpn->thp', queries, state_in, precision=HIGH) * inflow[:, :, None]
    skipped = head_params[2][None, :, None] * values
    return (within + carried + skipped).reshape(conv_out.shape[0], DI)

def global_tail(mixer_y, gate_z, embedded, mixer_gain, mixer_out, unpatch_weight, byte_acts):
    gated_norm = low(rms_scale(mixer_y * jax.nn.silu(gate_z), mixer_gain))
    branch = low_back(product(gated_norm, mixer_out))
    hidden = low(embedded + branch)
    byte_slots = low_back(product(hidden, unpatch_weight))
    return byte_acts + byte_slots.reshape(-1, D)

def local_section(stream, attn_gain, qkv_weight, attn_out, ffn_gain, gate_up, down_weight):
    row_count = stream.shape[0]
    normed = low(rms_scale(stream, attn_gain))
    triple = low(low_back(product(normed, qkv_weight)))
    triple = triple.reshape(row_count // PATCH, PATCH, 3, AHEADS, AHEAD_DIM)
    queries = triple[:, :, 0]
    key_rows = triple[:, :, 1]
    value_rows = triple[:, :, 2]
    scores = low_back(jnp.einsum('bqhd,bkhd->bhqk', queries, key_rows, precision=HIGH) * AHEAD_DIM ** (-0.5))
    position = jnp.arange(PATCH)
    causal = position[:, None] >= position[None, :]
    attn_probs = jax.nn.softmax(jnp.where(causal, scores, -1e+30), axis=-1)
    mixed_heads = low(low_back(jnp.einsum('bhqk,bkhd->bqhd', low(attn_probs), value_rows, precision=HIGH)))
    stream = stream + low_back(product(mixed_heads.reshape(row_count, D), attn_out))
    normed = low(rms_scale(stream, ffn_gain))
    gate_both = low_back(product(normed, gate_up))
    hidden = low(jax.nn.silu(gate_both[:, :FF]) * gate_both[:, FF:])
    return stream + low_back(product(hidden, down_weight))

def layer_forward(byte_acts, weights_all, resets):
    patch_weight, patch_gain, mixer_in, conv_weight, conv_bias, head_params, mixer_gain, mixer_out, unpatch_weight, attn_gain, qkv_weight, attn_out, ffn_gain, gate_up, down_weight = weights_all
    patches = byte_acts.reshape(-1, PATCH * D)
    patch_count = patches.shape[0]
    embedded, gate_z, conv_in, dt_raw = global_front(patches, patch_weight, patch_gain, mixer_in)
    flags_ext = jnp.concatenate([jnp.zeros((CONV - 1,), jnp.int32), resets])
    validity = tap_masks(flags_ext, patch_count)
    conv_ext = jnp.concatenate([jnp.zeros((CONV - 1, CONV_CH), jnp.float32), conv_in])
    conv_out = conv_apply(conv_ext, conv_weight, conv_bias, validity, patch_count)

    def block_step(state_in, pieces):
        conv_rows, dt_rows, flag_rows = pieces
        mixed_rows = block_output(conv_rows, dt_rows, head_params, state_in, flag_rows)
        state_out, decay_total = block_state(conv_rows, dt_rows, head_params, flag_rows)
        return (decay_total[:, None, None] * state_in + state_out, mixed_rows)
    block_count = patch_count // PATCH_DEV
    initial = jnp.zeros((MHEADS, MHEAD_DIM, NSTATE), jnp.float32)
    _, mixer_y = lax.scan(jax.checkpoint(block_step), initial, (conv_out.reshape(block_count, PATCH_DEV, CONV_CH), dt_raw.reshape(block_count, PATCH_DEV, MHEADS), resets.reshape(block_count, PATCH_DEV)))
    stream = global_tail(mixer_y.reshape(patch_count, DI), gate_z, embedded, mixer_gain, mixer_out, unpatch_weight, byte_acts)
    row_count = stream.shape[0]
    block_rows = math.gcd(row_count, 4096)

    def local_block(rows_in):
        return local_section(rows_in, attn_gain, qkv_weight, attn_out, ffn_gain, gate_up, down_weight)
    outputs = lax.map(jax.checkpoint(local_block), stream.reshape(row_count // block_rows, block_rows, D))
    return outputs.reshape(row_count, D)

def reference(byte_acts, resets, out_grad, patch_weight, patch_gain, mixer_in, conv_weight, conv_bias, head_params, mixer_gain, mixer_out, unpatch_weight, attn_gain, qkv_weight, attn_out, ffn_gain, gate_up, down_weight):
    weights_all = (patch_weight, patch_gain, mixer_in, conv_weight, conv_bias, head_params, mixer_gain, mixer_out, unpatch_weight, attn_gain, qkv_weight, attn_out, ffn_gain, gate_up, down_weight)
    float_args = tuple((piece.astype(jnp.float32) for piece in weights_all))

    def forward(acts_in, *params_in):
        return layer_forward(acts_in, params_in, resets)
    result, pullback = jax.vjp(forward, byte_acts.astype(jnp.float32), *float_args)
    gradients = pullback(out_grad.astype(jnp.float32))
    return (result.astype(jnp.bfloat16), gradients[0].astype(jnp.bfloat16), gradients[1], gradients[2], gradients[3], gradients[4], gradients[5], gradients[6], gradients[7], gradients[8], gradients[9], gradients[10], gradients[11], gradients[12], gradients[13], gradients[14], gradients[15])
```

```python
import functools

import jax
import jax.numpy as jnp
import numpy as np
from jax import lax
from jax.experimental import pallas as pl
from jax.experimental.pallas import tpu as pltpu
from jax.sharding import PartitionSpec as P

D = 1024
PATCH = 8
MHEADS = 32
MHEAD_DIM = 64
DI = 2048
NSTATE = 128
CONV = 4
AHEADS = 16
AHEAD_DIM = 64
FF = 4096
CONV_CH = 2304

EPS = 1e-05
HIGH = lax.Precision.HIGHEST
BF = jnp.bfloat16
F32 = jnp.float32


class Ring:
    def __init__(self, n):
        self.n = n
        self.depth = n // 8
        coords = [(i // 8, (i // 4) % 2, (i // 2) % 2, i % 2) for i in range(n)]

        def index(z, y, x, c):
            return ((z * 2 + y) * 2 + x) * 2 + c

        def flip(z, y, x, c, along_x):
            return index(z, y, 1 - x, c) if along_x else index(z, 1 - y, x, c)

        self.core = [(index(*p), index(*p) ^ 1) for p in coords]
        self.first = [(index(*p), flip(*p, p[3] == 0)) for p in coords]
        self.second = [(index(*p), flip(*p, p[3] == 1)) for p in coords]
        self.shift = [
            [(index(*p), index((p[0] + hop) % self.depth, *p[1:])) for p in coords]
            for hop in range(self.depth)
        ]
        table = np.zeros((n, n), np.int32)
        for me, (z, y, x, c) in enumerate(coords):
            place = 0
            for rc in range(2):
                owner = c ^ rc
                for r2 in range(2):
                    for r1 in range(2):
                        rx, ry = (r1, r2) if owner == 0 else (r2, r1)
                        for rz in range(self.depth):
                            table[me, place] = index((z + rz) % self.depth, y ^ ry, x ^ rx, owner)
                            place += 1
        self.table = table

    def order(self):
        return jnp.asarray(self.table)[lax.axis_index("seq")]


def swap(block, route):
    return lax.ppermute(block, "seq", route)


def after(value, earlier):
    return lax.optimization_barrier((value, earlier))[0]


def gather_weights(ring, shards):
    depth, count = ring.depth, len(shards)
    lines, firsts, pieces = [], [], []

    def along_z(place):
        shard = shards[place]
        if place >= 1:
            shard = after(shard, lines[place - 1])
        if place >= 2:
            shard = after(shard, firsts[place - 2])
        hops = [lax.ppermute(shard, "seq", ring.shift[hop]) for hop in range(1, depth)]
        lines.append([shard] + hops[::-1])

    along_z(0)
    for place in range(count):
        near = jnp.concatenate(lines[place], axis=0)
        if place >= 1:
            near = after(near, firsts[place - 1])
        across = swap(near, ring.first)
        firsts.append(across)
        if place + 1 < count:
            along_z(place + 1)
        mine = [near, across, swap(near, ring.second), swap(across, ring.second)]
        pieces.append(mine + [swap(piece, ring.core) for piece in mine])
    return pieces


def assemble_kernel(rows, per_piece, total, slots, table_ref, *refs):
    pieces, out_ref, held, in_sems, out_sems = refs[:-4], refs[-4], refs[-3], refs[-2], refs[-1]

    def load(place):
        source = pieces[place // per_piece].at[pl.ds((place % per_piece) * rows, rows)]
        slot = place % slots
        return pltpu.make_async_copy(source, held.at[slot], in_sems.at[slot])

    def store(place):
        start = pl.multiple_of(table_ref[place] * rows, rows)
        slot = place % slots
        return pltpu.make_async_copy(
            held.at[slot], out_ref.at[pl.ds(start, rows)], out_sems.at[slot]
        )

    lead = slots // 2
    for place in range(total + lead):
        if place < total:
            if place >= slots:
                store(place - slots).wait()
            load(place).start()
        if place >= lead:
            load(place - lead).wait()
            store(place - lead).start()
    for place in range(max(0, total - slots), total):
        store(place).wait()


def assemble(ring, pieces):
    n = ring.n
    per_piece = n // len(pieces)
    rows = pieces[0].shape[0] // per_piece
    columns = pieces[0].shape[1]
    if rows % 16:
        whole = jnp.concatenate(pieces, axis=0).reshape(n, rows, columns)
        back = jnp.argsort(ring.order())
        return jnp.take(whole, back, axis=0).reshape(n * rows, columns)
    slots = min(n, 16)
    return pl.pallas_call(
        functools.partial(assemble_kernel, rows, per_piece, n, slots),
        out_shape=jax.ShapeDtypeStruct((n * rows, columns), pieces[0].dtype),
        in_specs=[pl.BlockSpec(memory_space=pltpu.SMEM)]
        + [pl.BlockSpec(memory_space=pl.ANY)] * len(pieces),
        out_specs=pl.BlockSpec(memory_space=pl.ANY),
        scratch_shapes=[
            pltpu.VMEM((slots, rows, columns), pieces[0].dtype),
            pltpu.SemaphoreType.DMA((slots,)),
            pltpu.SemaphoreType.DMA((slots,)),
        ],
        compiler_params=pltpu.CompilerParams(vmem_limit_bytes=24 * 2**20),
        cost_estimate=pl.CostEstimate(
            flops=0, bytes_accessed=4 * n * rows * columns, transcendentals=0
        ),
    )(ring.order(), *pieces)


def gather_small(ring, vector):
    pieces = gather_weights(ring, [vector[None]])[0]
    return jnp.take(jnp.concatenate(pieces, axis=0), jnp.argsort(ring.order()), axis=0)


def scatter_sum(ring, part, wire):
    n, depth = ring.n, ring.depth
    quarter, eighth = n // 4, n // 8

    def send(block, route):
        return swap(block.astype(wire), route).astype(F32)

    one = send(part(n // 2, n), ring.core)
    two = send(part(quarter, n // 2) + one[quarter:], ring.second)
    three = send(part(eighth, quarter) + one[eighth:quarter] + two[eighth:], ring.first)
    total = (part(0, eighth) + one[:eighth] + two[:eighth] + three).astype(wire)
    held = total[0].astype(F32)
    for hop in range(1, depth):
        held = held + lax.ppermute(total[hop], "seq", ring.shift[hop]).astype(F32)
    return held


def blocks_kernel(count, table_ref, in_ref, out_ref):
    width = in_ref.shape[1] // count

    @pl.loop(0, count)
    def _(place):
        start = pl.multiple_of(table_ref[place] * width, width)
        out_ref[:, pl.ds(pl.multiple_of(place * width, width), width)] = in_ref[:, pl.ds(start, width)]


def column_blocks(ring, left):
    rows, width = left.shape
    n = ring.n
    block = width // n
    if block % 128 == 0:
        return pl.pallas_call(
            functools.partial(blocks_kernel, n),
            out_shape=jax.ShapeDtypeStruct(left.shape, left.dtype),
            in_specs=[
                pl.BlockSpec(memory_space=pltpu.SMEM),
                pl.BlockSpec(memory_space=pltpu.VMEM),
            ],
            out_specs=pl.BlockSpec(memory_space=pltpu.VMEM),
            compiler_params=pltpu.CompilerParams(vmem_limit_bytes=32 * 2**20),
        )(ring.order(), left)
    if rows * width >= 2**18:
        place = jnp.arange(width)
        source = jnp.repeat(ring.order() * block, block) + place % block
        picked = (place[:, None] == source[None, :]).astype(left.dtype)
        return dot(left, picked).astype(left.dtype)
    blocks = left.reshape(rows, n, block)
    return jnp.take(blocks, ring.order(), axis=1).reshape(rows, width)


def weight_grad(ring, left, right):
    width = left.shape[1]
    block = width // ring.n
    ordered = column_blocks(ring, left)

    def part(start, stop):
        product = lax.dot_general(
            ordered[:, start * block : stop * block],
            right,
            (((0,), (0,)), ((), ())),
            preferred_element_type=F32,
        )
        return product.reshape(stop - start, block, right.shape[1])

    return scatter_sum(ring, part, BF)


def dot(left, right):
    return jnp.dot(left, right, preferred_element_type=F32)


def dot_t(left, right):
    return lax.dot_general(left, right, (((1,), (1,)), ((), ())), preferred_element_type=F32)


def rms_scale(values, gain):
    return values * lax.rsqrt(jnp.mean(values * values, axis=-1, keepdims=True) + EPS) * gain


def rms_back(values, gain, grad):
    r = lax.rsqrt(jnp.mean(values * values, axis=-1, keepdims=True) + EPS)
    scaled = gain * grad
    inner = jnp.mean(values * scaled, axis=-1, keepdims=True)
    return r * scaled - values * (r * r * r) * inner, jnp.sum(values * r * grad, axis=0)


def silu(v):
    return v * jax.nn.sigmoid(v)


def silu_slope(v):
    s = jax.nn.sigmoid(v)
    return s * (1.0 + v * (1.0 - s))


def tap_masks(flags_ext, row_count):
    not_reset = 1.0 - flags_ext.astype(F32)
    validity = [jnp.ones((row_count,), F32)]
    for offset in range(1, CONV):
        validity.append(validity[-1] * not_reset[CONV - offset : CONV - offset + row_count])
    return validity


def conv_apply(conv_ext, conv_weight, conv_bias, validity, row_count):
    summed = conv_bias + conv_ext[CONV - 1 : CONV - 1 + row_count] * conv_weight[0]
    for offset in range(1, CONV):
        summed = (
            summed
            + validity[offset][:, None]
            * conv_ext[CONV - 1 - offset : CONV - 1 - offset + row_count]
            * conv_weight[offset]
        )
    return jax.nn.silu(summed)


def block_parts(conv_out, dt_raw, head_params, starts):
    row_count = conv_out.shape[0]
    values = conv_out[:, :DI].reshape(row_count, MHEADS, MHEAD_DIM)
    key_rows = conv_out[:, DI : DI + NSTATE]
    queries = conv_out[:, DI + NSTATE :]
    step_size = jax.nn.softplus(dt_raw + head_params[0])
    cumlog = jnp.cumsum(-step_size * jnp.exp(head_params[1]), axis=0)
    segment = jnp.cumsum(starts, axis=0, dtype=jnp.int32)
    return (values, key_rows, queries, step_size, cumlog, segment)


def block_state(conv_out, dt_raw, head_params, starts):
    values, key_rows, queries, step_size, cumlog, segment = block_parts(
        conv_out, dt_raw, head_params, starts
    )
    same_doc = (segment == segment[-1]).astype(F32)
    weighting = jnp.exp(cumlog[-1][None, :] - cumlog) * same_doc[:, None] * step_size
    state_out = jnp.einsum("rh,rhp,rn->hpn", weighting, values, key_rows, precision=HIGH)
    decay_total = jnp.exp(cumlog[-1]) * (segment[-1] == 0).astype(F32)
    return (state_out, decay_total)


def block_output(conv_out, dt_raw, head_params, state_in, starts):
    values, key_rows, queries, step_size, cumlog, segment = block_parts(
        conv_out, dt_raw, head_params, starts
    )
    position = jnp.arange(conv_out.shape[0])
    causal = (position[:, None] >= position[None, :]) & (segment[:, None] == segment[None, :])
    log_gaps = jnp.where(causal[:, :, None], cumlog[:, None, :] - cumlog[None, :, :], 0.0)
    decays = jnp.exp(log_gaps) * causal[:, :, None].astype(F32)
    scores = jnp.dot(queries, key_rows.T, precision=HIGH)
    mixing = scores[:, :, None] * decays * step_size[None, :, :]
    within = jnp.einsum("tsh,shp->thp", mixing, values, precision=HIGH)
    inflow = jnp.exp(cumlog) * (segment == 0).astype(F32)[:, None]
    carried = jnp.einsum("tn,hpn->thp", queries, state_in, precision=HIGH) * inflow[:, :, None]
    skipped = head_params[2][None, :, None] * values
    return (within + carried + skipped).reshape(conv_out.shape[0], DI)


def state_links(ring, logs, flags):
    n = ring.n
    place = jnp.arange(n)
    between = (place[None, None, :] > place[None, :, None]) & (
        place[None, None, :] < place[:, None, None]
    )
    gap = jnp.sum(jnp.where(between, logs[None, None, :], 0.0), axis=-1)
    cut = jnp.sum(jnp.where(between, flags[None, None, :], 0.0), axis=-1)
    later = place[:, None] > place[None, :]
    return jnp.exp(gap) * (later & (cut == 0)).astype(F32)


def pass_states(ring, states, links):
    n = ring.n
    rows = states.reshape(n, -1, NSTATE).astype(BF)
    spread = lax.all_to_all(rows, "seq", 0, 0, tiled=True)
    summed = jnp.einsum("de,erk->drk", links, spread.astype(F32), precision=HIGH)
    returned = lax.all_to_all(summed.astype(BF), "seq", 0, 0, tiled=True)
    return returned.astype(F32).reshape(MHEADS, MHEAD_DIM, NSTATE)


def attention(queries, key_rows, value_rows):
    scores = jnp.einsum(
        "bqhd,bkhd->bhqk", queries, key_rows, preferred_element_type=F32
    ) * AHEAD_DIM ** (-0.5)
    position = jnp.arange(PATCH)
    causal = position[:, None] >= position[None, :]
    probs = jax.nn.softmax(jnp.where(causal, scores, -1e30), axis=-1)
    mixed = jnp.einsum("bhqk,bkhd->bqhd", probs.astype(BF), value_rows, preferred_element_type=F32)
    return probs, mixed.astype(BF)


def attention_back(queries, key_rows, value_rows, probs, grad):
    d_probs = jnp.einsum("bqhd,bkhd->bhqk", grad, value_rows, preferred_element_type=F32)
    d_values = jnp.einsum("bhqk,bqhd->bkhd", probs.astype(BF), grad, preferred_element_type=F32)
    inner = jnp.sum(probs * d_probs, axis=-1, keepdims=True)
    d_scores = (probs * (d_probs - inner)).astype(BF)
    scale = AHEAD_DIM ** (-0.5)
    d_queries = scale * jnp.einsum("bhqk,bkhd->bqhd", d_scores, key_rows, preferred_element_type=F32)
    d_keys = scale * jnp.einsum("bhqk,bqhd->bkhd", d_scores, queries, preferred_element_type=F32)
    return d_queries, d_keys, d_values


def local(
    byte_acts,
    resets,
    out_grad,
    patch_weight,
    patch_gain,
    mixer_in,
    conv_weight,
    conv_bias,
    head_params,
    mixer_gain,
    mixer_out,
    unpatch_weight,
    attn_gain,
    qkv_weight,
    attn_out,
    ffn_gain,
    gate_up,
    down_weight,
):
    n = lax.axis_size("seq")
    me = lax.axis_index("seq")
    ring = Ring(n)

    def passed_along(block, distance):
        route = [(i - distance, i) for i in range(n) if 0 <= i - distance < n]
        return lax.ppermute(block, "seq", route)

    small = [patch_gain, conv_weight.reshape(-1), conv_bias, mixer_gain, attn_gain, ffn_gain]
    sizes = [piece.shape[0] for piece in small]
    cuts = list(np.cumsum(sizes))
    small_all = gather_small(ring, jnp.concatenate(small)).astype(F32)
    parts = jnp.split(small_all, cuts[:-1], axis=1)
    patch_gain_w = parts[0].reshape(-1)
    conv_weight_w = parts[1].reshape(n, CONV, -1).transpose(1, 0, 2).reshape(CONV, CONV_CH)
    conv_bias_w, mixer_gain_w, attn_gain_w, ffn_gain_w = [p.reshape(-1) for p in parts[2:]]

    shards = [patch_weight, mixer_in, mixer_out, unpatch_weight, qkv_weight, attn_out, gate_up, down_weight]
    wholes = [assemble(ring, pieces) for pieces in gather_weights(ring, shards)]
    patch_w, mixer_in_w, mixer_out_w, unpatch_w, qkv_w, attn_out_w, gate_up_w, down_w = wholes

    byte_wide = byte_acts.astype(F32)
    patches = byte_acts.reshape(-1, PATCH * D)
    patch_rows = patches.shape[0]
    embedded = dot(patches, patch_w)
    normed = rms_scale(embedded, patch_gain_w).astype(BF)
    projected = dot(normed, mixer_in_w)
    gate_z = projected[:, :DI]
    conv_in = projected[:, DI : DI + CONV_CH].astype(BF).astype(F32)
    dt_raw = projected[:, DI + CONV_CH :]

    logs = jnp.sum(-jax.nn.softplus(dt_raw + head_params[0]) * jnp.exp(head_params[1]), axis=0)
    flag = jnp.max(resets).astype(F32)
    links_all = gather_small(ring, jnp.concatenate([logs, flag[None]]))
    head = me * MHEADS // n
    links = state_links(
        ring, lax.dynamic_index_in_dim(links_all[:, :MHEADS], head, 1, False), links_all[:, MHEADS]
    )

    not_reset = 1.0 - resets.astype(F32)
    keep_tail = jnp.concatenate(
        [jnp.cumprod(not_reset[patch_rows - CONV + 2 :][::-1])[::-1], jnp.ones((1,), F32)]
    )
    tail_sent = (conv_in[patch_rows - CONV + 1 :] * keep_tail[:, None]).astype(BF)
    halo_rows = passed_along(tail_sent, 1)
    flags_ext = jnp.concatenate([jnp.zeros((CONV - 1,), jnp.int32), resets])
    validity = tap_masks(flags_ext, patch_rows)
    conv_ext = jnp.concatenate([halo_rows.astype(F32), conv_in])
    conv_out, conv_back = jax.vjp(
        functools.partial(conv_apply, validity=validity, row_count=patch_rows),
        conv_ext,
        conv_weight_w,
        conv_bias_w,
    )
    state_parts, state_back = jax.vjp(
        functools.partial(block_state, starts=resets), conv_out, dt_raw, head_params
    )
    local_state, decay_total = state_parts
    state_in = pass_states(ring, local_state, links)
    mixer_y, output_back = jax.vjp(
        functools.partial(block_output, starts=resets), conv_out, dt_raw, head_params, state_in
    )
    gate_act = silu(gate_z)
    gated = mixer_y * gate_act
    gated_norm = rms_scale(gated, mixer_gain_w).astype(BF)
    branch = dot(gated_norm, mixer_out_w)
    hidden = (embedded + branch).astype(BF)
    stream0 = byte_wide + dot(hidden, unpatch_w).reshape(-1, D)

    rows = stream0.shape[0]
    normed0 = rms_scale(stream0, attn_gain_w).astype(BF)
    triple = dot(normed0, qkv_w).astype(BF)
    triple_parts = triple.reshape(rows // PATCH, PATCH, 3, AHEADS, AHEAD_DIM)
    qkv = [triple_parts[:, :, i] for i in range(3)]
    probs, mixed = attention(*qkv)
    mixed = mixed.reshape(rows, D)
    stream1 = stream0 + dot(mixed, attn_out_w)
    normed1 = rms_scale(stream1, ffn_gain_w).astype(BF)
    gate_both = dot(normed1, gate_up_w)
    gate, up = gate_both[:, :FF], gate_both[:, FF:]
    act = silu(gate)
    hid = (act * up).astype(BF)
    layer_out = (stream1 + dot(hid, down_w)).astype(BF)

    d_out = out_grad.astype(F32)
    g_down = weight_grad(ring, hid, out_grad)
    d_hid = dot_t(out_grad, down_w)
    d_both = jnp.concatenate([d_hid * up * silu_slope(gate), d_hid * act], axis=1).astype(BF)
    g_gate_up = weight_grad(ring, normed1, d_both)
    d_stream1, g_ffn_gain = rms_back(stream1, ffn_gain_w, dot_t(d_both, gate_up_w))
    d_stream1 = d_out + d_stream1
    d_stream1_low = d_stream1.astype(BF)
    g_attn_out = weight_grad(ring, mixed, d_stream1_low)
    d_mixed = dot_t(d_stream1_low, attn_out_w).astype(BF)
    d_qkv = attention_back(*qkv, probs, d_mixed.reshape(rows // PATCH, PATCH, AHEADS, AHEAD_DIM))
    d_triple = jnp.stack(d_qkv, axis=2).astype(BF).reshape(rows, 3 * D)
    g_qkv = weight_grad(ring, normed0, d_triple)
    d_stream0, g_attn_gain = rms_back(stream0, attn_gain_w, dot_t(d_triple, qkv_w))
    d_stream0 = d_stream1 + d_stream0

    d_slots = d_stream0.astype(BF).reshape(patch_rows, PATCH * D)
    g_unpatch = weight_grad(ring, hidden, d_slots)
    d_hidden = dot_t(d_slots, unpatch_w)
    d_branch = d_hidden.astype(BF)
    g_mixer_out = weight_grad(ring, gated_norm, d_branch)
    d_gated, g_mixer_gain = rms_back(gated, mixer_gain_w, dot_t(d_branch, mixer_out_w))
    d_gate_z = d_gated * mixer_y * silu_slope(gate_z)
    output_grads = output_back(d_gated * gate_act)
    state_grad = pass_states(ring, output_grads[3], links.T)
    decay_grad = jnp.sum(state_grad * state_in, axis=(1, 2))
    state_cot = state_back((state_grad, decay_grad))
    conv_cot = conv_back(output_grads[0] + state_cot[0])
    returned = passed_along(conv_cot[0][: CONV - 1], -1)
    d_conv_in = conv_cot[0][CONV - 1 :] + jnp.concatenate(
        [jnp.zeros((patch_rows - CONV + 1, CONV_CH), F32), returned * keep_tail[:, None]]
    )
    d_dt = output_grads[1] + state_cot[1]
    d_projected = jnp.concatenate([d_gate_z, d_conv_in, d_dt], axis=1).astype(BF)
    g_mixer_in = weight_grad(ring, normed, d_projected)
    d_embedded, g_patch_gain = rms_back(embedded, patch_gain_w, dot_t(d_projected, mixer_in_w))
    d_embedded = (d_hidden + d_embedded).astype(BF)
    g_patch = weight_grad(ring, patches, d_embedded)
    input_grad = (d_stream0 + dot_t(d_embedded, patch_w).reshape(-1, D)).astype(BF)

    g_conv_weight = conv_cot[1].reshape(CONV, n, -1).transpose(1, 0, 2).reshape(n, -1)
    g_head = jnp.broadcast_to((output_grads[2] + state_cot[2]).reshape(1, -1), (n, 3 * MHEADS))
    g_small = [g_patch_gain, g_conv_weight, conv_cot[2], g_mixer_gain, g_attn_gain, g_ffn_gain, g_head]
    g_small = jnp.concatenate([piece.reshape(n, -1) for piece in g_small], axis=1)
    terms = jnp.take(g_small, ring.order(), axis=0)
    g_small = scatter_sum(ring, lambda start, stop: terms[start:stop], F32)
    s = jnp.split(g_small, cuts)
    return (
        layer_out,
        input_grad,
        g_patch,
        s[0],
        g_mixer_in,
        s[1].reshape(CONV, -1),
        s[2],
        s[6].reshape(3, MHEADS),
        s[3],
        g_mixer_out,
        g_unpatch,
        s[4],
        g_qkv,
        g_attn_out,
        s[5],
        g_gate_up,
        g_down,
    )


def solution(mesh):
    rows, vector = P("seq", None), P("seq")
    placed = (
        rows, vector, rows, rows, vector, rows, P(None, "seq"), vector, P(),
        vector, rows, rows, vector, rows, rows, vector, rows, rows,
    )
    returned = (
        rows, rows, rows, vector, rows, P(None, "seq"), vector, P(), vector,
        rows, rows, vector, rows, rows, vector, rows, rows,
    )
    return jax.shard_map(
        local, mesh=mesh, in_specs=placed, out_specs=returned, check_vma=False
    )
```

```python
import functools

import jax
import jax.numpy as jnp
import numpy as np
from jax import lax
from jax.experimental import pallas as pl
from jax.experimental.pallas import tpu as pltpu
from jax.sharding import PartitionSpec as P

D = 1024
PATCH = 8
MHEADS = 32
MHEAD_DIM = 64
DI = 2048
NSTATE = 128
CONV = 4
AHEADS = 16
AHEAD_DIM = 64
FF = 4096
CONV_CH = 2304

EPS = 1e-05
HIGH = lax.Precision.HIGHEST
BF = jnp.bfloat16
F32 = jnp.float32


class Ring:
    def __init__(self, n):
        self.n = n
        self.depth = n // 8
        coords = [(i // 8, (i // 4) % 2, (i // 2) % 2, i % 2) for i in range(n)]

        def index(z, y, x, c):
            return ((z * 2 + y) * 2 + x) * 2 + c

        def flip(z, y, x, c, along_x):
            return index(z, y, 1 - x, c) if along_x else index(z, 1 - y, x, c)

        self.core = [(index(*p), index(*p) ^ 1) for p in coords]
        self.first = [(index(*p), flip(*p, p[3] == 0)) for p in coords]
        self.second = [(index(*p), flip(*p, p[3] == 1)) for p in coords]
        self.bits = [1 << b for b in range(self.depth.bit_length() - 1)]
        self.along = {
            bit: [(index(*p), index(p[0] ^ bit, *p[1:])) for p in coords] for bit in self.bits
        }
        table = np.zeros((n, n), np.int32)
        for me, (z, y, x, c) in enumerate(coords):
            place = 0
            for rc in range(2):
                owner = c ^ rc
                for r2 in range(2):
                    for r1 in range(2):
                        rx, ry = (r1, r2) if owner == 0 else (r2, r1)
                        for rz in range(self.depth):
                            table[me, place] = index(z ^ rz, y ^ ry, x ^ rx, owner)
                            place += 1
        self.table = table

    def order(self):
        return jnp.asarray(self.table)[lax.axis_index("seq")]


def swap(block, route):
    return lax.ppermute(block, "seq", route)


def joined(pieces):
    return jnp.concatenate(pieces, axis=0) if len(pieces) > 1 else pieces[0]


def gather_near(ring, pieces, bits):
    for bit in bits:
        block = joined(pieces)
        pieces = [block, swap(block, ring.along[bit])]
    return pieces


def gather_near_low(ring, pieces):
    return gather_near(ring, pieces, ring.bits[: len(ring.bits) // 2])


def gather_near_high(ring, pieces):
    return gather_near(ring, pieces, ring.bits[len(ring.bits) // 2 :])


def gather_first(ring, pieces):
    block = joined(pieces)
    return [block, swap(block, ring.first)]


def gather_second(ring, pieces):
    block = joined(pieces)
    return [block, swap(block, ring.second)]


def gather_core(ring, pieces):
    return pieces + [swap(piece, ring.core) for piece in pieces]


GATHER = [gather_near_low, gather_near_high, gather_first, gather_second, gather_core]


def flat_kernel(*refs):
    out, first = refs[-1], 0
    for ref in refs[:-1]:
        rows = ref.shape[0]
        for column in range(0, ref.shape[1], D):
            out[pl.ds(first, rows)] = ref[:, pl.ds(column, D)]
            first += rows


def flat_rows(shards):
    total = sum(shard.shape[0] * shard.shape[1] // D for shard in shards)
    return pl.pallas_call(
        flat_kernel,
        out_shape=jax.ShapeDtypeStruct((total, D), BF),
        in_specs=[pl.BlockSpec(memory_space=pltpu.VMEM)] * len(shards),
        out_specs=pl.BlockSpec(memory_space=pltpu.VMEM),
    )(*shards)


def unpack_kernel(n, slots, shapes, flat_ref, *refs):
    outs, (held, in_sems, out_sems) = refs[:-3], refs[-3:]
    total = held.shape[1]

    def load(place):
        source = flat_ref.at[pl.ds(pl.multiple_of(place * total, 16), total)]
        return pltpu.make_async_copy(source, held.at[place % slots], in_sems.at[place % slots])

    def stores(place):
        offset, copies = 0, []
        for out, (rows, columns) in zip(outs, shapes):
            start = pl.multiple_of(place * rows, 16)
            for first in range(0, columns, D):
                source = held.at[place % slots, pl.ds(offset, rows)]
                target = out.at[pl.ds(start, rows), pl.ds(first, D)]
                sem = out_sems.at[place % slots, len(copies)]
                copies.append(pltpu.make_async_copy(source, target, sem))
                offset += rows
        return copies

    lead = slots // 2

    @pl.loop(0, n + lead)
    def _(time):
        @pl.when(time < n)
        def _():
            @pl.when(time >= slots)
            def _():
                for copy in stores(time - slots):
                    copy.wait()

            load(time).start()

        @pl.when(time >= lead)
        def _():
            load(time - lead).wait()
            for copy in stores(time - lead):
                copy.start()

    @pl.loop(n - slots, n)
    def _(place):
        for copy in stores(place):
            copy.wait()


def gather_flat(n, shards):
    if any(shard.shape[0] % 16 for shard in shards):
        return lambda: [lax.all_gather(shard, "seq", axis=0, tiled=True) for shard in shards]
    shapes = [shard.shape for shard in shards]
    flat = flat_rows(shards)
    total, slots = flat.shape[0], 8
    blocks = sum(columns // D for _, columns in shapes)
    flat = lax.all_gather(flat, "seq", axis=0, tiled=True)

    def unpack():
        return pl.pallas_call(
            functools.partial(unpack_kernel, n, slots, shapes),
            out_shape=[jax.ShapeDtypeStruct((n * rows, columns), BF) for rows, columns in shapes],
            in_specs=[pl.BlockSpec(memory_space=pltpu.HBM)],
            out_specs=[pl.BlockSpec(memory_space=pltpu.HBM)] * len(shapes),
            scratch_shapes=[
                pltpu.VMEM((slots, total, D), BF),
                pltpu.SemaphoreType.DMA((slots,)),
                pltpu.SemaphoreType.DMA((slots, blocks)),
            ],
            compiler_params=pltpu.CompilerParams(vmem_limit_bytes=24 * 2**20),
            cost_estimate=pl.CostEstimate(
                flops=0, bytes_accessed=4 * n * total * D, transcendentals=0
            ),
        )(flat)

    return unpack


def gather_rows(ring, shard):
    pieces = [shard]
    for phase in GATHER:
        pieces = phase(ring, pieces)
    return pieces


def gather_small(ring, vector):
    pieces = gather_rows(ring, vector[None])
    return jnp.take(jnp.concatenate(pieces, axis=0), jnp.argsort(ring.order()), axis=0)


class Live:
    def fence(self):
        vars(self).update(lax.optimization_barrier(dict(vars(self))))


def summed_grad(left, right):
    product = lax.dot_general(left, right, (((0,), (0,)), ((), ())), preferred_element_type=F32)
    summed = lax.psum_scatter(product.astype(BF), "seq", scatter_dimension=0, tiled=True)
    return summed.astype(F32)


def flat_grad_kernel(hid_ref, grad_ref, normed_ref, both_ref, out_ref):
    devices, block = out_ref.shape[:2]
    parts = block // SUM_ROWS

    def product(left, right):
        return lax.dot_general(
            left, right, (((0,), (0,)), ((), ())), preferred_element_type=F32
        ).astype(BF)

    @pl.when(pl.program_id(0) < 4)
    def _():
        few = devices // parts
        for part in range(parts):
            cut = pl.ds(part * few * block, few * block)
            found = product(hid_ref[:, cut], grad_ref[...])
            out_ref[pl.ds(part * few, few)] = found.reshape(few, block, D)

    @pl.when(pl.program_id(0) >= 4)
    def _():
        for part in range(parts):
            found = product(normed_ref[...], both_ref[:, pl.ds(part * D, D)])
            cut = pl.ds(part * SUM_ROWS, SUM_ROWS)
            out_ref[:, cut] = found.reshape(devices, SUM_ROWS, D)


def flat_grads(n, hid, out_grad, normed, both):
    rows, block, devices = hid.shape[0], hid.shape[1] // n, n // 4

    def late(step):
        return jnp.maximum(step - 4, 0)

    return pl.pallas_call(
        flat_grad_kernel,
        grid=(12,),
        out_shape=jax.ShapeDtypeStruct((n, 3 * block, D), BF),
        in_specs=[
            pl.BlockSpec((rows, devices * block), lambda i: (0, jnp.minimum(i, 3))),
            pl.BlockSpec((rows, D), lambda i: (0, 0)),
            pl.BlockSpec((rows, devices * SUM_ROWS), lambda i: (0, late(i) % 4)),
            pl.BlockSpec((rows, FF), lambda i: (0, late(i) // 4)),
        ],
        out_specs=pl.BlockSpec(
            (devices, block, D), lambda i: (i % 4, jnp.minimum(i // 4, 1) + late(i) // 4, 0)
        ),
        compiler_params=pltpu.CompilerParams(vmem_limit_bytes=32 * 2**20),
        cost_estimate=pl.CostEstimate(
            flops=6 * rows * FF * D, bytes_accessed=2**25, transcendentals=0
        ),
    )(hid, out_grad, normed, both)


def dot(left, right):
    return jnp.dot(left, right, preferred_element_type=F32)


def dot_t(left, right):
    return lax.dot_general(left, right, (((1,), (1,)), ((), ())), preferred_element_type=F32)


def rms_scale(values, gain):
    return values * lax.rsqrt(jnp.mean(values * values, axis=-1, keepdims=True) + EPS) * gain


def rms_back(values, gain, grad):
    r = lax.rsqrt(jnp.mean(values * values, axis=-1, keepdims=True) + EPS)
    scaled = gain * grad
    inner = jnp.mean(values * scaled, axis=-1, keepdims=True)
    return r * scaled - values * (r * r * r) * inner, jnp.sum(values * r * grad, axis=0)


def silu(v):
    return v * jax.nn.sigmoid(v)


def silu_slope(v):
    s = jax.nn.sigmoid(v)
    return s * (1.0 + v * (1.0 - s))


def tap_masks(flags_ext, row_count):
    not_reset = 1.0 - flags_ext.astype(F32)
    validity = [jnp.ones((row_count,), F32)]
    for offset in range(1, CONV):
        validity.append(validity[-1] * not_reset[CONV - offset : CONV - offset + row_count])
    return validity


def conv_apply(conv_ext, conv_weight, conv_bias, validity, row_count):
    summed = conv_bias + conv_ext[CONV - 1 : CONV - 1 + row_count] * conv_weight[0]
    for offset in range(1, CONV):
        summed = (
            summed
            + validity[offset][:, None]
            * conv_ext[CONV - 1 - offset : CONV - 1 - offset + row_count]
            * conv_weight[offset]
        )
    return jax.nn.silu(summed)


def block_parts(conv_out, dt_raw, head_params, starts):
    row_count = conv_out.shape[0]
    values = conv_out[:, :DI].reshape(row_count, MHEADS, MHEAD_DIM)
    key_rows = conv_out[:, DI : DI + NSTATE]
    queries = conv_out[:, DI + NSTATE :]
    step_size = jax.nn.softplus(dt_raw + head_params[0])
    cumlog = jnp.cumsum(-step_size * jnp.exp(head_params[1]), axis=0)
    segment = jnp.cumsum(starts, axis=0, dtype=jnp.int32)
    return (values, key_rows, queries, step_size, cumlog, segment)


def block_state(conv_out, dt_raw, head_params, starts):
    values, key_rows, queries, step_size, cumlog, segment = block_parts(
        conv_out, dt_raw, head_params, starts
    )
    same_doc = (segment == segment[-1]).astype(F32)
    weighting = jnp.exp(cumlog[-1][None, :] - cumlog) * same_doc[:, None] * step_size
    state_out = jnp.einsum("rh,rhp,rn->hpn", weighting, values, key_rows, precision=HIGH)
    decay_total = jnp.exp(cumlog[-1]) * (segment[-1] == 0).astype(F32)
    return (state_out, decay_total)


def block_output(conv_out, dt_raw, head_params, state_in, starts):
    values, key_rows, queries, step_size, cumlog, segment = block_parts(
        conv_out, dt_raw, head_params, starts
    )
    position = jnp.arange(conv_out.shape[0])
    causal = (position[:, None] >= position[None, :]) & (segment[:, None] == segment[None, :])
    log_gaps = jnp.where(causal[:, :, None], cumlog[:, None, :] - cumlog[None, :, :], 0.0)
    decays = jnp.exp(log_gaps) * causal[:, :, None].astype(F32)
    scores = jnp.dot(queries, key_rows.T, precision=HIGH)
    mixing = scores[:, :, None] * decays * step_size[None, :, :]
    within = jnp.einsum("tsh,shp->thp", mixing, values, precision=HIGH)
    inflow = jnp.exp(cumlog) * (segment == 0).astype(F32)[:, None]
    carried = jnp.einsum("tn,hpn->thp", queries, state_in, precision=HIGH) * inflow[:, :, None]
    skipped = head_params[2][None, :, None] * values
    return (within + carried + skipped).reshape(conv_out.shape[0], DI)


MESH = pl.DeviceIdType.MESH


class Place:
    def __init__(self, n):
        self.n, self.depth = n, n // 8
        self.me = me = lax.axis_index("seq")
        self.z, self.y, self.x, self.c = me // 8, (me // 4) % 2, (me // 2) % 2, me % 2

    def flipped(self, rz, ry, rx, rc):
        z, bit = 0, 1
        while bit < self.depth:
            z = z + ((self.z // bit + rz // bit) % 2) * bit
            bit *= 2
        y, x, c = (self.y + ry) % 2, (self.x + rx) % 2, (self.c + rc) % 2
        return ((z * 2 + y) * 2 + x) * 2 + c

    def split(self, place):
        depth = self.depth
        rz, r1, r2 = place % depth, (place // depth) % 2, (place // (2 * depth)) % 2
        return rz, r1, r2, place // (4 * depth)

    def device(self, place):
        rz, r1, r2, rc = self.split(place)
        owner = (self.c + rc) % 2
        return self.flipped(rz, r2 + owner * (r1 - r2), r1 + owner * (r2 - r1), rc)

    def place_there(self, place):
        rz, r1, r2, rc = self.split(place)
        s1, s2 = r1 + rc * (r2 - r1), r2 + rc * (r1 - r2)
        return ((rc * 2 + s2) * 2 + s1) * self.depth + rz

    def halves(self):
        steps, bit = [], 1
        while bit < self.depth:
            steps.append((bit, self.flipped(bit, 0, 0, 0)))
            bit *= 2
        steps.append((self.depth, self.flipped(0, self.c, 1 - self.c, 0)))
        steps.append((2 * self.depth, self.flipped(0, 1 - self.c, self.c, 0)))
        steps.append((4 * self.depth, self.flipped(0, 0, 0, 1)))
        return steps


def greet(n):
    barrier = pltpu.get_barrier_semaphore()
    me = lax.axis_index("seq")

    @pl.loop(1, n)
    def _(hop):
        other = lax.rem(me + hop, n)
        pl.semaphore_signal(barrier, inc=1, device_id=(other,), device_id_type=MESH)

    pl.semaphore_wait(barrier, n - 1)


def remote(source, target, send_sem, recv_sem, device):
    return pltpu.make_async_remote_copy(
        src_ref=source,
        dst_ref=target,
        send_sem=send_sem,
        recv_sem=recv_sem,
        device_id=(device,),
        device_id_type=MESH,
    )


def landed(ref, sem):
    pltpu.make_async_copy(ref, ref, sem).wait()


def rows_of(place, count, rows):
    return pl.ds(pl.multiple_of(place * rows, rows), count * rows)


GATHER_TIMES = [0, 1, 2, 3, 5, 6]


def gather_kernel(n, chunks, *refs):
    count = len(refs) // 2 - 1
    shards, wholes, (own_sem, send_sem, recv_sem) = refs[:count], refs[count : 2 * count], refs[2 * count :]
    here = Place(n)
    greet(n)
    owns = []
    for index in range(count):
        rows = shards[index].shape[0]
        target = wholes[index].at[rows_of(here.me, 1, rows)]
        owns.append(pltpu.make_async_copy(shards[index], target, own_sem.at[index]))
        owns[-1].start()
    for own in owns:
        own.wait()
    steps = here.halves()

    def block(chunk, place):
        index, first, rows, column, columns = chunks[chunk]
        start = here.device(place) * shards[index].shape[0] + first
        return wholes[index].at[pl.ds(pl.multiple_of(start, 16), rows), pl.ds(column, columns)]

    def sending(chunk, step, place):
        blocks, partner = steps[step]
        there = blocks + place
        ref = block(chunk, place)
        return remote(ref, ref, send_sem.at[chunk, there], recv_sem.at[chunk, there], partner)

    def arrive(chunk, step):
        blocks = steps[step][0]

        @pl.loop(blocks, 2 * blocks)
        def _(place):
            landed(block(chunk, place), recv_sem.at[chunk, place])

    def send(chunk, step):
        @pl.loop(0, steps[step][0])
        def _(place):
            sending(chunk, step, place).start()

    for time in range(len(chunks) + GATHER_TIMES[-1]):
        for step in range(len(steps), -1, -1):
            chunk = time - GATHER_TIMES[step]
            if 0 <= chunk < len(chunks):
                if step > 0:
                    arrive(chunk, step - 1)
                if step < len(steps):
                    send(chunk, step)
    for chunk in range(len(chunks)):
        for step in range(len(steps)):

            @pl.loop(0, steps[step][0])
            def _(place):
                sending(chunk, step, place).wait_send()


def gather_weights(n, shards, cuts):
    if n != 32 or any(shard.shape[0] % 16 for shard in shards):
        return [lax.all_gather(shard, "seq", axis=0, tiled=True) for shard in shards]
    chunks = [
        (index, first, rows, column, min(columns, shard.shape[1] - column))
        for index, (shard, (rows, columns)) in enumerate(zip(shards, cuts))
        for first in range(0, shard.shape[0], rows)
        for column in range(0, shard.shape[1], columns)
    ]
    sems = [pltpu.SemaphoreType.DMA((len(chunks), n))] * 2
    return pl.pallas_call(
        functools.partial(gather_kernel, n, chunks),
        out_shape=[
            jax.ShapeDtypeStruct((n * shard.shape[0], shard.shape[1]), shard.dtype) for shard in shards
        ],
        in_specs=[pl.BlockSpec(memory_space=pltpu.VMEM)] * len(shards),
        out_specs=[pl.BlockSpec(memory_space=pltpu.HBM)] * len(shards),
        scratch_shapes=[pltpu.SemaphoreType.DMA((len(shards),))] + sems,
        compiler_params=pltpu.CompilerParams(
            collective_id=0, has_side_effects=True, vmem_limit_bytes=16 * 2**20
        ),
        cost_estimate=pl.CostEstimate(flops=0, bytes_accessed=2**25, transcendentals=0),
    )(*shards)


SUM_ROWS, SUM_COLUMNS, SUM_SLOTS = 32, 512, 8
SUM_TIMES = [0, 1, 3, 4, 6, 7]


class Sums:
    def __init__(self, here, find, left, right, out, kept, sent, got, send_sem, recv_sem):
        self.here, self.find, self.left, self.right, self.out = here, find, left, right, out
        self.kept, self.sent, self.got = kept, sent, got
        self.send_sem, self.recv_sem = send_sem, recv_sem
        self.steps = here.halves()[::-1]
        self.chunks = got.shape[0]
        self.times = self.chunks + SUM_TIMES[-1]

    def copy(self, chunk, step):
        blocks, partner = self.steps[step]
        cut = pl.ds(blocks * SUM_ROWS, blocks * SUM_ROWS)
        return remote(
            self.sent.at[chunk % SUM_SLOTS, cut],
            self.got.at[chunk, cut],
            self.send_sem.at[chunk, step],
            self.recv_sem.at[chunk, step],
            partner,
        )

    def sent_all(self, chunk):
        for step in range(len(self.steps)):
            self.copy(chunk, step).wait_send()

    def product(self, chunk, first, rows):
        which, column = self.find(chunk)
        left = self.left[which, pl.ds(first, rows)]
        start = pl.multiple_of(column * SUM_COLUMNS, SUM_COLUMNS)
        return dot(left, self.right[:, pl.ds(start, SUM_COLUMNS)])

    def begin(self, chunk):
        half = self.here.n // 2 * SUM_ROWS
        slot = chunk % SUM_SLOTS

        @pl.when(chunk >= SUM_SLOTS)
        def _():
            self.sent_all(chunk - SUM_SLOTS)

        self.sent[slot, pl.ds(half, half)] = self.product(chunk, half, half).astype(BF)
        self.copy(chunk, 0).start()
        self.kept[slot] = self.product(chunk, 0, half)

    def go_on(self, chunk, step):
        slot, rows = chunk % SUM_SLOTS, self.steps[step - 1][0] * SUM_ROWS
        self.copy(chunk, step - 1).wait_recv()
        total = self.kept[slot, pl.ds(0, rows)] + self.got[chunk, pl.ds(rows, rows)].astype(F32)
        if step == len(self.steps):
            start = pl.multiple_of(chunk * SUM_COLUMNS, SUM_COLUMNS)
            self.out[:, pl.ds(start, SUM_COLUMNS)] = total
            return
        half = rows // 2
        self.sent[slot, pl.ds(half, half)] = total[half:].astype(BF)
        self.copy(chunk, step).start()
        self.kept[slot, pl.ds(0, half)] = total[:half]

    def run(self, first, stop):
        @pl.loop(first, stop)
        def _(time):
            for step in range(len(self.steps), -1, -1):
                chunk = time - SUM_TIMES[step]

                @pl.when((chunk >= 0) & (chunk < self.chunks))
                def _():
                    if step == 0:
                        self.begin(chunk)
                    else:
                        self.go_on(chunk, step)

    def end(self):
        @pl.loop(max(0, self.chunks - SUM_SLOTS), self.chunks)
        def _(chunk):
            self.sent_all(chunk)


def sums_scratch(n, chunks):
    rows, phases = n * SUM_ROWS, n.bit_length() - 1
    return [
        pltpu.VMEM((SUM_SLOTS, rows // 2, SUM_COLUMNS), F32),
        pltpu.VMEM((SUM_SLOTS, rows, SUM_COLUMNS), BF),
        pltpu.VMEM((chunks, rows, SUM_COLUMNS), BF),
        pltpu.SemaphoreType.DMA((chunks, phases)),
        pltpu.SemaphoreType.DMA((chunks, phases)),
    ]


def local_find(chunk):
    return (chunk + 6) // 8, chunk


def last_find(chunk):
    late, rest = chunk // 16, chunk - 16
    return late * (1 + (rest + 7) // 16 + (rest + 5) // 16), chunk


def last_kernel(
    n, grad_ref, parted_ref, small_ref, left_ref, right_ref,
    d_weight_ref, d_small_ref, out_ref,
    known, small_kept, small_got, g_send, g_recv, t_send, t_recv, *scratch
):
    here = Place(n)
    rows = grad_ref.shape[0]
    greet(n)
    known[pl.ds(0, rows)] = grad_ref[...]
    small_kept[...] = small_ref[...]
    sums = Sums(here, last_find, left_ref, right_ref, out_ref, *scratch)
    steps = here.halves()
    copies = []
    for step in range(len(steps)):
        blocks, partner = steps[step]
        source, target = pl.ds(0, blocks * rows), pl.ds(blocks * rows, blocks * rows)
        gather = remote(known.at[source], known.at[target], g_send.at[step], g_recv.at[step], partner)
        gather.start()
        blocks, partner = steps[::-1][step]
        cut, mine = pl.ds(blocks * LOG_ROWS, blocks * LOG_ROWS), pl.ds(0, blocks * LOG_ROWS)
        told = remote(small_kept.at[cut], small_got.at[cut], t_send.at[step], t_recv.at[step], partner)
        told.start()
        copies += [gather, told]
        sums.run(3 * step, 3 * step + 3)
        gather.wait_recv()
        told.wait_recv()
        small_kept[mine] = small_kept[mine] + small_got[cut]
    sums.run(3 * len(steps), sums.times)
    d_small_ref[...] = small_kept[pl.ds(0, LOG_ROWS)]
    d_weight_ref[...] = lax.dot_general(
        parted_ref[...], known[...], (((0,), (0,)), ((), ())), preferred_element_type=F32
    )
    for copy in copies:
        copy.wait_send()
    sums.end()


def last_sums(n, grad, parted, small, lefts, right):
    rows, width = grad.shape[0], parted.shape[1]
    phases, chunks = n.bit_length() - 1, right.shape[1] // SUM_COLUMNS
    return pl.pallas_call(
        functools.partial(last_kernel, n),
        out_shape=[
            jax.ShapeDtypeStruct((width, D), F32),
            jax.ShapeDtypeStruct((LOG_ROWS, 128), F32),
            jax.ShapeDtypeStruct((SUM_ROWS, right.shape[1]), F32),
        ],
        in_specs=[pl.BlockSpec(memory_space=pltpu.VMEM)] * 5,
        out_specs=[pl.BlockSpec(memory_space=pltpu.VMEM)] * 3,
        scratch_shapes=[
            pltpu.VMEM((n * rows, D), BF),
            pltpu.VMEM(small.shape, F32),
            pltpu.VMEM(small.shape, F32),
        ]
        + [pltpu.SemaphoreType.DMA((phases,))] * 4
        + sums_scratch(n, chunks),
        compiler_params=pltpu.CompilerParams(
            collective_id=1, has_side_effects=True, vmem_limit_bytes=60 * 2**20
        ),
        cost_estimate=pl.CostEstimate(flops=2**32, bytes_accessed=2**24, transcendentals=0),
    )(grad, parted, small, lefts, right)


LOG_ROWS = 8


def states_kernel(
    n, reverse, states_ref, logs_ref, left_ref, right_ref, out_ref, sum_ref, spread, logs, summed,
    s_send, s_recv, l_send, l_recv, b_send, b_recv, *scratch
):
    me = lax.axis_index("seq")
    rows = states_ref.shape[0] // n
    greet(n)
    sums = None
    if scratch:
        sums = Sums(Place(n), local_find, left_ref, right_ref, sum_ref, *scratch)

    def spreading(other):
        return remote(
            states_ref.at[rows_of(other, 1, rows)],
            spread.at[rows_of(me, 1, rows)],
            s_send.at[other],
            s_recv.at[me],
            other,
        )

    def telling(other):
        target = logs.at[rows_of(me, 1, LOG_ROWS)]
        return remote(logs_ref, target, l_send.at[other], l_recv.at[me], other)

    def returning(other):
        return remote(
            summed.at[rows_of(other, 1, rows)],
            out_ref.at[rows_of(me, 1, rows)],
            b_send.at[other],
            b_recv.at[me],
            other,
        )

    @pl.loop(1, n)
    def _(hop):
        other = lax.rem(me + hop, n)
        spreading(other).start()
        telling(other).start()

    own = pltpu.make_async_copy(
        states_ref.at[rows_of(me, 1, rows)], spread.at[rows_of(me, 1, rows)], s_recv.at[me]
    )
    own_logs = pltpu.make_async_copy(logs_ref, logs.at[rows_of(me, 1, LOG_ROWS)], l_recv.at[me])
    own.start()
    own_logs.start()
    if sums:
        sums.run(0, 4)

    @pl.loop(0, n)
    def _(other):
        landed(spread.at[rows_of(other, 1, rows)], s_recv.at[other])
        landed(logs.at[rows_of(other, 1, LOG_ROWS)], l_recv.at[other])

    head = me * MHEADS // n
    lane = lax.broadcasted_iota(jnp.int32, (LOG_ROWS, 128), 1)
    row = lax.broadcasted_iota(jnp.int32, (LOG_ROWS, 128), 0)

    def join(step, total):
        place = n - 1 - step if reverse else step
        cut = rows_of(place, 1, rows)
        summed[cut] = total.astype(BF)
        told = logs[rows_of(place, 1, LOG_ROWS)]
        log = jnp.sum(jnp.where((lane == head) & (row == 0), told, 0.0), keepdims=True)
        flag = jnp.sum(jnp.where((lane == MHEADS) & (row == 0), told, 0.0), keepdims=True)
        decay = jnp.where(flag > 0.0, 0.0, jnp.exp(log))
        return decay * total + spread[cut].astype(F32)

    lax.fori_loop(0, n, join, jnp.zeros((rows, NSTATE), F32))

    @pl.loop(1, n)
    def _(hop):
        returning(lax.rem(me + hop, n)).start()

    own_back = pltpu.make_async_copy(
        summed.at[rows_of(me, 1, rows)], out_ref.at[rows_of(me, 1, rows)], b_recv.at[me]
    )
    own_back.start()
    if sums:
        sums.run(4, sums.times)
        sums.end()

    @pl.loop(0, n)
    def _(other):
        landed(out_ref.at[rows_of(other, 1, rows)], b_recv.at[other])

    @pl.loop(1, n)
    def _(hop):
        other = lax.rem(me + hop, n)
        spreading(other).wait_send()
        telling(other).wait_send()
        returning(other).wait_send()


def pass_states(n, states, logs, lefts=None, right=None):
    total, reverse = MHEADS * MHEAD_DIM, lefts is not None
    told = jnp.zeros((LOG_ROWS, 128), F32).at[0, : logs.shape[0]].set(logs)
    summing = reverse and n == 32
    chunks = right.shape[1] // SUM_COLUMNS if summing else 0
    small = jnp.zeros((LOG_ROWS, 128), F32)
    operands = [states.reshape(total, NSTATE).astype(BF), told]
    operands += [lefts, right] if summing else [small, small]
    out, found = pl.pallas_call(
        functools.partial(states_kernel, n, reverse),
        out_shape=[
            jax.ShapeDtypeStruct((total, NSTATE), BF),
            jax.ShapeDtypeStruct((SUM_ROWS, chunks * SUM_COLUMNS) if summing else (LOG_ROWS, 128), F32),
        ],
        in_specs=[pl.BlockSpec(memory_space=pltpu.VMEM)] * 4,
        out_specs=[pl.BlockSpec(memory_space=pltpu.VMEM)] * 2,
        scratch_shapes=[
            pltpu.VMEM((total, NSTATE), BF),
            pltpu.VMEM((n * LOG_ROWS, 128), F32),
            pltpu.VMEM((total, NSTATE), BF),
        ]
        + [pltpu.SemaphoreType.DMA((n,))] * 6
        + (sums_scratch(n, chunks) if summing else []),
        compiler_params=pltpu.CompilerParams(
            collective_id=3 if reverse else 2,
            has_side_effects=True,
            vmem_limit_bytes=(48 if summing else 16) * 2**20,
        ),
        cost_estimate=pl.CostEstimate(flops=2**22, bytes_accessed=2**21, transcendentals=0),
    )(*operands)
    return out.astype(F32).reshape(MHEADS, MHEAD_DIM, NSTATE), found


ATTN_ROWS = 128


def tile_mask():
    row = lax.broadcasted_iota(jnp.int32, (ATTN_ROWS, ATTN_ROWS), 0)
    column = lax.broadcasted_iota(jnp.int32, (ATTN_ROWS, ATTN_ROWS), 1)
    return (row // PATCH == column // PATCH) & (row >= column)


def head_mask(which):
    lane = lax.broadcasted_iota(jnp.int32, (1, 2 * AHEAD_DIM), 1)
    return lane // AHEAD_DIM == which


def only(values, mask):
    return jnp.where(mask, values, jnp.zeros_like(values))


def tile_probs(queries, key_rows, mask):
    scores = dot_t(queries, key_rows) * AHEAD_DIM ** (-0.5)
    scores = jnp.where(mask, scores, -1e30)
    raised = jnp.exp(scores - jnp.max(scores, axis=-1, keepdims=True))
    return raised / jnp.sum(raised, axis=-1, keepdims=True)


def attention_kernel(triple_ref, out_ref):
    mask = tile_mask()
    width = 2 * AHEAD_DIM
    for pair in range(AHEADS // 2):
        queries, key_rows, value_rows = [
            triple_ref[:, part * D + pair * width : part * D + (pair + 1) * width] for part in range(3)
        ]
        total = None
        for which in range(2):
            lanes = head_mask(which)
            probs = tile_probs(only(queries, lanes), key_rows, mask)
            mixed = dot(probs.astype(BF), only(value_rows, lanes))
            total = mixed if total is None else total + mixed
        out_ref[:, pair * width : (pair + 1) * width] = total.astype(BF)


def attention(triple):
    rows = triple.shape[0]
    return pl.pallas_call(
        attention_kernel,
        grid=(rows // ATTN_ROWS,),
        out_shape=jax.ShapeDtypeStruct((rows, D), BF),
        in_specs=[pl.BlockSpec((ATTN_ROWS, 3 * D), lambda i: (i, 0))],
        out_specs=pl.BlockSpec((ATTN_ROWS, D), lambda i: (i, 0)),
    )(triple)


def attention_back_kernel(triple_ref, grad_ref, out_ref):
    mask = tile_mask()
    width = 2 * AHEAD_DIM
    scale = AHEAD_DIM ** (-0.5)
    rows_first = (((0,), (0,)), ((), ()))
    for pair in range(AHEADS // 2):
        lo, hi = pair * width, (pair + 1) * width
        queries, key_rows, value_rows = [
            triple_ref[:, part * D + lo : part * D + hi] for part in range(3)
        ]
        grad = grad_ref[:, lo:hi]
        totals = [None, None, None]
        for which in range(2):
            lanes = head_mask(which)
            probs = tile_probs(only(queries, lanes), key_rows, mask)
            grad_one = only(grad, lanes)
            d_probs = dot_t(grad_one, value_rows)
            d_scores = probs * (d_probs - jnp.sum(probs * d_probs, axis=-1, keepdims=True))
            d_scores = d_scores.astype(BF)
            found = [
                scale * dot(d_scores, only(key_rows, lanes)),
                scale
                * lax.dot_general(
                    d_scores, only(queries, lanes), rows_first, preferred_element_type=F32
                ),
                lax.dot_general(
                    probs.astype(BF), grad_one, rows_first, preferred_element_type=F32
                ),
            ]
            totals = found if which == 0 else [a + b for a, b in zip(totals, found)]
        for part in range(3):
            out_ref[:, part * D + lo : part * D + hi] = totals[part].astype(BF)


def attention_back(triple, grad):
    rows = triple.shape[0]
    return pl.pallas_call(
        attention_back_kernel,
        grid=(rows // ATTN_ROWS,),
        out_shape=jax.ShapeDtypeStruct((rows, 3 * D), BF),
        in_specs=[
            pl.BlockSpec((ATTN_ROWS, 3 * D), lambda i: (i, 0)),
            pl.BlockSpec((ATTN_ROWS, D), lambda i: (i, 0)),
        ],
        out_specs=pl.BlockSpec((ATTN_ROWS, 3 * D), lambda i: (i, 0)),
    )(triple, grad)


def local(
    byte_acts,
    resets,
    out_grad,
    patch_weight,
    patch_gain,
    mixer_in,
    conv_weight,
    conv_bias,
    head_params,
    mixer_gain,
    mixer_out,
    unpatch_weight,
    attn_gain,
    qkv_weight,
    attn_out,
    ffn_gain,
    gate_up,
    down_weight,
):
    n = lax.axis_size("seq")
    me = lax.axis_index("seq")
    ring = Ring(n)

    def passed_along(block, distance):
        route = [(i - distance, i) for i in range(n) if 0 <= i - distance < n]
        return lax.ppermute(block, "seq", route)

    live = Live()
    order = ring.order()

    byte_wide = byte_acts.astype(F32)
    patches = byte_acts.reshape(-1, PATCH * D)
    patch_rows = patches.shape[0]
    unpack_early = gather_flat(n, [unpatch_weight, qkv_weight, attn_out])
    unpack_late = gather_flat(n, [gate_up, down_weight])
    small = [patch_gain, conv_weight.reshape(-1), conv_bias, mixer_gain, attn_gain, ffn_gain]
    cuts = list(np.cumsum([piece.shape[0] for piece in small]))
    small_all = gather_small(ring, jnp.concatenate(small)).astype(F32)
    parts = jnp.split(small_all, cuts[:-1], axis=1)
    live.patch_gain = parts[0].reshape(-1)
    live.conv_weight = parts[1].reshape(n, CONV, -1).transpose(1, 0, 2).reshape(CONV, CONV_CH)
    live.conv_bias, live.mixer_gain, live.attn_gain, live.ffn_gain = [
        piece.reshape(-1) for piece in parts[2:]
    ]
    live.fence()

    live.patch_w, live.mixer_in, live.mixer_out = gather_weights(
        n,
        [patch_weight, jnp.pad(mixer_in, ((0, 0), (0, -mixer_in.shape[1] % 128))), mixer_out],
        [(32, D), (16, 2304), (32, D)],
    )
    live.embedded = dot(patches, live.patch_w)
    live.normed = rms_scale(live.embedded, live.patch_gain).astype(BF)
    projected = dot(live.normed, live.mixer_in)
    live.gate_z = projected[:, :DI]
    conv_in = projected[:, DI : DI + CONV_CH].astype(BF).astype(F32)
    dt_raw = projected[:, DI + CONV_CH : DI + CONV_CH + MHEADS]
    logs = jnp.sum(-jax.nn.softplus(dt_raw + head_params[0]) * jnp.exp(head_params[1]), axis=0)
    flag = jnp.max(resets).astype(F32)
    live.logs = jnp.concatenate([logs, flag[None]])
    not_reset = 1.0 - resets.astype(F32)
    keep_tail = jnp.concatenate(
        [jnp.cumprod(not_reset[patch_rows - CONV + 2 :][::-1])[::-1], jnp.ones((1,), F32)]
    )
    tail_sent = (conv_in[patch_rows - CONV + 1 :] * keep_tail[:, None]).astype(BF)
    halo_rows = passed_along(tail_sent, 1)
    flags_ext = jnp.concatenate([jnp.zeros((CONV - 1,), jnp.int32), resets])
    validity = tap_masks(flags_ext, patch_rows)
    conv_ext = jnp.concatenate([halo_rows.astype(F32), conv_in])
    conv_out, conv_back = jax.vjp(
        functools.partial(conv_apply, validity=validity, row_count=patch_rows),
        conv_ext,
        live.conv_weight,
        live.conv_bias,
    )
    state_parts, state_back = jax.vjp(
        functools.partial(block_state, starts=resets), conv_out, dt_raw, head_params
    )
    local_state, decay_total = state_parts
    live.state_in, _ = pass_states(n, local_state, live.logs)
    live.fence()

    mixer_y, output_back = jax.vjp(
        functools.partial(block_output, starts=resets),
        conv_out,
        dt_raw,
        head_params,
        live.state_in,
    )
    gate_act = silu(live.gate_z)
    gated = mixer_y * gate_act
    live.gated_norm = rms_scale(gated, live.mixer_gain).astype(BF)
    branch = dot(live.gated_norm, live.mixer_out)
    live.hidden = (live.embedded + branch).astype(BF)
    live.unpatch, live.qkv_w, live.attn_out = unpack_early()
    slots = dot(live.hidden, live.unpatch)
    live.stream0 = byte_wide + slots.reshape(-1, D)
    live.normed0 = rms_scale(live.stream0, live.attn_gain).astype(BF)
    live.fence()

    rows = byte_wide.shape[0]
    live.triple = dot(live.normed0, live.qkv_w).astype(BF)
    live.mixed = attention(live.triple)
    live.stream1 = live.stream0 + dot(live.mixed, live.attn_out)
    live.normed1 = rms_scale(live.stream1, live.ffn_gain).astype(BF)
    live.gate_up, live.down_w = unpack_late()
    both = dot(live.normed1, live.gate_up)
    live.both = both.astype(BF)
    live.hid = (silu(both[:, :FF]) * both[:, FF:]).astype(BF)
    parted = patches.reshape(patch_rows, n, -1).transpose(1, 0, 2)
    live.parted = lax.all_to_all(parted, "seq", 0, 0, tiled=True)
    live.fence()

    small_slice = n == 32

    def in_order(values):
        blocks = values.reshape(n, -1, values.shape[-1])
        return jnp.take(blocks, order, axis=0).reshape(-1, values.shape[-1])

    def lefts_of(values):
        if not small_slice:
            return values
        turned = in_order(values.T).reshape(n, -1, SUM_ROWS, values.shape[0])
        return turned.transpose(1, 0, 2, 3).reshape(-1, n * SUM_ROWS, values.shape[0])

    layer_out = (live.stream1 + dot(live.hid, live.down_w)).astype(BF)
    d_hid = dot_t(out_grad, live.down_w)
    gate, up = live.both[:, :FF].astype(F32), live.both[:, FF:].astype(F32)
    d_both = jnp.concatenate([d_hid * up * silu_slope(gate), d_hid * silu(gate)], axis=1).astype(BF)
    if small_slice:
        block = down_weight.shape[0]
        flat = flat_grads(n, live.hid, out_grad, live.normed1, d_both)
        found = lax.psum_scatter(flat, "seq", scatter_dimension=0, tiled=True)[0].astype(F32)
        g_down = found[:block]
        g_gate_up = found[block:].reshape(-1, SUM_ROWS, D).transpose(1, 0, 2)
        g_gate_up = g_gate_up.reshape(SUM_ROWS, -1)
    else:
        g_down = summed_grad(live.hid, out_grad)
        g_gate_up = summed_grad(live.normed1, d_both)
    d_normed1 = dot_t(d_both, live.gate_up)
    d_stream1, g_ffn_gain = rms_back(live.stream1, live.ffn_gain, d_normed1)
    d_stream1 = out_grad.astype(F32) + d_stream1
    d_stream1_low = d_stream1.astype(BF)
    d_mixed = dot_t(d_stream1_low, live.attn_out).astype(BF)
    d_triple = attention_back(live.triple, d_mixed)
    d_stream0, g_attn_gain = rms_back(live.stream0, live.attn_gain, dot_t(d_triple, live.qkv_w))
    live.d_stream0 = d_stream1 + d_stream0
    d_slots = live.d_stream0.astype(BF).reshape(patch_rows, PATCH * D)
    d_hidden = dot_t(d_slots, live.unpatch)
    d_branch = d_hidden.astype(BF)
    d_gated, g_mixer_gain = rms_back(gated, live.mixer_gain, dot_t(d_branch, live.mixer_out))
    d_gate_z = d_gated * mixer_y * silu_slope(live.gate_z)
    output_grads = output_back(d_gated * gate_act)
    state_grad, found = pass_states(
        n,
        output_grads[3],
        live.logs,
        jnp.concatenate([lefts_of(live.mixed), lefts_of(live.normed0)], axis=0),
        jnp.concatenate([d_stream1_low, d_triple], axis=1),
    )
    g_attn_out, g_qkv = found[:, :D], found[:, D:]
    decay_grad = jnp.sum(state_grad * live.state_in, axis=(1, 2))
    state_cot = state_back((state_grad, decay_grad))
    conv_cot = conv_back(output_grads[0] + state_cot[0])
    returned = passed_along(conv_cot[0][: CONV - 1], -1)
    d_conv_in = conv_cot[0][CONV - 1 :] + jnp.concatenate(
        [jnp.zeros((patch_rows - CONV + 1, CONV_CH), F32), returned * keep_tail[:, None]]
    )
    d_dt = output_grads[1] + state_cot[1]
    d_projected = jnp.concatenate([d_gate_z, d_conv_in, d_dt], axis=1).astype(BF)
    d_projected = jnp.pad(d_projected, ((0, 0), (0, -d_projected.shape[1] % 128)))
    d_embedded, g_patch_gain = rms_back(
        live.embedded, live.patch_gain, dot_t(d_projected, live.mixer_in)
    )
    d_embedded = (d_hidden + d_embedded).astype(BF)
    d_patches = dot_t(d_embedded, live.patch_w).reshape(-1, D)
    input_grad = (live.d_stream0 + d_patches).astype(BF)

    g_conv_weight = conv_cot[1].reshape(CONV, n, -1).transpose(1, 0, 2).reshape(n, -1)
    g_head = jnp.broadcast_to((output_grads[2] + state_cot[2]).reshape(1, -1), (n, 3 * MHEADS))
    g_small = [g_patch_gain, g_conv_weight, conv_cot[2], g_mixer_gain, g_attn_gain, g_ffn_gain, g_head]
    g_small = jnp.concatenate([piece.reshape(n, -1) for piece in g_small], axis=1)
    small_width = g_small.shape[1]
    g_small = jnp.pad(g_small, ((0, 0), (0, LOG_ROWS * 128 - small_width)))
    g_small = g_small.reshape(n * LOG_ROWS, 128)
    if small_slice:
        lefts = [lefts_of(live.hidden), lefts_of(live.normed), lefts_of(live.gated_norm)]
        d_projected = jnp.pad(d_projected, ((0, 0), (0, -d_projected.shape[1] % SUM_COLUMNS)))
        g_patch, g_small, found = last_sums(
            n,
            d_embedded,
            in_order(live.parted),
            in_order(g_small),
            jnp.concatenate(lefts, axis=0),
            jnp.concatenate([d_slots, d_projected, d_branch, d_branch], axis=1),
        )
        g_unpatch = found[:, : PATCH * D]
        g_mixer_in = found[:, PATCH * D : PATCH * D + mixer_in.shape[1]]
        g_mixer_out = found[:, found.shape[1] - 2 * D :].reshape(SUM_ROWS, 2, D)
        g_mixer_out = g_mixer_out.transpose(1, 0, 2).reshape(-1, D)
    else:
        g_attn_out = summed_grad(live.mixed, d_stream1_low)
        g_qkv = summed_grad(live.normed0, d_triple)
        known = lax.all_gather(d_embedded, "seq", axis=0, tiled=True)
        g_patch = dot(live.parted.reshape(n * patch_rows, -1).T, known)
        g_small = lax.psum_scatter(g_small, "seq", scatter_dimension=0, tiled=True)
        g_unpatch = summed_grad(live.hidden, d_slots)
        g_mixer_in = summed_grad(live.normed, d_projected)[:, : mixer_in.shape[1]]
        g_mixer_out = summed_grad(live.gated_norm, d_branch)
    g_small = g_small.reshape(-1)[:small_width]
    s = jnp.split(g_small, cuts)
    return (
        layer_out,
        input_grad,
        g_patch,
        s[0],
        g_mixer_in,
        s[1].reshape(CONV, -1),
        s[2],
        s[6].reshape(3, MHEADS),
        s[3],
        g_mixer_out,
        g_unpatch,
        s[4],
        g_qkv,
        g_attn_out,
        s[5],
        g_gate_up,
        g_down,
    )


def solution(mesh):
    rows, vector = P("seq", None), P("seq")
    placed = (
        rows, vector, rows, rows, vector, rows, P(None, "seq"), vector, P(),
        vector, rows, rows, vector, rows, rows, vector, rows, rows,
    )
    returned = (
        rows, rows, rows, vector, rows, P(None, "seq"), vector, P(), vector,
        rows, rows, vector, rows, rows, vector, rows, rows,
    )
    return jax.shard_map(
        local, mesh=mesh, in_specs=placed, out_specs=returned, check_vma=False
    )
```

```python
import functools

import jax
import jax.numpy as jnp
import numpy as np
from jax import lax
from jax.experimental import pallas as pl
from jax.experimental.pallas import tpu as pltpu
from jax.sharding import PartitionSpec as P

D = 1024
PATCH = 8
MHEADS = 32
MHEAD_DIM = 64
DI = 2048
NSTATE = 128
CONV = 4
AHEADS = 16
AHEAD_DIM = 64
FF = 4096
CONV_CH = 2304

EPS = 1e-05
HIGH = lax.Precision.HIGHEST
BF = jnp.bfloat16
F32 = jnp.float32


class Ring:
    def __init__(self, n):
        self.n = n
        self.depth = n // 8
        coords = [(i // 8, (i // 4) % 2, (i // 2) % 2, i % 2) for i in range(n)]

        def index(z, y, x, c):
            return ((z * 2 + y) * 2 + x) * 2 + c

        def flip(z, y, x, c, along_x):
            return index(z, y, 1 - x, c) if along_x else index(z, 1 - y, x, c)

        self.core = [(index(*p), index(*p) ^ 1) for p in coords]
        self.first = [(index(*p), flip(*p, p[3] == 0)) for p in coords]
        self.second = [(index(*p), flip(*p, p[3] == 1)) for p in coords]
        self.bits = [1 << b for b in range(self.depth.bit_length() - 1)]
        self.along = {
            bit: [(index(*p), index(p[0] ^ bit, *p[1:])) for p in coords] for bit in self.bits
        }
        table = np.zeros((n, n), np.int32)
        for me, (z, y, x, c) in enumerate(coords):
            place = 0
            for rc in range(2):
                owner = c ^ rc
                for r2 in range(2):
                    for r1 in range(2):
                        rx, ry = (r1, r2) if owner == 0 else (r2, r1)
                        for rz in range(self.depth):
                            table[me, place] = index(z ^ rz, y ^ ry, x ^ rx, owner)
                            place += 1
        self.table = table

    def order(self):
        return jnp.asarray(self.table)[lax.axis_index("seq")]


def swap(block, route):
    return lax.ppermute(block, "seq", route)


def flat_kernel(*refs):
    out, first = refs[-1], 0
    for ref in refs[:-1]:
        rows = ref.shape[0]
        for column in range(0, ref.shape[1], D):
            out[pl.ds(first, rows)] = ref[:, pl.ds(column, D)]
            first += rows


def flat_rows(shards):
    total = sum(shard.shape[0] * shard.shape[1] // D for shard in shards)
    return pl.pallas_call(
        flat_kernel,
        out_shape=jax.ShapeDtypeStruct((total, D), BF),
        in_specs=[pl.BlockSpec(memory_space=pltpu.VMEM)] * len(shards),
        out_specs=pl.BlockSpec(memory_space=pltpu.VMEM),
    )(*shards)


def gather_flat(n, shards):
    return lax.all_gather(flat_rows(shards), "seq", axis=0)


def flat_block(n, rows, place):
    return pl.BlockSpec((n, rows, D), lambda i: (0, place(i), 0))


def whole_of(ref):
    return ref[...].reshape(-1, ref.shape[-1])


def flat_dot_kernel(values_ref, flat_ref, out_ref):
    out_ref[...] = dot(values_ref[...], whole_of(flat_ref)).astype(out_ref.dtype)


def flat_dot(values, flat, first, count, kind):
    n, rows = flat.shape[0], values.shape[0]
    return pl.pallas_call(
        flat_dot_kernel,
        grid=(count,),
        out_shape=jax.ShapeDtypeStruct((rows, count * D), kind),
        in_specs=[
            pl.BlockSpec((rows, D), lambda i: (0, 0)),
            flat_block(n, D // n, lambda i: first + i),
        ],
        out_specs=pl.BlockSpec((rows, D), lambda i: (0, i)),
        compiler_params=pltpu.CompilerParams(vmem_limit_bytes=56 * 2**20),
        cost_estimate=pl.CostEstimate(
            flops=2 * rows * D * D * count, bytes_accessed=2 * D * D * count, transcendentals=0
        ),
    )(values, flat)


def flat_dot_t_kernel(values_ref, flat_ref, out_ref):
    found = dot_t(values_ref[...], whole_of(flat_ref))

    @pl.when(pl.program_id(0) == 0)
    def _():
        out_ref[...] = found

    @pl.when(pl.program_id(0) > 0)
    def _():
        out_ref[...] += found


def flat_dot_t(values, flat, first, count):
    n, rows = flat.shape[0], values.shape[0]
    return pl.pallas_call(
        flat_dot_t_kernel,
        grid=(count,),
        out_shape=jax.ShapeDtypeStruct((rows, D), F32),
        in_specs=[
            pl.BlockSpec((rows, D), lambda i: (0, i)),
            flat_block(n, D // n, lambda i: first + i),
        ],
        out_specs=pl.BlockSpec((rows, D), lambda i: (0, 0)),
        compiler_params=pltpu.CompilerParams(vmem_limit_bytes=56 * 2**20),
        cost_estimate=pl.CostEstimate(
            flops=2 * rows * D * D * count, bytes_accessed=2 * D * D * count, transcendentals=0
        ),
    )(values, flat)


def input_grad_kernel(direct_ref, grad_ref, weight_ref, out_ref):
    out_ref[...] = (direct_ref[...] + dot_t(grad_ref[...], weight_ref[...])).astype(BF)


def input_gradient(direct, grad, weight):
    rows, columns = direct.shape
    return pl.pallas_call(
        input_grad_kernel,
        grid=(columns // D,),
        out_shape=jax.ShapeDtypeStruct((rows, columns), BF),
        in_specs=[
            pl.BlockSpec((rows, D), lambda i: (0, i)),
            pl.BlockSpec((rows, D), lambda i: (0, 0)),
            pl.BlockSpec((D, D), lambda i: (i, 0)),
        ],
        out_specs=pl.BlockSpec((rows, D), lambda i: (0, i)),
        compiler_params=pltpu.CompilerParams(vmem_limit_bytes=56 * 2**20),
        cost_estimate=pl.CostEstimate(
            flops=2 * rows * columns * D, bytes_accessed=2 * columns * D, transcendentals=0
        ),
    )(direct, grad, weight)


class Live:
    def fence(self):
        vars(self).update(lax.optimization_barrier(dict(vars(self))))


def summed_grad(left, right):
    product = lax.dot_general(left, right, (((0,), (0,)), ((), ())), preferred_element_type=F32)
    summed = lax.psum_scatter(product.astype(BF), "seq", scatter_dimension=0, tiled=True)
    return summed.astype(F32)


def flat_grad_kernel(hid_ref, grad_ref, normed_ref, both_ref, out_ref):
    devices, block = out_ref.shape[:2]
    parts = block // SUM_ROWS

    def product(left, right):
        return lax.dot_general(
            left, right, (((0,), (0,)), ((), ())), preferred_element_type=F32
        ).astype(BF)

    @pl.when(pl.program_id(0) < 4)
    def _():
        few = devices // parts
        for part in range(parts):
            cut = pl.ds(part * few * block, few * block)
            found = product(hid_ref[:, cut], grad_ref[...])
            out_ref[pl.ds(part * few, few)] = found.reshape(few, block, D)

    @pl.when(pl.program_id(0) >= 4)
    def _():
        for part in range(parts):
            found = product(normed_ref[...], both_ref[0, :, pl.ds(part * D, D)])
            cut = pl.ds(part * SUM_ROWS, SUM_ROWS)
            out_ref[:, cut] = found.reshape(devices, SUM_ROWS, D)


def flat_grads(n, hid, out_grad, normed, both):
    rows, block, devices = hid.shape[0], hid.shape[1] // n, n // 4

    def late(step):
        return jnp.maximum(step - 4, 0)

    return pl.pallas_call(
        flat_grad_kernel,
        grid=(12,),
        out_shape=jax.ShapeDtypeStruct((n, 3 * block, D), BF),
        in_specs=[
            pl.BlockSpec((rows, devices * block), lambda i: (0, jnp.minimum(i, 3))),
            pl.BlockSpec((rows, D), lambda i: (0, 0)),
            pl.BlockSpec((rows, devices * SUM_ROWS), lambda i: (0, late(i) % 4)),
            pl.BlockSpec((1, rows, FF), lambda i: (late(i) // 4, 0, 0)),
        ],
        out_specs=pl.BlockSpec(
            (devices, block, D), lambda i: (i % 4, jnp.minimum(i // 4, 1) + late(i) // 4, 0)
        ),
        compiler_params=pltpu.CompilerParams(vmem_limit_bytes=32 * 2**20),
        cost_estimate=pl.CostEstimate(
            flops=6 * rows * FF * D, bytes_accessed=2**25, transcendentals=0
        ),
    )(hid, out_grad, normed, both)


def dot(left, right):
    return jnp.dot(left, right, preferred_element_type=F32)


def dot_t(left, right):
    return lax.dot_general(left, right, (((1,), (1,)), ((), ())), preferred_element_type=F32)


def rms_scale(values, gain):
    return values * lax.rsqrt(jnp.mean(values * values, axis=-1, keepdims=True) + EPS) * gain


def rms_back(values, gain, grad):
    r = lax.rsqrt(jnp.mean(values * values, axis=-1, keepdims=True) + EPS)
    scaled = gain * grad
    inner = jnp.mean(values * scaled, axis=-1, keepdims=True)
    return r * scaled - values * (r * r * r) * inner, jnp.sum(values * r * grad, axis=0)


def silu(v):
    return v * jax.nn.sigmoid(v)


def silu_slope(v):
    s = jax.nn.sigmoid(v)
    return s * (1.0 + v * (1.0 - s))


def tap_masks(flags_ext, row_count):
    not_reset = 1.0 - flags_ext.astype(F32)
    validity = [jnp.ones((row_count,), F32)]
    for offset in range(1, CONV):
        validity.append(validity[-1] * not_reset[CONV - offset : CONV - offset + row_count])
    return validity


def conv_apply(conv_ext, conv_weight, conv_bias, validity, row_count):
    summed = conv_bias + conv_ext[CONV - 1 : CONV - 1 + row_count] * conv_weight[0]
    for offset in range(1, CONV):
        summed = (
            summed
            + validity[offset][:, None]
            * conv_ext[CONV - 1 - offset : CONV - 1 - offset + row_count]
            * conv_weight[offset]
        )
    return jax.nn.silu(summed)


def block_parts(conv_out, dt_raw, head_params, starts):
    row_count = conv_out.shape[0]
    values = conv_out[:, :DI].reshape(row_count, MHEADS, MHEAD_DIM)
    key_rows = conv_out[:, DI : DI + NSTATE]
    queries = conv_out[:, DI + NSTATE :]
    step_size = jax.nn.softplus(dt_raw + head_params[0])
    cumlog = jnp.cumsum(-step_size * jnp.exp(head_params[1]), axis=0)
    segment = jnp.cumsum(starts, axis=0, dtype=jnp.int32)
    return (values, key_rows, queries, step_size, cumlog, segment)


def block_state(conv_out, dt_raw, head_params, starts):
    values, key_rows, queries, step_size, cumlog, segment = block_parts(
        conv_out, dt_raw, head_params, starts
    )
    same_doc = (segment == segment[-1]).astype(F32)
    weighting = jnp.exp(cumlog[-1][None, :] - cumlog) * same_doc[:, None] * step_size
    state_out = jnp.einsum("rh,rhp,rn->hpn", weighting, values, key_rows, precision=HIGH)
    decay_total = jnp.exp(cumlog[-1]) * (segment[-1] == 0).astype(F32)
    return (state_out, decay_total)


def block_output(conv_out, dt_raw, head_params, state_in, starts):
    values, key_rows, queries, step_size, cumlog, segment = block_parts(
        conv_out, dt_raw, head_params, starts
    )
    position = jnp.arange(conv_out.shape[0])
    causal = (position[:, None] >= position[None, :]) & (segment[:, None] == segment[None, :])
    log_gaps = jnp.where(causal[:, :, None], cumlog[:, None, :] - cumlog[None, :, :], 0.0)
    decays = jnp.exp(log_gaps) * causal[:, :, None].astype(F32)
    scores = jnp.dot(queries, key_rows.T, precision=HIGH)
    mixing = scores[:, :, None] * decays * step_size[None, :, :]
    within = jnp.einsum("tsh,shp->thp", mixing, values, precision=HIGH)
    inflow = jnp.exp(cumlog) * (segment == 0).astype(F32)[:, None]
    carried = jnp.einsum("tn,hpn->thp", queries, state_in, precision=HIGH) * inflow[:, :, None]
    skipped = head_params[2][None, :, None] * values
    return (within + carried + skipped).reshape(conv_out.shape[0], DI)


MESH = pl.DeviceIdType.MESH


class Place:
    def __init__(self, n):
        self.n, self.depth = n, n // 8
        self.me = me = lax.axis_index("seq")
        self.z, self.y, self.x, self.c = me // 8, (me // 4) % 2, (me // 2) % 2, me % 2

    def flipped(self, rz, ry, rx, rc):
        z, bit = 0, 1
        while bit < self.depth:
            z = z + ((self.z // bit + rz // bit) % 2) * bit
            bit *= 2
        y, x, c = (self.y + ry) % 2, (self.x + rx) % 2, (self.c + rc) % 2
        return ((z * 2 + y) * 2 + x) * 2 + c

    def split(self, place):
        depth = self.depth
        rz, r1, r2 = place % depth, (place // depth) % 2, (place // (2 * depth)) % 2
        return rz, r1, r2, place // (4 * depth)

    def device(self, place):
        rz, r1, r2, rc = self.split(place)
        owner = (self.c + rc) % 2
        return self.flipped(rz, r2 + owner * (r1 - r2), r1 + owner * (r2 - r1), rc)

    def place_there(self, place):
        rz, r1, r2, rc = self.split(place)
        s1, s2 = r1 + rc * (r2 - r1), r2 + rc * (r1 - r2)
        return ((rc * 2 + s2) * 2 + s1) * self.depth + rz

    def halves(self):
        steps, bit = [], 1
        while bit < self.depth:
            steps.append((bit, self.flipped(bit, 0, 0, 0)))
            bit *= 2
        steps.append((self.depth, self.flipped(0, self.c, 1 - self.c, 0)))
        steps.append((2 * self.depth, self.flipped(0, 1 - self.c, self.c, 0)))
        steps.append((4 * self.depth, self.flipped(0, 0, 0, 1)))
        return steps


def greet(n):
    barrier = pltpu.get_barrier_semaphore()
    me = lax.axis_index("seq")

    @pl.loop(1, n)
    def _(hop):
        other = lax.rem(me + hop, n)
        pl.semaphore_signal(barrier, inc=1, device_id=(other,), device_id_type=MESH)

    pl.semaphore_wait(barrier, n - 1)


def remote(source, target, send_sem, recv_sem, device):
    return pltpu.make_async_remote_copy(
        src_ref=source,
        dst_ref=target,
        send_sem=send_sem,
        recv_sem=recv_sem,
        device_id=(device,),
        device_id_type=MESH,
    )


def landed(ref, sem):
    pltpu.make_async_copy(ref, ref, sem).wait()


def rows_of(place, count, rows):
    return pl.ds(pl.multiple_of(place * rows, rows), count * rows)


GATHER_TIMES = [0, 1, 2, 3, 5, 6]


EMBED_ROWS = 1024


def gather_kernel(n, chunks, embed_time, *refs):
    count = (len(refs) - 11) // 2
    shards, patches_ref, wholes = refs[:count], refs[count], refs[count + 1 : -10]
    embedded_ref, parted_ref, total, held, held_sem, own_sem = refs[-10:-4]
    send_sem, recv_sem, part_send, part_recv = refs[-4:]
    here = Place(n)
    greet(n)
    owns = []
    for index in range(count):
        rows = shards[index].shape[0]
        target = wholes[index].at[rows_of(here.me, 1, rows)]
        owns.append(pltpu.make_async_copy(shards[index], target, own_sem.at[index]))
        owns[-1].start()
    for own in owns:
        own.wait()
    steps = here.halves()

    def block(chunk, place):
        index, first, rows, column, columns = chunks[chunk]
        start = here.device(place) * shards[index].shape[0] + first
        return wholes[index].at[pl.ds(pl.multiple_of(start, 16), rows), pl.ds(column, columns)]

    def sending(chunk, step, place):
        blocks, partner = steps[step]
        there = blocks + place
        ref = block(chunk, place)
        return remote(ref, ref, send_sem.at[chunk, there], recv_sem.at[chunk, there], partner)

    def arrive(chunk, step):
        blocks = steps[step][0]

        @pl.loop(blocks, 2 * blocks)
        def _(place):
            landed(block(chunk, place), recv_sem.at[chunk, place])

    def send(chunk, step):
        @pl.loop(0, steps[step][0])
        def _(place):
            sending(chunk, step, place).start()

    rows, width = patches_ref.shape[0], patches_ref.shape[1] // n

    def part_of(place):
        start = pl.multiple_of(here.device(place) * width, 128)
        return patches_ref.at[:, pl.ds(start, width)]

    def parting(place):
        there = here.place_there(place)
        target = parted_ref.at[rows_of(there, 1, rows)]
        return remote(
            part_of(place), target, part_send.at[place], part_recv.at[there], here.device(place)
        )

    pieces = wholes[0].shape[0] // EMBED_ROWS

    def fetch(piece):
        source = wholes[0].at[pl.ds(piece * EMBED_ROWS, EMBED_ROWS)]
        return pltpu.make_async_copy(source, held.at[piece % 2], held_sem.at[piece % 2])

    def embed(piece):
        if piece == 0:
            fetch(0).start()
        if piece + 1 < pieces:
            fetch(piece + 1).start()
        fetch(piece).wait()
        found = dot(patches_ref[:, pl.ds(piece * EMBED_ROWS, EMBED_ROWS)], held[piece % 2])
        total[...] = found if piece == 0 else total[...] + found

    done = 0
    own_part = pltpu.make_async_copy(part_of(0), parted_ref.at[rows_of(0, 1, rows)], part_recv.at[0])
    for time in range(len(chunks) + GATHER_TIMES[-1]):
        if time == embed_time:
            own_part.start()

            @pl.loop(1, n)
            def _(place):
                parting(place).start()

        for step in range(len(steps), -1, -1):
            chunk = time - GATHER_TIMES[step]
            if 0 <= chunk < len(chunks):
                if step > 0:
                    arrive(chunk, step - 1)
                if step < len(steps):
                    send(chunk, step)
        for _ in range(2):
            if time >= embed_time and done < pieces:
                embed(done)
                done += 1
    for piece in range(done, pieces):
        embed(piece)
    embedded_ref[...] = total[...]

    @pl.loop(0, n)
    def _(place):
        landed(parted_ref.at[rows_of(place, 1, rows)], part_recv.at[place])

    @pl.loop(1, n)
    def _(place):
        parting(place).wait_send()

    for chunk in range(len(chunks)):
        for step in range(len(steps)):

            @pl.loop(0, steps[step][0])
            def _(place):
                sending(chunk, step, place).wait_send()


def gather_weights(n, shards, cuts, patches):
    if n != 32 or any(shard.shape[0] % 16 for shard in shards):
        wholes = [lax.all_gather(shard, "seq", axis=0, tiled=True) for shard in shards]
        parted = patches.reshape(patches.shape[0], n, -1).transpose(1, 0, 2)
        parted = lax.all_to_all(parted, "seq", 0, 0, tiled=True)
        return wholes + [dot(patches, wholes[0]), parted.reshape(-1, parted.shape[-1])]
    rows = patches.shape[0]
    embed_time = shards[0].shape[0] // cuts[0][0] + GATHER_TIMES[-1]
    chunks = [
        (index, first, rows, column, min(columns, shard.shape[1] - column))
        for index, (shard, (rows, columns)) in enumerate(zip(shards, cuts))
        for first in range(0, shard.shape[0], rows)
        for column in range(0, shard.shape[1], columns)
    ]
    sems = [pltpu.SemaphoreType.DMA((len(chunks), n))] * 2
    return pl.pallas_call(
        functools.partial(gather_kernel, n, chunks, embed_time),
        out_shape=[
            jax.ShapeDtypeStruct((n * shard.shape[0], shard.shape[1]), shard.dtype) for shard in shards
        ]
        + [
            jax.ShapeDtypeStruct((rows, D), F32),
            jax.ShapeDtypeStruct((n * rows, patches.shape[1] // n), BF),
        ],
        in_specs=[pl.BlockSpec(memory_space=pltpu.VMEM)] * (len(shards) + 1),
        out_specs=[pl.BlockSpec(memory_space=pltpu.HBM)] * len(shards)
        + [pl.BlockSpec(memory_space=pltpu.VMEM)] * 2,
        scratch_shapes=[
            pltpu.VMEM((rows, D), F32),
            pltpu.VMEM((2, EMBED_ROWS, D), BF),
            pltpu.SemaphoreType.DMA((2,)),
            pltpu.SemaphoreType.DMA((len(shards),)),
        ]
        + sems
        + [pltpu.SemaphoreType.DMA((n,))] * 2,
        compiler_params=pltpu.CompilerParams(
            collective_id=0, has_side_effects=True, vmem_limit_bytes=24 * 2**20
        ),
        cost_estimate=pl.CostEstimate(flops=0, bytes_accessed=2**25, transcendentals=0),
    )(*shards, patches)


SUM_ROWS, SUM_COLUMNS, SUM_SLOTS = 32, 512, 8
SUM_TIMES = [0, 1, 3, 4, 6, 7]


class Sums:
    def __init__(self, here, find, left, right, out, kept, sent, got, send_sem, recv_sem):
        self.here, self.find, self.left, self.right, self.out = here, find, left, right, out
        self.kept, self.sent, self.got = kept, sent, got
        self.send_sem, self.recv_sem = send_sem, recv_sem
        self.steps = here.halves()[::-1]
        self.chunks = got.shape[0]
        self.times = self.chunks + SUM_TIMES[-1]

    def copy(self, chunk, step):
        blocks, partner = self.steps[step]
        cut = pl.ds(blocks * SUM_ROWS, blocks * SUM_ROWS)
        return remote(
            self.sent.at[chunk % SUM_SLOTS, cut],
            self.got.at[chunk, cut],
            self.send_sem.at[chunk, step],
            self.recv_sem.at[chunk, step],
            partner,
        )

    def sent_all(self, chunk):
        for step in range(len(self.steps)):
            self.copy(chunk, step).wait_send()

    def product(self, chunk, first, rows):
        which, column = self.find(chunk)
        left = self.left[which, pl.ds(first, rows)]
        start = pl.multiple_of(column * SUM_COLUMNS, SUM_COLUMNS)
        return dot(left, self.right[:, pl.ds(start, SUM_COLUMNS)])

    def begin(self, chunk):
        half = self.here.n // 2 * SUM_ROWS
        slot = chunk % SUM_SLOTS

        @pl.when(chunk >= SUM_SLOTS)
        def _():
            self.sent_all(chunk - SUM_SLOTS)

        self.sent[slot, pl.ds(half, half)] = self.product(chunk, half, half).astype(BF)
        self.copy(chunk, 0).start()
        self.kept[slot] = self.product(chunk, 0, half)

    def go_on(self, chunk, step):
        slot, rows = chunk % SUM_SLOTS, self.steps[step - 1][0] * SUM_ROWS
        self.copy(chunk, step - 1).wait_recv()
        total = self.kept[slot, pl.ds(0, rows)] + self.got[chunk, pl.ds(rows, rows)].astype(F32)
        if step == len(self.steps):
            self.out(chunk, total)
            return
        half = rows // 2
        self.sent[slot, pl.ds(half, half)] = total[half:].astype(BF)
        self.copy(chunk, step).start()
        self.kept[slot, pl.ds(0, half)] = total[:half]

    def run(self, first, stop):
        @pl.loop(first, stop)
        def _(time):
            for step in range(len(self.steps), -1, -1):
                chunk = time - SUM_TIMES[step]

                @pl.when((chunk >= 0) & (chunk < self.chunks))
                def _():
                    if step == 0:
                        self.begin(chunk)
                    else:
                        self.go_on(chunk, step)

    def end(self):
        @pl.loop(max(0, self.chunks - SUM_SLOTS), self.chunks)
        def _(chunk):
            self.sent_all(chunk)


def turn(order_ref, left_ref, values_ref):
    for index in range(values_ref.shape[0]):
        left_ref[index] = dot_t(order_ref[...], values_ref[index]).astype(BF)


def lefts_scratch(n, lefts):
    return [pltpu.VMEM((lefts.shape[0], n * SUM_ROWS, lefts.shape[1]), BF)]


def sums_scratch(n, chunks):
    rows, phases = n * SUM_ROWS, n.bit_length() - 1
    return [
        pltpu.VMEM((SUM_SLOTS, rows // 2, SUM_COLUMNS), F32),
        pltpu.VMEM((SUM_SLOTS, rows, SUM_COLUMNS), BF),
        pltpu.VMEM((chunks, rows, SUM_COLUMNS), BF),
        pltpu.SemaphoreType.DMA((chunks, phases)),
        pltpu.SemaphoreType.DMA((chunks, phases)),
    ]


def columns_of(chunk):
    return pl.ds(pl.multiple_of(chunk * SUM_COLUMNS, SUM_COLUMNS), SUM_COLUMNS)


def local_find(chunk):
    return (chunk + 6) // 8, chunk


def last_find(chunk):
    late, rest = chunk // 16, chunk - 16
    return late * (1 + (rest + 7) // 16 + (rest + 5) // 16), chunk


def last_kernel(
    n, grad_ref, parted_ref, small_ref, order_ref, values_ref, right_ref,
    d_weight_ref, d_small_ref, d_unpatch_ref, d_in_ref, d_out_ref,
    known, small_kept, small_got, g_send, g_recv, t_send, t_recv, left_ref, *scratch
):
    here = Place(n)
    rows = grad_ref.shape[0]
    greet(n)
    known[pl.ds(0, rows)] = grad_ref[...]

    @pl.loop(0, n)
    def _(place):
        device = here.device(place)
        small_kept[rows_of(place, 1, LOG_ROWS)] = small_ref[rows_of(device, 1, LOG_ROWS)]

    turn(order_ref, left_ref, values_ref)
    spare = d_in_ref.shape[1] % SUM_COLUMNS

    def store(chunk, total):
        @pl.when(chunk < 16)
        def _():
            d_unpatch_ref[:, columns_of(chunk)] = total

        @pl.when((chunk >= 16) & (chunk < 24))
        def _():
            d_in_ref[:, columns_of(chunk - 16)] = total

        @pl.when(chunk == 24)
        def _():
            d_in_ref[:, pl.ds(8 * SUM_COLUMNS, spare)] = total[:, :spare]

        @pl.when(chunk >= 25)
        def _():
            part = (chunk - 25) // 2
            d_out_ref[rows_of(part, 1, SUM_ROWS), columns_of((chunk - 25) % 2)] = total

    sums = Sums(here, last_find, left_ref, right_ref, store, *scratch)
    steps = here.halves()
    copies = []
    for step in range(len(steps)):
        blocks, partner = steps[step]
        source, target = pl.ds(0, blocks * rows), pl.ds(blocks * rows, blocks * rows)
        gather = remote(known.at[source], known.at[target], g_send.at[step], g_recv.at[step], partner)
        gather.start()
        blocks, partner = steps[::-1][step]
        cut, mine = pl.ds(blocks * LOG_ROWS, blocks * LOG_ROWS), pl.ds(0, blocks * LOG_ROWS)
        told = remote(small_kept.at[cut], small_got.at[cut], t_send.at[step], t_recv.at[step], partner)
        told.start()
        copies += [gather, told]
        sums.run(3 * step, 3 * step + 3)
        gather.wait_recv()
        told.wait_recv()
        small_kept[mine] = small_kept[mine] + small_got[cut]
    sums.run(3 * len(steps), sums.times)
    d_small_ref[...] = small_kept[pl.ds(0, LOG_ROWS)]
    d_weight_ref[...] = lax.dot_general(
        parted_ref[...], known[...], (((0,), (0,)), ((), ())), preferred_element_type=F32
    )
    for copy in copies:
        copy.wait_send()
    sums.end()


def last_sums(n, grad, parted, small, order, lefts, right, projections):
    rows, width = grad.shape[0], parted.shape[1]
    phases, chunks = n.bit_length() - 1, right.shape[1] // SUM_COLUMNS
    return pl.pallas_call(
        functools.partial(last_kernel, n),
        out_shape=[
            jax.ShapeDtypeStruct((width, D), F32),
            jax.ShapeDtypeStruct((LOG_ROWS, 128), F32),
            jax.ShapeDtypeStruct((SUM_ROWS, PATCH * D), F32),
            jax.ShapeDtypeStruct((SUM_ROWS, projections), F32),
            jax.ShapeDtypeStruct((2 * SUM_ROWS, D), F32),
        ],
        in_specs=[pl.BlockSpec(memory_space=pltpu.VMEM)] * 6,
        out_specs=[pl.BlockSpec(memory_space=pltpu.VMEM)] * 5,
        scratch_shapes=[
            pltpu.VMEM((n * rows, D), BF),
            pltpu.VMEM(small.shape, F32),
            pltpu.VMEM(small.shape, F32),
        ]
        + [pltpu.SemaphoreType.DMA((phases,))] * 4
        + lefts_scratch(n, lefts)
        + sums_scratch(n, chunks),
        compiler_params=pltpu.CompilerParams(
            collective_id=1, has_side_effects=True, vmem_limit_bytes=62 * 2**20
        ),
        cost_estimate=pl.CostEstimate(flops=2**32, bytes_accessed=2**24, transcendentals=0),
    )(grad, parted, small, order, lefts, right)


LOG_ROWS = 8


def states_kernel(
    n, reverse, states_ref, logs_ref, order_ref, values_ref, right_ref, out_ref, sum_ref,
    spread, logs, summed, s_send, s_recv, l_send, l_recv, b_send, b_recv, *scratch
):
    me = lax.axis_index("seq")
    rows = states_ref.shape[0] // n
    greet(n)
    sums = None

    def store(chunk, total):
        sum_ref[:, columns_of(chunk)] = total

    if scratch:
        left_ref = scratch[0]
        sums = Sums(Place(n), local_find, left_ref, right_ref, store, *scratch[1:])

    def spreading(other):
        return remote(
            states_ref.at[rows_of(other, 1, rows)],
            spread.at[rows_of(me, 1, rows)],
            s_send.at[other],
            s_recv.at[me],
            other,
        )

    def telling(other):
        target = logs.at[rows_of(me, 1, LOG_ROWS)]
        return remote(logs_ref, target, l_send.at[other], l_recv.at[me], other)

    def returning(other):
        return remote(
            summed.at[rows_of(other, 1, rows)],
            out_ref.at[rows_of(me, 1, rows)],
            b_send.at[other],
            b_recv.at[me],
            other,
        )

    @pl.loop(1, n)
    def _(hop):
        other = lax.rem(me + hop, n)
        spreading(other).start()
        telling(other).start()

    own = pltpu.make_async_copy(
        states_ref.at[rows_of(me, 1, rows)], spread.at[rows_of(me, 1, rows)], s_recv.at[me]
    )
    own_logs = pltpu.make_async_copy(logs_ref, logs.at[rows_of(me, 1, LOG_ROWS)], l_recv.at[me])
    own.start()
    own_logs.start()
    if sums:
        turn(order_ref, left_ref, values_ref)
        sums.run(0, 4)

    @pl.loop(0, n)
    def _(other):
        landed(spread.at[rows_of(other, 1, rows)], s_recv.at[other])
        landed(logs.at[rows_of(other, 1, LOG_ROWS)], l_recv.at[other])

    head = me * MHEADS // n
    lane = lax.broadcasted_iota(jnp.int32, (LOG_ROWS, 128), 1)
    row = lax.broadcasted_iota(jnp.int32, (LOG_ROWS, 128), 0)

    def join(step, total):
        place = n - 1 - step if reverse else step
        cut = rows_of(place, 1, rows)
        summed[cut] = total.astype(BF)
        told = logs[rows_of(place, 1, LOG_ROWS)]
        log = jnp.sum(jnp.where((lane == head) & (row == 0), told, 0.0), keepdims=True)
        flag = jnp.sum(jnp.where((lane == MHEADS) & (row == 0), told, 0.0), keepdims=True)
        decay = jnp.where(flag > 0.0, 0.0, jnp.exp(log))
        return decay * total + spread[cut].astype(F32)

    lax.fori_loop(0, n, join, jnp.zeros((rows, NSTATE), F32))

    @pl.loop(1, n)
    def _(hop):
        returning(lax.rem(me + hop, n)).start()

    own_back = pltpu.make_async_copy(
        summed.at[rows_of(me, 1, rows)], out_ref.at[rows_of(me, 1, rows)], b_recv.at[me]
    )
    own_back.start()
    if sums:
        sums.run(4, sums.times)
        sums.end()

    @pl.loop(0, n)
    def _(other):
        landed(out_ref.at[rows_of(other, 1, rows)], b_recv.at[other])

    @pl.loop(1, n)
    def _(hop):
        other = lax.rem(me + hop, n)
        spreading(other).wait_send()
        telling(other).wait_send()
        returning(other).wait_send()


def pass_states(n, states, logs, reverse, order=None, lefts=None, right=None):
    total = MHEADS * MHEAD_DIM
    told = jnp.zeros((LOG_ROWS, 128), F32).at[0, : logs.shape[0]].set(logs)
    summing = lefts is not None
    chunks = right.shape[1] // SUM_COLUMNS if summing else 0
    small = jnp.zeros((LOG_ROWS, 128), F32)
    operands = [states.reshape(total, NSTATE).astype(BF), told]
    operands += [order, lefts, right] if summing else [small] * 3
    out, found = pl.pallas_call(
        functools.partial(states_kernel, n, reverse),
        out_shape=[
            jax.ShapeDtypeStruct((total, NSTATE), BF),
            jax.ShapeDtypeStruct((SUM_ROWS, chunks * SUM_COLUMNS) if summing else (LOG_ROWS, 128), F32),
        ],
        in_specs=[pl.BlockSpec(memory_space=pltpu.VMEM)] * 5,
        out_specs=[pl.BlockSpec(memory_space=pltpu.VMEM)] * 2,
        scratch_shapes=[
            pltpu.VMEM((total, NSTATE), BF),
            pltpu.VMEM((n * LOG_ROWS, 128), F32),
            pltpu.VMEM((total, NSTATE), BF),
        ]
        + [pltpu.SemaphoreType.DMA((n,))] * 6
        + (lefts_scratch(n, lefts) + sums_scratch(n, chunks) if summing else []),
        compiler_params=pltpu.CompilerParams(
            collective_id=3 if reverse else 2,
            has_side_effects=True,
            vmem_limit_bytes=(48 if summing else 16) * 2**20,
        ),
        cost_estimate=pl.CostEstimate(flops=2**22, bytes_accessed=2**21, transcendentals=0),
    )(*operands)
    return out.astype(F32).reshape(MHEADS, MHEAD_DIM, NSTATE), found


FF_TILE = D


def feed_forward_kernel(
    stream_ref, normed_ref, gate_w_ref, up_w_ref, down_ref, out_ref, gate_ref, up_ref, hid_ref, total
):
    step = pl.program_id(0)
    gate, up = dot(normed_ref[...], whole_of(gate_w_ref)), dot(normed_ref[...], whole_of(up_w_ref))
    hid = (silu(gate) * up).astype(BF)
    gate_ref[...], up_ref[...], hid_ref[...] = gate.astype(BF), up.astype(BF), hid
    found = dot(hid, whole_of(down_ref))

    @pl.when(step == 0)
    def _():
        total[...] = stream_ref[...] + found

    @pl.when(step > 0)
    def _():
        total[...] += found

    @pl.when(step == pl.num_programs(0) - 1)
    def _():
        out_ref[...] = total[...].astype(BF)


def late_blocks(n):
    tiles, block = FF // FF_TILE, FF // n
    return [
        flat_block(n, D // n, lambda i: i),
        flat_block(n, D // n, lambda i: i + tiles),
        pl.BlockSpec((n // tiles, block, D), lambda i: (i, 2 * FF // n // block, 0)),
    ]


def feed_forward(stream, normed, flat):
    rows, tiles = stream.shape[0], FF // FF_TILE
    wide = pl.BlockSpec((rows, D), lambda i: (0, 0))
    tile = pl.BlockSpec((rows, FF_TILE), lambda i: (0, i))
    return pl.pallas_call(
        feed_forward_kernel,
        grid=(tiles,),
        out_shape=[jax.ShapeDtypeStruct((rows, D), BF)]
        + [jax.ShapeDtypeStruct((rows, FF), BF)] * 3,
        in_specs=[
            wide,
            wide,
            *late_blocks(flat.shape[0]),
        ],
        out_specs=[wide, tile, tile, tile],
        scratch_shapes=[pltpu.VMEM((rows, D), F32)],
        compiler_params=pltpu.CompilerParams(vmem_limit_bytes=52 * 2**20),
        cost_estimate=pl.CostEstimate(
            flops=6 * rows * D * FF, bytes_accessed=2**25, transcendentals=rows * FF
        ),
    )(stream, normed, flat, flat, flat)


def feed_forward_back_kernel(
    grad_ref, stream_ref, gain_ref, gate_ref, up_ref, gate_w_ref, up_w_ref, down_ref,
    both_ref, d_stream_ref, d_low_ref, d_gain_ref, total,
):
    step = pl.program_id(0)
    d_hid = dot_t(grad_ref[...], whole_of(down_ref))
    gate, up = gate_ref[...].astype(F32), up_ref[...].astype(F32)
    s = jax.nn.sigmoid(gate)
    d_gate = (d_hid * up * (s * (1.0 + gate * (1.0 - s)))).astype(BF)
    d_up = (d_hid * (gate * s)).astype(BF)
    both_ref[0], both_ref[1] = d_gate, d_up
    found = dot_t(d_gate, whole_of(gate_w_ref)) + dot_t(d_up, whole_of(up_w_ref))

    @pl.when(step == 0)
    def _():
        total[...] = found

    @pl.when(step > 0)
    def _():
        total[...] += found

    @pl.when(step == pl.num_programs(0) - 1)
    def _():
        stream, d_normed = stream_ref[...], total[...]
        r = lax.rsqrt(jnp.mean(stream * stream, axis=-1, keepdims=True) + EPS)
        scaled = gain_ref[...] * d_normed
        inner = jnp.mean(stream * scaled, axis=-1, keepdims=True)
        d_stream = grad_ref[...].astype(F32) + r * scaled - stream * (r * r * r) * inner
        d_stream_ref[...] = d_stream
        d_low_ref[...] = d_stream.astype(BF)
        d_gain_ref[...] = jnp.sum(stream * r * d_normed, axis=0, keepdims=True)


def feed_forward_back(grad, stream, gain, gate, up, flat):
    rows, tiles = stream.shape[0], FF // FF_TILE
    wide = pl.BlockSpec((rows, D), lambda i: (0, 0))
    tile = pl.BlockSpec((rows, FF_TILE), lambda i: (0, i))
    narrow = pl.BlockSpec((1, D), lambda i: (0, 0))
    both, d_stream, d_low, d_gain = pl.pallas_call(
        feed_forward_back_kernel,
        grid=(tiles,),
        out_shape=[
            jax.ShapeDtypeStruct((2, rows, FF), BF),
            jax.ShapeDtypeStruct((rows, D), F32),
            jax.ShapeDtypeStruct((rows, D), BF),
            jax.ShapeDtypeStruct((1, D), F32),
        ],
        in_specs=[
            wide,
            wide,
            narrow,
            tile,
            tile,
            *late_blocks(flat.shape[0]),
        ],
        out_specs=[pl.BlockSpec((2, rows, FF_TILE), lambda i: (0, 0, i)), wide, wide, narrow],
        scratch_shapes=[pltpu.VMEM((rows, D), F32)],
        compiler_params=pltpu.CompilerParams(vmem_limit_bytes=56 * 2**20),
        cost_estimate=pl.CostEstimate(
            flops=6 * rows * D * FF, bytes_accessed=2**25, transcendentals=rows * FF
        ),
    )(grad, stream, gain[None], gate, up, flat, flat, flat)
    return both, d_stream, d_low, d_gain[0]


ATTN_ROWS = 128


def tile_mask():
    row = lax.broadcasted_iota(jnp.int32, (ATTN_ROWS, ATTN_ROWS), 0)
    column = lax.broadcasted_iota(jnp.int32, (ATTN_ROWS, ATTN_ROWS), 1)
    return (row // PATCH == column // PATCH) & (row >= column)


def head_mask(which):
    lane = lax.broadcasted_iota(jnp.int32, (1, 2 * AHEAD_DIM), 1)
    return lane // AHEAD_DIM == which


def only(values, mask):
    return jnp.where(mask, values, jnp.zeros_like(values))


def tile_probs(queries, key_rows, mask):
    scores = dot_t(queries, key_rows) * AHEAD_DIM ** (-0.5)
    scores = jnp.where(mask, scores, -1e30)
    raised = jnp.exp(scores - jnp.max(scores, axis=-1, keepdims=True))
    return raised / jnp.sum(raised, axis=-1, keepdims=True)


def attention_kernel(triple_ref, out_ref):
    mask = tile_mask()
    width = 2 * AHEAD_DIM
    for pair in range(AHEADS // 2):
        queries, key_rows, value_rows = [
            triple_ref[:, part * D + pair * width : part * D + (pair + 1) * width] for part in range(3)
        ]
        total = None
        for which in range(2):
            lanes = head_mask(which)
            probs = tile_probs(only(queries, lanes), key_rows, mask)
            mixed = dot(probs.astype(BF), only(value_rows, lanes))
            total = mixed if total is None else total + mixed
        out_ref[:, pair * width : (pair + 1) * width] = total.astype(BF)


def attention(triple):
    rows = triple.shape[0]
    return pl.pallas_call(
        attention_kernel,
        grid=(rows // ATTN_ROWS,),
        out_shape=jax.ShapeDtypeStruct((rows, D), BF),
        in_specs=[pl.BlockSpec((ATTN_ROWS, 3 * D), lambda i: (i, 0))],
        out_specs=pl.BlockSpec((ATTN_ROWS, D), lambda i: (i, 0)),
    )(triple)


def attention_back_kernel(triple_ref, grad_ref, out_ref):
    mask = tile_mask()
    width = 2 * AHEAD_DIM
    scale = AHEAD_DIM ** (-0.5)
    rows_first = (((0,), (0,)), ((), ()))
    for pair in range(AHEADS // 2):
        lo, hi = pair * width, (pair + 1) * width
        queries, key_rows, value_rows = [
            triple_ref[:, part * D + lo : part * D + hi] for part in range(3)
        ]
        grad = grad_ref[:, lo:hi]
        totals = [None, None, None]
        for which in range(2):
            lanes = head_mask(which)
            probs = tile_probs(only(queries, lanes), key_rows, mask)
            grad_one = only(grad, lanes)
            d_probs = dot_t(grad_one, value_rows)
            d_scores = probs * (d_probs - jnp.sum(probs * d_probs, axis=-1, keepdims=True))
            d_scores = d_scores.astype(BF)
            found = [
                scale * dot(d_scores, only(key_rows, lanes)),
                scale
                * lax.dot_general(
                    d_scores, only(queries, lanes), rows_first, preferred_element_type=F32
                ),
                lax.dot_general(
                    probs.astype(BF), grad_one, rows_first, preferred_element_type=F32
                ),
            ]
            totals = found if which == 0 else [a + b for a, b in zip(totals, found)]
        for part in range(3):
            out_ref[:, part * D + lo : part * D + hi] = totals[part].astype(BF)


def attention_back(triple, grad):
    rows = triple.shape[0]
    return pl.pallas_call(
        attention_back_kernel,
        grid=(rows // ATTN_ROWS,),
        out_shape=jax.ShapeDtypeStruct((rows, 3 * D), BF),
        in_specs=[
            pl.BlockSpec((ATTN_ROWS, 3 * D), lambda i: (i, 0)),
            pl.BlockSpec((ATTN_ROWS, D), lambda i: (i, 0)),
        ],
        out_specs=pl.BlockSpec((ATTN_ROWS, 3 * D), lambda i: (i, 0)),
    )(triple, grad)


def local(
    byte_acts,
    resets,
    out_grad,
    patch_weight,
    patch_gain,
    mixer_in,
    conv_weight,
    conv_bias,
    head_params,
    mixer_gain,
    mixer_out,
    unpatch_weight,
    attn_gain,
    qkv_weight,
    attn_out,
    ffn_gain,
    gate_up,
    down_weight,
):
    n = lax.axis_size("seq")
    me = lax.axis_index("seq")
    ring = Ring(n)

    def passed_along(block, distance):
        route = [(i - distance, i) for i in range(n) if 0 <= i - distance < n]
        return lax.ppermute(block, "seq", route)

    live = Live()
    order = ring.order()

    byte_wide = byte_acts.astype(F32)
    patches = byte_acts.reshape(-1, PATCH * D)
    patch_rows = patches.shape[0]
    early = gather_flat(n, [unpatch_weight, qkv_weight, attn_out])
    late = gather_flat(n, [gate_up, down_weight])
    small = [patch_gain, conv_weight.reshape(-1), conv_bias, mixer_gain, attn_gain, ffn_gain]
    cuts = list(np.cumsum([piece.shape[0] for piece in small]))
    small_shard = jnp.concatenate(small)
    small_shard = jnp.pad(small_shard, (0, -small_shard.shape[0] % 2048)).reshape(-1, 128)
    live.patch_w, live.mixer_in, live.mixer_out, small_all, embedded, live.parted = gather_weights(
        n,
        [
            patch_weight,
            jnp.pad(mixer_in, ((0, 0), (0, -mixer_in.shape[1] % 128))),
            mixer_out,
            small_shard,
        ],
        [(32, D), (16, 2304), (32, D), (16, 128)],
        patches,
    )
    small_all = small_all.reshape(n, -1)[:, : cuts[-1]].astype(F32)
    parts = jnp.split(small_all, cuts[:-1], axis=1)
    live.patch_gain = parts[0].reshape(-1)
    live.conv_weight = parts[1].reshape(n, CONV, -1).transpose(1, 0, 2).reshape(CONV, CONV_CH)
    live.conv_bias, live.mixer_gain, live.attn_gain, live.ffn_gain = [
        piece.reshape(-1) for piece in parts[2:]
    ]
    live.embedded = embedded
    live.normed = rms_scale(live.embedded, live.patch_gain).astype(BF)
    projected = dot(live.normed, live.mixer_in)
    live.gate_z = projected[:, :DI]
    conv_in = projected[:, DI : DI + CONV_CH].astype(BF).astype(F32)
    dt_raw = projected[:, DI + CONV_CH : DI + CONV_CH + MHEADS]
    logs = jnp.sum(-jax.nn.softplus(dt_raw + head_params[0]) * jnp.exp(head_params[1]), axis=0)
    flag = jnp.max(resets).astype(F32)
    live.logs = jnp.concatenate([logs, flag[None]])
    not_reset = 1.0 - resets.astype(F32)
    keep_tail = jnp.concatenate(
        [jnp.cumprod(not_reset[patch_rows - CONV + 2 :][::-1])[::-1], jnp.ones((1,), F32)]
    )
    tail_sent = (conv_in[patch_rows - CONV + 1 :] * keep_tail[:, None]).astype(BF)
    halo_rows = passed_along(tail_sent, 1)
    flags_ext = jnp.concatenate([jnp.zeros((CONV - 1,), jnp.int32), resets])
    validity = tap_masks(flags_ext, patch_rows)
    conv_ext = jnp.concatenate([halo_rows.astype(F32), conv_in])
    conv_out, conv_back = jax.vjp(
        functools.partial(conv_apply, validity=validity, row_count=patch_rows),
        conv_ext,
        live.conv_weight,
        live.conv_bias,
    )
    state_parts, state_back = jax.vjp(
        functools.partial(block_state, starts=resets), conv_out, dt_raw, head_params
    )
    local_state, decay_total = state_parts
    live.state_in, _ = pass_states(n, local_state, live.logs, False)
    live.fence()

    mixer_y, output_back = jax.vjp(
        functools.partial(block_output, starts=resets),
        conv_out,
        dt_raw,
        head_params,
        live.state_in,
    )
    gate_act = silu(live.gate_z)
    gated = mixer_y * gate_act
    live.gated_norm = rms_scale(gated, live.mixer_gain).astype(BF)
    branch = dot(live.gated_norm, live.mixer_out)
    live.hidden = (live.embedded + branch).astype(BF)
    live.early = early
    slots = flat_dot(live.hidden, live.early, 0, PATCH, F32)
    live.stream0 = byte_wide + slots.reshape(-1, D)
    live.normed0 = rms_scale(live.stream0, live.attn_gain).astype(BF)
    live.fence()

    rows = byte_wide.shape[0]
    live.triple = flat_dot(live.normed0, live.early, PATCH, 3, BF)
    live.mixed = attention(live.triple)
    live.stream1 = live.stream0 + flat_dot(live.mixed, live.early, PATCH + 3, 1, F32)
    live.normed1 = rms_scale(live.stream1, live.ffn_gain).astype(BF)
    live.late = late
    layer_out, gate, up, hid = feed_forward(live.stream1, live.normed1, live.late)
    live.gate, live.up, live.hid = gate, up, hid
    live.fence()

    small_slice = n == 32

    def lefts_of(*values):
        parts = []
        for value in values:
            cut = value.reshape(value.shape[0], n, -1, SUM_ROWS).transpose(2, 0, 1, 3)
            parts.append(cut.reshape(-1, value.shape[0], n * SUM_ROWS))
        return jnp.concatenate(parts, axis=0)

    if small_slice:
        place = jnp.arange(n * SUM_ROWS)
        source = jnp.repeat(order * SUM_ROWS, SUM_ROWS) + place % SUM_ROWS
        live.order = (place[None, :] == source[:, None]).astype(BF)

    d_both, d_stream1, d_stream1_low, g_ffn_gain = feed_forward_back(
        out_grad, live.stream1, live.ffn_gain, live.gate, live.up, live.late
    )
    if small_slice:
        block = down_weight.shape[0]
        flat = flat_grads(n, live.hid, out_grad, live.normed1, d_both)
        found = lax.psum_scatter(flat, "seq", scatter_dimension=0, tiled=True)[0].astype(F32)
        g_down = found[:block]
        g_gate_up = found[block:].reshape(-1, SUM_ROWS, D).transpose(1, 0, 2)
        g_gate_up = g_gate_up.reshape(SUM_ROWS, -1)
    else:
        g_down = summed_grad(live.hid, out_grad)
        g_gate_up = summed_grad(live.normed1, jnp.concatenate([d_both[0], d_both[1]], axis=1))
    d_mixed = flat_dot_t(d_stream1_low, live.early, PATCH + 3, 1).astype(BF)
    d_triple = attention_back(live.triple, d_mixed)
    d_stream0, g_attn_gain = rms_back(live.stream0, live.attn_gain, flat_dot_t(d_triple, live.early, PATCH, 3))
    live.d_stream0 = (d_stream1 + d_stream0).reshape(patch_rows, PATCH * D)
    d_slots = live.d_stream0.astype(BF)
    d_hidden = flat_dot_t(d_slots, live.early, 0, PATCH)
    d_branch = d_hidden.astype(BF)
    d_gated, g_mixer_gain = rms_back(gated, live.mixer_gain, dot_t(d_branch, live.mixer_out))
    d_gate_z = d_gated * mixer_y * silu_slope(live.gate_z)
    output_grads = output_back(d_gated * gate_act)
    summed = []
    if small_slice:
        summed = [
            live.order,
            jnp.stack([live.mixed, live.normed0]),
            jnp.concatenate([d_stream1_low, d_triple], axis=1),
        ]
    state_grad, found = pass_states(n, output_grads[3], live.logs, True, *summed)
    g_attn_out, g_qkv = found[:, :D], found[:, D:]
    decay_grad = jnp.sum(state_grad * live.state_in, axis=(1, 2))
    state_cot = state_back((state_grad, decay_grad))
    conv_cot = conv_back(output_grads[0] + state_cot[0])
    returned = passed_along(conv_cot[0][: CONV - 1], -1)
    d_conv_in = conv_cot[0][CONV - 1 :] + jnp.concatenate(
        [jnp.zeros((patch_rows - CONV + 1, CONV_CH), F32), returned * keep_tail[:, None]]
    )
    d_dt = output_grads[1] + state_cot[1]
    d_projected = jnp.concatenate([d_gate_z, d_conv_in, d_dt], axis=1).astype(BF)
    d_projected = jnp.pad(d_projected, ((0, 0), (0, -d_projected.shape[1] % 128)))
    d_embedded, g_patch_gain = rms_back(
        live.embedded, live.patch_gain, dot_t(d_projected, live.mixer_in)
    )
    d_embedded = (d_hidden + d_embedded).astype(BF)
    input_grad = input_gradient(live.d_stream0, d_embedded, live.patch_w).reshape(-1, D)

    g_conv_weight = conv_cot[1].reshape(CONV, n, -1).transpose(1, 0, 2).reshape(n, -1)
    g_head = jnp.broadcast_to((output_grads[2] + state_cot[2]).reshape(1, -1), (n, 3 * MHEADS))
    g_small = [g_patch_gain, g_conv_weight, conv_cot[2], g_mixer_gain, g_attn_gain, g_ffn_gain, g_head]
    g_small = jnp.concatenate([piece.reshape(n, -1) for piece in g_small], axis=1)
    small_width = g_small.shape[1]
    g_small = jnp.pad(g_small, ((0, 0), (0, LOG_ROWS * 128 - small_width)))
    g_small = g_small.reshape(n * LOG_ROWS, 128)
    if small_slice:
        d_projected = jnp.pad(d_projected, ((0, 0), (0, -d_projected.shape[1] % SUM_COLUMNS)))
        g_patch, g_small, g_unpatch, g_mixer_in, g_mixer_out = last_sums(
            n,
            d_embedded,
            live.parted,
            g_small,
            live.order,
            lefts_of(live.hidden, live.normed, live.gated_norm),
            jnp.concatenate([d_slots, d_projected, d_branch, d_branch], axis=1),
            mixer_in.shape[1],
        )
    else:
        g_attn_out = summed_grad(live.mixed, d_stream1_low)
        g_qkv = summed_grad(live.normed0, d_triple)
        known = lax.all_gather(d_embedded, "seq", axis=0, tiled=True)
        g_patch = dot(live.parted.T, known)
        g_small = lax.psum_scatter(g_small, "seq", scatter_dimension=0, tiled=True)
        g_unpatch = summed_grad(live.hidden, d_slots)
        g_mixer_in = summed_grad(live.normed, d_projected)[:, : mixer_in.shape[1]]
        g_mixer_out = summed_grad(live.gated_norm, d_branch)
    g_small = g_small.reshape(-1)[:small_width]
    s = jnp.split(g_small, cuts)
    return (
        layer_out,
        input_grad,
        g_patch,
        s[0],
        g_mixer_in,
        s[1].reshape(CONV, -1),
        s[2],
        s[6].reshape(3, MHEADS),
        s[3],
        g_mixer_out,
        g_unpatch,
        s[4],
        g_qkv,
        g_attn_out,
        s[5],
        g_gate_up,
        g_down,
    )


def solution(mesh):
    rows, vector = P("seq", None), P("seq")
    placed = (
        rows, vector, rows, rows, vector, rows, P(None, "seq"), vector, P(),
        vector, rows, rows, vector, rows, rows, vector, rows, rows,
    )
    returned = (
        rows, rows, rows, vector, rows, P(None, "seq"), vector, P(), vector,
        rows, rows, vector, rows, rows, vector, rows, rows,
    )
    return jax.shard_map(
        local, mesh=mesh, in_specs=placed, out_specs=returned, check_vma=False
    )
```

```python
import functools

import jax
import jax.numpy as jnp
import numpy as np
from jax import lax
from jax.experimental import pallas as pl
from jax.experimental.pallas import tpu as pltpu
from jax.sharding import PartitionSpec as P

D = 1024
PATCH = 8
MHEADS = 32
MHEAD_DIM = 64
DI = 2048
NSTATE = 128
CONV = 4
AHEADS = 16
AHEAD_DIM = 64
FF = 4096
CONV_CH = 2304

EPS = 1e-05
HIGH = lax.Precision.HIGHEST
BF = jnp.bfloat16
F32 = jnp.float32


class Ring:
    def __init__(self, n):
        self.n = n
        self.depth = n // 8
        coords = [(i // 8, (i // 4) % 2, (i // 2) % 2, i % 2) for i in range(n)]

        def index(z, y, x, c):
            return ((z * 2 + y) * 2 + x) * 2 + c

        def flip(z, y, x, c, along_x):
            return index(z, y, 1 - x, c) if along_x else index(z, 1 - y, x, c)

        self.core = [(index(*p), index(*p) ^ 1) for p in coords]
        self.first = [(index(*p), flip(*p, p[3] == 0)) for p in coords]
        self.second = [(index(*p), flip(*p, p[3] == 1)) for p in coords]
        self.bits = [1 << b for b in range(self.depth.bit_length() - 1)]
        self.along = {
            bit: [(index(*p), index(p[0] ^ bit, *p[1:])) for p in coords] for bit in self.bits
        }
        table = np.zeros((n, n), np.int32)
        for me, (z, y, x, c) in enumerate(coords):
            place = 0
            for rc in range(2):
                owner = c ^ rc
                for r2 in range(2):
                    for r1 in range(2):
                        rx, ry = (r1, r2) if owner == 0 else (r2, r1)
                        for rz in range(self.depth):
                            table[me, place] = index(z ^ rz, y ^ ry, x ^ rx, owner)
                            place += 1
        self.table = table

    def order(self):
        return jnp.asarray(self.table)[lax.axis_index("seq")]


def swap(block, route):
    return lax.ppermute(block, "seq", route)


def flat_kernel(*refs):
    out, first = refs[-1], 0
    for ref in refs[:-1]:
        rows = ref.shape[0]
        for column in range(0, ref.shape[1], D):
            out[pl.ds(first, rows)] = ref[:, pl.ds(column, D)]
            first += rows


def flat_rows(shards):
    total = sum(shard.shape[0] * shard.shape[1] // D for shard in shards)
    return pl.pallas_call(
        flat_kernel,
        out_shape=jax.ShapeDtypeStruct((total, D), BF),
        in_specs=[pl.BlockSpec(memory_space=pltpu.VMEM)] * len(shards),
        out_specs=pl.BlockSpec(memory_space=pltpu.VMEM),
    )(*shards)


def gather_flat(n, shards):
    return lax.all_gather(flat_rows(shards), "seq", axis=0)


def flat_block(n, rows, place):
    return pl.BlockSpec((n, rows, D), lambda i: (0, place(i), 0))


def whole_of(ref):
    return ref[...].reshape(-1, ref.shape[-1])


def flat_dot_kernel(values_ref, flat_ref, out_ref):
    out_ref[...] = dot(values_ref[...], whole_of(flat_ref)).astype(out_ref.dtype)


def flat_dot(values, flat, first, count, kind):
    n, rows = flat.shape[0], values.shape[0]
    return pl.pallas_call(
        flat_dot_kernel,
        grid=(count,),
        out_shape=jax.ShapeDtypeStruct((rows, count * D), kind),
        in_specs=[
            pl.BlockSpec((rows, D), lambda i: (0, 0)),
            flat_block(n, D // n, lambda i: first + i),
        ],
        out_specs=pl.BlockSpec((rows, D), lambda i: (0, i)),
        compiler_params=pltpu.CompilerParams(vmem_limit_bytes=56 * 2**20),
        cost_estimate=pl.CostEstimate(
            flops=2 * rows * D * D * count, bytes_accessed=2 * D * D * count, transcendentals=0
        ),
    )(values, flat)


def flat_dot_t_kernel(values_ref, flat_ref, out_ref, total):
    few = values_ref.shape[0] < 256
    step = pl.program_id(0)
    if few:
        found = dot_t(whole_of(flat_ref), values_ref[...])
    else:
        found = dot_t(values_ref[...], whole_of(flat_ref))

    @pl.when(step == 0)
    def _():
        total[...] = found

    @pl.when(step > 0)
    def _():
        total[...] += found

    @pl.when(step == pl.num_programs(0) - 1)
    def _():
        out_ref[...] = total[...].T if few else total[...]


def flat_dot_t(values, flat, first, count):
    n, rows = flat.shape[0], values.shape[0]
    return pl.pallas_call(
        flat_dot_t_kernel,
        grid=(count,),
        out_shape=jax.ShapeDtypeStruct((rows, D), F32),
        in_specs=[
            pl.BlockSpec((rows, D), lambda i: (0, i)),
            flat_block(n, D // n, lambda i: first + i),
        ],
        out_specs=pl.BlockSpec((rows, D), lambda i: (0, 0)),
        scratch_shapes=[pltpu.VMEM((D, rows) if rows < 256 else (rows, D), F32)],
        compiler_params=pltpu.CompilerParams(vmem_limit_bytes=56 * 2**20),
        cost_estimate=pl.CostEstimate(
            flops=2 * rows * D * D * count, bytes_accessed=2 * D * D * count, transcendentals=0
        ),
    )(values, flat)


def input_grad_kernel(direct_ref, grad_ref, weight_ref, out_ref):
    out_ref[...] = (direct_ref[...] + dot_t(weight_ref[...], grad_ref[...]).T).astype(BF)


def input_gradient(direct, grad, weight):
    rows, columns = direct.shape
    return pl.pallas_call(
        input_grad_kernel,
        grid=(columns // D,),
        out_shape=jax.ShapeDtypeStruct((rows, columns), BF),
        in_specs=[
            pl.BlockSpec((rows, D), lambda i: (0, i)),
            pl.BlockSpec((rows, D), lambda i: (0, 0)),
            pl.BlockSpec((D, D), lambda i: (i, 0)),
        ],
        out_specs=pl.BlockSpec((rows, D), lambda i: (0, i)),
        compiler_params=pltpu.CompilerParams(vmem_limit_bytes=56 * 2**20),
        cost_estimate=pl.CostEstimate(
            flops=2 * rows * columns * D, bytes_accessed=2 * columns * D, transcendentals=0
        ),
    )(direct, grad, weight)


class Live:
    def fence(self):
        vars(self).update(lax.optimization_barrier(dict(vars(self))))


def summed_grad(left, right):
    product = lax.dot_general(left, right, (((0,), (0,)), ((), ())), preferred_element_type=F32)
    summed = lax.psum_scatter(product.astype(BF), "seq", scatter_dimension=0, tiled=True)
    return summed.astype(F32)


def flat_grad_kernel(hid_ref, grad_ref, normed_ref, both_ref, out_ref):
    devices, block = out_ref.shape[:2]
    parts = block // SUM_ROWS

    def product(left, right):
        return lax.dot_general(
            left, right, (((0,), (0,)), ((), ())), preferred_element_type=F32
        ).astype(BF)

    @pl.when(pl.program_id(0) < 4)
    def _():
        few = devices // parts
        for part in range(parts):
            cut = pl.ds(part * few * block, few * block)
            found = product(hid_ref[:, cut], grad_ref[...])
            out_ref[pl.ds(part * few, few)] = found.reshape(few, block, D)

    @pl.when(pl.program_id(0) >= 4)
    def _():
        for part in range(parts):
            found = product(normed_ref[...], both_ref[0, :, pl.ds(part * D, D)])
            cut = pl.ds(part * SUM_ROWS, SUM_ROWS)
            out_ref[:, cut] = found.reshape(devices, SUM_ROWS, D)


def flat_grads(n, hid, out_grad, normed, both):
    rows, block, devices = hid.shape[0], hid.shape[1] // n, n // 4

    def late(step):
        return jnp.maximum(step - 4, 0)

    return pl.pallas_call(
        flat_grad_kernel,
        grid=(12,),
        out_shape=jax.ShapeDtypeStruct((n, 3 * block, D), BF),
        in_specs=[
            pl.BlockSpec((rows, devices * block), lambda i: (0, jnp.minimum(i, 3))),
            pl.BlockSpec((rows, D), lambda i: (0, 0)),
            pl.BlockSpec((rows, devices * SUM_ROWS), lambda i: (0, late(i) % 4)),
            pl.BlockSpec((1, rows, FF), lambda i: (late(i) // 4, 0, 0)),
        ],
        out_specs=pl.BlockSpec(
            (devices, block, D), lambda i: (i % 4, jnp.minimum(i // 4, 1) + late(i) // 4, 0)
        ),
        compiler_params=pltpu.CompilerParams(vmem_limit_bytes=56 * 2**20),
        cost_estimate=pl.CostEstimate(
            flops=6 * rows * FF * D, bytes_accessed=2**25, transcendentals=0
        ),
    )(hid, out_grad, normed, both)


def dot(left, right):
    return jnp.dot(left, right, preferred_element_type=F32)


def dot_t(left, right):
    return lax.dot_general(left, right, (((1,), (1,)), ((), ())), preferred_element_type=F32)


def rms_scale(values, gain):
    return values * lax.rsqrt(jnp.mean(values * values, axis=-1, keepdims=True) + EPS) * gain


def rms_back(values, gain, grad):
    r = lax.rsqrt(jnp.mean(values * values, axis=-1, keepdims=True) + EPS)
    scaled = gain * grad
    inner = jnp.mean(values * scaled, axis=-1, keepdims=True)
    return r * scaled - values * (r * r * r) * inner, jnp.sum(values * r * grad, axis=0)


def silu(v):
    return v * jax.nn.sigmoid(v)


def silu_slope(v):
    s = jax.nn.sigmoid(v)
    return s * (1.0 + v * (1.0 - s))


def tap_masks(flags_ext, row_count):
    not_reset = 1.0 - flags_ext.astype(F32)
    validity = [jnp.ones((row_count,), F32)]
    for offset in range(1, CONV):
        validity.append(validity[-1] * not_reset[CONV - offset : CONV - offset + row_count])
    return validity


def conv_apply(conv_ext, conv_weight, conv_bias, validity, row_count):
    summed = conv_bias + conv_ext[CONV - 1 : CONV - 1 + row_count] * conv_weight[0]
    for offset in range(1, CONV):
        summed = (
            summed
            + validity[offset][:, None]
            * conv_ext[CONV - 1 - offset : CONV - 1 - offset + row_count]
            * conv_weight[offset]
        )
    return jax.nn.silu(summed)


def block_parts(conv_out, dt_raw, head_params, starts):
    row_count = conv_out.shape[0]
    values = conv_out[:, :DI].reshape(row_count, MHEADS, MHEAD_DIM)
    key_rows = conv_out[:, DI : DI + NSTATE]
    queries = conv_out[:, DI + NSTATE :]
    step_size = jax.nn.softplus(dt_raw + head_params[0])
    cumlog = jnp.cumsum(-step_size * jnp.exp(head_params[1]), axis=0)
    segment = jnp.cumsum(starts, axis=0, dtype=jnp.int32)
    return (values, key_rows, queries, step_size, cumlog, segment)


def block_state(conv_out, dt_raw, head_params, starts):
    values, key_rows, queries, step_size, cumlog, segment = block_parts(
        conv_out, dt_raw, head_params, starts
    )
    same_doc = (segment == segment[-1]).astype(F32)
    weighting = jnp.exp(cumlog[-1][None, :] - cumlog) * same_doc[:, None] * step_size
    state_out = jnp.einsum("rh,rhp,rn->hpn", weighting, values, key_rows, precision=HIGH)
    decay_total = jnp.exp(cumlog[-1]) * (segment[-1] == 0).astype(F32)
    return (state_out, decay_total)


def block_output(conv_out, dt_raw, head_params, state_in, starts):
    values, key_rows, queries, step_size, cumlog, segment = block_parts(
        conv_out, dt_raw, head_params, starts
    )
    position = jnp.arange(conv_out.shape[0])
    causal = (position[:, None] >= position[None, :]) & (segment[:, None] == segment[None, :])
    log_gaps = jnp.where(causal[:, :, None], cumlog[:, None, :] - cumlog[None, :, :], 0.0)
    decays = jnp.exp(log_gaps) * causal[:, :, None].astype(F32)
    scores = jnp.dot(queries, key_rows.T, precision=HIGH)
    mixing = scores[:, :, None] * decays * step_size[None, :, :]
    within = jnp.einsum("tsh,shp->thp", mixing, values, precision=HIGH)
    inflow = jnp.exp(cumlog) * (segment == 0).astype(F32)[:, None]
    carried = jnp.einsum("tn,hpn->thp", queries, state_in, precision=HIGH) * inflow[:, :, None]
    skipped = head_params[2][None, :, None] * values
    return (within + carried + skipped).reshape(conv_out.shape[0], DI)


MESH = pl.DeviceIdType.MESH


class Place:
    def __init__(self, n):
        self.n, self.depth = n, n // 8
        self.me = me = lax.axis_index("seq")
        self.z, self.y, self.x, self.c = me // 8, (me // 4) % 2, (me // 2) % 2, me % 2

    def flipped(self, rz, ry, rx, rc):
        z, bit = 0, 1
        while bit < self.depth:
            z = z + ((self.z // bit + rz // bit) % 2) * bit
            bit *= 2
        y, x, c = (self.y + ry) % 2, (self.x + rx) % 2, (self.c + rc) % 2
        return ((z * 2 + y) * 2 + x) * 2 + c

    def split(self, place):
        depth = self.depth
        rz, r1, r2 = place % depth, (place // depth) % 2, (place // (2 * depth)) % 2
        return rz, r1, r2, place // (4 * depth)

    def device(self, place):
        rz, r1, r2, rc = self.split(place)
        owner = (self.c + rc) % 2
        return self.flipped(rz, r2 + owner * (r1 - r2), r1 + owner * (r2 - r1), rc)

    def place_there(self, place):
        rz, r1, r2, rc = self.split(place)
        s1, s2 = r1 + rc * (r2 - r1), r2 + rc * (r1 - r2)
        return ((rc * 2 + s2) * 2 + s1) * self.depth + rz

    def halves(self):
        steps, bit = [], 1
        while bit < self.depth:
            steps.append((bit, self.flipped(bit, 0, 0, 0)))
            bit *= 2
        steps.append((self.depth, self.flipped(0, self.c, 1 - self.c, 0)))
        steps.append((2 * self.depth, self.flipped(0, 1 - self.c, self.c, 0)))
        steps.append((4 * self.depth, self.flipped(0, 0, 0, 1)))
        return steps


def greet(n):
    barrier = pltpu.get_barrier_semaphore()
    me = lax.axis_index("seq")

    @pl.loop(1, n)
    def _(hop):
        other = lax.rem(me + hop, n)
        pl.semaphore_signal(barrier, inc=1, device_id=(other,), device_id_type=MESH)

    pl.semaphore_wait(barrier, n - 1)


def remote(source, target, send_sem, recv_sem, device):
    return pltpu.make_async_remote_copy(
        src_ref=source,
        dst_ref=target,
        send_sem=send_sem,
        recv_sem=recv_sem,
        device_id=(device,),
        device_id_type=MESH,
    )


def landed(ref, sem):
    pltpu.make_async_copy(ref, ref, sem).wait()


def rows_of(place, count, rows):
    return pl.ds(pl.multiple_of(place * rows, rows), count * rows)


GATHER_TIMES = [0, 1, 2, 3, 5, 6]


EMBED_ROWS = 1024


def gather_kernel(n, chunks, embed_time, *refs):
    count = (len(refs) - 11) // 2
    shards, patches_ref, wholes = refs[:count], refs[count], refs[count + 1 : -10]
    embedded_ref, parted_ref, total, held, held_sem, own_sem = refs[-10:-4]
    send_sem, recv_sem, part_send, part_recv = refs[-4:]
    here = Place(n)
    greet(n)
    owns = []
    for index in range(count):
        rows = shards[index].shape[0]
        target = wholes[index].at[rows_of(here.me, 1, rows)]
        owns.append(pltpu.make_async_copy(shards[index], target, own_sem.at[index]))
        owns[-1].start()
    for own in owns:
        own.wait()
    steps = here.halves()

    def block(chunk, place):
        index, first, rows, column, columns = chunks[chunk]
        start = here.device(place) * shards[index].shape[0] + first
        return wholes[index].at[pl.ds(pl.multiple_of(start, 16), rows), pl.ds(column, columns)]

    def sending(chunk, step, place):
        blocks, partner = steps[step]
        there = blocks + place
        ref = block(chunk, place)
        return remote(ref, ref, send_sem.at[chunk, there], recv_sem.at[chunk, there], partner)

    def arrive(chunk, step):
        blocks = steps[step][0]

        @pl.loop(blocks, 2 * blocks)
        def _(place):
            landed(block(chunk, place), recv_sem.at[chunk, place])

    def send(chunk, step):
        @pl.loop(0, steps[step][0])
        def _(place):
            sending(chunk, step, place).start()

    rows, width = patches_ref.shape[0], patches_ref.shape[1] // n

    def part_of(place):
        start = pl.multiple_of(here.device(place) * width, 128)
        return patches_ref.at[:, pl.ds(start, width)]

    def parting(place):
        there = here.place_there(place)
        target = parted_ref.at[rows_of(there, 1, rows)]
        return remote(
            part_of(place), target, part_send.at[place], part_recv.at[there], here.device(place)
        )

    pieces = wholes[0].shape[0] // EMBED_ROWS

    def fetch(piece):
        source = wholes[0].at[pl.ds(piece * EMBED_ROWS, EMBED_ROWS)]
        return pltpu.make_async_copy(source, held.at[piece % 2], held_sem.at[piece % 2])

    def embed(piece):
        if piece == 0:
            fetch(0).start()
        if piece + 1 < pieces:
            fetch(piece + 1).start()
        fetch(piece).wait()
        found = dot(patches_ref[:, pl.ds(piece * EMBED_ROWS, EMBED_ROWS)], held[piece % 2])
        total[...] = found if piece == 0 else total[...] + found

    done = 0
    own_part = pltpu.make_async_copy(part_of(0), parted_ref.at[rows_of(0, 1, rows)], part_recv.at[0])
    for time in range(len(chunks) + GATHER_TIMES[-1]):
        if time == embed_time:
            own_part.start()

            @pl.loop(1, n)
            def _(place):
                parting(place).start()

        for step in range(len(steps), -1, -1):
            chunk = time - GATHER_TIMES[step]
            if 0 <= chunk < len(chunks):
                if step > 0:
                    arrive(chunk, step - 1)
                if step < len(steps):
                    send(chunk, step)
        for _ in range(2):
            if time >= embed_time and done < pieces:
                embed(done)
                done += 1
    for piece in range(done, pieces):
        embed(piece)
    embedded_ref[...] = total[...]

    @pl.loop(0, n)
    def _(place):
        landed(parted_ref.at[rows_of(place, 1, rows)], part_recv.at[place])

    @pl.loop(1, n)
    def _(place):
        parting(place).wait_send()

    for chunk in range(len(chunks)):
        for step in range(len(steps)):

            @pl.loop(0, steps[step][0])
            def _(place):
                sending(chunk, step, place).wait_send()


def gather_weights(n, shards, cuts, patches):
    if n != 32 or any(shard.shape[0] % 16 for shard in shards):
        wholes = [lax.all_gather(shard, "seq", axis=0, tiled=True) for shard in shards]
        parted = patches.reshape(patches.shape[0], n, -1).transpose(1, 0, 2)
        parted = lax.all_to_all(parted, "seq", 0, 0, tiled=True)
        return wholes + [dot(patches, wholes[0]), parted.reshape(-1, parted.shape[-1])]
    rows = patches.shape[0]
    embed_time = shards[0].shape[0] // cuts[0][0] + GATHER_TIMES[-1]
    chunks = [
        (index, first, rows, column, min(columns, shard.shape[1] - column))
        for index, (shard, (rows, columns)) in enumerate(zip(shards, cuts))
        for first in range(0, shard.shape[0], rows)
        for column in range(0, shard.shape[1], columns)
    ]
    sems = [pltpu.SemaphoreType.DMA((len(chunks), n))] * 2
    return pl.pallas_call(
        functools.partial(gather_kernel, n, chunks, embed_time),
        out_shape=[
            jax.ShapeDtypeStruct((n * shard.shape[0], shard.shape[1]), shard.dtype) for shard in shards
        ]
        + [
            jax.ShapeDtypeStruct((rows, D), F32),
            jax.ShapeDtypeStruct((n * rows, patches.shape[1] // n), BF),
        ],
        in_specs=[pl.BlockSpec(memory_space=pltpu.VMEM)] * (len(shards) + 1),
        out_specs=[pl.BlockSpec(memory_space=pltpu.HBM)] * len(shards)
        + [pl.BlockSpec(memory_space=pltpu.VMEM)] * 2,
        scratch_shapes=[
            pltpu.VMEM((rows, D), F32),
            pltpu.VMEM((2, EMBED_ROWS, D), BF),
            pltpu.SemaphoreType.DMA((2,)),
            pltpu.SemaphoreType.DMA((len(shards),)),
        ]
        + sems
        + [pltpu.SemaphoreType.DMA((n,))] * 2,
        compiler_params=pltpu.CompilerParams(
            collective_id=0, has_side_effects=True, vmem_limit_bytes=24 * 2**20
        ),
        cost_estimate=pl.CostEstimate(flops=0, bytes_accessed=2**25, transcendentals=0),
    )(*shards, patches)


SUM_ROWS, SUM_COLUMNS, SUM_SLOTS = 32, 512, 8
SUM_TIMES = [0, 1, 3, 4, 6, 7]


def columns_of(chunk):
    return pl.ds(pl.multiple_of(chunk * SUM_COLUMNS, SUM_COLUMNS), SUM_COLUMNS)


class Sums:
    def __init__(self, here, sources, out, kept, sent, got, send_sem, recv_sem):
        self.here, self.sources, self.out = here, sources, out
        self.kept, self.sent, self.got = kept, sent, got
        self.send_sem, self.recv_sem = send_sem, recv_sem
        self.steps = here.halves()[::-1]
        self.chunks = got.shape[0]
        self.times = self.chunks + SUM_TIMES[-1]

    def copy(self, chunk, step):
        blocks, partner = self.steps[step]
        cut = pl.ds(blocks * SUM_ROWS, blocks * SUM_ROWS)
        return remote(
            self.sent.at[chunk % SUM_SLOTS, cut],
            self.got.at[chunk, cut],
            self.send_sem.at[chunk, step],
            self.recv_sem.at[chunk, step],
            partner,
        )

    def sent_all(self, chunk):
        for step in range(len(self.steps)):
            self.copy(chunk, step).wait_send()

    def begin(self, chunk):
        half = self.here.n // 2 * SUM_ROWS
        slot = chunk % SUM_SLOTS

        @pl.when(chunk >= SUM_SLOTS)
        def _():
            self.sent_all(chunk - SUM_SLOTS)

        for first, stop, find, left, right in self.sources:

            @pl.when((chunk >= first) & (chunk < stop))
            def _():
                which, column = find(chunk - first)

                def product(row):
                    return dot(left[which, pl.ds(row, half)], right[:, columns_of(column)])

                self.sent[slot, pl.ds(half, half)] = product(half).astype(BF)
                self.copy(chunk, 0).start()
                self.kept[slot] = product(0)

    def go_on(self, chunk, step):
        slot, rows = chunk % SUM_SLOTS, self.steps[step - 1][0] * SUM_ROWS
        self.copy(chunk, step - 1).wait_recv()
        total = self.kept[slot, pl.ds(0, rows)] + self.got[chunk, pl.ds(rows, rows)].astype(F32)
        if step == len(self.steps):
            self.out(chunk, total)
            return
        half = rows // 2
        self.sent[slot, pl.ds(half, half)] = total[half:].astype(BF)
        self.copy(chunk, step).start()
        self.kept[slot, pl.ds(0, half)] = total[:half]

    def at(self, time):
        for step in range(len(self.steps), -1, -1):
            chunk = time - SUM_TIMES[step]

            @pl.when((chunk >= 0) & (chunk < self.chunks))
            def _():
                if step == 0:
                    self.begin(chunk)
                else:
                    self.go_on(chunk, step)

    def run(self, first, stop):
        pl.loop(first, stop)(self.at)

    def end(self):
        @pl.loop(max(0, self.chunks - SUM_SLOTS), self.chunks)
        def _(chunk):
            self.sent_all(chunk)


def turn(order_ref, left_ref, values_ref):
    for index in range(values_ref.shape[0]):
        left_ref[index] = dot_t(order_ref[...], values_ref[index]).astype(BF)


def lefts_scratch(n, lefts):
    return [pltpu.VMEM((lefts.shape[0], n * SUM_ROWS, lefts.shape[1]), BF)]


def sums_scratch(n, chunks):
    rows, phases = n * SUM_ROWS, n.bit_length() - 1
    return [
        pltpu.VMEM((SUM_SLOTS, rows // 2, SUM_COLUMNS), F32),
        pltpu.VMEM((SUM_SLOTS, rows, SUM_COLUMNS), BF),
        pltpu.VMEM((chunks, rows, SUM_COLUMNS), BF),
        pltpu.SemaphoreType.DMA((chunks, phases)),
        pltpu.SemaphoreType.DMA((chunks, phases)),
    ]


def local_find(chunk):
    return (chunk + 6) // 8, chunk


def unpatch_find(chunk):
    return 0, chunk


def last_find(chunk):
    return (chunk + 7) // 16 + (chunk + 5) // 16, chunk


def last_kernel(
    n, grad_ref, parted_ref, small_ref, order_ref, values_ref, right_ref,
    d_weight_ref, d_small_ref, d_in_ref, d_out_ref,
    known, small_kept, small_got, g_send, g_recv, t_send, t_recv, left_ref, *scratch
):
    here = Place(n)
    rows = grad_ref.shape[0]
    greet(n)
    known[pl.ds(0, rows)] = grad_ref[...]

    @pl.loop(0, n)
    def _(place):
        device = here.device(place)
        small_kept[rows_of(place, 1, LOG_ROWS)] = small_ref[rows_of(device, 1, LOG_ROWS)]

    turn(order_ref, left_ref, values_ref)
    spare = d_in_ref.shape[1] % SUM_COLUMNS

    def store(chunk, total):
        @pl.when(chunk < 8)
        def _():
            d_in_ref[:, columns_of(chunk)] = total

        @pl.when(chunk == 8)
        def _():
            d_in_ref[:, pl.ds(8 * SUM_COLUMNS, spare)] = total[:, :spare]

        @pl.when(chunk >= 9)
        def _():
            part = (chunk - 9) // 2
            d_out_ref[rows_of(part, 1, SUM_ROWS), columns_of((chunk - 9) % 2)] = total

    sums = Sums(here, [(0, 13, last_find, left_ref, right_ref)], store, *scratch)
    steps = here.halves()
    copies = []
    for step in range(len(steps)):
        blocks, partner = steps[step]
        source, target = pl.ds(0, blocks * rows), pl.ds(blocks * rows, blocks * rows)
        gather = remote(known.at[source], known.at[target], g_send.at[step], g_recv.at[step], partner)
        gather.start()
        blocks, partner = steps[::-1][step]
        cut, mine = pl.ds(blocks * LOG_ROWS, blocks * LOG_ROWS), pl.ds(0, blocks * LOG_ROWS)
        told = remote(small_kept.at[cut], small_got.at[cut], t_send.at[step], t_recv.at[step], partner)
        told.start()
        copies += [gather, told]
        sums.run(2 * step, 2 * step + 2)
        gather.wait_recv()
        told.wait_recv()
        small_kept[mine] = small_kept[mine] + small_got[cut]
    sums.run(2 * len(steps), sums.times)
    d_small_ref[...] = small_kept[pl.ds(0, LOG_ROWS)]
    d_weight_ref[...] = lax.dot_general(
        parted_ref[...], known[...], (((0,), (0,)), ((), ())), preferred_element_type=F32
    )
    for copy in copies:
        copy.wait_send()
    sums.end()


def last_sums(n, grad, parted, small, order, lefts, right, projections):
    rows, width = grad.shape[0], parted.shape[1]
    phases, chunks = n.bit_length() - 1, right.shape[1] // SUM_COLUMNS
    return pl.pallas_call(
        functools.partial(last_kernel, n),
        out_shape=[
            jax.ShapeDtypeStruct((width, D), F32),
            jax.ShapeDtypeStruct((LOG_ROWS, 128), F32),
            jax.ShapeDtypeStruct((SUM_ROWS, projections), F32),
            jax.ShapeDtypeStruct((2 * SUM_ROWS, D), F32),
        ],
        in_specs=[pl.BlockSpec(memory_space=pltpu.VMEM)] * 6,
        out_specs=[pl.BlockSpec(memory_space=pltpu.VMEM)] * 4,
        scratch_shapes=[
            pltpu.VMEM((n * rows, D), BF),
            pltpu.VMEM(small.shape, F32),
            pltpu.VMEM(small.shape, F32),
        ]
        + [pltpu.SemaphoreType.DMA((phases,))] * 4
        + lefts_scratch(n, lefts)
        + sums_scratch(n, chunks),
        compiler_params=pltpu.CompilerParams(
            collective_id=1, has_side_effects=True, vmem_limit_bytes=62 * 2**20
        ),
        cost_estimate=pl.CostEstimate(flops=2**32, bytes_accessed=2**24, transcendentals=0),
    )(grad, parted, small, order, lefts, right)


LOG_ROWS = 8


class Exchange:
    def __init__(self, n, reverse, states, logs_in, out, spread, logs, summed, *sems):
        self.n, self.reverse = n, reverse
        self.me = lax.axis_index("seq")
        self.states, self.logs_in, self.out = states, logs_in, out
        self.spread, self.logs, self.summed = spread, logs, summed
        self.sems = sems
        self.rows = states.shape[0] // n

    def spreading(self, other):
        send, recv = self.sems[:2]
        source = self.states.at[rows_of(other, 1, self.rows)]
        target = self.spread.at[rows_of(self.me, 1, self.rows)]
        return remote(source, target, send.at[other], recv.at[self.me], other)

    def telling(self, other):
        send, recv = self.sems[2:4]
        target = self.logs.at[rows_of(self.me, 1, LOG_ROWS)]
        return remote(self.logs_in, target, send.at[other], recv.at[self.me], other)

    def returning(self, other):
        send, recv = self.sems[4:6]
        source = self.summed.at[rows_of(other, 1, self.rows)]
        target = self.out.at[rows_of(self.me, 1, self.rows)]
        return remote(source, target, send.at[other], recv.at[self.me], other)

    def tell(self):
        @pl.loop(1, self.n)
        def _(hop):
            self.telling(lax.rem(self.me + hop, self.n)).start()

        target = self.logs.at[rows_of(self.me, 1, LOG_ROWS)]
        pltpu.make_async_copy(self.logs_in, target, self.sems[3].at[self.me]).start()

    def start(self):
        @pl.loop(1, self.n)
        def _(hop):
            self.spreading(lax.rem(self.me + hop, self.n)).start()

        mine = rows_of(self.me, 1, self.rows)
        recv = self.sems[1].at[self.me]
        pltpu.make_async_copy(self.states.at[mine], self.spread.at[mine], recv).start()

    def join(self):
        n, rows, summed, spread = self.n, self.rows, self.summed, self.spread

        @pl.loop(0, n)
        def _(other):
            landed(spread.at[rows_of(other, 1, rows)], self.sems[1].at[other])
            landed(self.logs.at[rows_of(other, 1, LOG_ROWS)], self.sems[3].at[other])

        head = self.me * MHEADS // n
        lane = lax.broadcasted_iota(jnp.int32, (LOG_ROWS, 128), 1)
        row = lax.broadcasted_iota(jnp.int32, (LOG_ROWS, 128), 0)

        def step(count, total):
            place = n - 1 - count if self.reverse else count
            cut = rows_of(place, 1, rows)
            summed[cut] = total.astype(BF)
            told = self.logs[rows_of(place, 1, LOG_ROWS)]
            log = jnp.sum(jnp.where((lane == head) & (row == 0), told, 0.0), keepdims=True)
            flag = jnp.sum(jnp.where((lane == MHEADS) & (row == 0), told, 0.0), keepdims=True)
            decay = jnp.where(flag > 0.0, 0.0, jnp.exp(log))
            return decay * total + spread[cut].astype(F32)

        lax.fori_loop(0, n, step, jnp.zeros((rows, NSTATE), F32))

        @pl.loop(1, n)
        def _(hop):
            self.returning(lax.rem(self.me + hop, n)).start()

        mine = rows_of(self.me, 1, rows)
        recv = self.sems[5].at[self.me]
        pltpu.make_async_copy(summed.at[mine], self.out.at[mine], recv).start()

    def arrive(self):
        @pl.loop(0, self.n)
        def _(other):
            landed(self.out.at[rows_of(other, 1, self.rows)], self.sems[5].at[other])

    def end(self):
        @pl.loop(1, self.n)
        def _(hop):
            other = lax.rem(self.me + hop, self.n)
            self.spreading(other).wait_send()
            self.telling(other).wait_send()
            self.returning(other).wait_send()


def exchange_scratch(n):
    total = MHEADS * MHEAD_DIM
    return [
        pltpu.VMEM((total, NSTATE), BF),
        pltpu.VMEM((n * LOG_ROWS, 128), F32),
        pltpu.VMEM((total, NSTATE), BF),
    ] + [pltpu.SemaphoreType.DMA((n,))] * 6


def states_kernel(n, reverse, states_ref, logs_ref, out_ref, *scratch):
    greet(n)
    exchange = Exchange(n, reverse, states_ref, logs_ref, out_ref, *scratch)
    exchange.tell()
    exchange.start()
    exchange.join()
    exchange.arrive()
    exchange.end()


def told_logs(logs):
    return jnp.zeros((LOG_ROWS, 128), F32).at[0, : logs.shape[0]].set(logs)


def pass_states(n, states, logs, reverse):
    total = MHEADS * MHEAD_DIM
    return pl.pallas_call(
        functools.partial(states_kernel, n, reverse),
        out_shape=jax.ShapeDtypeStruct((total, NSTATE), BF),
        in_specs=[pl.BlockSpec(memory_space=pltpu.VMEM)] * 2,
        out_specs=pl.BlockSpec(memory_space=pltpu.VMEM),
        scratch_shapes=exchange_scratch(n),
        compiler_params=pltpu.CompilerParams(
            collective_id=3 if reverse else 2, has_side_effects=True, vmem_limit_bytes=16 * 2**20
        ),
        cost_estimate=pl.CostEstimate(flops=2**22, bytes_accessed=2**21, transcendentals=0),
    )(states.reshape(total, NSTATE).astype(BF), told_logs(logs))


NN, NT, TN = ((1,), (0,)), ((1,), (1,)), ((0,), (0,))


def in_parts(value, count):
    if value.dtype == BF:
        return [value]
    parts = []
    for _ in range(count):
        parts.append(value.astype(BF))
        value = value - parts[-1].astype(F32)
    return parts


def dot_fine(left, right, dims, count=2):
    total = None
    for i, a in enumerate(in_parts(left, count)):
        for j, b in enumerate(in_parts(right, count)):
            if i + j < count:
                found = lax.dot_general(a, b, (dims, ((), ())), preferred_element_type=F32)
                total = found if total is None else total + found
    return total


def mixer_back_kernel(
    n, logs_ref, order_ref, values_ref, right_ref, hidden_ref, slots_ref,
    dy_ref, x_ref, keys_ref, queries_ref, state_ref, steps_ref, marks_ref, head_ref,
    dx_ref, dkeys_ref, dqueries_ref, d_dt_ref, d_head_ref, sum_ref, unpatch_ref,
    scores, d_scores, d_step, d_cum, d_turned, grads, back, left_ref, hidden_left, *scratch
):
    rows, width = x_ref.shape[0], 2 * MHEAD_DIM
    greet(n)
    exchange = Exchange(n, True, grads, logs_ref, back, *scratch[:9])

    def store(chunk, total):
        @pl.when(chunk < 16)
        def _():
            unpatch_ref[:, columns_of(chunk)] = total

        @pl.when(chunk >= 16)
        def _():
            sum_ref[:, columns_of(chunk - 16)] = total

    sources = [
        (0, 16, unpatch_find, hidden_left, slots_ref),
        (16, 24, local_find, left_ref, right_ref),
    ]
    sums = Sums(Place(n), sources, store, *scratch[9:])
    exchange.tell()
    turn(order_ref, hidden_left, hidden_ref)
    turn(order_ref, left_ref, values_ref)

    head_lane = lax.broadcasted_iota(jnp.int32, (1, MHEADS), 1)
    lanes = lax.broadcasted_iota(jnp.int32, (1, width), 1)
    halves = [lanes < MHEAD_DIM, lanes >= MHEAD_DIM]
    step, cum = steps_ref[0, :rows, :MHEADS], steps_ref[1, :rows, :MHEADS]
    turned_step, turned_cum = steps_ref.at[3], steps_ref.at[4]
    reach = marks_ref[0][:, :rows]
    from_before, to_after = marks_ref[1][:, 0:1], marks_ref[1][:, 1:2]
    last_cum = cum[rows - 1 : rows]
    to_end = jnp.exp(last_cum - cum) * to_after

    def column(values, head):
        return jnp.sum(jnp.where(head_lane == head, values, 0.0), axis=1, keepdims=True)

    def at_head(head, values):
        return jnp.where(head_lane == head, values, 0.0)

    def of_pair(pair, values):
        return jnp.where(halves[0], column(values, 2 * pair), column(values, 2 * pair + 1))

    def columns(pair):
        return pl.ds(pl.multiple_of(pair * width, width), width)

    scores[...] = dot_fine(queries_ref[...], keys_ref[...], NT)
    d_scores[...] = jnp.zeros_like(d_scores)
    d_step[...] = jnp.zeros_like(d_step)
    d_cum[...] = jnp.zeros_like(d_cum)
    d_turned[...] = jnp.zeros_like(d_turned)
    dqueries_ref[...] = jnp.zeros_like(dqueries_ref)
    d_head_ref[...] = jnp.zeros_like(d_head_ref)

    @pl.loop(0, MHEADS // 2)
    def _(pair):
        sums.at(pair)
        x, dy, state = x_ref[:, columns(pair)], dy_ref[:, columns(pair)], state_ref[columns(pair)]
        dx = of_pair(pair, head_ref[2:3]) * dy
        inflow = jnp.exp(of_pair(pair, cum)) * from_before
        dy_in = dy * inflow
        carried = dy_in * dot_fine(queries_ref[...], state, NT)
        dqueries_ref[...] += dot_fine(dy_in, state, NN)
        grads[columns(pair)] = dot_fine(dy_in, queries_ref[...], TN).astype(BF)
        for which, half in enumerate(halves):
            head = 2 * pair + which
            mine = pl.ds(head, 1)
            gap = column(cum, head) - turned_cum[mine, :rows]
            decay = jnp.exp(jnp.where(reach > 0.0, gap, 0.0)) * reach
            weighted = scores[...] * decay
            step_row = turned_step[mine, :rows]
            mixing = weighted * step_row
            d_mixing = dot_fine(dy, jnp.where(half, x, 0.0), NT)
            dx += dot_fine(mixing, jnp.where(half, dy, 0.0), TN)
            d_scores[...] += d_mixing * decay * step_row
            d_gap = d_mixing * mixing
            d_turned[0, mine, :rows] = jnp.sum(d_mixing * weighted, axis=0, keepdims=True)
            d_turned[1, mine, :rows] = -jnp.sum(d_gap, axis=0, keepdims=True)
            moved = jnp.sum(d_gap, axis=1, keepdims=True)
            moved += jnp.sum(jnp.where(half, carried, 0.0), axis=1, keepdims=True)
            d_cum[...] += at_head(head, moved)
            skipped = jnp.sum(jnp.where(half, dy * x, 0.0), keepdims=True)
            d_head_ref[2:3] += at_head(head, skipped)
        dx_ref[:, columns(pair)] = dx

    dkeys_ref[...] = dot_fine(d_scores[...], queries_ref[...], TN)
    dqueries_ref[...] += dot_fine(d_scores[...], keys_ref[...], NN)
    exchange.start()
    sums.run(16, 20)
    exchange.join()
    sums.run(20, 24)
    exchange.arrive()

    @pl.loop(0, MHEADS // 2)
    def _(pair):
        @pl.when(pair < 7)
        def _():
            sums.at(24 + pair)

        x, state, grad = x_ref[:, columns(pair)], state_ref[columns(pair)], back[columns(pair)]
        weight = of_pair(pair, to_end * step)
        d_weighted = dot_fine(keys_ref[...], grad, NT)
        dkeys_ref[...] += dot_fine(x * weight, grad, NN)
        dx_ref[:, columns(pair)] += weight * d_weighted
        kept = grad.astype(F32) * state.astype(F32)
        for which, half in enumerate(halves):
            head = 2 * pair + which
            d_weight = jnp.sum(jnp.where(half, x * d_weighted, 0.0), axis=1, keepdims=True)
            d_step[...] += at_head(head, d_weight * column(to_end, head))
            moved = d_weight * column(to_end * step, head)
            d_cum[...] -= at_head(head, moved)
            d_decay = jnp.sum(kept[which * MHEAD_DIM : (which + 1) * MHEAD_DIM], keepdims=True)
            ended = jnp.sum(moved, keepdims=True)
            ended += d_decay * jnp.exp(column(last_cum, head)) * from_before[rows - 1 : rows]
            d_cum[rows - 1 : rows] += at_head(head, ended)

    d_steps = d_step[...] + d_turned[0].T[:rows, :MHEADS]
    d_cums = d_cum[...] + d_turned[1].T[:rows, :MHEADS]
    later = lax.broadcasted_iota(jnp.int32, (rows, rows), 0) <= lax.broadcasted_iota(
        jnp.int32, (rows, rows), 1
    )
    d_logs = dot_fine(later.astype(BF), d_cums, NN, 3)
    rate = jnp.exp(head_ref[1:2])
    d_raw = (d_steps - rate * d_logs) * steps_ref[2, :rows, :MHEADS]
    d_dt_ref[...] = d_raw
    d_head_ref[0:1] = jnp.sum(d_raw, axis=0, keepdims=True)
    d_head_ref[1:2] = -rate * jnp.sum(step * d_logs, axis=0, keepdims=True)
    sums.run(31, sums.times)
    sums.end()
    exchange.end()


def mixer_back(n, logs, order, values, right, hidden, slots, dy, conv_out, state_in, dt_raw, head_params, starts):
    rows = conv_out.shape[0]
    x, keys, queries, step, cum, segment = block_parts(conv_out, dt_raw, head_params, starts)
    slope = jax.nn.sigmoid(dt_raw + head_params[0])
    square = [jnp.pad(v, ((0, 128 - v.shape[0]), (0, 128 - v.shape[1]))) for v in (step.T, cum.T)]
    tall = [jnp.pad(v, ((0, 128 - rows), (0, 128 - MHEADS))) for v in (step, cum, slope)]
    steps = jnp.stack(tall + square)
    position = jnp.arange(rows)
    reach = (position[:, None] >= position[None, :]) & (segment[:, None] == segment[None, :])
    ends = jnp.stack([segment == 0, segment == segment[-1]], axis=1)
    marks = jnp.stack(
        [jnp.pad(v.astype(F32), ((0, 0), (0, 128 - v.shape[1]))) for v in (reach, ends)]
    )
    total = MHEADS * MHEAD_DIM
    narrow = jax.ShapeDtypeStruct((rows, NSTATE), F32)
    return pl.pallas_call(
        functools.partial(mixer_back_kernel, n),
        out_shape=[
            jax.ShapeDtypeStruct((rows, DI), F32),
            narrow,
            narrow,
            jax.ShapeDtypeStruct((rows, MHEADS), F32),
            jax.ShapeDtypeStruct((8, MHEADS), F32),
            jax.ShapeDtypeStruct((SUM_ROWS, right.shape[1]), F32),
            jax.ShapeDtypeStruct((SUM_ROWS, slots.shape[1]), F32),
        ],
        in_specs=[pl.BlockSpec(memory_space=pltpu.VMEM)] * 14,
        out_specs=[pl.BlockSpec(memory_space=pltpu.VMEM)] * 7,
        scratch_shapes=[
            pltpu.VMEM((rows, rows), F32),
            pltpu.VMEM((rows, rows), F32),
            pltpu.VMEM((rows, MHEADS), F32),
            pltpu.VMEM((rows, MHEADS), F32),
            pltpu.VMEM((2, 128, 128), F32),
            pltpu.VMEM((total, NSTATE), BF),
            pltpu.VMEM((total, NSTATE), BF),
        ]
        + lefts_scratch(n, values)
        + lefts_scratch(n, hidden)
        + exchange_scratch(n)
        + sums_scratch(n, 24),
        compiler_params=pltpu.CompilerParams(
            collective_id=3, has_side_effects=True, vmem_limit_bytes=62 * 2**20
        ),
        cost_estimate=pl.CostEstimate(flops=2**32, bytes_accessed=2**24, transcendentals=2**20),
    )(
        told_logs(logs), order, values, right, hidden, slots, dy, conv_out[:, :DI], keys, queries,
        state_in, steps, marks, head_params,
    )


FF_TILE = D


def feed_forward_kernel(
    stream_ref, normed_ref, gate_w_ref, up_w_ref, down_ref, out_ref, gate_ref, up_ref, hid_ref, total
):
    step = pl.program_id(0)
    gate, up = dot(normed_ref[...], whole_of(gate_w_ref)), dot(normed_ref[...], whole_of(up_w_ref))
    hid = (silu(gate) * up).astype(BF)
    gate_ref[...], up_ref[...], hid_ref[...] = gate.astype(BF), up.astype(BF), hid
    found = dot(hid, down_ref[...])

    @pl.when(step == 0)
    def _():
        total[...] = stream_ref[...] + found

    @pl.when(step > 0)
    def _():
        total[...] += found

    @pl.when(step == pl.num_programs(0) - 1)
    def _():
        out_ref[...] = total[...].astype(BF)


def feed_forward_blocks(n):
    tiles, first = FF // FF_TILE, PATCH + 4
    return [
        flat_block(n, D // n, lambda i: first + i),
        flat_block(n, D // n, lambda i: first + tiles + i),
        pl.BlockSpec((FF_TILE, D), lambda i: (i, 0)),
    ]


def feed_forward(stream, normed, flat, down):
    rows, tiles = stream.shape[0], FF // FF_TILE
    wide = pl.BlockSpec((rows, D), lambda i: (0, 0))
    tile = pl.BlockSpec((rows, FF_TILE), lambda i: (0, i))
    return pl.pallas_call(
        feed_forward_kernel,
        grid=(tiles,),
        out_shape=[jax.ShapeDtypeStruct((rows, D), BF)]
        + [jax.ShapeDtypeStruct((rows, FF), BF)] * 3,
        in_specs=[
            wide,
            wide,
            *feed_forward_blocks(flat.shape[0]),
        ],
        out_specs=[wide, tile, tile, tile],
        scratch_shapes=[pltpu.VMEM((rows, D), F32)],
        compiler_params=pltpu.CompilerParams(vmem_limit_bytes=52 * 2**20),
        cost_estimate=pl.CostEstimate(
            flops=6 * rows * D * FF, bytes_accessed=2**25, transcendentals=rows * FF
        ),
    )(stream, normed, flat, flat, down)


def feed_forward_back_kernel(
    grad_ref, stream_ref, gain_ref, gate_ref, up_ref, gate_w_ref, up_w_ref, down_ref,
    both_ref, d_stream_ref, d_low_ref, d_gain_ref, total,
):
    step = pl.program_id(0)
    d_hid = dot_t(grad_ref[...], down_ref[...])
    gate, up = gate_ref[...].astype(F32), up_ref[...].astype(F32)
    s = jax.nn.sigmoid(gate)
    d_gate = (d_hid * up * (s * (1.0 + gate * (1.0 - s)))).astype(BF)
    d_up = (d_hid * (gate * s)).astype(BF)
    both_ref[0], both_ref[1] = d_gate, d_up
    found = dot_t(d_gate, whole_of(gate_w_ref)) + dot_t(d_up, whole_of(up_w_ref))

    @pl.when(step == 0)
    def _():
        total[...] = found

    @pl.when(step > 0)
    def _():
        total[...] += found

    @pl.when(step == pl.num_programs(0) - 1)
    def _():
        stream, d_normed = stream_ref[...], total[...]
        r = lax.rsqrt(jnp.mean(stream * stream, axis=-1, keepdims=True) + EPS)
        scaled = gain_ref[...] * d_normed
        inner = jnp.mean(stream * scaled, axis=-1, keepdims=True)
        d_stream = grad_ref[...].astype(F32) + r * scaled - stream * (r * r * r) * inner
        d_stream_ref[...] = d_stream
        d_low_ref[...] = d_stream.astype(BF)
        d_gain_ref[...] = jnp.sum(stream * r * d_normed, axis=0, keepdims=True)


def feed_forward_back(grad, stream, gain, gate, up, flat, down):
    rows, tiles = stream.shape[0], FF // FF_TILE
    wide = pl.BlockSpec((rows, D), lambda i: (0, 0))
    tile = pl.BlockSpec((rows, FF_TILE), lambda i: (0, i))
    narrow = pl.BlockSpec((1, D), lambda i: (0, 0))
    both, d_stream, d_low, d_gain = pl.pallas_call(
        feed_forward_back_kernel,
        grid=(tiles,),
        out_shape=[
            jax.ShapeDtypeStruct((2, rows, FF), BF),
            jax.ShapeDtypeStruct((rows, D), F32),
            jax.ShapeDtypeStruct((rows, D), BF),
            jax.ShapeDtypeStruct((1, D), F32),
        ],
        in_specs=[
            wide,
            wide,
            narrow,
            tile,
            tile,
            *feed_forward_blocks(flat.shape[0]),
        ],
        out_specs=[pl.BlockSpec((2, rows, FF_TILE), lambda i: (0, 0, i)), wide, wide, narrow],
        scratch_shapes=[pltpu.VMEM((rows, D), F32)],
        compiler_params=pltpu.CompilerParams(vmem_limit_bytes=56 * 2**20),
        cost_estimate=pl.CostEstimate(
            flops=6 * rows * D * FF, bytes_accessed=2**25, transcendentals=rows * FF
        ),
    )(grad, stream, gain[None], gate, up, flat, flat, down)
    return both, d_stream, d_low, d_gain[0]


ATTN_ROWS = 128


def tile_mask():
    row = lax.broadcasted_iota(jnp.int32, (ATTN_ROWS, 2 * ATTN_ROWS), 0)
    column = lax.broadcasted_iota(jnp.int32, (ATTN_ROWS, 2 * ATTN_ROWS), 1) % ATTN_ROWS
    return (row // PATCH == column // PATCH) & (row >= column)


def first_head():
    return lax.broadcasted_iota(jnp.int32, (1, 2 * AHEAD_DIM), 1) < AHEAD_DIM


def one_below_other(pair):
    lanes, zeros = first_head(), jnp.zeros_like(pair)
    return jnp.concatenate([jnp.where(lanes, pair, zeros), jnp.where(lanes, zeros, pair)], axis=0)


def by_head(values, reduce):
    first = reduce(values[:, :ATTN_ROWS], axis=-1, keepdims=True)
    second = reduce(values[:, ATTN_ROWS:], axis=-1, keepdims=True)
    shape = (values.shape[0], ATTN_ROWS)
    return jnp.concatenate(
        [jnp.broadcast_to(first, shape), jnp.broadcast_to(second, shape)], axis=1
    )


def pair_probs(queries, key_rows, mask):
    scores = jnp.where(mask, dot_t(queries, key_rows) * AHEAD_DIM ** (-0.5), -1e30)
    raised = jnp.exp(scores - by_head(scores, jnp.max))
    return raised / by_head(raised, jnp.sum)


def attention_kernel(triple_ref, out_ref):
    mask = tile_mask()
    width = 2 * AHEAD_DIM
    for pair in range(AHEADS // 2):
        queries, key_rows, value_rows = [
            triple_ref[:, part * D + pair * width : part * D + (pair + 1) * width] for part in range(3)
        ]
        probs = pair_probs(queries, one_below_other(key_rows), mask)
        mixed = dot(probs.astype(BF), one_below_other(value_rows))
        out_ref[:, pair * width : (pair + 1) * width] = mixed.astype(BF)


def attention(triple):
    rows = triple.shape[0]
    return pl.pallas_call(
        attention_kernel,
        grid=(rows // ATTN_ROWS,),
        out_shape=jax.ShapeDtypeStruct((rows, D), BF),
        in_specs=[pl.BlockSpec((ATTN_ROWS, 3 * D), lambda i: (i, 0))],
        out_specs=pl.BlockSpec((ATTN_ROWS, D), lambda i: (i, 0)),
    )(triple)


def attention_back_kernel(triple_ref, grad_ref, out_ref):
    mask = tile_mask()
    width = 2 * AHEAD_DIM
    scale = AHEAD_DIM ** (-0.5)

    def of_keys(left, right):
        found = lax.dot_general(left, right, (((0,), (0,)), ((), ())), preferred_element_type=F32)
        return jnp.where(first_head(), found[:ATTN_ROWS], found[ATTN_ROWS:])

    for pair in range(AHEADS // 2):
        lo, hi = pair * width, (pair + 1) * width
        queries, key_rows, value_rows = [
            triple_ref[:, part * D + lo : part * D + hi] for part in range(3)
        ]
        grad = grad_ref[:, lo:hi]
        key_rows = one_below_other(key_rows)
        probs = pair_probs(queries, key_rows, mask)
        d_probs = dot_t(grad, one_below_other(value_rows))
        d_scores = (probs * (d_probs - by_head(probs * d_probs, jnp.sum))).astype(BF)
        out_ref[:, lo:hi] = (scale * dot(d_scores, key_rows)).astype(BF)
        out_ref[:, D + lo : D + hi] = (scale * of_keys(d_scores, queries)).astype(BF)
        out_ref[:, 2 * D + lo : 2 * D + hi] = of_keys(probs.astype(BF), grad).astype(BF)


def attention_back(triple, grad):
    rows = triple.shape[0]
    return pl.pallas_call(
        attention_back_kernel,
        grid=(rows // ATTN_ROWS,),
        out_shape=jax.ShapeDtypeStruct((rows, 3 * D), BF),
        in_specs=[
            pl.BlockSpec((ATTN_ROWS, 3 * D), lambda i: (i, 0)),
            pl.BlockSpec((ATTN_ROWS, D), lambda i: (i, 0)),
        ],
        out_specs=pl.BlockSpec((ATTN_ROWS, 3 * D), lambda i: (i, 0)),
    )(triple, grad)


def local(
    byte_acts,
    resets,
    out_grad,
    patch_weight,
    patch_gain,
    mixer_in,
    conv_weight,
    conv_bias,
    head_params,
    mixer_gain,
    mixer_out,
    unpatch_weight,
    attn_gain,
    qkv_weight,
    attn_out,
    ffn_gain,
    gate_up,
    down_weight,
):
    n = lax.axis_size("seq")
    me = lax.axis_index("seq")
    ring = Ring(n)

    def passed_along(block, distance):
        route = [(i - distance, i) for i in range(n) if 0 <= i - distance < n]
        return lax.ppermute(block, "seq", route)

    live = Live()
    order = ring.order()

    byte_wide = byte_acts.astype(F32)
    patches = byte_acts.reshape(-1, PATCH * D)
    patch_rows = patches.shape[0]
    early = gather_flat(n, [unpatch_weight, qkv_weight, attn_out, gate_up])
    late = lax.all_gather(down_weight, "seq", axis=0, tiled=True)
    small = [patch_gain, conv_weight.reshape(-1), conv_bias, mixer_gain, attn_gain, ffn_gain]
    cuts = list(np.cumsum([piece.shape[0] for piece in small]))
    small_shard = jnp.concatenate(small)
    small_shard = jnp.pad(small_shard, (0, -small_shard.shape[0] % 2048)).reshape(-1, 128)
    live.patch_w, live.mixer_in, live.mixer_out, small_all, embedded, live.parted = gather_weights(
        n,
        [
            patch_weight,
            jnp.pad(mixer_in, ((0, 0), (0, -mixer_in.shape[1] % 128))),
            mixer_out,
            small_shard,
        ],
        [(32, D), (16, 2304), (32, D), (16, 128)],
        patches,
    )
    small_all = small_all.reshape(n, -1)[:, : cuts[-1]].astype(F32)
    parts = jnp.split(small_all, cuts[:-1], axis=1)
    live.patch_gain = parts[0].reshape(-1)
    live.conv_weight = parts[1].reshape(n, CONV, -1).transpose(1, 0, 2).reshape(CONV, CONV_CH)
    live.conv_bias, live.mixer_gain, live.attn_gain, live.ffn_gain = [
        piece.reshape(-1) for piece in parts[2:]
    ]
    live.embedded = embedded
    live.normed = rms_scale(live.embedded, live.patch_gain).astype(BF)
    projected = dot(live.normed, live.mixer_in)
    live.gate_z = projected[:, :DI]
    conv_in = projected[:, DI : DI + CONV_CH].astype(BF).astype(F32)
    dt_raw = projected[:, DI + CONV_CH : DI + CONV_CH + MHEADS]
    logs = jnp.sum(-jax.nn.softplus(dt_raw + head_params[0]) * jnp.exp(head_params[1]), axis=0)
    flag = jnp.max(resets).astype(F32)
    live.logs = jnp.concatenate([logs, flag[None]])
    not_reset = 1.0 - resets.astype(F32)
    keep_tail = jnp.concatenate(
        [jnp.cumprod(not_reset[patch_rows - CONV + 2 :][::-1])[::-1], jnp.ones((1,), F32)]
    )
    tail_sent = (conv_in[patch_rows - CONV + 1 :] * keep_tail[:, None]).astype(BF)
    halo_rows = passed_along(tail_sent, 1)
    flags_ext = jnp.concatenate([jnp.zeros((CONV - 1,), jnp.int32), resets])
    validity = tap_masks(flags_ext, patch_rows)
    conv_ext = jnp.concatenate([halo_rows.astype(F32), conv_in])
    conv_out, conv_back = jax.vjp(
        functools.partial(conv_apply, validity=validity, row_count=patch_rows),
        conv_ext,
        live.conv_weight,
        live.conv_bias,
    )
    state_parts, state_back = jax.vjp(
        functools.partial(block_state, starts=resets), conv_out, dt_raw, head_params
    )
    local_state, decay_total = state_parts
    live.state_in = pass_states(n, local_state, live.logs, False)
    live.fence()

    mixer_y, output_back = jax.vjp(
        functools.partial(block_output, starts=resets),
        conv_out,
        dt_raw,
        head_params,
        live.state_in.astype(F32).reshape(MHEADS, MHEAD_DIM, NSTATE),
    )
    gate_act = silu(live.gate_z)
    gated = mixer_y * gate_act
    live.gated_norm = rms_scale(gated, live.mixer_gain).astype(BF)
    branch = dot(live.gated_norm, live.mixer_out)
    live.hidden = (live.embedded + branch).astype(BF)
    live.early = early
    slots = flat_dot(live.hidden, live.early, 0, PATCH, F32)
    live.stream0 = byte_wide + slots.reshape(-1, D)
    live.normed0 = rms_scale(live.stream0, live.attn_gain).astype(BF)
    live.fence()

    rows = byte_wide.shape[0]
    live.triple = flat_dot(live.normed0, live.early, PATCH, 3, BF)
    live.mixed = attention(live.triple)
    live.stream1 = live.stream0 + flat_dot(live.mixed, live.early, PATCH + 3, 1, F32)
    live.normed1 = rms_scale(live.stream1, live.ffn_gain).astype(BF)
    live.late = late
    layer_out, gate, up, hid = feed_forward(live.stream1, live.normed1, live.early, live.late)
    live.gate, live.up, live.hid = gate, up, hid
    live.fence()

    small_slice = n == 32

    def lefts_of(*values):
        parts = []
        for value in values:
            cut = value.reshape(value.shape[0], n, -1, SUM_ROWS).transpose(2, 0, 1, 3)
            parts.append(cut.reshape(-1, value.shape[0], n * SUM_ROWS))
        return jnp.concatenate(parts, axis=0)

    if small_slice:
        place = jnp.arange(n * SUM_ROWS)
        source = jnp.repeat(order * SUM_ROWS, SUM_ROWS) + place % SUM_ROWS
        live.order = (place[None, :] == source[:, None]).astype(BF)

    d_both, d_stream1, d_stream1_low, g_ffn_gain = feed_forward_back(
        out_grad, live.stream1, live.ffn_gain, live.gate, live.up, live.early, live.late
    )
    if small_slice:
        block = down_weight.shape[0]
        flat = flat_grads(n, live.hid, out_grad, live.normed1, d_both)
        found = lax.psum_scatter(flat, "seq", scatter_dimension=0, tiled=True)[0].astype(F32)
        g_down = found[:block]
        g_gate_up = found[block:].reshape(-1, SUM_ROWS, D).transpose(1, 0, 2)
        g_gate_up = g_gate_up.reshape(SUM_ROWS, -1)
    else:
        g_down = summed_grad(live.hid, out_grad)
        g_gate_up = summed_grad(live.normed1, jnp.concatenate([d_both[0], d_both[1]], axis=1))
    d_mixed = flat_dot_t(d_stream1_low, live.early, PATCH + 3, 1).astype(BF)
    d_triple = attention_back(live.triple, d_mixed)
    d_stream0, g_attn_gain = rms_back(live.stream0, live.attn_gain, flat_dot_t(d_triple, live.early, PATCH, 3))
    live.d_stream0 = (d_stream1 + d_stream0).reshape(patch_rows, PATCH * D)
    d_slots = live.d_stream0.astype(BF)
    d_hidden = flat_dot_t(d_slots, live.early, 0, PATCH)
    d_branch = d_hidden.astype(BF)
    d_gated, g_mixer_gain = rms_back(gated, live.mixer_gain, dot_t(d_branch, live.mixer_out))
    d_gate_z = d_gated * mixer_y * silu_slope(live.gate_z)
    if small_slice:
        dx, dkeys, dqueries, d_dt, g_head, found, g_unpatch = mixer_back(
            n,
            live.logs,
            live.order,
            jnp.stack([live.mixed, live.normed0]),
            jnp.concatenate([d_stream1_low, d_triple], axis=1),
            live.hidden[None],
            d_slots,
            d_gated * gate_act,
            conv_out,
            live.state_in,
            dt_raw,
            head_params,
            resets,
        )
        g_attn_out, g_qkv = found[:, :D], found[:, D:]
        conv_cot = conv_back(jnp.concatenate([dx, dkeys, dqueries], axis=1))
        g_head = g_head[:3]
    else:
        output_grads = output_back(d_gated * gate_act)
        state_grad = pass_states(n, output_grads[3], live.logs, True).astype(F32)
        state_grad = state_grad.reshape(MHEADS, MHEAD_DIM, NSTATE)
        state_in = live.state_in.astype(F32).reshape(MHEADS, MHEAD_DIM, NSTATE)
        state_cot = state_back((state_grad, jnp.sum(state_grad * state_in, axis=(1, 2))))
        conv_cot = conv_back(output_grads[0] + state_cot[0])
        d_dt = output_grads[1] + state_cot[1]
        g_head = output_grads[2] + state_cot[2]
    returned = passed_along(conv_cot[0][: CONV - 1], -1)
    d_conv_in = conv_cot[0][CONV - 1 :] + jnp.concatenate(
        [jnp.zeros((patch_rows - CONV + 1, CONV_CH), F32), returned * keep_tail[:, None]]
    )
    d_projected = jnp.concatenate([d_gate_z, d_conv_in, d_dt], axis=1).astype(BF)
    d_projected = jnp.pad(d_projected, ((0, 0), (0, -d_projected.shape[1] % 128)))
    d_embedded, g_patch_gain = rms_back(
        live.embedded, live.patch_gain, dot_t(d_projected, live.mixer_in)
    )
    d_embedded = (d_hidden + d_embedded).astype(BF)
    input_grad = input_gradient(live.d_stream0, d_embedded, live.patch_w).reshape(-1, D)

    g_conv_weight = conv_cot[1].reshape(CONV, n, -1).transpose(1, 0, 2).reshape(n, -1)
    g_head = jnp.broadcast_to(g_head.reshape(1, -1), (n, 3 * MHEADS))
    g_small = [g_patch_gain, g_conv_weight, conv_cot[2], g_mixer_gain, g_attn_gain, g_ffn_gain, g_head]
    g_small = jnp.concatenate([piece.reshape(n, -1) for piece in g_small], axis=1)
    small_width = g_small.shape[1]
    g_small = jnp.pad(g_small, ((0, 0), (0, LOG_ROWS * 128 - small_width)))
    g_small = g_small.reshape(n * LOG_ROWS, 128)
    if small_slice:
        d_projected = jnp.pad(d_projected, ((0, 0), (0, -d_projected.shape[1] % SUM_COLUMNS)))
        g_patch, g_small, g_mixer_in, g_mixer_out = last_sums(
            n,
            d_embedded,
            live.parted,
            g_small,
            live.order,
            lefts_of(live.normed, live.gated_norm),
            jnp.concatenate([d_projected, d_branch, d_branch], axis=1),
            mixer_in.shape[1],
        )
    else:
        g_attn_out = summed_grad(live.mixed, d_stream1_low)
        g_qkv = summed_grad(live.normed0, d_triple)
        known = lax.all_gather(d_embedded, "seq", axis=0, tiled=True)
        g_patch = dot(live.parted.T, known)
        g_small = lax.psum_scatter(g_small, "seq", scatter_dimension=0, tiled=True)
        g_unpatch = summed_grad(live.hidden, d_slots)
        g_mixer_in = summed_grad(live.normed, d_projected)[:, : mixer_in.shape[1]]
        g_mixer_out = summed_grad(live.gated_norm, d_branch)
    g_small = g_small.reshape(-1)[:small_width]
    s = jnp.split(g_small, cuts)
    return (
        layer_out,
        input_grad,
        g_patch,
        s[0],
        g_mixer_in,
        s[1].reshape(CONV, -1),
        s[2],
        s[6].reshape(3, MHEADS),
        s[3],
        g_mixer_out,
        g_unpatch,
        s[4],
        g_qkv,
        g_attn_out,
        s[5],
        g_gate_up,
        g_down,
    )


def solution(mesh):
    rows, vector = P("seq", None), P("seq")
    placed = (
        rows, vector, rows, rows, vector, rows, P(None, "seq"), vector, P(),
        vector, rows, rows, vector, rows, rows, vector, rows, rows,
    )
    returned = (
        rows, rows, rows, vector, rows, P(None, "seq"), vector, P(), vector,
        rows, rows, vector, rows, rows, vector, rows, rows,
    )
    return jax.shard_map(
        local, mesh=mesh, in_specs=placed, out_specs=returned, check_vma=False
    )
```

```python
import functools

import jax
import jax.numpy as jnp
import numpy as np
from jax import lax
from jax.experimental import pallas as pl
from jax.experimental.pallas import tpu as pltpu
from jax.sharding import PartitionSpec as P

D = 1024
PATCH = 8
MHEADS = 32
MHEAD_DIM = 64
DI = 2048
NSTATE = 128
CONV = 4
AHEADS = 16
AHEAD_DIM = 64
FF = 4096
CONV_CH = 2304

EPS = 1e-05
HIGH = lax.Precision.HIGHEST
BF = jnp.bfloat16
F32 = jnp.float32


class Ring:
    def __init__(self, n):
        self.n = n
        self.depth = n // 8
        coords = [(i // 8, (i // 4) % 2, (i // 2) % 2, i % 2) for i in range(n)]

        def index(z, y, x, c):
            return ((z * 2 + y) * 2 + x) * 2 + c

        def flip(z, y, x, c, along_x):
            return index(z, y, 1 - x, c) if along_x else index(z, 1 - y, x, c)

        self.core = [(index(*p), index(*p) ^ 1) for p in coords]
        self.first = [(index(*p), flip(*p, p[3] == 0)) for p in coords]
        self.second = [(index(*p), flip(*p, p[3] == 1)) for p in coords]
        self.bits = [1 << b for b in range(self.depth.bit_length() - 1)]
        self.along = {
            bit: [(index(*p), index(p[0] ^ bit, *p[1:])) for p in coords] for bit in self.bits
        }
        table = np.zeros((n, n), np.int32)
        for me, (z, y, x, c) in enumerate(coords):
            place = 0
            for rc in range(2):
                owner = c ^ rc
                for r2 in range(2):
                    for r1 in range(2):
                        rx, ry = (r1, r2) if owner == 0 else (r2, r1)
                        for rz in range(self.depth):
                            table[me, place] = index(z ^ rz, y ^ ry, x ^ rx, owner)
                            place += 1
        self.table = table

    def order(self):
        return jnp.asarray(self.table)[lax.axis_index("seq")]


def swap(block, route):
    return lax.ppermute(block, "seq", route)


def flat_kernel(*refs):
    out, first = refs[-1], 0
    for ref in refs[:-1]:
        rows = ref.shape[0]
        for column in range(0, ref.shape[1], D):
            out[pl.ds(first, rows)] = ref[:, pl.ds(column, D)]
            first += rows


def flat_rows(shards):
    total = sum(shard.shape[0] * shard.shape[1] // D for shard in shards)
    return pl.pallas_call(
        flat_kernel,
        out_shape=jax.ShapeDtypeStruct((total, D), BF),
        in_specs=[pl.BlockSpec(memory_space=pltpu.VMEM)] * len(shards),
        out_specs=pl.BlockSpec(memory_space=pltpu.VMEM),
    )(*shards)


def gather_flat(n, shards):
    return lax.all_gather(flat_rows(shards), "seq", axis=0)


def flat_block(n, rows, place):
    return pl.BlockSpec((n, rows, D), lambda i: (0, place(i), 0))


def whole_of(ref):
    return ref[...].reshape(-1, ref.shape[-1])


def flat_dot_kernel(values_ref, flat_ref, out_ref):
    out_ref[...] = dot(values_ref[...], whole_of(flat_ref)).astype(out_ref.dtype)


def flat_dot(values, flat, first, count, kind):
    n, rows = flat.shape[0], values.shape[0]
    return pl.pallas_call(
        flat_dot_kernel,
        grid=(count,),
        out_shape=jax.ShapeDtypeStruct((rows, count * D), kind),
        in_specs=[
            pl.BlockSpec((rows, D), lambda i: (0, 0)),
            flat_block(n, D // n, lambda i: first + i),
        ],
        out_specs=pl.BlockSpec((rows, D), lambda i: (0, i)),
        compiler_params=pltpu.CompilerParams(vmem_limit_bytes=56 * 2**20),
        cost_estimate=pl.CostEstimate(
            flops=2 * rows * D * D * count, bytes_accessed=2 * D * D * count, transcendentals=0
        ),
    )(values, flat)


def flat_dot_t_kernel(values_ref, flat_ref, out_ref, total):
    few = values_ref.shape[0] < 256
    step = pl.program_id(0)
    if few:
        found = dot_t(whole_of(flat_ref), values_ref[...])
    else:
        found = dot_t(values_ref[...], whole_of(flat_ref))

    @pl.when(step == 0)
    def _():
        total[...] = found

    @pl.when(step > 0)
    def _():
        total[...] += found

    @pl.when(step == pl.num_programs(0) - 1)
    def _():
        out_ref[...] = total[...].T if few else total[...]


def flat_dot_t(values, flat, first, count):
    n, rows = flat.shape[0], values.shape[0]
    return pl.pallas_call(
        flat_dot_t_kernel,
        grid=(count,),
        out_shape=jax.ShapeDtypeStruct((rows, D), F32),
        in_specs=[
            pl.BlockSpec((rows, D), lambda i: (0, i)),
            flat_block(n, D // n, lambda i: first + i),
        ],
        out_specs=pl.BlockSpec((rows, D), lambda i: (0, 0)),
        scratch_shapes=[pltpu.VMEM((D, rows) if rows < 256 else (rows, D), F32)],
        compiler_params=pltpu.CompilerParams(vmem_limit_bytes=56 * 2**20),
        cost_estimate=pl.CostEstimate(
            flops=2 * rows * D * D * count, bytes_accessed=2 * D * D * count, transcendentals=0
        ),
    )(values, flat)


class Live:
    def fence(self):
        vars(self).update(lax.optimization_barrier(dict(vars(self))))


def summed_grad(left, right):
    product = lax.dot_general(left, right, (((0,), (0,)), ((), ())), preferred_element_type=F32)
    summed = lax.psum_scatter(product.astype(BF), "seq", scatter_dimension=0, tiled=True)
    return summed.astype(F32)


def turned_product(left, right):
    found = lax.dot_general(left, right, (((0,), (0,)), ((), ())), preferred_element_type=F32)
    return found.astype(BF)


def down_grad_kernel(hid_ref, grad_ref, out_ref):
    devices, block = out_ref.shape[:2]
    few = 256 // block
    for first in range(0, devices, few):
        found = turned_product(hid_ref[:, pl.ds(first * block, 256)], grad_ref[...])
        out_ref[pl.ds(first, few)] = found.reshape(few, block, D)


def down_grad(n, hid, out_grad):
    rows, block, devices = hid.shape[0], hid.shape[1] // n, n // 4
    return pl.pallas_call(
        down_grad_kernel,
        grid=(4,),
        out_shape=jax.ShapeDtypeStruct((n, 3 * block, D), BF),
        in_specs=[
            pl.BlockSpec((rows, devices * block), lambda i: (0, i)),
            pl.BlockSpec((rows, D), lambda i: (0, 0)),
        ],
        out_specs=pl.BlockSpec((devices, block, D), lambda i: (i, 0, 0)),
        compiler_params=pltpu.CompilerParams(vmem_limit_bytes=56 * 2**20),
        cost_estimate=pl.CostEstimate(
            flops=2 * rows * FF * D, bytes_accessed=2**24, transcendentals=0
        ),
    )(hid, out_grad)


def gate_up_grad_kernel(normed_ref, both_ref, flat_ref, out_ref):
    del flat_ref
    devices, block = out_ref.shape[:2]
    for part in range(block // SUM_ROWS):
        found = turned_product(normed_ref[...], both_ref[0, :, pl.ds(part * D, D)])
        out_ref[:, pl.ds(part * SUM_ROWS, SUM_ROWS)] = found.reshape(devices, SUM_ROWS, D)


def gate_up_grad(normed, both, flat):
    n, rows, devices = flat.shape[0], normed.shape[0], flat.shape[0] // 4
    return pl.pallas_call(
        gate_up_grad_kernel,
        grid=(8,),
        out_shape=jax.ShapeDtypeStruct(flat.shape, BF),
        in_specs=[
            pl.BlockSpec((rows, devices * SUM_ROWS), lambda i: (0, i % 4)),
            pl.BlockSpec((1, rows, FF), lambda i: (i // 4, 0, 0)),
            pl.BlockSpec(memory_space=pltpu.HBM),
        ],
        out_specs=pl.BlockSpec((devices, flat.shape[1] // 3, D), lambda i: (i % 4, 1 + i // 4, 0)),
        input_output_aliases={2: 0},
        compiler_params=pltpu.CompilerParams(vmem_limit_bytes=56 * 2**20),
        cost_estimate=pl.CostEstimate(
            flops=4 * rows * FF * D, bytes_accessed=2**25, transcendentals=0
        ),
    )(normed, both, flat)


def dot(left, right):
    return jnp.dot(left, right, preferred_element_type=F32)


def dot_t(left, right):
    return lax.dot_general(left, right, (((1,), (1,)), ((), ())), preferred_element_type=F32)


def rms_scale(values, gain):
    return values * lax.rsqrt(jnp.mean(values * values, axis=-1, keepdims=True) + EPS) * gain


def rms_back(values, gain, grad):
    r = lax.rsqrt(jnp.mean(values * values, axis=-1, keepdims=True) + EPS)
    scaled = gain * grad
    inner = jnp.mean(values * scaled, axis=-1, keepdims=True)
    return r * scaled - values * (r * r * r) * inner, jnp.sum(values * r * grad, axis=0)


def silu(v):
    return v * jax.nn.sigmoid(v)


def silu_slope(v):
    s = jax.nn.sigmoid(v)
    return s * (1.0 + v * (1.0 - s))


def tap_masks(flags_ext, row_count):
    not_reset = 1.0 - flags_ext.astype(F32)
    validity = [jnp.ones((row_count,), F32)]
    for offset in range(1, CONV):
        validity.append(validity[-1] * not_reset[CONV - offset : CONV - offset + row_count])
    return validity


def conv_apply(conv_ext, conv_weight, conv_bias, validity, row_count):
    summed = conv_bias + conv_ext[CONV - 1 : CONV - 1 + row_count] * conv_weight[0]
    for offset in range(1, CONV):
        summed = (
            summed
            + validity[offset][:, None]
            * conv_ext[CONV - 1 - offset : CONV - 1 - offset + row_count]
            * conv_weight[offset]
        )
    return jax.nn.silu(summed)


def block_parts(conv_out, dt_raw, head_params, starts):
    row_count = conv_out.shape[0]
    values = conv_out[:, :DI].reshape(row_count, MHEADS, MHEAD_DIM)
    key_rows = conv_out[:, DI : DI + NSTATE]
    queries = conv_out[:, DI + NSTATE :]
    step_size = jax.nn.softplus(dt_raw + head_params[0])
    cumlog = jnp.cumsum(-step_size * jnp.exp(head_params[1]), axis=0)
    segment = jnp.cumsum(starts, axis=0, dtype=jnp.int32)
    return (values, key_rows, queries, step_size, cumlog, segment)


def block_state(conv_out, dt_raw, head_params, starts):
    values, key_rows, queries, step_size, cumlog, segment = block_parts(
        conv_out, dt_raw, head_params, starts
    )
    same_doc = (segment == segment[-1]).astype(F32)
    weighting = jnp.exp(cumlog[-1][None, :] - cumlog) * same_doc[:, None] * step_size
    state_out = jnp.einsum("rh,rhp,rn->hpn", weighting, values, key_rows, precision=HIGH)
    decay_total = jnp.exp(cumlog[-1]) * (segment[-1] == 0).astype(F32)
    return (state_out, decay_total)


def block_output(conv_out, dt_raw, head_params, state_in, starts):
    values, key_rows, queries, step_size, cumlog, segment = block_parts(
        conv_out, dt_raw, head_params, starts
    )
    position = jnp.arange(conv_out.shape[0])
    causal = (position[:, None] >= position[None, :]) & (segment[:, None] == segment[None, :])
    log_gaps = jnp.where(causal[:, :, None], cumlog[:, None, :] - cumlog[None, :, :], 0.0)
    decays = jnp.exp(log_gaps) * causal[:, :, None].astype(F32)
    scores = jnp.dot(queries, key_rows.T, precision=HIGH)
    mixing = scores[:, :, None] * decays * step_size[None, :, :]
    within = jnp.einsum("tsh,shp->thp", mixing, values, precision=HIGH)
    inflow = jnp.exp(cumlog) * (segment == 0).astype(F32)[:, None]
    carried = jnp.einsum("tn,hpn->thp", queries, state_in, precision=HIGH) * inflow[:, :, None]
    skipped = head_params[2][None, :, None] * values
    return (within + carried + skipped).reshape(conv_out.shape[0], DI)


MESH = pl.DeviceIdType.MESH


class Place:
    def __init__(self, n):
        self.n, self.depth = n, n // 8
        self.me = me = lax.axis_index("seq")
        self.z, self.y, self.x, self.c = me // 8, (me // 4) % 2, (me // 2) % 2, me % 2

    def flipped(self, rz, ry, rx, rc):
        z, bit = 0, 1
        while bit < self.depth:
            z = z + ((self.z // bit + rz // bit) % 2) * bit
            bit *= 2
        y, x, c = (self.y + ry) % 2, (self.x + rx) % 2, (self.c + rc) % 2
        return ((z * 2 + y) * 2 + x) * 2 + c

    def split(self, place):
        depth = self.depth
        rz, r1, r2 = place % depth, (place // depth) % 2, (place // (2 * depth)) % 2
        return rz, r1, r2, place // (4 * depth)

    def device(self, place):
        rz, r1, r2, rc = self.split(place)
        owner = (self.c + rc) % 2
        return self.flipped(rz, r2 + owner * (r1 - r2), r1 + owner * (r2 - r1), rc)

    def place_there(self, place):
        rz, r1, r2, rc = self.split(place)
        s1, s2 = r1 + rc * (r2 - r1), r2 + rc * (r1 - r2)
        return ((rc * 2 + s2) * 2 + s1) * self.depth + rz

    def halves(self):
        steps, bit = [], 1
        while bit < self.depth:
            steps.append((bit, self.flipped(bit, 0, 0, 0)))
            bit *= 2
        steps.append((self.depth, self.flipped(0, self.c, 1 - self.c, 0)))
        steps.append((2 * self.depth, self.flipped(0, 1 - self.c, self.c, 0)))
        steps.append((4 * self.depth, self.flipped(0, 0, 0, 1)))
        return steps


def greet(n):
    barrier = pltpu.get_barrier_semaphore()
    me = lax.axis_index("seq")

    @pl.loop(1, n)
    def _(hop):
        other = lax.rem(me + hop, n)
        pl.semaphore_signal(barrier, inc=1, device_id=(other,), device_id_type=MESH)

    pl.semaphore_wait(barrier, n - 1)


def remote(source, target, send_sem, recv_sem, device):
    return pltpu.make_async_remote_copy(
        src_ref=source,
        dst_ref=target,
        send_sem=send_sem,
        recv_sem=recv_sem,
        device_id=(device,),
        device_id_type=MESH,
    )


def landed(ref, sem):
    pltpu.make_async_copy(ref, ref, sem).wait()


def rows_of(place, count, rows):
    return pl.ds(pl.multiple_of(place * rows, rows), count * rows)


GATHER_TIMES = [0, 1, 2, 3, 5, 6]
EMBED_TIMES = [2, 4, 6, 8, 10, 11]


def gather_kernel(n, chunks, *refs):
    count = (len(refs) - 13) // 2
    shards, patches_ref, weight_ref = refs[:count], refs[count], refs[count + 1]
    wholes = refs[count + 2 : -11]
    embedded_ref, parted_ref, product, got, own_sem = refs[-11:-6]
    send_sem, recv_sem, part_send, part_recv, sum_send, sum_recv = refs[-6:]
    here = Place(n)
    greet(n)
    owns = []
    for index in range(count):
        rows = shards[index].shape[0]
        target = wholes[index].at[rows_of(here.me, 1, rows)]
        owns.append(pltpu.make_async_copy(shards[index], target, own_sem.at[index]))
        owns[-1].start()
    for own in owns:
        own.wait()
    steps = here.halves()

    def block(chunk, place):
        index, first, rows, column, columns = chunks[chunk]
        start = here.device(place) * shards[index].shape[0] + first
        return wholes[index].at[pl.ds(pl.multiple_of(start, 16), rows), pl.ds(column, columns)]

    def sending(chunk, step, place):
        blocks, partner = steps[step]
        there = blocks + place
        ref = block(chunk, place)
        return remote(ref, ref, send_sem.at[chunk, there], recv_sem.at[chunk, there], partner)

    def arrive(chunk, step):
        blocks = steps[step][0]

        @pl.loop(blocks, 2 * blocks)
        def _(place):
            landed(block(chunk, place), recv_sem.at[chunk, place])

    def send(chunk, step):
        @pl.loop(0, steps[step][0])
        def _(place):
            sending(chunk, step, place).start()

    rows, width = patches_ref.shape[0], patches_ref.shape[1] // n

    def part_of(place):
        start = pl.multiple_of(here.device(place) * width, 128)
        return patches_ref.at[:, pl.ds(start, width)]

    def parting(place):
        there = here.place_there(place)
        target = parted_ref.at[rows_of(there, 1, rows)]
        return remote(
            part_of(place), target, part_send.at[place], part_recv.at[there], here.device(place)
        )

    half = n // 2
    own_part = pltpu.make_async_copy(part_of(0), parted_ref.at[rows_of(0, 1, rows)], part_recv.at[0])
    own_part.start()

    @pl.loop(1, n)
    def _(hop):
        parting(n - hop).start()

    def multiply(first):
        @pl.loop(first, first + half)
        def _(place):
            landed(parted_ref.at[rows_of(place, 1, rows)], part_recv.at[place])

        @pl.loop(0, half // 4)
        def _(index):
            cut = rows_of(first // 4 + index, 1, 4 * rows)
            product[cut] = dot(parted_ref[cut], weight_ref[...])

    def summing(step):
        blocks, partner = steps[len(steps) - 1 - step]
        cut = pl.ds(blocks * rows, blocks * rows)
        return remote(product.at[cut], got.at[cut], sum_send.at[step], sum_recv.at[step], partner)

    def add(step):
        blocks = steps[len(steps) - 1 - step][0]
        summing(step).wait_recv()
        mine, cut = pl.ds(0, blocks * rows), pl.ds(blocks * rows, blocks * rows)
        product[mine] += got[cut]

    def embed(time):
        if time == EMBED_TIMES[0]:
            multiply(half)
            summing(0).start()
            multiply(0)
        for step in range(len(steps)):
            if time == EMBED_TIMES[step + 1]:
                add(step)
                if step + 1 < len(steps):
                    summing(step + 1).start()

    for time in range(max(len(chunks) + GATHER_TIMES[-1], EMBED_TIMES[-1] + 1)):
        for step in range(len(steps), -1, -1):
            chunk = time - GATHER_TIMES[step]
            if 0 <= chunk < len(chunks):
                if step > 0:
                    arrive(chunk, step - 1)
                if step < len(steps):
                    send(chunk, step)
        embed(time)
    embedded_ref[...] = product[pl.ds(0, rows)]

    @pl.loop(1, n)
    def _(place):
        parting(place).wait_send()

    for step in range(len(steps)):
        summing(step).wait_send()
    for chunk in range(len(chunks)):
        for step in range(len(steps)):

            @pl.loop(0, steps[step][0])
            def _(place):
                sending(chunk, step, place).wait_send()


def gather_weights(n, shards, cuts, patches, patch_weight):
    if n != 32 or any(shard.shape[0] % 16 for shard in shards):
        wholes = [lax.all_gather(shard, "seq", axis=0, tiled=True) for shard in shards]
        parted = patches.reshape(patches.shape[0], n, -1).transpose(1, 0, 2)
        parted = lax.all_to_all(parted, "seq", 0, 0, tiled=True)
        parted = parted.reshape(-1, parted.shape[-1])
        product = dot(parted, patch_weight)
        return wholes + [
            lax.psum_scatter(product, "seq", scatter_dimension=0, tiled=True),
            parted,
        ]
    rows, phases = patches.shape[0], n.bit_length() - 1
    chunks = [
        (index, first, rows, column, min(columns, shard.shape[1] - column))
        for index, (shard, (rows, columns)) in enumerate(zip(shards, cuts))
        for first in range(0, shard.shape[0], rows)
        for column in range(0, shard.shape[1], columns)
    ]
    sems = [pltpu.SemaphoreType.DMA((len(chunks), n))] * 2
    return pl.pallas_call(
        functools.partial(gather_kernel, n, chunks),
        out_shape=[
            jax.ShapeDtypeStruct((n * shard.shape[0], shard.shape[1]), shard.dtype) for shard in shards
        ]
        + [
            jax.ShapeDtypeStruct((rows, D), F32),
            jax.ShapeDtypeStruct((n * rows, patches.shape[1] // n), BF),
        ],
        in_specs=[pl.BlockSpec(memory_space=pltpu.VMEM)] * (len(shards) + 2),
        out_specs=[pl.BlockSpec(memory_space=pltpu.HBM)] * len(shards)
        + [pl.BlockSpec(memory_space=pltpu.VMEM)] * 2,
        scratch_shapes=[
            pltpu.VMEM((n * rows, D), F32),
            pltpu.VMEM((n * rows, D), F32),
            pltpu.SemaphoreType.DMA((len(shards),)),
        ]
        + sems
        + [pltpu.SemaphoreType.DMA((n,))] * 2
        + [pltpu.SemaphoreType.DMA((phases,))] * 2,
        compiler_params=pltpu.CompilerParams(
            collective_id=0, has_side_effects=True, vmem_limit_bytes=32 * 2**20
        ),
        cost_estimate=pl.CostEstimate(flops=0, bytes_accessed=2**25, transcendentals=0),
    )(*shards, patches, patch_weight)


SUM_ROWS, SUM_COLUMNS, SUM_SLOTS = 32, 512, 8
SUM_TIMES = [0, 1, 3, 4, 6, 7]


def columns_of(chunk):
    return pl.ds(pl.multiple_of(chunk * SUM_COLUMNS, SUM_COLUMNS), SUM_COLUMNS)


class Sums:
    def __init__(self, here, sources, out, kept, sent, got, send_sem, recv_sem):
        self.here, self.sources, self.out = here, sources, out
        self.kept, self.sent, self.got = kept, sent, got
        self.send_sem, self.recv_sem = send_sem, recv_sem
        self.steps = here.halves()[::-1]
        self.chunks = got.shape[0]
        self.times = self.chunks + SUM_TIMES[-1]

    def copy(self, chunk, step):
        blocks, partner = self.steps[step]
        cut = pl.ds(blocks * SUM_ROWS, blocks * SUM_ROWS)
        return remote(
            self.sent.at[chunk % SUM_SLOTS, cut],
            self.got.at[chunk, cut],
            self.send_sem.at[chunk, step],
            self.recv_sem.at[chunk, step],
            partner,
        )

    def sent_all(self, chunk):
        for step in range(len(self.steps)):
            self.copy(chunk, step).wait_send()

    def begin(self, chunk):
        half = self.here.n // 2 * SUM_ROWS
        slot = chunk % SUM_SLOTS

        @pl.when(chunk >= SUM_SLOTS)
        def _():
            self.sent_all(chunk - SUM_SLOTS)

        for first, stop, find, left, right in self.sources:

            @pl.when((chunk >= first) & (chunk < stop))
            def _():
                which, column = find(chunk - first)

                def product(row):
                    return dot(left[which, pl.ds(row, half)], right[:, columns_of(column)])

                self.sent[slot, pl.ds(half, half)] = product(half).astype(BF)
                self.copy(chunk, 0).start()
                self.kept[slot] = product(0)

    def go_on(self, chunk, step):
        slot, rows = chunk % SUM_SLOTS, self.steps[step - 1][0] * SUM_ROWS
        self.copy(chunk, step - 1).wait_recv()
        total = self.kept[slot, pl.ds(0, rows)] + self.got[chunk, pl.ds(rows, rows)].astype(F32)
        if step == len(self.steps):
            self.out(chunk, total)
            return
        half = rows // 2
        self.sent[slot, pl.ds(half, half)] = total[half:].astype(BF)
        self.copy(chunk, step).start()
        self.kept[slot, pl.ds(0, half)] = total[:half]

    def at(self, time):
        for step in range(len(self.steps), -1, -1):
            chunk = time - SUM_TIMES[step]

            @pl.when((chunk >= 0) & (chunk < self.chunks))
            def _():
                if step == 0:
                    self.begin(chunk)
                else:
                    self.go_on(chunk, step)

    def run(self, first, stop):
        pl.loop(first, stop)(self.at)

    def end(self):
        @pl.loop(max(0, self.chunks - SUM_SLOTS), self.chunks)
        def _(chunk):
            self.sent_all(chunk)


def turn(order_ref, left_ref, values_ref):
    for index in range(values_ref.shape[0]):
        left_ref[index] = dot_t(order_ref[...], values_ref[index]).astype(BF)


def lefts_scratch(n, lefts):
    return [pltpu.VMEM((lefts.shape[0], n * SUM_ROWS, lefts.shape[1]), BF)]


def sums_scratch(n, chunks):
    rows, phases = n * SUM_ROWS, n.bit_length() - 1
    return [
        pltpu.VMEM((SUM_SLOTS, rows // 2, SUM_COLUMNS), F32),
        pltpu.VMEM((SUM_SLOTS, rows, SUM_COLUMNS), BF),
        pltpu.VMEM((chunks, rows, SUM_COLUMNS), BF),
        pltpu.SemaphoreType.DMA((chunks, phases)),
        pltpu.SemaphoreType.DMA((chunks, phases)),
    ]


def last_find(chunk):
    return (chunk + 7) // 16 + (chunk + 5) // 16, chunk


def last_kernel(
    n, grad_ref, parted_ref, small_ref, order_ref, values_ref, right_ref, direct_ref, weight_ref,
    d_weight_ref, d_small_ref, d_in_ref, d_out_ref, input_ref,
    back, d_patches, b_send, b_recv, known, small_kept, small_got, g_send, g_recv, t_send, t_recv, left_ref, *scratch
):
    here = Place(n)
    rows = grad_ref.shape[0]
    greet(n)
    known[pl.ds(0, rows)] = grad_ref[...]

    @pl.loop(0, n)
    def _(place):
        device = here.device(place)
        small_kept[rows_of(place, 1, LOG_ROWS)] = small_ref[rows_of(device, 1, LOG_ROWS)]

    turn(order_ref, left_ref, values_ref)
    spare = d_in_ref.shape[1] % SUM_COLUMNS

    def store(chunk, total):
        @pl.when(chunk < 8)
        def _():
            d_in_ref[:, columns_of(chunk)] = total

        @pl.when(chunk == 8)
        def _():
            d_in_ref[:, pl.ds(8 * SUM_COLUMNS, spare)] = total[:, :spare]

        @pl.when(chunk >= 9)
        def _():
            part = (chunk - 9) // 2
            d_out_ref[rows_of(part, 1, SUM_ROWS), columns_of((chunk - 9) % 2)] = total

    sums = Sums(here, [(0, 13, last_find, left_ref, right_ref)], store, *scratch)
    steps = here.halves()
    copies = []
    for step in range(len(steps)):
        blocks, partner = steps[step]
        source, target = pl.ds(0, blocks * rows), pl.ds(blocks * rows, blocks * rows)
        gather = remote(known.at[source], known.at[target], g_send.at[step], g_recv.at[step], partner)
        gather.start()
        blocks, partner = steps[::-1][step]
        cut, mine = pl.ds(blocks * LOG_ROWS, blocks * LOG_ROWS), pl.ds(0, blocks * LOG_ROWS)
        told = remote(small_kept.at[cut], small_got.at[cut], t_send.at[step], t_recv.at[step], partner)
        told.start()
        copies += [gather, told]
        sums.run(2 * step, 2 * step + 2)
        gather.wait_recv()
        told.wait_recv()
        small_kept[mine] = small_kept[mine] + small_got[cut]
    width = weight_ref.shape[0]
    back[...] = dot_t(known[...], weight_ref[...]).astype(BF)
    mine = pl.ds(pl.multiple_of(here.me * width, 128), width)

    def returning(place):
        source, target = back.at[rows_of(place, 1, rows)], d_patches.at[:, mine]
        there = here.place_there(place)
        return remote(source, target, b_send.at[place], b_recv.at[there], here.device(place))

    @pl.loop(1, n)
    def _(place):
        returning(place).start()

    pltpu.make_async_copy(back.at[pl.ds(0, rows)], d_patches.at[:, mine], b_recv.at[0]).start()
    sums.run(2 * len(steps), 2 * len(steps) + 1)
    d_weight_ref[...] = lax.dot_general(
        parted_ref[...], known[...], (((0,), (0,)), ((), ())), preferred_element_type=F32
    )
    sums.run(2 * len(steps) + 1, sums.times)

    @pl.loop(0, n)
    def _(place):
        cut = pl.ds(pl.multiple_of(here.device(place) * width, 128), width)
        landed(d_patches.at[:, cut], b_recv.at[place])

    input_ref[...] = (direct_ref[...] + d_patches[...].astype(F32)).astype(BF)

    @pl.loop(1, n)
    def _(place):
        returning(place).wait_send()

    d_small_ref[...] = small_kept[pl.ds(0, LOG_ROWS)]
    for copy in copies:
        copy.wait_send()
    sums.end()


def last_sums(n, grad, parted, small, order, lefts, right, direct, weight, projections):
    rows, width = grad.shape[0], parted.shape[1]
    phases, chunks = n.bit_length() - 1, right.shape[1] // SUM_COLUMNS
    return pl.pallas_call(
        functools.partial(last_kernel, n),
        out_shape=[
            jax.ShapeDtypeStruct((width, D), F32),
            jax.ShapeDtypeStruct((LOG_ROWS, 128), F32),
            jax.ShapeDtypeStruct((SUM_ROWS, projections), F32),
            jax.ShapeDtypeStruct((2 * SUM_ROWS, D), F32),
            jax.ShapeDtypeStruct(direct.shape, BF),
        ],
        in_specs=[pl.BlockSpec(memory_space=pltpu.VMEM)] * 8,
        out_specs=[pl.BlockSpec(memory_space=pltpu.VMEM)] * 5,
        scratch_shapes=[
            pltpu.VMEM((n * rows, width), BF),
            pltpu.VMEM(direct.shape, BF),
            pltpu.SemaphoreType.DMA((n,)),
            pltpu.SemaphoreType.DMA((n,)),
            pltpu.VMEM((n * rows, D), BF),
            pltpu.VMEM(small.shape, F32),
            pltpu.VMEM(small.shape, F32),
        ]
        + [pltpu.SemaphoreType.DMA((phases,))] * 4
        + lefts_scratch(n, lefts)
        + sums_scratch(n, chunks),
        compiler_params=pltpu.CompilerParams(
            collective_id=1, has_side_effects=True, vmem_limit_bytes=62 * 2**20
        ),
        cost_estimate=pl.CostEstimate(flops=2**32, bytes_accessed=2**24, transcendentals=0),
    )(grad, parted, small, order, lefts, right, direct, weight)


LOG_ROWS = 8


class Exchange:
    def __init__(self, n, reverse, states, logs_in, out, spread, logs, summed, *sems):
        self.n, self.reverse = n, reverse
        self.me = lax.axis_index("seq")
        self.states, self.logs_in, self.out = states, logs_in, out
        self.spread, self.logs, self.summed = spread, logs, summed
        self.sems = sems
        self.rows = states.shape[0] // n

    def spreading(self, other):
        send, recv = self.sems[:2]
        source = self.states.at[rows_of(other, 1, self.rows)]
        target = self.spread.at[rows_of(self.me, 1, self.rows)]
        return remote(source, target, send.at[other], recv.at[self.me], other)

    def telling(self, other):
        send, recv = self.sems[2:4]
        target = self.logs.at[rows_of(self.me, 1, LOG_ROWS)]
        return remote(self.logs_in, target, send.at[other], recv.at[self.me], other)

    def returning(self, other):
        send, recv = self.sems[4:6]
        source = self.summed.at[rows_of(other, 1, self.rows)]
        target = self.out.at[rows_of(self.me, 1, self.rows)]
        return remote(source, target, send.at[other], recv.at[self.me], other)

    def tell(self):
        @pl.loop(1, self.n)
        def _(hop):
            self.telling(lax.rem(self.me + hop, self.n)).start()

        target = self.logs.at[rows_of(self.me, 1, LOG_ROWS)]
        pltpu.make_async_copy(self.logs_in, target, self.sems[3].at[self.me]).start()

    def start(self):
        @pl.loop(1, self.n)
        def _(hop):
            self.spreading(lax.rem(self.me + hop, self.n)).start()

        mine = rows_of(self.me, 1, self.rows)
        recv = self.sems[1].at[self.me]
        pltpu.make_async_copy(self.states.at[mine], self.spread.at[mine], recv).start()

    def join(self):
        n, rows, summed, spread = self.n, self.rows, self.summed, self.spread

        @pl.loop(0, n)
        def _(other):
            landed(spread.at[rows_of(other, 1, rows)], self.sems[1].at[other])
            landed(self.logs.at[rows_of(other, 1, LOG_ROWS)], self.sems[3].at[other])

        head = self.me * MHEADS // n
        lane = lax.broadcasted_iota(jnp.int32, (LOG_ROWS, 128), 1)
        row = lax.broadcasted_iota(jnp.int32, (LOG_ROWS, 128), 0)

        def step(count, total):
            place = n - 1 - count if self.reverse else count
            cut = rows_of(place, 1, rows)
            summed[cut] = total.astype(BF)
            told = self.logs[rows_of(place, 1, LOG_ROWS)]
            log = jnp.sum(jnp.where((lane == head) & (row == 0), told, 0.0), keepdims=True)
            flag = jnp.sum(jnp.where((lane == MHEADS) & (row == 0), told, 0.0), keepdims=True)
            decay = jnp.where(flag > 0.0, 0.0, jnp.exp(log))
            return decay * total + spread[cut].astype(F32)

        lax.fori_loop(0, n, step, jnp.zeros((rows, NSTATE), F32))

        @pl.loop(1, n)
        def _(hop):
            self.returning(lax.rem(self.me + hop, n)).start()

        mine = rows_of(self.me, 1, rows)
        recv = self.sems[5].at[self.me]
        pltpu.make_async_copy(summed.at[mine], self.out.at[mine], recv).start()

    def arrive(self):
        @pl.loop(0, self.n)
        def _(other):
            landed(self.out.at[rows_of(other, 1, self.rows)], self.sems[5].at[other])

    def end(self):
        @pl.loop(1, self.n)
        def _(hop):
            other = lax.rem(self.me + hop, self.n)
            self.spreading(other).wait_send()
            self.telling(other).wait_send()
            self.returning(other).wait_send()


def exchange_scratch(n):
    total = MHEADS * MHEAD_DIM
    return [
        pltpu.VMEM((total, NSTATE), BF),
        pltpu.VMEM((n * LOG_ROWS, 128), F32),
        pltpu.VMEM((total, NSTATE), BF),
    ] + [pltpu.SemaphoreType.DMA((n,))] * 6


def states_kernel(n, reverse, states_ref, logs_ref, out_ref, *scratch):
    greet(n)
    exchange = Exchange(n, reverse, states_ref, logs_ref, out_ref, *scratch)
    exchange.tell()
    exchange.start()
    exchange.join()
    exchange.arrive()
    exchange.end()


def told_logs(logs):
    return jnp.zeros((LOG_ROWS, 128), F32).at[0, : logs.shape[0]].set(logs)


def pass_states(n, states, logs, reverse):
    total = MHEADS * MHEAD_DIM
    return pl.pallas_call(
        functools.partial(states_kernel, n, reverse),
        out_shape=jax.ShapeDtypeStruct((total, NSTATE), BF),
        in_specs=[pl.BlockSpec(memory_space=pltpu.VMEM)] * 2,
        out_specs=pl.BlockSpec(memory_space=pltpu.VMEM),
        scratch_shapes=exchange_scratch(n),
        compiler_params=pltpu.CompilerParams(
            collective_id=3 if reverse else 2, has_side_effects=True, vmem_limit_bytes=16 * 2**20
        ),
        cost_estimate=pl.CostEstimate(flops=2**22, bytes_accessed=2**21, transcendentals=0),
    )(states.reshape(total, NSTATE).astype(BF), told_logs(logs))


NN, NT, TN = ((1,), (0,)), ((1,), (1,)), ((0,), (0,))


def in_parts(value, count):
    if value.dtype == BF:
        return [value]
    parts = []
    for _ in range(count):
        parts.append(value.astype(BF))
        value = value - parts[-1].astype(F32)
    return parts


def dot_fine(left, right, dims, count=2):
    total = None
    for i, a in enumerate(in_parts(left, count)):
        for j, b in enumerate(in_parts(right, count)):
            if i + j < count:
                found = lax.dot_general(a, b, (dims, ((), ())), preferred_element_type=F32)
                total = found if total is None else total + found
    return total


def mixer_back_kernel(
    n, logs_ref, order_ref, mixed_ref, normed_ref, out_right_ref, qkv_right_ref, hidden_ref, slots_ref,
    dy_ref, x_ref, keys_ref, queries_ref, state_ref, steps_ref, marks_ref, head_ref,
    dx_ref, d_dt_ref, d_head_ref, d_out_ref, d_qkv_ref, unpatch_ref, dkeys_ref, dqueries_ref,
    scores, d_scores, d_step, d_cum, d_turned, grads, back, left_ref, hidden_left, *scratch
):
    rows, width = x_ref.shape[0], 2 * MHEAD_DIM
    greet(n)
    exchange = Exchange(n, True, grads, logs_ref, back, *scratch[:9])

    def store(chunk, total):
        for (first, stop, *_), target in zip(sources, (unpatch_ref, d_out_ref, d_qkv_ref)):

            @pl.when((chunk >= first) & (chunk < stop))
            def _():
                target[:, columns_of(chunk - first)] = total

    def find(which):
        return lambda chunk: (which, chunk)

    sources = [
        (0, 16, find(0), hidden_left, slots_ref),
        (16, 18, find(0), left_ref, out_right_ref),
        (18, 24, find(1), left_ref, qkv_right_ref),
    ]
    sums = Sums(Place(n), sources, store, *scratch[9:])
    exchange.tell()
    turn(order_ref, hidden_left, hidden_ref)
    left_ref[0] = dot_t(order_ref[...], mixed_ref[...]).astype(BF)
    left_ref[1] = dot_t(order_ref[...], normed_ref[...]).astype(BF)

    head_lane = lax.broadcasted_iota(jnp.int32, (1, MHEADS), 1)
    lanes = lax.broadcasted_iota(jnp.int32, (1, width), 1)
    halves = [lanes < MHEAD_DIM, lanes >= MHEAD_DIM]
    step, cum = steps_ref[0, :rows, :MHEADS], steps_ref[1, :rows, :MHEADS]
    turned_step, turned_cum = steps_ref.at[3], steps_ref.at[4]
    reach = marks_ref[0][:, :rows]
    from_before, to_after = marks_ref[1][:, 0:1], marks_ref[1][:, 1:2]
    last_cum = cum[rows - 1 : rows]
    to_end = jnp.exp(last_cum - cum) * to_after

    def column(values, head):
        return jnp.sum(jnp.where(head_lane == head, values, 0.0), axis=1, keepdims=True)

    def at_head(head, values):
        return jnp.where(head_lane == head, values, 0.0)

    def of_pair(pair, values):
        return jnp.where(halves[0], column(values, 2 * pair), column(values, 2 * pair + 1))

    def columns(pair):
        return pl.ds(pl.multiple_of(pair * width, width), width)

    scores[...] = dot_fine(queries_ref[...], keys_ref[...], NT)
    d_scores[...] = jnp.zeros_like(d_scores)
    d_step[...] = jnp.zeros_like(d_step)
    d_cum[...] = jnp.zeros_like(d_cum)
    d_turned[...] = jnp.zeros_like(d_turned)
    dqueries_ref[...] = jnp.zeros_like(dqueries_ref)
    d_head_ref[...] = jnp.zeros_like(d_head_ref)

    @pl.loop(0, MHEADS // 2)
    def _(pair):
        sums.at(pair)
        x, dy, state = x_ref[:, columns(pair)], dy_ref[:, columns(pair)], state_ref[columns(pair)]
        dx = of_pair(pair, head_ref[2:3]) * dy
        inflow = jnp.exp(of_pair(pair, cum)) * from_before
        dy_in = dy * inflow
        carried = dy_in * dot_fine(queries_ref[...], state, NT)
        dqueries_ref[...] += dot_fine(dy_in, state, NN)
        grads[columns(pair)] = dot_fine(dy_in, queries_ref[...], TN).astype(BF)
        for which, half in enumerate(halves):
            head = 2 * pair + which
            mine = pl.ds(head, 1)
            gap = column(cum, head) - turned_cum[mine, :rows]
            decay = jnp.exp(jnp.where(reach > 0.0, gap, 0.0)) * reach
            weighted = scores[...] * decay
            step_row = turned_step[mine, :rows]
            mixing = weighted * step_row
            d_mixing = dot_fine(dy, jnp.where(half, x, 0.0), NT)
            dx += dot_fine(mixing, jnp.where(half, dy, 0.0), TN)
            d_scores[...] += d_mixing * decay * step_row
            d_gap = d_mixing * mixing
            d_turned[0, mine, :rows] = jnp.sum(d_mixing * weighted, axis=0, keepdims=True)
            d_turned[1, mine, :rows] = -jnp.sum(d_gap, axis=0, keepdims=True)
            moved = jnp.sum(d_gap, axis=1, keepdims=True)
            moved += jnp.sum(jnp.where(half, carried, 0.0), axis=1, keepdims=True)
            d_cum[...] += at_head(head, moved)
            skipped = jnp.sum(jnp.where(half, dy * x, 0.0), keepdims=True)
            d_head_ref[2:3] += at_head(head, skipped)
        dx_ref[:, columns(pair)] = dx

    dkeys_ref[...] = dot_fine(d_scores[...], queries_ref[...], TN)
    dqueries_ref[...] += dot_fine(d_scores[...], keys_ref[...], NN)
    exchange.start()
    sums.run(16, 20)
    exchange.join()
    sums.run(20, 24)
    exchange.arrive()

    @pl.loop(0, MHEADS // 2)
    def _(pair):
        @pl.when(pair < 7)
        def _():
            sums.at(24 + pair)

        x, state, grad = x_ref[:, columns(pair)], state_ref[columns(pair)], back[columns(pair)]
        weight = of_pair(pair, to_end * step)
        d_weighted = dot_fine(keys_ref[...], grad, NT)
        dkeys_ref[...] += dot_fine(x * weight, grad, NN)
        dx_ref[:, columns(pair)] += weight * d_weighted
        kept = grad.astype(F32) * state.astype(F32)
        for which, half in enumerate(halves):
            head = 2 * pair + which
            d_weight = jnp.sum(jnp.where(half, x * d_weighted, 0.0), axis=1, keepdims=True)
            d_step[...] += at_head(head, d_weight * column(to_end, head))
            moved = d_weight * column(to_end * step, head)
            d_cum[...] -= at_head(head, moved)
            d_decay = jnp.sum(kept[which * MHEAD_DIM : (which + 1) * MHEAD_DIM], keepdims=True)
            ended = jnp.sum(moved, keepdims=True)
            ended += d_decay * jnp.exp(column(last_cum, head)) * from_before[rows - 1 : rows]
            d_cum[rows - 1 : rows] += at_head(head, ended)

    d_steps = d_step[...] + d_turned[0].T[:rows, :MHEADS]
    d_cums = d_cum[...] + d_turned[1].T[:rows, :MHEADS]
    later = lax.broadcasted_iota(jnp.int32, (rows, rows), 0) <= lax.broadcasted_iota(
        jnp.int32, (rows, rows), 1
    )
    d_logs = dot_fine(later.astype(BF), d_cums, NN, 3)
    rate = jnp.exp(head_ref[1:2])
    d_raw = (d_steps - rate * d_logs) * steps_ref[2, :rows, :MHEADS]
    d_dt_ref[...] = d_raw
    d_head_ref[0:1] = jnp.sum(d_raw, axis=0, keepdims=True)
    d_head_ref[1:2] = -rate * jnp.sum(step * d_logs, axis=0, keepdims=True)
    dx_ref[:, pl.ds(DI, NSTATE)] = dkeys_ref[...]
    dx_ref[:, pl.ds(DI + NSTATE, NSTATE)] = dqueries_ref[...]
    sums.run(31, sums.times)
    sums.end()
    exchange.end()


def mixer_tables(dt_raw, head_params, starts):
    rows = dt_raw.shape[0]
    step = jax.nn.softplus(dt_raw + head_params[0])
    cum = jnp.cumsum(-step * jnp.exp(head_params[1]), axis=0)
    segment = jnp.cumsum(starts, axis=0, dtype=jnp.int32)
    slope = jax.nn.sigmoid(dt_raw + head_params[0])
    square = [jnp.pad(v, ((0, 128 - v.shape[0]), (0, 128 - v.shape[1]))) for v in (step.T, cum.T)]
    tall = [jnp.pad(v, ((0, 128 - rows), (0, 128 - MHEADS))) for v in (step, cum, slope)]
    position = jnp.arange(rows)
    reach = (position[:, None] >= position[None, :]) & (segment[:, None] == segment[None, :])
    ends = jnp.stack([segment == 0, segment == segment[-1]], axis=1)
    marks = [jnp.pad(v.astype(F32), ((0, 0), (0, 128 - v.shape[1]))) for v in (reach, ends)]
    return jnp.stack(tall + square), jnp.stack(marks)


def mixer_back(told, order, values, rights, hidden, slots, dy, conv_out, state_in, steps, marks, head_params):
    n, rows = lax.axis_size("seq"), conv_out.shape[0]
    x, keys, queries = jnp.split(conv_out, [DI, DI + NSTATE], axis=1)
    total = MHEADS * MHEAD_DIM
    wide = sum(right.shape[1] for right in rights)
    return pl.pallas_call(
        functools.partial(mixer_back_kernel, n),
        out_shape=[
            jax.ShapeDtypeStruct((rows, CONV_CH), F32),
            jax.ShapeDtypeStruct((rows, MHEADS), F32),
            jax.ShapeDtypeStruct((8, MHEADS), F32),
        ]
        + [jax.ShapeDtypeStruct((SUM_ROWS, right.shape[1]), F32) for right in rights]
        + [jax.ShapeDtypeStruct((SUM_ROWS, slots.shape[1]), F32)],
        in_specs=[pl.BlockSpec(memory_space=pltpu.VMEM)] * 16,
        out_specs=[pl.BlockSpec(memory_space=pltpu.VMEM)] * 6,
        scratch_shapes=[
            pltpu.VMEM((rows, NSTATE), F32),
            pltpu.VMEM((rows, NSTATE), F32),
            pltpu.VMEM((rows, rows), F32),
            pltpu.VMEM((rows, rows), F32),
            pltpu.VMEM((rows, MHEADS), F32),
            pltpu.VMEM((rows, MHEADS), F32),
            pltpu.VMEM((2, 128, 128), F32),
            pltpu.VMEM((total, NSTATE), BF),
            pltpu.VMEM((total, NSTATE), BF),
        ]
        + [pltpu.VMEM((2, n * SUM_ROWS, values[0].shape[0]), BF)]
        + lefts_scratch(n, hidden)
        + exchange_scratch(n)
        + sums_scratch(n, 24),
        compiler_params=pltpu.CompilerParams(
            collective_id=3, has_side_effects=True, vmem_limit_bytes=62 * 2**20
        ),
        cost_estimate=pl.CostEstimate(flops=2**32, bytes_accessed=2**24, transcendentals=2**20),
    )(
        told, order, *values, *rights, hidden, slots, dy, x, keys, queries,
        state_in, steps, marks, head_params,
    )


FF_TILE = D


def feed_forward_kernel(normed_ref, gate_w_ref, up_w_ref, gate_ref, up_ref, hid_ref):
    gate, up = dot(normed_ref[...], whole_of(gate_w_ref)), dot(normed_ref[...], whole_of(up_w_ref))
    gate_ref[...], up_ref[...] = gate.astype(BF), up.astype(BF)
    hid_ref[...] = (silu(gate) * up).astype(BF)


def feed_forward_blocks(n):
    tiles, first = FF // FF_TILE, PATCH + 4
    return [
        flat_block(n, D // n, lambda i: first + i),
        flat_block(n, D // n, lambda i: first + tiles + i),
        pl.BlockSpec((FF_TILE, D), lambda i: (i, 0)),
    ]


def feed_forward(normed, flat):
    rows = normed.shape[0]
    tile = pl.BlockSpec((rows, FF_TILE), lambda i: (0, i))
    return pl.pallas_call(
        feed_forward_kernel,
        grid=(FF // FF_TILE,),
        out_shape=[jax.ShapeDtypeStruct((rows, FF), BF)] * 3,
        in_specs=[pl.BlockSpec((rows, D), lambda i: (0, 0)), *feed_forward_blocks(flat.shape[0])[:2]],
        out_specs=[tile, tile, tile],
        compiler_params=pltpu.CompilerParams(vmem_limit_bytes=56 * 2**20),
        cost_estimate=pl.CostEstimate(
            flops=4 * rows * D * FF, bytes_accessed=2**25, transcendentals=rows * FF
        ),
    )(normed, flat, flat)


def feed_forward_back_kernel(
    grad_ref, stream_ref, gain_ref, gate_ref, up_ref, hid_ref, gate_w_ref, up_w_ref, down_ref,
    out_ref, both_ref, d_stream_ref, d_low_ref, d_gain_ref, layer, total,
):
    step = pl.program_id(0)
    added = dot(hid_ref[...], down_ref[...])

    @pl.when(step == 0)
    def _():
        layer[...] = stream_ref[...] + added

    @pl.when(step > 0)
    def _():
        layer[...] += added

    d_hid = dot_t(grad_ref[...], down_ref[...])
    gate, up = gate_ref[...].astype(F32), up_ref[...].astype(F32)
    s = jax.nn.sigmoid(gate)
    d_gate = (d_hid * up * (s * (1.0 + gate * (1.0 - s)))).astype(BF)
    d_up = (d_hid * (gate * s)).astype(BF)
    both_ref[0], both_ref[1] = d_gate, d_up
    found = dot_t(d_gate, whole_of(gate_w_ref)) + dot_t(d_up, whole_of(up_w_ref))

    @pl.when(step == 0)
    def _():
        total[...] = found

    @pl.when(step > 0)
    def _():
        total[...] += found

    @pl.when(step == pl.num_programs(0) - 1)
    def _():
        out_ref[...] = layer[...].astype(BF)
        stream, d_normed = stream_ref[...], total[...]
        r = lax.rsqrt(jnp.mean(stream * stream, axis=-1, keepdims=True) + EPS)
        scaled = gain_ref[...] * d_normed
        inner = jnp.mean(stream * scaled, axis=-1, keepdims=True)
        d_stream = grad_ref[...].astype(F32) + r * scaled - stream * (r * r * r) * inner
        d_stream_ref[...] = d_stream
        d_low_ref[...] = d_stream.astype(BF)
        d_gain_ref[...] = jnp.sum(stream * r * d_normed, axis=0, keepdims=True)


def feed_forward_back(grad, stream, gain, gate, up, hid, flat, down):
    rows, tiles = stream.shape[0], FF // FF_TILE
    wide = pl.BlockSpec((rows, D), lambda i: (0, 0))
    tile = pl.BlockSpec((rows, FF_TILE), lambda i: (0, i))
    narrow = pl.BlockSpec((1, D), lambda i: (0, 0))
    out, both, d_stream, d_low, d_gain = pl.pallas_call(
        feed_forward_back_kernel,
        grid=(tiles,),
        out_shape=[
            jax.ShapeDtypeStruct((rows, D), BF),
            jax.ShapeDtypeStruct((2, rows, FF), BF),
            jax.ShapeDtypeStruct((rows, D), F32),
            jax.ShapeDtypeStruct((rows, D), BF),
            jax.ShapeDtypeStruct((1, D), F32),
        ],
        in_specs=[
            wide,
            wide,
            narrow,
            tile,
            tile,
            tile,
            *feed_forward_blocks(flat.shape[0]),
        ],
        out_specs=[wide, pl.BlockSpec((2, rows, FF_TILE), lambda i: (0, 0, i)), wide, wide, narrow],
        scratch_shapes=[pltpu.VMEM((rows, D), F32)] * 2,
        compiler_params=pltpu.CompilerParams(vmem_limit_bytes=60 * 2**20),
        cost_estimate=pl.CostEstimate(
            flops=8 * rows * D * FF, bytes_accessed=2**25, transcendentals=rows * FF
        ),
    )(grad, stream, gain[None], gate, up, hid, flat, flat, down)
    return out, both, d_stream, d_low, d_gain[0]


ATTN_ROWS = 128


def tile_mask():
    row = lax.broadcasted_iota(jnp.int32, (ATTN_ROWS, 2 * ATTN_ROWS), 0)
    column = lax.broadcasted_iota(jnp.int32, (ATTN_ROWS, 2 * ATTN_ROWS), 1) % ATTN_ROWS
    return (row // PATCH == column // PATCH) & (row >= column)


def first_head():
    return lax.broadcasted_iota(jnp.int32, (1, 2 * AHEAD_DIM), 1) < AHEAD_DIM


def one_below_other(pair):
    lanes, zeros = first_head(), jnp.zeros_like(pair)
    return jnp.concatenate([jnp.where(lanes, pair, zeros), jnp.where(lanes, zeros, pair)], axis=0)


def by_head(values, reduce):
    first = reduce(values[:, :ATTN_ROWS], axis=-1, keepdims=True)
    second = reduce(values[:, ATTN_ROWS:], axis=-1, keepdims=True)
    shape = (values.shape[0], ATTN_ROWS)
    return jnp.concatenate(
        [jnp.broadcast_to(first, shape), jnp.broadcast_to(second, shape)], axis=1
    )


def pair_probs(queries, key_rows, mask):
    scores = jnp.where(mask, dot_t(queries, key_rows) * AHEAD_DIM ** (-0.5), -1e30)
    raised = jnp.exp(scores - by_head(scores, jnp.max))
    return raised / by_head(raised, jnp.sum)


def attention_kernel(triple_ref, out_ref):
    mask = tile_mask()
    width = 2 * AHEAD_DIM
    for pair in range(AHEADS // 2):
        queries, key_rows, value_rows = [
            triple_ref[:, part * D + pair * width : part * D + (pair + 1) * width] for part in range(3)
        ]
        probs = pair_probs(queries, one_below_other(key_rows), mask)
        mixed = dot(probs.astype(BF), one_below_other(value_rows))
        out_ref[:, pair * width : (pair + 1) * width] = mixed.astype(BF)


def attention(triple):
    rows = triple.shape[0]
    return pl.pallas_call(
        attention_kernel,
        grid=(rows // ATTN_ROWS,),
        out_shape=jax.ShapeDtypeStruct((rows, D), BF),
        in_specs=[pl.BlockSpec((ATTN_ROWS, 3 * D), lambda i: (i, 0))],
        out_specs=pl.BlockSpec((ATTN_ROWS, D), lambda i: (i, 0)),
    )(triple)


def attention_back_kernel(
    triple_ref, low_ref, d_stream_ref, stream_ref, gain_ref, out_w_ref, q_ref, k_ref, v_ref,
    out_ref, d_out_ref, d_gain_ref,
):
    mask = tile_mask()
    width = 2 * AHEAD_DIM
    scale = AHEAD_DIM ** (-0.5)

    def of_keys(left, right):
        found = lax.dot_general(left, right, (((0,), (0,)), ((), ())), preferred_element_type=F32)
        return jnp.where(first_head(), found[:ATTN_ROWS], found[ATTN_ROWS:])

    grads = dot_t(low_ref[...], whole_of(out_w_ref)).astype(BF)
    for pair in range(AHEADS // 2):
        lo, hi = pair * width, (pair + 1) * width
        queries, key_rows, value_rows = [
            triple_ref[:, part * D + lo : part * D + hi] for part in range(3)
        ]
        grad = grads[:, lo:hi]
        key_rows = one_below_other(key_rows)
        probs = pair_probs(queries, key_rows, mask)
        d_probs = dot_t(grad, one_below_other(value_rows))
        d_scores = (probs * (d_probs - by_head(probs * d_probs, jnp.sum))).astype(BF)
        out_ref[:, lo:hi] = (scale * dot(d_scores, key_rows)).astype(BF)
        out_ref[:, D + lo : D + hi] = (scale * of_keys(d_scores, queries)).astype(BF)
        out_ref[:, 2 * D + lo : 2 * D + hi] = of_keys(probs.astype(BF), grad).astype(BF)

    d_normed = None
    for part, ref in enumerate((q_ref, k_ref, v_ref)):
        found = dot_t(out_ref[:, part * D : (part + 1) * D], whole_of(ref))
        d_normed = found if part == 0 else d_normed + found
    stream = stream_ref[...]
    r = lax.rsqrt(jnp.mean(stream * stream, axis=-1, keepdims=True) + EPS)
    scaled = gain_ref[...] * d_normed
    inner = jnp.mean(stream * scaled, axis=-1, keepdims=True)
    d_out_ref[...] = d_stream_ref[...] + r * scaled - stream * (r * r * r) * inner
    gained = jnp.sum(stream * r * d_normed, axis=0, keepdims=True)

    @pl.when(pl.program_id(0) == 0)
    def _():
        d_gain_ref[...] = gained

    @pl.when(pl.program_id(0) > 0)
    def _():
        d_gain_ref[...] += gained


def attention_back(triple, low, d_stream, stream, gain, flat):
    rows, n = triple.shape[0], flat.shape[0]
    wide = pl.BlockSpec((ATTN_ROWS, 3 * D), lambda i: (i, 0))
    tile = pl.BlockSpec((ATTN_ROWS, D), lambda i: (i, 0))
    narrow = pl.BlockSpec((1, D), lambda i: (0, 0))

    def block(place):
        return flat_block(n, D // n, lambda i: place)

    d_triple, d_out, d_gain = pl.pallas_call(
        attention_back_kernel,
        grid=(rows // ATTN_ROWS,),
        out_shape=[
            jax.ShapeDtypeStruct((rows, 3 * D), BF),
            jax.ShapeDtypeStruct((rows, D), F32),
            jax.ShapeDtypeStruct((1, D), F32),
        ],
        in_specs=[wide, tile, tile, tile, narrow]
        + [block(PATCH + 3), block(PATCH), block(PATCH + 1), block(PATCH + 2)],
        out_specs=[wide, tile, narrow],
        compiler_params=pltpu.CompilerParams(vmem_limit_bytes=56 * 2**20),
        cost_estimate=pl.CostEstimate(
            flops=8 * rows * D * D, bytes_accessed=2**24, transcendentals=0
        ),
    )(triple, low, d_stream, stream, gain[None], flat, flat, flat, flat)
    return d_triple, d_out, d_gain[0]


def local(
    byte_acts,
    resets,
    out_grad,
    patch_weight,
    patch_gain,
    mixer_in,
    conv_weight,
    conv_bias,
    head_params,
    mixer_gain,
    mixer_out,
    unpatch_weight,
    attn_gain,
    qkv_weight,
    attn_out,
    ffn_gain,
    gate_up,
    down_weight,
):
    n = lax.axis_size("seq")
    me = lax.axis_index("seq")
    ring = Ring(n)

    def passed_along(block, distance):
        route = [(i - distance, i) for i in range(n) if 0 <= i - distance < n]
        return lax.ppermute(block, "seq", route)

    live = Live()
    order = ring.order()

    byte_wide = byte_acts.astype(F32)
    patches = byte_acts.reshape(-1, PATCH * D)
    patch_rows = patches.shape[0]
    early = gather_flat(n, [unpatch_weight, qkv_weight, attn_out, gate_up])
    late = lax.all_gather(down_weight, "seq", axis=0, tiled=True)
    small = [patch_gain, conv_weight.reshape(-1), conv_bias, mixer_gain, attn_gain, ffn_gain]
    cuts = list(np.cumsum([piece.shape[0] for piece in small]))
    small_shard = jnp.concatenate(small)
    small_shard = jnp.pad(small_shard, (0, -small_shard.shape[0] % 2048)).reshape(-1, 128)
    live.mixer_in, live.mixer_out, small_all, live.embedded, live.parted = gather_weights(
        n,
        [
            jnp.pad(mixer_in, ((0, 0), (0, -mixer_in.shape[1] % 128))),
            mixer_out,
            small_shard,
        ],
        [(16, 2304), (32, D), (16, 128)],
        patches,
        patch_weight,
    )
    small_all = small_all.reshape(n, -1)[:, : cuts[-1]].astype(F32)
    parts = jnp.split(small_all, cuts[:-1], axis=1)
    live.patch_gain = parts[0].reshape(-1)
    live.conv_weight = parts[1].reshape(n, CONV, -1).transpose(1, 0, 2).reshape(CONV, CONV_CH)
    live.conv_bias, live.mixer_gain, live.attn_gain, live.ffn_gain = [
        piece.reshape(-1) for piece in parts[2:]
    ]
    live.normed = rms_scale(live.embedded, live.patch_gain).astype(BF)
    projected = dot(live.normed, live.mixer_in)
    live.gate_z = projected[:, :DI]
    conv_in = projected[:, DI : DI + CONV_CH].astype(BF).astype(F32)
    dt_raw = projected[:, DI + CONV_CH : DI + CONV_CH + MHEADS]
    logs = jnp.sum(-jax.nn.softplus(dt_raw + head_params[0]) * jnp.exp(head_params[1]), axis=0)
    flag = jnp.max(resets).astype(F32)
    live.logs = jnp.concatenate([logs, flag[None]])
    not_reset = 1.0 - resets.astype(F32)
    keep_tail = jnp.concatenate(
        [jnp.cumprod(not_reset[patch_rows - CONV + 2 :][::-1])[::-1], jnp.ones((1,), F32)]
    )
    tail_sent = (conv_in[patch_rows - CONV + 1 :] * keep_tail[:, None]).astype(BF)
    halo_rows = passed_along(tail_sent, 1)
    flags_ext = jnp.concatenate([jnp.zeros((CONV - 1,), jnp.int32), resets])
    validity = tap_masks(flags_ext, patch_rows)
    conv_ext = jnp.concatenate([halo_rows.astype(F32), conv_in])
    conv_out, conv_back = jax.vjp(
        functools.partial(conv_apply, validity=validity, row_count=patch_rows),
        conv_ext,
        live.conv_weight,
        live.conv_bias,
    )
    state_parts, state_back = jax.vjp(
        functools.partial(block_state, starts=resets), conv_out, dt_raw, head_params
    )
    local_state, decay_total = state_parts
    live.state_in = pass_states(n, local_state, live.logs, False)
    live.fence()

    mixer_y, output_back = jax.vjp(
        functools.partial(block_output, starts=resets),
        conv_out,
        dt_raw,
        head_params,
        live.state_in.astype(F32).reshape(MHEADS, MHEAD_DIM, NSTATE),
    )
    gate_act = silu(live.gate_z)
    gated = mixer_y * gate_act
    live.gated_norm = rms_scale(gated, live.mixer_gain).astype(BF)
    branch = dot(live.gated_norm, live.mixer_out)
    live.hidden = (live.embedded + branch).astype(BF)
    live.early = early
    slots = flat_dot(live.hidden, live.early, 0, PATCH, F32)
    live.stream0 = byte_wide + slots.reshape(-1, D)
    live.normed0 = rms_scale(live.stream0, live.attn_gain).astype(BF)
    live.fence()

    rows = byte_wide.shape[0]
    live.triple = flat_dot(live.normed0, live.early, PATCH, 3, BF)
    live.mixed = attention(live.triple)
    live.stream1 = live.stream0 + flat_dot(live.mixed, live.early, PATCH + 3, 1, F32)
    live.normed1 = rms_scale(live.stream1, live.ffn_gain).astype(BF)
    live.gate, live.up, live.hid = feed_forward(live.normed1, live.early)
    small_slice = n == 32
    if small_slice:
        live.flat = down_grad(n, live.hid, out_grad)

    def lefts_of(*values):
        parts = []
        for value in values:
            cut = value.reshape(value.shape[0], n, -1, SUM_ROWS).transpose(2, 0, 1, 3)
            parts.append(cut.reshape(-1, value.shape[0], n * SUM_ROWS))
        return jnp.concatenate(parts, axis=0)

    if small_slice:
        place = jnp.arange(n * SUM_ROWS)
        source = jnp.repeat(order * SUM_ROWS, SUM_ROWS) + place % SUM_ROWS
        live.order = (place[None, :] == source[:, None]).astype(BF)
        live.last_lefts = lefts_of(live.normed, live.gated_norm)
        live.steps, live.marks = mixer_tables(dt_raw, head_params, resets)
        live.told = told_logs(live.logs)
    live.fence()

    layer_out, d_both, d_stream1, d_stream1_low, g_ffn_gain = feed_forward_back(
        out_grad, live.stream1, live.ffn_gain, live.gate, live.up, live.hid, live.early, late
    )
    if small_slice:
        block = down_weight.shape[0]
        flat = gate_up_grad(live.normed1, d_both, live.flat)
        found = lax.psum_scatter(flat, "seq", scatter_dimension=0, tiled=True)[0].astype(F32)
        g_down = found[:block]
        g_gate_up = found[block:].reshape(-1, SUM_ROWS, D).transpose(1, 0, 2)
        g_gate_up = g_gate_up.reshape(SUM_ROWS, -1)
    else:
        g_down = summed_grad(live.hid, out_grad)
        g_gate_up = summed_grad(live.normed1, jnp.concatenate([d_both[0], d_both[1]], axis=1))
    d_triple, d_stream0, g_attn_gain = attention_back(
        live.triple, d_stream1_low, d_stream1, live.stream0, live.attn_gain, live.early
    )
    live.d_stream0 = d_stream0.reshape(patch_rows, PATCH * D)

    d_slots = live.d_stream0.astype(BF)
    d_hidden = flat_dot_t(d_slots, live.early, 0, PATCH)
    d_branch = d_hidden.astype(BF)
    d_gated, g_mixer_gain = rms_back(gated, live.mixer_gain, dot_t(d_branch, live.mixer_out))
    d_gate_z = d_gated * mixer_y * silu_slope(live.gate_z)
    if small_slice:
        d_conv_out, d_dt, g_head, g_attn_out, g_qkv, g_unpatch = mixer_back(
            live.told,
            live.order,
            [live.mixed, live.normed0],
            [d_stream1_low, d_triple],
            live.hidden[None],
            d_slots,
            d_gated * gate_act,
            conv_out,
            live.state_in,
            live.steps,
            live.marks,
            head_params,
        )
        conv_cot = conv_back(d_conv_out)
        g_head = g_head[:3]
    else:
        output_grads = output_back(d_gated * gate_act)
        state_grad = pass_states(n, output_grads[3], live.logs, True).astype(F32)
        state_grad = state_grad.reshape(MHEADS, MHEAD_DIM, NSTATE)
        state_in = live.state_in.astype(F32).reshape(MHEADS, MHEAD_DIM, NSTATE)
        state_cot = state_back((state_grad, jnp.sum(state_grad * state_in, axis=(1, 2))))
        conv_cot = conv_back(output_grads[0] + state_cot[0])
        d_dt = output_grads[1] + state_cot[1]
        g_head = output_grads[2] + state_cot[2]
    returned = passed_along(conv_cot[0][: CONV - 1], -1)
    d_conv_in = conv_cot[0][CONV - 1 :] + jnp.concatenate(
        [jnp.zeros((patch_rows - CONV + 1, CONV_CH), F32), returned * keep_tail[:, None]]
    )
    d_projected = jnp.concatenate([d_gate_z, d_conv_in, d_dt], axis=1).astype(BF)
    d_projected = jnp.pad(d_projected, ((0, 0), (0, -d_projected.shape[1] % 128)))
    d_embedded, g_patch_gain = rms_back(
        live.embedded, live.patch_gain, dot_t(d_projected, live.mixer_in)
    )
    d_embedded = (d_hidden + d_embedded).astype(BF)

    g_conv_weight = conv_cot[1].reshape(CONV, n, -1).transpose(1, 0, 2).reshape(n, -1)
    g_head = jnp.broadcast_to(g_head.reshape(1, -1), (n, 3 * MHEADS))
    g_small = [g_patch_gain, g_conv_weight, conv_cot[2], g_mixer_gain, g_attn_gain, g_ffn_gain, g_head]
    g_small = jnp.concatenate([piece.reshape(n, -1) for piece in g_small], axis=1)
    small_width = g_small.shape[1]
    g_small = jnp.pad(g_small, ((0, 0), (0, LOG_ROWS * 128 - small_width)))
    g_small = g_small.reshape(n * LOG_ROWS, 128)
    if small_slice:
        d_projected = jnp.pad(d_projected, ((0, 0), (0, -d_projected.shape[1] % SUM_COLUMNS)))
        g_patch, g_small, g_mixer_in, g_mixer_out, input_grad = last_sums(
            n,
            d_embedded,
            live.parted,
            g_small,
            live.order,
            live.last_lefts,
            jnp.concatenate([d_projected, d_branch, d_branch], axis=1),
            live.d_stream0,
            patch_weight,
            mixer_in.shape[1],
        )
    else:
        g_attn_out = summed_grad(live.mixed, d_stream1_low)
        g_qkv = summed_grad(live.normed0, d_triple)
        known = lax.all_gather(d_embedded, "seq", axis=0, tiled=True)
        g_patch = dot(live.parted.T, known)
        d_parted = dot_t(known, patch_weight).astype(BF).reshape(n, patch_rows, -1)
        d_parted = lax.all_to_all(d_parted, "seq", 0, 0, tiled=True)
        d_parted = d_parted.transpose(1, 0, 2).reshape(patch_rows, -1).astype(F32)
        input_grad = (live.d_stream0 + d_parted).astype(BF)
        g_small = lax.psum_scatter(g_small, "seq", scatter_dimension=0, tiled=True)
        g_unpatch = summed_grad(live.hidden, d_slots)
        g_mixer_in = summed_grad(live.normed, d_projected)[:, : mixer_in.shape[1]]
        g_mixer_out = summed_grad(live.gated_norm, d_branch)
    g_small = g_small.reshape(-1)[:small_width]
    s = jnp.split(g_small, cuts)
    return (
        layer_out,
        input_grad.reshape(-1, D),
        g_patch,
        s[0],
        g_mixer_in,
        s[1].reshape(CONV, -1),
        s[2],
        s[6].reshape(3, MHEADS),
        s[3],
        g_mixer_out,
        g_unpatch,
        s[4],
        g_qkv,
        g_attn_out,
        s[5],
        g_gate_up,
        g_down,
    )


def solution(mesh):
    rows, vector = P("seq", None), P("seq")
    placed = (
        rows, vector, rows, rows, vector, rows, P(None, "seq"), vector, P(),
        vector, rows, rows, vector, rows, rows, vector, rows, rows,
    )
    returned = (
        rows, rows, rows, vector, rows, P(None, "seq"), vector, P(), vector,
        rows, rows, vector, rows, rows, vector, rows, rows,
    )
    return jax.shard_map(
        local, mesh=mesh, in_specs=placed, out_specs=returned, check_vma=False
    )
```

```python
import functools

import jax
import jax.numpy as jnp
import numpy as np
from jax import lax
from jax.experimental import pallas as pl
from jax.experimental.pallas import tpu as pltpu
from jax.sharding import PartitionSpec as P

D = 1024
PATCH = 8
MHEADS = 32
MHEAD_DIM = 64
DI = 2048
NSTATE = 128
CONV = 4
AHEADS = 16
AHEAD_DIM = 64
FF = 4096
CONV_CH = 2304

EPS = 1e-05
HIGH = lax.Precision.HIGHEST
BF = jnp.bfloat16
F32 = jnp.float32


class Ring:
    def __init__(self, n):
        self.n = n
        self.depth = n // 8
        coords = [(i // 8, (i // 4) % 2, (i // 2) % 2, i % 2) for i in range(n)]

        def index(z, y, x, c):
            return ((z * 2 + y) * 2 + x) * 2 + c

        def flip(z, y, x, c, along_x):
            return index(z, y, 1 - x, c) if along_x else index(z, 1 - y, x, c)

        self.core = [(index(*p), index(*p) ^ 1) for p in coords]
        self.first = [(index(*p), flip(*p, p[3] == 0)) for p in coords]
        self.second = [(index(*p), flip(*p, p[3] == 1)) for p in coords]
        self.bits = [1 << b for b in range(self.depth.bit_length() - 1)]
        self.along = {
            bit: [(index(*p), index(p[0] ^ bit, *p[1:])) for p in coords] for bit in self.bits
        }
        table = np.zeros((n, n), np.int32)
        for me, (z, y, x, c) in enumerate(coords):
            place = 0
            for rc in range(2):
                owner = c ^ rc
                for r2 in range(2):
                    for r1 in range(2):
                        rx, ry = (r1, r2) if owner == 0 else (r2, r1)
                        for rz in range(self.depth):
                            table[me, place] = index((z + rz) % self.depth, y ^ ry, x ^ rx, owner)
                            place += 1
        self.table = table

    def order(self):
        return jnp.asarray(self.table)[lax.axis_index("seq")]


def swap(block, route):
    return lax.ppermute(block, "seq", route)


def flat_kernel(*refs):
    out, first = refs[-1], 0
    for ref in refs[:-1]:
        rows = ref.shape[0]
        for column in range(0, ref.shape[1], D):
            out[pl.ds(first, rows)] = ref[:, pl.ds(column, D)]
            first += rows


def flat_rows(shards):
    total = sum(shard.shape[0] * shard.shape[1] // D for shard in shards)
    return pl.pallas_call(
        flat_kernel,
        out_shape=jax.ShapeDtypeStruct((total, D), BF),
        in_specs=[pl.BlockSpec(memory_space=pltpu.VMEM)] * len(shards),
        out_specs=pl.BlockSpec(memory_space=pltpu.VMEM),
    )(*shards)


def gather_flat(n, shards):
    return lax.all_gather(flat_rows(shards), "seq", axis=0)


def flat_block(n, rows, place):
    return pl.BlockSpec((n, rows, D), lambda i: (0, place(i), 0))


def whole_of(ref):
    return ref[...].reshape(-1, ref.shape[-1])


def flat_dot_kernel(values_ref, flat_ref, out_ref):
    out_ref[...] = dot(values_ref[...], whole_of(flat_ref)).astype(out_ref.dtype)


def flat_dot(values, flat, first, count, kind):
    n, rows = flat.shape[0], values.shape[0]
    return pl.pallas_call(
        flat_dot_kernel,
        grid=(count,),
        out_shape=jax.ShapeDtypeStruct((rows, count * D), kind),
        in_specs=[
            pl.BlockSpec((rows, D), lambda i: (0, 0)),
            flat_block(n, D // n, lambda i: first + i),
        ],
        out_specs=pl.BlockSpec((rows, D), lambda i: (0, i)),
        compiler_params=pltpu.CompilerParams(vmem_limit_bytes=56 * 2**20),
        cost_estimate=pl.CostEstimate(
            flops=2 * rows * D * D * count, bytes_accessed=2 * D * D * count, transcendentals=0
        ),
    )(values, flat)


def flat_dot_t_kernel(values_ref, flat_ref, out_ref, total):
    few = values_ref.shape[0] < 256
    step = pl.program_id(0)
    if few:
        found = dot_t(whole_of(flat_ref), values_ref[...])
    else:
        found = dot_t(values_ref[...], whole_of(flat_ref))

    @pl.when(step == 0)
    def _():
        total[...] = found

    @pl.when(step > 0)
    def _():
        total[...] += found

    @pl.when(step == pl.num_programs(0) - 1)
    def _():
        out_ref[...] = total[...].T if few else total[...]


def flat_dot_t(values, flat, first, count):
    n, rows = flat.shape[0], values.shape[0]
    return pl.pallas_call(
        flat_dot_t_kernel,
        grid=(count,),
        out_shape=jax.ShapeDtypeStruct((rows, D), F32),
        in_specs=[
            pl.BlockSpec((rows, D), lambda i: (0, i)),
            flat_block(n, D // n, lambda i: first + i),
        ],
        out_specs=pl.BlockSpec((rows, D), lambda i: (0, 0)),
        scratch_shapes=[pltpu.VMEM((D, rows) if rows < 256 else (rows, D), F32)],
        compiler_params=pltpu.CompilerParams(vmem_limit_bytes=56 * 2**20),
        cost_estimate=pl.CostEstimate(
            flops=2 * rows * D * D * count, bytes_accessed=2 * D * D * count, transcendentals=0
        ),
    )(values, flat)


class Live:
    def fence(self):
        vars(self).update(lax.optimization_barrier(dict(vars(self))))


def summed_grad(left, right):
    product = lax.dot_general(left, right, (((0,), (0,)), ((), ())), preferred_element_type=F32)
    summed = lax.psum_scatter(product.astype(BF), "seq", scatter_dimension=0, tiled=True)
    return summed.astype(F32)


def turned_product(left, right):
    found = lax.dot_general(left, right, (((0,), (0,)), ((), ())), preferred_element_type=F32)
    return found.astype(BF)


def down_grad_kernel(hid_ref, grad_ref, out_ref):
    devices, block = out_ref.shape[:2]
    few = 256 // block
    for first in range(0, devices, few):
        found = turned_product(hid_ref[:, pl.ds(first * block, 256)], grad_ref[...])
        out_ref[pl.ds(first, few)] = found.reshape(few, block, D)


def down_grad(n, hid, out_grad):
    rows, block, devices = hid.shape[0], hid.shape[1] // n, n // 4
    return pl.pallas_call(
        down_grad_kernel,
        grid=(4,),
        out_shape=jax.ShapeDtypeStruct((n, 3 * block, D), BF),
        in_specs=[
            pl.BlockSpec((rows, devices * block), lambda i: (0, i)),
            pl.BlockSpec((rows, D), lambda i: (0, 0)),
        ],
        out_specs=pl.BlockSpec((devices, block, D), lambda i: (i, 0, 0)),
        compiler_params=pltpu.CompilerParams(vmem_limit_bytes=56 * 2**20),
        cost_estimate=pl.CostEstimate(
            flops=2 * rows * FF * D, bytes_accessed=2**24, transcendentals=0
        ),
    )(hid, out_grad)


def gate_up_grad_kernel(normed_ref, both_ref, flat_ref, out_ref):
    del flat_ref
    devices, block = out_ref.shape[:2]
    for part in range(block // SUM_ROWS):
        found = turned_product(normed_ref[...], both_ref[0, :, pl.ds(part * D, D)])
        out_ref[:, pl.ds(part * SUM_ROWS, SUM_ROWS)] = found.reshape(devices, SUM_ROWS, D)


def gate_up_grad(normed, both, flat):
    n, rows, devices = flat.shape[0], normed.shape[0], flat.shape[0] // 4
    return pl.pallas_call(
        gate_up_grad_kernel,
        grid=(8,),
        out_shape=jax.ShapeDtypeStruct(flat.shape, BF),
        in_specs=[
            pl.BlockSpec((rows, devices * SUM_ROWS), lambda i: (0, i % 4)),
            pl.BlockSpec((1, rows, FF), lambda i: (i // 4, 0, 0)),
            pl.BlockSpec(memory_space=pltpu.HBM),
        ],
        out_specs=pl.BlockSpec((devices, flat.shape[1] // 3, D), lambda i: (i % 4, 1 + i // 4, 0)),
        input_output_aliases={2: 0},
        compiler_params=pltpu.CompilerParams(vmem_limit_bytes=56 * 2**20),
        cost_estimate=pl.CostEstimate(
            flops=4 * rows * FF * D, bytes_accessed=2**25, transcendentals=0
        ),
    )(normed, both, flat)


def dot(left, right):
    return jnp.dot(left, right, preferred_element_type=F32)


def dot_t(left, right):
    return lax.dot_general(left, right, (((1,), (1,)), ((), ())), preferred_element_type=F32)


def rms_scale(values, gain):
    return values * lax.rsqrt(jnp.mean(values * values, axis=-1, keepdims=True) + EPS) * gain


def rms_back(values, gain, grad):
    r = lax.rsqrt(jnp.mean(values * values, axis=-1, keepdims=True) + EPS)
    scaled = gain * grad
    inner = jnp.mean(values * scaled, axis=-1, keepdims=True)
    return r * scaled - values * (r * r * r) * inner, jnp.sum(values * r * grad, axis=0)


def silu(v):
    return v * jax.nn.sigmoid(v)


def silu_slope(v):
    s = jax.nn.sigmoid(v)
    return s * (1.0 + v * (1.0 - s))


def tap_masks(flags_ext, row_count):
    not_reset = 1.0 - flags_ext.astype(F32)
    validity = [jnp.ones((row_count,), F32)]
    for offset in range(1, CONV):
        validity.append(validity[-1] * not_reset[CONV - offset : CONV - offset + row_count])
    return validity


def conv_apply(conv_ext, conv_weight, conv_bias, validity, row_count):
    summed = conv_bias + conv_ext[CONV - 1 : CONV - 1 + row_count] * conv_weight[0]
    for offset in range(1, CONV):
        summed = (
            summed
            + validity[offset][:, None]
            * conv_ext[CONV - 1 - offset : CONV - 1 - offset + row_count]
            * conv_weight[offset]
        )
    return jax.nn.silu(summed)


def block_parts(conv_out, dt_raw, head_params, starts):
    row_count = conv_out.shape[0]
    values = conv_out[:, :DI].reshape(row_count, MHEADS, MHEAD_DIM)
    key_rows = conv_out[:, DI : DI + NSTATE]
    queries = conv_out[:, DI + NSTATE :]
    step_size = jax.nn.softplus(dt_raw + head_params[0])
    cumlog = jnp.cumsum(-step_size * jnp.exp(head_params[1]), axis=0)
    segment = jnp.cumsum(starts, axis=0, dtype=jnp.int32)
    return (values, key_rows, queries, step_size, cumlog, segment)


def block_state(conv_out, dt_raw, head_params, starts):
    values, key_rows, queries, step_size, cumlog, segment = block_parts(
        conv_out, dt_raw, head_params, starts
    )
    same_doc = (segment == segment[-1]).astype(F32)
    weighting = jnp.exp(cumlog[-1][None, :] - cumlog) * same_doc[:, None] * step_size
    state_out = jnp.einsum("rh,rhp,rn->hpn", weighting, values, key_rows, precision=HIGH)
    decay_total = jnp.exp(cumlog[-1]) * (segment[-1] == 0).astype(F32)
    return (state_out, decay_total)


def block_output(conv_out, dt_raw, head_params, state_in, starts):
    values, key_rows, queries, step_size, cumlog, segment = block_parts(
        conv_out, dt_raw, head_params, starts
    )
    position = jnp.arange(conv_out.shape[0])
    causal = (position[:, None] >= position[None, :]) & (segment[:, None] == segment[None, :])
    log_gaps = jnp.where(causal[:, :, None], cumlog[:, None, :] - cumlog[None, :, :], 0.0)
    decays = jnp.exp(log_gaps) * causal[:, :, None].astype(F32)
    scores = jnp.dot(queries, key_rows.T, precision=HIGH)
    mixing = scores[:, :, None] * decays * step_size[None, :, :]
    within = jnp.einsum("tsh,shp->thp", mixing, values, precision=HIGH)
    inflow = jnp.exp(cumlog) * (segment == 0).astype(F32)[:, None]
    carried = jnp.einsum("tn,hpn->thp", queries, state_in, precision=HIGH) * inflow[:, :, None]
    skipped = head_params[2][None, :, None] * values
    return (within + carried + skipped).reshape(conv_out.shape[0], DI)


MESH = pl.DeviceIdType.MESH


class Place:
    def __init__(self, n):
        self.n, self.depth = n, n // 8
        self.me = me = lax.axis_index("seq")
        self.z, self.y, self.x, self.c = me // 8, (me // 4) % 2, (me // 2) % 2, me % 2

    def flipped(self, rz, ry, rx, rc):
        z, bit = 0, 1
        while bit < self.depth:
            z = z + ((self.z // bit + rz // bit) % 2) * bit
            bit *= 2
        y, x, c = (self.y + ry) % 2, (self.x + rx) % 2, (self.c + rc) % 2
        return ((z * 2 + y) * 2 + x) * 2 + c

    def split(self, place):
        depth = self.depth
        rz, r1, r2 = place % depth, (place // depth) % 2, (place // (2 * depth)) % 2
        return rz, r1, r2, place // (4 * depth)

    def device(self, place):
        rz, r1, r2, rc = self.split(place)
        owner = (self.c + rc) % 2
        return self.flipped(rz, r2 + owner * (r1 - r2), r1 + owner * (r2 - r1), rc)

    def place_there(self, place):
        rz, r1, r2, rc = self.split(place)
        s1, s2 = r1 + rc * (r2 - r1), r2 + rc * (r1 - r2)
        return ((rc * 2 + s2) * 2 + s1) * self.depth + rz

    def sum_steps(self):
        steps = [(blocks, blocks, partner) for blocks, partner in self.halves()[:-4:-1]]
        above = self.me + ((self.z + 1) % self.depth - self.z) * 8
        return steps + [(block, 1, above) for block in range(self.depth - 1, 0, -1)]

    def halves(self):
        steps, bit = [], 1
        while bit < self.depth:
            steps.append((bit, self.flipped(bit, 0, 0, 0)))
            bit *= 2
        steps.append((self.depth, self.flipped(0, self.c, 1 - self.c, 0)))
        steps.append((2 * self.depth, self.flipped(0, 1 - self.c, self.c, 0)))
        steps.append((4 * self.depth, self.flipped(0, 0, 0, 1)))
        return steps


def greet(n):
    barrier = pltpu.get_barrier_semaphore()
    me = lax.axis_index("seq")

    @pl.loop(1, n)
    def _(hop):
        other = lax.rem(me + hop, n)
        pl.semaphore_signal(barrier, inc=1, device_id=(other,), device_id_type=MESH)

    pl.semaphore_wait(barrier, n - 1)


def remote(source, target, send_sem, recv_sem, device):
    return pltpu.make_async_remote_copy(
        src_ref=source,
        dst_ref=target,
        send_sem=send_sem,
        recv_sem=recv_sem,
        device_id=(device,),
        device_id_type=MESH,
    )


def landed(ref, sem):
    pltpu.make_async_copy(ref, ref, sem).wait()


def rows_of(place, count, rows):
    return pl.ds(pl.multiple_of(place * rows, rows), count * rows)


GATHER_TIMES = [0, 1, 2, 3, 5, 6]
EMBED_TIMES = [2, 4, 6, 8, 10, 11]


def gather_kernel(n, chunks, *refs):
    count = (len(refs) - 13) // 2
    shards, patches_ref, weight_ref = refs[:count], refs[count], refs[count + 1]
    wholes = refs[count + 2 : -11]
    embedded_ref, parted_ref, product, got, own_sem = refs[-11:-6]
    send_sem, recv_sem, part_send, part_recv, sum_send, sum_recv = refs[-6:]
    here = Place(n)
    greet(n)
    owns = []
    for index in range(count):
        rows = shards[index].shape[0]
        target = wholes[index].at[rows_of(here.me, 1, rows)]
        owns.append(pltpu.make_async_copy(shards[index], target, own_sem.at[index]))
        owns[-1].start()
    for own in owns:
        own.wait()
    steps = here.halves()

    def block(chunk, place):
        index, first, rows, column, columns = chunks[chunk]
        start = here.device(place) * shards[index].shape[0] + first
        return wholes[index].at[pl.ds(pl.multiple_of(start, 16), rows), pl.ds(column, columns)]

    def sending(chunk, step, place):
        blocks, partner = steps[step]
        there = blocks + place
        ref = block(chunk, place)
        return remote(ref, ref, send_sem.at[chunk, there], recv_sem.at[chunk, there], partner)

    def arrive(chunk, step):
        blocks = steps[step][0]

        @pl.loop(blocks, 2 * blocks)
        def _(place):
            landed(block(chunk, place), recv_sem.at[chunk, place])

    def send(chunk, step):
        @pl.loop(0, steps[step][0])
        def _(place):
            sending(chunk, step, place).start()

    rows, width = patches_ref.shape[0], patches_ref.shape[1] // n

    def part_of(place):
        start = pl.multiple_of(here.device(place) * width, 128)
        return patches_ref.at[:, pl.ds(start, width)]

    def parting(place):
        there = here.place_there(place)
        target = parted_ref.at[rows_of(there, 1, rows)]
        return remote(
            part_of(place), target, part_send.at[place], part_recv.at[there], here.device(place)
        )

    half = n // 2
    own_part = pltpu.make_async_copy(part_of(0), parted_ref.at[rows_of(0, 1, rows)], part_recv.at[0])
    own_part.start()

    @pl.loop(1, n)
    def _(hop):
        parting(n - hop).start()

    def multiply(first):
        @pl.loop(first, first + half)
        def _(place):
            landed(parted_ref.at[rows_of(place, 1, rows)], part_recv.at[place])

        @pl.loop(0, half // 4)
        def _(index):
            cut = rows_of(first // 4 + index, 1, 4 * rows)
            product[cut] = dot(parted_ref[cut], weight_ref[...])

    def summing(step):
        blocks, partner = steps[len(steps) - 1 - step]
        cut = pl.ds(blocks * rows, blocks * rows)
        return remote(product.at[cut], got.at[cut], sum_send.at[step], sum_recv.at[step], partner)

    def add(step):
        blocks = steps[len(steps) - 1 - step][0]
        summing(step).wait_recv()
        mine, cut = pl.ds(0, blocks * rows), pl.ds(blocks * rows, blocks * rows)
        product[mine] += got[cut]

    def embed(time):
        if time == EMBED_TIMES[0]:
            multiply(half)
            summing(0).start()
            multiply(0)
        for step in range(len(steps)):
            if time == EMBED_TIMES[step + 1]:
                add(step)
                if step + 1 < len(steps):
                    summing(step + 1).start()

    for time in range(max(len(chunks) + GATHER_TIMES[-1], EMBED_TIMES[-1] + 1)):
        for step in range(len(steps), -1, -1):
            chunk = time - GATHER_TIMES[step]
            if 0 <= chunk < len(chunks):
                if step > 0:
                    arrive(chunk, step - 1)
                if step < len(steps):
                    send(chunk, step)
        embed(time)
    embedded_ref[...] = product[pl.ds(0, rows)]

    @pl.loop(1, n)
    def _(place):
        parting(place).wait_send()

    for step in range(len(steps)):
        summing(step).wait_send()
    for chunk in range(len(chunks)):
        for step in range(len(steps)):

            @pl.loop(0, steps[step][0])
            def _(place):
                sending(chunk, step, place).wait_send()


def gather_weights(n, shards, cuts, patches, patch_weight):
    if n != 32 or any(shard.shape[0] % 16 for shard in shards):
        wholes = [lax.all_gather(shard, "seq", axis=0, tiled=True) for shard in shards]
        parted = patches.reshape(patches.shape[0], n, -1).transpose(1, 0, 2)
        parted = lax.all_to_all(parted, "seq", 0, 0, tiled=True)
        parted = parted.reshape(-1, parted.shape[-1])
        product = dot(parted, patch_weight)
        return wholes + [
            lax.psum_scatter(product, "seq", scatter_dimension=0, tiled=True),
            parted,
        ]
    rows, phases = patches.shape[0], n.bit_length() - 1
    chunks = [
        (index, first, rows, column, min(columns, shard.shape[1] - column))
        for index, (shard, (rows, columns)) in enumerate(zip(shards, cuts))
        for first in range(0, shard.shape[0], rows)
        for column in range(0, shard.shape[1], columns)
    ]
    sems = [pltpu.SemaphoreType.DMA((len(chunks), n))] * 2
    return pl.pallas_call(
        functools.partial(gather_kernel, n, chunks),
        out_shape=[
            jax.ShapeDtypeStruct((n * shard.shape[0], shard.shape[1]), shard.dtype) for shard in shards
        ]
        + [
            jax.ShapeDtypeStruct((rows, D), F32),
            jax.ShapeDtypeStruct((n * rows, patches.shape[1] // n), BF),
        ],
        in_specs=[pl.BlockSpec(memory_space=pltpu.VMEM)] * (len(shards) + 2),
        out_specs=[pl.BlockSpec(memory_space=pltpu.HBM)] * len(shards)
        + [pl.BlockSpec(memory_space=pltpu.VMEM)] * 2,
        scratch_shapes=[
            pltpu.VMEM((n * rows, D), F32),
            pltpu.VMEM((n * rows, D), F32),
            pltpu.SemaphoreType.DMA((len(shards),)),
        ]
        + sems
        + [pltpu.SemaphoreType.DMA((n,))] * 2
        + [pltpu.SemaphoreType.DMA((phases,))] * 2,
        compiler_params=pltpu.CompilerParams(
            collective_id=0, has_side_effects=True, vmem_limit_bytes=32 * 2**20
        ),
        cost_estimate=pl.CostEstimate(flops=0, bytes_accessed=2**25, transcendentals=0),
    )(*shards, patches, patch_weight)


SUM_ROWS, SUM_COLUMNS, SUM_SLOTS = 32, 512, 8
SUM_TIMES = [0, 1, 3, 4, 5, 6, 7]


def columns_of(chunk):
    return pl.ds(pl.multiple_of(chunk * SUM_COLUMNS, SUM_COLUMNS), SUM_COLUMNS)


class Sums:
    def __init__(self, here, sources, out, kept, sent, got, send_sem, recv_sem):
        self.here, self.sources, self.out = here, sources, out
        self.kept, self.sent, self.got = kept, sent, got
        self.send_sem, self.recv_sem = send_sem, recv_sem
        self.steps = here.sum_steps()
        self.chunks = got.shape[0]
        self.times = self.chunks + SUM_TIMES[-1]

    def copy(self, chunk, step):
        first, blocks, partner = self.steps[step]
        cut = pl.ds(first * SUM_ROWS, blocks * SUM_ROWS)
        return remote(
            self.sent.at[chunk % SUM_SLOTS, cut],
            self.got.at[chunk, cut],
            self.send_sem.at[chunk, step],
            self.recv_sem.at[chunk, step],
            partner,
        )

    def sent_all(self, chunk):
        for step in range(len(self.steps)):
            self.copy(chunk, step).wait_send()

    def begin(self, chunk):
        half = self.here.n // 2 * SUM_ROWS
        slot = chunk % SUM_SLOTS

        @pl.when(chunk >= SUM_SLOTS)
        def _():
            self.sent_all(chunk - SUM_SLOTS)

        for first, stop, find, left, right in self.sources:

            @pl.when((chunk >= first) & (chunk < stop))
            def _():
                which, column = find(chunk - first)

                def product(row):
                    return dot(left[which, pl.ds(row, half)], right[:, columns_of(column)])

                self.sent[slot, pl.ds(half, half)] = product(half).astype(BF)
                self.copy(chunk, 0).start()
                self.kept[slot] = product(0)

    def go_on(self, chunk, step):
        slot, (first, blocks, _) = chunk % SUM_SLOTS, self.steps[step - 1]
        self.copy(chunk, step - 1).wait_recv()
        got = self.got[chunk, pl.ds(first * SUM_ROWS, blocks * SUM_ROWS)].astype(F32)
        start = (first - blocks) * SUM_ROWS
        total = self.kept[slot, pl.ds(start, blocks * SUM_ROWS)] + got
        if step == len(self.steps):
            self.out(chunk, total)
            return
        next_first, next_blocks, _ = self.steps[step]
        sent = total[next_first * SUM_ROWS - start :][: next_blocks * SUM_ROWS]
        self.sent[slot, pl.ds(next_first * SUM_ROWS, next_blocks * SUM_ROWS)] = sent.astype(BF)
        self.copy(chunk, step).start()
        if blocks > 1:
            self.kept[slot, pl.ds(0, next_first * SUM_ROWS)] = total[: next_first * SUM_ROWS]

    def at(self, time):
        for step in range(len(self.steps), -1, -1):
            chunk = time - SUM_TIMES[step]

            @pl.when((chunk >= 0) & (chunk < self.chunks))
            def _():
                if step == 0:
                    self.begin(chunk)
                else:
                    self.go_on(chunk, step)

    def run(self, first, stop):
        pl.loop(first, stop)(self.at)

    def end(self):
        @pl.loop(max(0, self.chunks - SUM_SLOTS), self.chunks)
        def _(chunk):
            self.sent_all(chunk)


def turn(order_ref, left_ref, values_ref):
    for index in range(values_ref.shape[0]):
        left_ref[index] = dot_t(order_ref[...], values_ref[index]).astype(BF)


def lefts_scratch(n, lefts):
    return [pltpu.VMEM((lefts.shape[0], n * SUM_ROWS, lefts.shape[1]), BF)]


def sums_scratch(n, chunks):
    rows, phases = n * SUM_ROWS, n // 8 + 2
    return [
        pltpu.VMEM((SUM_SLOTS, rows // 2, SUM_COLUMNS), F32),
        pltpu.VMEM((SUM_SLOTS, rows, SUM_COLUMNS), BF),
        pltpu.VMEM((chunks, rows, SUM_COLUMNS), BF),
        pltpu.SemaphoreType.DMA((chunks, phases)),
        pltpu.SemaphoreType.DMA((chunks, phases)),
    ]


def last_find(chunk):
    return (chunk + 7) // 16 + (chunk + 5) // 16, chunk


def last_kernel(
    n, grad_ref, parted_ref, small_ref, order_ref, values_ref, right_ref, direct_ref, weight_ref,
    d_weight_ref, d_small_ref, d_in_ref, d_out_ref, input_ref,
    back, d_patches, b_send, b_recv, known, small_kept, small_got, g_send, g_recv, t_send, t_recv, left_ref, *scratch
):
    here = Place(n)
    rows = grad_ref.shape[0]
    greet(n)
    known[pl.ds(0, rows)] = grad_ref[...]

    @pl.loop(0, n)
    def _(place):
        device = here.device(place)
        small_kept[rows_of(place, 1, LOG_ROWS)] = small_ref[rows_of(device, 1, LOG_ROWS)]

    turn(order_ref, left_ref, values_ref)
    spare = d_in_ref.shape[1] % SUM_COLUMNS

    def store(chunk, total):
        @pl.when(chunk < 8)
        def _():
            d_in_ref[:, columns_of(chunk)] = total

        @pl.when(chunk == 8)
        def _():
            d_in_ref[:, pl.ds(8 * SUM_COLUMNS, spare)] = total[:, :spare]

        @pl.when(chunk >= 9)
        def _():
            part = (chunk - 9) // 2
            d_out_ref[rows_of(part, 1, SUM_ROWS), columns_of((chunk - 9) % 2)] = total

    sums = Sums(here, [(0, 13, last_find, left_ref, right_ref)], store, *scratch)
    steps = here.halves()
    copies = []
    for step in range(len(steps)):
        blocks, partner = steps[step]
        source, target = pl.ds(0, blocks * rows), pl.ds(blocks * rows, blocks * rows)
        gather = remote(known.at[source], known.at[target], g_send.at[step], g_recv.at[step], partner)
        gather.start()
        blocks, partner = steps[::-1][step]
        cut, mine = pl.ds(blocks * LOG_ROWS, blocks * LOG_ROWS), pl.ds(0, blocks * LOG_ROWS)
        told = remote(small_kept.at[cut], small_got.at[cut], t_send.at[step], t_recv.at[step], partner)
        told.start()
        copies += [gather, told]
        sums.run(2 * step, 2 * step + 2)
        gather.wait_recv()
        told.wait_recv()
        small_kept[mine] = small_kept[mine] + small_got[cut]
    width = weight_ref.shape[0]
    back[...] = dot_t(known[...], weight_ref[...]).astype(BF)
    mine = pl.ds(pl.multiple_of(here.me * width, 128), width)

    def returning(place):
        source, target = back.at[rows_of(place, 1, rows)], d_patches.at[:, mine]
        there = here.place_there(place)
        return remote(source, target, b_send.at[place], b_recv.at[there], here.device(place))

    @pl.loop(1, n)
    def _(place):
        returning(place).start()

    pltpu.make_async_copy(back.at[pl.ds(0, rows)], d_patches.at[:, mine], b_recv.at[0]).start()
    sums.run(2 * len(steps), 2 * len(steps) + 1)
    d_weight_ref[...] = lax.dot_general(
        parted_ref[...], known[...], (((0,), (0,)), ((), ())), preferred_element_type=F32
    )
    sums.run(2 * len(steps) + 1, sums.times)

    @pl.loop(0, n)
    def _(place):
        cut = pl.ds(pl.multiple_of(here.device(place) * width, 128), width)
        landed(d_patches.at[:, cut], b_recv.at[place])

    input_ref[...] = (direct_ref[...] + d_patches[...].astype(F32)).astype(BF)

    @pl.loop(1, n)
    def _(place):
        returning(place).wait_send()

    d_small_ref[...] = small_kept[pl.ds(0, LOG_ROWS)]
    for copy in copies:
        copy.wait_send()
    sums.end()


def last_sums(n, grad, parted, small, order, lefts, right, direct, weight, projections):
    rows, width = grad.shape[0], parted.shape[1]
    phases, chunks = n.bit_length() - 1, right.shape[1] // SUM_COLUMNS
    return pl.pallas_call(
        functools.partial(last_kernel, n),
        out_shape=[
            jax.ShapeDtypeStruct((width, D), F32),
            jax.ShapeDtypeStruct((LOG_ROWS, 128), F32),
            jax.ShapeDtypeStruct((SUM_ROWS, projections), F32),
            jax.ShapeDtypeStruct((2 * SUM_ROWS, D), F32),
            jax.ShapeDtypeStruct(direct.shape, BF),
        ],
        in_specs=[pl.BlockSpec(memory_space=pltpu.VMEM)] * 8,
        out_specs=[pl.BlockSpec(memory_space=pltpu.VMEM)] * 5,
        scratch_shapes=[
            pltpu.VMEM((n * rows, width), BF),
            pltpu.VMEM(direct.shape, BF),
            pltpu.SemaphoreType.DMA((n,)),
            pltpu.SemaphoreType.DMA((n,)),
            pltpu.VMEM((n * rows, D), BF),
            pltpu.VMEM(small.shape, F32),
            pltpu.VMEM(small.shape, F32),
        ]
        + [pltpu.SemaphoreType.DMA((phases,))] * 4
        + lefts_scratch(n, lefts)
        + sums_scratch(n, chunks),
        compiler_params=pltpu.CompilerParams(
            collective_id=1, has_side_effects=True, vmem_limit_bytes=62 * 2**20
        ),
        cost_estimate=pl.CostEstimate(flops=2**32, bytes_accessed=2**24, transcendentals=0),
    )(grad, parted, small, order, lefts, right, direct, weight)


LOG_ROWS = 8


class Exchange:
    def __init__(self, n, reverse, states, logs_in, out, spread, logs, summed, *sems):
        self.n, self.reverse = n, reverse
        self.me = lax.axis_index("seq")
        self.states, self.logs_in, self.out = states, logs_in, out
        self.spread, self.logs, self.summed = spread, logs, summed
        self.sems = sems
        self.rows = states.shape[0] // n

    def spreading(self, other):
        send, recv = self.sems[:2]
        source = self.states.at[rows_of(other, 1, self.rows)]
        target = self.spread.at[rows_of(self.me, 1, self.rows)]
        return remote(source, target, send.at[other], recv.at[self.me], other)

    def telling(self, other):
        send, recv = self.sems[2:4]
        target = self.logs.at[rows_of(self.me, 1, LOG_ROWS)]
        return remote(self.logs_in, target, send.at[other], recv.at[self.me], other)

    def returning(self, other):
        send, recv = self.sems[4:6]
        source = self.summed.at[rows_of(other, 1, self.rows)]
        target = self.out.at[rows_of(self.me, 1, self.rows)]
        return remote(source, target, send.at[other], recv.at[self.me], other)

    def tell(self):
        @pl.loop(1, self.n)
        def _(hop):
            self.telling(lax.rem(self.me + hop, self.n)).start()

        target = self.logs.at[rows_of(self.me, 1, LOG_ROWS)]
        pltpu.make_async_copy(self.logs_in, target, self.sems[3].at[self.me]).start()

    def start(self):
        @pl.loop(1, self.n)
        def _(hop):
            self.spreading(lax.rem(self.me + hop, self.n)).start()

        mine = rows_of(self.me, 1, self.rows)
        recv = self.sems[1].at[self.me]
        pltpu.make_async_copy(self.states.at[mine], self.spread.at[mine], recv).start()

    def join(self):
        n, rows, summed, spread = self.n, self.rows, self.summed, self.spread

        @pl.loop(0, n)
        def _(other):
            landed(spread.at[rows_of(other, 1, rows)], self.sems[1].at[other])
            landed(self.logs.at[rows_of(other, 1, LOG_ROWS)], self.sems[3].at[other])

        head = self.me * MHEADS // n
        lane = lax.broadcasted_iota(jnp.int32, (LOG_ROWS, 128), 1)
        row = lax.broadcasted_iota(jnp.int32, (LOG_ROWS, 128), 0)

        def step(count, total):
            place = n - 1 - count if self.reverse else count
            cut = rows_of(place, 1, rows)
            summed[cut] = total.astype(BF)
            told = self.logs[rows_of(place, 1, LOG_ROWS)]
            log = jnp.sum(jnp.where((lane == head) & (row == 0), told, 0.0), keepdims=True)
            flag = jnp.sum(jnp.where((lane == MHEADS) & (row == 0), told, 0.0), keepdims=True)
            decay = jnp.where(flag > 0.0, 0.0, jnp.exp(log))
            return decay * total + spread[cut].astype(F32)

        lax.fori_loop(0, n, step, jnp.zeros((rows, NSTATE), F32))

        @pl.loop(1, n)
        def _(hop):
            self.returning(lax.rem(self.me + hop, n)).start()

        mine = rows_of(self.me, 1, rows)
        recv = self.sems[5].at[self.me]
        pltpu.make_async_copy(summed.at[mine], self.out.at[mine], recv).start()

    def arrive(self):
        @pl.loop(0, self.n)
        def _(other):
            landed(self.out.at[rows_of(other, 1, self.rows)], self.sems[5].at[other])

    def end(self):
        @pl.loop(1, self.n)
        def _(hop):
            other = lax.rem(self.me + hop, self.n)
            self.spreading(other).wait_send()
            self.telling(other).wait_send()
            self.returning(other).wait_send()


def exchange_scratch(n):
    total = MHEADS * MHEAD_DIM
    return [
        pltpu.VMEM((total, NSTATE), BF),
        pltpu.VMEM((n * LOG_ROWS, 128), F32),
        pltpu.VMEM((total, NSTATE), BF),
    ] + [pltpu.SemaphoreType.DMA((n,))] * 6


def states_kernel(n, reverse, states_ref, logs_ref, out_ref, *scratch):
    greet(n)
    exchange = Exchange(n, reverse, states_ref, logs_ref, out_ref, *scratch)
    exchange.tell()
    exchange.start()
    exchange.join()
    exchange.arrive()
    exchange.end()


def told_logs(logs):
    return jnp.zeros((LOG_ROWS, 128), F32).at[0, : logs.shape[0]].set(logs)


def pass_states(n, states, logs, reverse):
    total = MHEADS * MHEAD_DIM
    return pl.pallas_call(
        functools.partial(states_kernel, n, reverse),
        out_shape=jax.ShapeDtypeStruct((total, NSTATE), BF),
        in_specs=[pl.BlockSpec(memory_space=pltpu.VMEM)] * 2,
        out_specs=pl.BlockSpec(memory_space=pltpu.VMEM),
        scratch_shapes=exchange_scratch(n),
        compiler_params=pltpu.CompilerParams(
            collective_id=3 if reverse else 2, has_side_effects=True, vmem_limit_bytes=16 * 2**20
        ),
        cost_estimate=pl.CostEstimate(flops=2**22, bytes_accessed=2**21, transcendentals=0),
    )(states.reshape(total, NSTATE).astype(BF), told_logs(logs))


NN, NT, TN = ((1,), (0,)), ((1,), (1,)), ((0,), (0,))


def in_parts(value, count):
    if value.dtype == BF:
        return [value]
    parts = []
    for _ in range(count):
        parts.append(value.astype(BF))
        value = value - parts[-1].astype(F32)
    return parts


def dot_fine(left, right, dims, count=2):
    total = None
    for i, a in enumerate(in_parts(left, count)):
        for j, b in enumerate(in_parts(right, count)):
            if i + j < count:
                found = lax.dot_general(a, b, (dims, ((), ())), preferred_element_type=F32)
                total = found if total is None else total + found
    return total


def mixer_back_kernel(
    n, logs_ref, order_ref, mixed_ref, normed_ref, out_right_ref, qkv_right_ref, hidden_ref, slots_ref,
    dy_ref, x_ref, keys_ref, queries_ref, state_ref, steps_ref, marks_ref, head_ref,
    dx_ref, d_dt_ref, d_head_ref, d_out_ref, d_qkv_ref, unpatch_ref, dkeys_ref, dqueries_ref,
    scores, d_scores, d_step, d_cum, d_turned, grads, back, left_ref, hidden_left, *scratch
):
    rows, width = x_ref.shape[0], 2 * MHEAD_DIM
    greet(n)
    exchange = Exchange(n, True, grads, logs_ref, back, *scratch[:9])

    def store(chunk, total):
        for (first, stop, *_), target in zip(sources, (unpatch_ref, d_out_ref, d_qkv_ref)):

            @pl.when((chunk >= first) & (chunk < stop))
            def _():
                target[:, columns_of(chunk - first)] = total

    def find(which):
        return lambda chunk: (which, chunk)

    sources = [
        (0, 16, find(0), hidden_left, slots_ref),
        (16, 18, find(0), left_ref, out_right_ref),
        (18, 24, find(1), left_ref, qkv_right_ref),
    ]
    sums = Sums(Place(n), sources, store, *scratch[9:])
    exchange.tell()
    turn(order_ref, hidden_left, hidden_ref)
    left_ref[0] = dot_t(order_ref[...], mixed_ref[...]).astype(BF)
    left_ref[1] = dot_t(order_ref[...], normed_ref[...]).astype(BF)

    head_lane = lax.broadcasted_iota(jnp.int32, (1, MHEADS), 1)
    lanes = lax.broadcasted_iota(jnp.int32, (1, width), 1)
    halves = [lanes < MHEAD_DIM, lanes >= MHEAD_DIM]
    step, cum = steps_ref[0, :rows, :MHEADS], steps_ref[1, :rows, :MHEADS]
    turned_step, turned_cum = steps_ref.at[3], steps_ref.at[4]
    reach = marks_ref[0][:, :rows]
    from_before, to_after = marks_ref[1][:, 0:1], marks_ref[1][:, 1:2]
    last_cum = cum[rows - 1 : rows]
    to_end = jnp.exp(last_cum - cum) * to_after

    def column(values, head):
        return jnp.sum(jnp.where(head_lane == head, values, 0.0), axis=1, keepdims=True)

    def at_head(head, values):
        return jnp.where(head_lane == head, values, 0.0)

    def of_pair(pair, values):
        return jnp.where(halves[0], column(values, 2 * pair), column(values, 2 * pair + 1))

    def columns(pair):
        return pl.ds(pl.multiple_of(pair * width, width), width)

    scores[...] = dot_fine(queries_ref[...], keys_ref[...], NT)
    d_scores[...] = jnp.zeros_like(d_scores)
    d_step[...] = jnp.zeros_like(d_step)
    d_cum[...] = jnp.zeros_like(d_cum)
    d_turned[...] = jnp.zeros_like(d_turned)
    dqueries_ref[...] = jnp.zeros_like(dqueries_ref)
    d_head_ref[...] = jnp.zeros_like(d_head_ref)

    @pl.loop(0, MHEADS // 2)
    def _(pair):
        sums.at(pair)
        x, dy, state = x_ref[:, columns(pair)], dy_ref[:, columns(pair)], state_ref[columns(pair)]
        dx = of_pair(pair, head_ref[2:3]) * dy
        inflow = jnp.exp(of_pair(pair, cum)) * from_before
        dy_in = dy * inflow
        carried = dy_in * dot_fine(queries_ref[...], state, NT)
        dqueries_ref[...] += dot_fine(dy_in, state, NN)
        grads[columns(pair)] = dot_fine(dy_in, queries_ref[...], TN).astype(BF)
        for which, half in enumerate(halves):
            head = 2 * pair + which
            mine = pl.ds(head, 1)
            gap = column(cum, head) - turned_cum[mine, :rows]
            decay = jnp.exp(jnp.where(reach > 0.0, gap, 0.0)) * reach
            weighted = scores[...] * decay
            step_row = turned_step[mine, :rows]
            mixing = weighted * step_row
            d_mixing = dot_fine(dy, jnp.where(half, x, 0.0), NT)
            dx += dot_fine(mixing, jnp.where(half, dy, 0.0), TN)
            d_scores[...] += d_mixing * decay * step_row
            d_gap = d_mixing * mixing
            d_turned[0, mine, :rows] = jnp.sum(d_mixing * weighted, axis=0, keepdims=True)
            d_turned[1, mine, :rows] = -jnp.sum(d_gap, axis=0, keepdims=True)
            moved = jnp.sum(d_gap, axis=1, keepdims=True)
            moved += jnp.sum(jnp.where(half, carried, 0.0), axis=1, keepdims=True)
            d_cum[...] += at_head(head, moved)
            skipped = jnp.sum(jnp.where(half, dy * x, 0.0), keepdims=True)
            d_head_ref[2:3] += at_head(head, skipped)
        dx_ref[:, columns(pair)] = dx

    dkeys_ref[...] = dot_fine(d_scores[...], queries_ref[...], TN)
    dqueries_ref[...] += dot_fine(d_scores[...], keys_ref[...], NN)
    exchange.start()
    sums.run(16, 20)
    exchange.join()
    sums.run(20, 24)
    exchange.arrive()

    @pl.loop(0, MHEADS // 2)
    def _(pair):
        @pl.when(pair < 7)
        def _():
            sums.at(24 + pair)

        x, state, grad = x_ref[:, columns(pair)], state_ref[columns(pair)], back[columns(pair)]
        weight = of_pair(pair, to_end * step)
        d_weighted = dot_fine(keys_ref[...], grad, NT)
        dkeys_ref[...] += dot_fine(x * weight, grad, NN)
        dx_ref[:, columns(pair)] += weight * d_weighted
        kept = grad.astype(F32) * state.astype(F32)
        for which, half in enumerate(halves):
            head = 2 * pair + which
            d_weight = jnp.sum(jnp.where(half, x * d_weighted, 0.0), axis=1, keepdims=True)
            d_step[...] += at_head(head, d_weight * column(to_end, head))
            moved = d_weight * column(to_end * step, head)
            d_cum[...] -= at_head(head, moved)
            d_decay = jnp.sum(kept[which * MHEAD_DIM : (which + 1) * MHEAD_DIM], keepdims=True)
            ended = jnp.sum(moved, keepdims=True)
            ended += d_decay * jnp.exp(column(last_cum, head)) * from_before[rows - 1 : rows]
            d_cum[rows - 1 : rows] += at_head(head, ended)

    d_steps = d_step[...] + d_turned[0].T[:rows, :MHEADS]
    d_cums = d_cum[...] + d_turned[1].T[:rows, :MHEADS]
    later = lax.broadcasted_iota(jnp.int32, (rows, rows), 0) <= lax.broadcasted_iota(
        jnp.int32, (rows, rows), 1
    )
    d_logs = dot_fine(later.astype(BF), d_cums, NN, 3)
    rate = jnp.exp(head_ref[1:2])
    d_raw = (d_steps - rate * d_logs) * steps_ref[2, :rows, :MHEADS]
    d_dt_ref[...] = d_raw
    d_head_ref[0:1] = jnp.sum(d_raw, axis=0, keepdims=True)
    d_head_ref[1:2] = -rate * jnp.sum(step * d_logs, axis=0, keepdims=True)
    dx_ref[:, pl.ds(DI, NSTATE)] = dkeys_ref[...]
    dx_ref[:, pl.ds(DI + NSTATE, NSTATE)] = dqueries_ref[...]
    sums.run(31, sums.times)
    sums.end()
    exchange.end()


def mixer_tables(dt_raw, head_params, starts):
    rows = dt_raw.shape[0]
    step = jax.nn.softplus(dt_raw + head_params[0])
    cum = jnp.cumsum(-step * jnp.exp(head_params[1]), axis=0)
    segment = jnp.cumsum(starts, axis=0, dtype=jnp.int32)
    slope = jax.nn.sigmoid(dt_raw + head_params[0])
    square = [jnp.pad(v, ((0, 128 - v.shape[0]), (0, 128 - v.shape[1]))) for v in (step.T, cum.T)]
    tall = [jnp.pad(v, ((0, 128 - rows), (0, 128 - MHEADS))) for v in (step, cum, slope)]
    position = jnp.arange(rows)
    reach = (position[:, None] >= position[None, :]) & (segment[:, None] == segment[None, :])
    ends = jnp.stack([segment == 0, segment == segment[-1]], axis=1)
    marks = [jnp.pad(v.astype(F32), ((0, 0), (0, 128 - v.shape[1]))) for v in (reach, ends)]
    return jnp.stack(tall + square), jnp.stack(marks)


def mixer_back(told, order, values, rights, hidden, slots, dy, conv_out, state_in, steps, marks, head_params):
    n, rows = lax.axis_size("seq"), conv_out.shape[0]
    x, keys, queries = jnp.split(conv_out, [DI, DI + NSTATE], axis=1)
    total = MHEADS * MHEAD_DIM
    wide = sum(right.shape[1] for right in rights)
    return pl.pallas_call(
        functools.partial(mixer_back_kernel, n),
        out_shape=[
            jax.ShapeDtypeStruct((rows, CONV_CH), F32),
            jax.ShapeDtypeStruct((rows, MHEADS), F32),
            jax.ShapeDtypeStruct((8, MHEADS), F32),
        ]
        + [jax.ShapeDtypeStruct((SUM_ROWS, right.shape[1]), F32) for right in rights]
        + [jax.ShapeDtypeStruct((SUM_ROWS, slots.shape[1]), F32)],
        in_specs=[pl.BlockSpec(memory_space=pltpu.VMEM)] * 16,
        out_specs=[pl.BlockSpec(memory_space=pltpu.VMEM)] * 6,
        scratch_shapes=[
            pltpu.VMEM((rows, NSTATE), F32),
            pltpu.VMEM((rows, NSTATE), F32),
            pltpu.VMEM((rows, rows), F32),
            pltpu.VMEM((rows, rows), F32),
            pltpu.VMEM((rows, MHEADS), F32),
            pltpu.VMEM((rows, MHEADS), F32),
            pltpu.VMEM((2, 128, 128), F32),
            pltpu.VMEM((total, NSTATE), BF),
            pltpu.VMEM((total, NSTATE), BF),
        ]
        + [pltpu.VMEM((2, n * SUM_ROWS, values[0].shape[0]), BF)]
        + lefts_scratch(n, hidden)
        + exchange_scratch(n)
        + sums_scratch(n, 24),
        compiler_params=pltpu.CompilerParams(
            collective_id=3, has_side_effects=True, vmem_limit_bytes=62 * 2**20
        ),
        cost_estimate=pl.CostEstimate(flops=2**32, bytes_accessed=2**24, transcendentals=2**20),
    )(
        told, order, *values, *rights, hidden, slots, dy, x, keys, queries,
        state_in, steps, marks, head_params,
    )


FF_TILE = D


def feed_forward_kernel(normed_ref, gate_w_ref, up_w_ref, gate_ref, up_ref, hid_ref):
    gate, up = dot(normed_ref[...], whole_of(gate_w_ref)), dot(normed_ref[...], whole_of(up_w_ref))
    gate_ref[...], up_ref[...] = gate.astype(BF), up.astype(BF)
    hid_ref[...] = (silu(gate) * up).astype(BF)


def feed_forward_blocks(n):
    tiles, first = FF // FF_TILE, PATCH + 4
    return [
        flat_block(n, D // n, lambda i: first + i),
        flat_block(n, D // n, lambda i: first + tiles + i),
        pl.BlockSpec((FF_TILE, D), lambda i: (i, 0)),
    ]


def feed_forward(normed, flat):
    rows = normed.shape[0]
    tile = pl.BlockSpec((rows, FF_TILE), lambda i: (0, i))
    return pl.pallas_call(
        feed_forward_kernel,
        grid=(FF // FF_TILE,),
        out_shape=[jax.ShapeDtypeStruct((rows, FF), BF)] * 3,
        in_specs=[pl.BlockSpec((rows, D), lambda i: (0, 0)), *feed_forward_blocks(flat.shape[0])[:2]],
        out_specs=[tile, tile, tile],
        compiler_params=pltpu.CompilerParams(vmem_limit_bytes=56 * 2**20),
        cost_estimate=pl.CostEstimate(
            flops=4 * rows * D * FF, bytes_accessed=2**25, transcendentals=rows * FF
        ),
    )(normed, flat, flat)


def feed_forward_back_kernel(
    grad_ref, stream_ref, gain_ref, gate_ref, up_ref, hid_ref, gate_w_ref, up_w_ref, down_ref,
    out_ref, both_ref, d_stream_ref, d_low_ref, d_gain_ref, layer, total,
):
    step = pl.program_id(0)
    added = dot(hid_ref[...], down_ref[...])

    @pl.when(step == 0)
    def _():
        layer[...] = stream_ref[...] + added

    @pl.when(step > 0)
    def _():
        layer[...] += added

    d_hid = dot_t(grad_ref[...], down_ref[...])
    gate, up = gate_ref[...].astype(F32), up_ref[...].astype(F32)
    s = jax.nn.sigmoid(gate)
    d_gate = (d_hid * up * (s * (1.0 + gate * (1.0 - s)))).astype(BF)
    d_up = (d_hid * (gate * s)).astype(BF)
    both_ref[0], both_ref[1] = d_gate, d_up
    found = dot_t(d_gate, whole_of(gate_w_ref)) + dot_t(d_up, whole_of(up_w_ref))

    @pl.when(step == 0)
    def _():
        total[...] = found

    @pl.when(step > 0)
    def _():
        total[...] += found

    @pl.when(step == pl.num_programs(0) - 1)
    def _():
        out_ref[...] = layer[...].astype(BF)
        stream, d_normed = stream_ref[...], total[...]
        r = lax.rsqrt(jnp.mean(stream * stream, axis=-1, keepdims=True) + EPS)
        scaled = gain_ref[...] * d_normed
        inner = jnp.mean(stream * scaled, axis=-1, keepdims=True)
        d_stream = grad_ref[...].astype(F32) + r * scaled - stream * (r * r * r) * inner
        d_stream_ref[...] = d_stream
        d_low_ref[...] = d_stream.astype(BF)
        d_gain_ref[...] = jnp.sum(stream * r * d_normed, axis=0, keepdims=True)


def feed_forward_back(grad, stream, gain, gate, up, hid, flat, down):
    rows, tiles = stream.shape[0], FF // FF_TILE
    wide = pl.BlockSpec((rows, D), lambda i: (0, 0))
    tile = pl.BlockSpec((rows, FF_TILE), lambda i: (0, i))
    narrow = pl.BlockSpec((1, D), lambda i: (0, 0))
    out, both, d_stream, d_low, d_gain = pl.pallas_call(
        feed_forward_back_kernel,
        grid=(tiles,),
        out_shape=[
            jax.ShapeDtypeStruct((rows, D), BF),
            jax.ShapeDtypeStruct((2, rows, FF), BF),
            jax.ShapeDtypeStruct((rows, D), F32),
            jax.ShapeDtypeStruct((rows, D), BF),
            jax.ShapeDtypeStruct((1, D), F32),
        ],
        in_specs=[
            wide,
            wide,
            narrow,
            tile,
            tile,
            tile,
            *feed_forward_blocks(flat.shape[0]),
        ],
        out_specs=[wide, pl.BlockSpec((2, rows, FF_TILE), lambda i: (0, 0, i)), wide, wide, narrow],
        scratch_shapes=[pltpu.VMEM((rows, D), F32)] * 2,
        compiler_params=pltpu.CompilerParams(vmem_limit_bytes=60 * 2**20),
        cost_estimate=pl.CostEstimate(
            flops=8 * rows * D * FF, bytes_accessed=2**25, transcendentals=rows * FF
        ),
    )(grad, stream, gain[None], gate, up, hid, flat, flat, down)
    return out, both, d_stream, d_low, d_gain[0]


ATTN_ROWS, BACK_ROWS = 128, 256


def tile_mask():
    row = lax.broadcasted_iota(jnp.int32, (ATTN_ROWS, 2 * ATTN_ROWS), 0)
    column = lax.broadcasted_iota(jnp.int32, (ATTN_ROWS, 2 * ATTN_ROWS), 1) % ATTN_ROWS
    return (row // PATCH == column // PATCH) & (row >= column)


def first_head():
    return lax.broadcasted_iota(jnp.int32, (1, 2 * AHEAD_DIM), 1) < AHEAD_DIM


def one_below_other(pair):
    lanes, zeros = first_head(), jnp.zeros_like(pair)
    return jnp.concatenate([jnp.where(lanes, pair, zeros), jnp.where(lanes, zeros, pair)], axis=0)


def by_head(values, reduce):
    first = reduce(values[:, :ATTN_ROWS], axis=-1, keepdims=True)
    second = reduce(values[:, ATTN_ROWS:], axis=-1, keepdims=True)
    shape = (values.shape[0], ATTN_ROWS)
    return jnp.concatenate(
        [jnp.broadcast_to(first, shape), jnp.broadcast_to(second, shape)], axis=1
    )


def pair_probs(queries, key_rows, mask):
    scores = jnp.where(mask, dot_t(queries, key_rows) * AHEAD_DIM ** (-0.5), -1e30)
    raised = jnp.exp(scores - by_head(scores, jnp.max))
    return raised / by_head(raised, jnp.sum)


def attention_kernel(triple_ref, out_ref):
    mask = tile_mask()
    width = 2 * AHEAD_DIM
    for pair in range(AHEADS // 2):
        queries, key_rows, value_rows = [
            triple_ref[:, part * D + pair * width : part * D + (pair + 1) * width] for part in range(3)
        ]
        probs = pair_probs(queries, one_below_other(key_rows), mask)
        mixed = dot(probs.astype(BF), one_below_other(value_rows))
        out_ref[:, pair * width : (pair + 1) * width] = mixed.astype(BF)


def attention(triple):
    rows = triple.shape[0]
    return pl.pallas_call(
        attention_kernel,
        grid=(rows // ATTN_ROWS,),
        out_shape=jax.ShapeDtypeStruct((rows, D), BF),
        in_specs=[pl.BlockSpec((ATTN_ROWS, 3 * D), lambda i: (i, 0))],
        out_specs=pl.BlockSpec((ATTN_ROWS, D), lambda i: (i, 0)),
    )(triple)


def attention_back_kernel(
    triple_ref, low_ref, d_stream_ref, stream_ref, gain_ref, out_w_ref, q_ref, k_ref, v_ref,
    out_ref, d_out_ref, d_gain_ref,
):
    mask = tile_mask()
    width = 2 * AHEAD_DIM
    scale = AHEAD_DIM ** (-0.5)

    def of_keys(left, right):
        found = lax.dot_general(left, right, (((0,), (0,)), ((), ())), preferred_element_type=F32)
        return jnp.where(first_head(), found[:ATTN_ROWS], found[ATTN_ROWS:])

    grads = dot_t(low_ref[...], whole_of(out_w_ref)).astype(BF)
    for first in range(0, BACK_ROWS, ATTN_ROWS):
        rows = slice(first, first + ATTN_ROWS)
        for pair in range(AHEADS // 2):
            lo, hi = pair * width, (pair + 1) * width
            queries, key_rows, value_rows = [
                triple_ref[rows, part * D + lo : part * D + hi] for part in range(3)
            ]
            grad = grads[rows, lo:hi]
            key_rows = one_below_other(key_rows)
            probs = pair_probs(queries, key_rows, mask)
            d_probs = dot_t(grad, one_below_other(value_rows))
            d_scores = (probs * (d_probs - by_head(probs * d_probs, jnp.sum))).astype(BF)
            out_ref[rows, lo:hi] = (scale * dot(d_scores, key_rows)).astype(BF)
            out_ref[rows, D + lo : D + hi] = (scale * of_keys(d_scores, queries)).astype(BF)
            d_values = of_keys(probs.astype(BF), grad)
            out_ref[rows, 2 * D + lo : 2 * D + hi] = d_values.astype(BF)

    d_normed = None
    for part, ref in enumerate((q_ref, k_ref, v_ref)):
        found = dot_t(out_ref[:, part * D : (part + 1) * D], whole_of(ref))
        d_normed = found if part == 0 else d_normed + found
    stream = stream_ref[...]
    r = lax.rsqrt(jnp.mean(stream * stream, axis=-1, keepdims=True) + EPS)
    scaled = gain_ref[...] * d_normed
    inner = jnp.mean(stream * scaled, axis=-1, keepdims=True)
    d_out_ref[...] = d_stream_ref[...] + r * scaled - stream * (r * r * r) * inner
    gained = jnp.sum(stream * r * d_normed, axis=0, keepdims=True)

    @pl.when(pl.program_id(0) == 0)
    def _():
        d_gain_ref[...] = gained

    @pl.when(pl.program_id(0) > 0)
    def _():
        d_gain_ref[...] += gained


def attention_back(triple, low, d_stream, stream, gain, flat):
    rows, n = triple.shape[0], flat.shape[0]
    wide = pl.BlockSpec((BACK_ROWS, 3 * D), lambda i: (i, 0))
    tile = pl.BlockSpec((BACK_ROWS, D), lambda i: (i, 0))
    narrow = pl.BlockSpec((1, D), lambda i: (0, 0))

    def block(place):
        return flat_block(n, D // n, lambda i: place)

    d_triple, d_out, d_gain = pl.pallas_call(
        attention_back_kernel,
        grid=(rows // BACK_ROWS,),
        out_shape=[
            jax.ShapeDtypeStruct((rows, 3 * D), BF),
            jax.ShapeDtypeStruct((rows, D), F32),
            jax.ShapeDtypeStruct((1, D), F32),
        ],
        in_specs=[wide, tile, tile, tile, narrow]
        + [block(PATCH + 3), block(PATCH), block(PATCH + 1), block(PATCH + 2)],
        out_specs=[wide, tile, narrow],
        compiler_params=pltpu.CompilerParams(vmem_limit_bytes=56 * 2**20),
        cost_estimate=pl.CostEstimate(
            flops=8 * rows * D * D, bytes_accessed=2**24, transcendentals=0
        ),
    )(triple, low, d_stream, stream, gain[None], flat, flat, flat, flat)
    return d_triple, d_out, d_gain[0]


def local(
    byte_acts,
    resets,
    out_grad,
    patch_weight,
    patch_gain,
    mixer_in,
    conv_weight,
    conv_bias,
    head_params,
    mixer_gain,
    mixer_out,
    unpatch_weight,
    attn_gain,
    qkv_weight,
    attn_out,
    ffn_gain,
    gate_up,
    down_weight,
):
    n = lax.axis_size("seq")
    me = lax.axis_index("seq")
    ring = Ring(n)

    def passed_along(block, distance):
        route = [(i - distance, i) for i in range(n) if 0 <= i - distance < n]
        return lax.ppermute(block, "seq", route)

    live = Live()
    order = ring.order()

    byte_wide = byte_acts.astype(F32)
    patches = byte_acts.reshape(-1, PATCH * D)
    patch_rows = patches.shape[0]
    early = gather_flat(n, [unpatch_weight, qkv_weight, attn_out, gate_up])
    late = lax.all_gather(down_weight, "seq", axis=0, tiled=True)
    small = [patch_gain, conv_weight.reshape(-1), conv_bias, mixer_gain, attn_gain, ffn_gain]
    cuts = list(np.cumsum([piece.shape[0] for piece in small]))
    small_shard = jnp.concatenate(small)
    small_shard = jnp.pad(small_shard, (0, -small_shard.shape[0] % 2048)).reshape(-1, 128)
    live.mixer_in, live.mixer_out, small_all, live.embedded, live.parted = gather_weights(
        n,
        [
            jnp.pad(mixer_in, ((0, 0), (0, -mixer_in.shape[1] % 128))),
            mixer_out,
            small_shard,
        ],
        [(16, 2304), (32, D), (16, 128)],
        patches,
        patch_weight,
    )
    small_all = small_all.reshape(n, -1)[:, : cuts[-1]].astype(F32)
    parts = jnp.split(small_all, cuts[:-1], axis=1)
    live.patch_gain = parts[0].reshape(-1)
    live.conv_weight = parts[1].reshape(n, CONV, -1).transpose(1, 0, 2).reshape(CONV, CONV_CH)
    live.conv_bias, live.mixer_gain, live.attn_gain, live.ffn_gain = [
        piece.reshape(-1) for piece in parts[2:]
    ]
    live.normed = rms_scale(live.embedded, live.patch_gain).astype(BF)
    projected = dot(live.normed, live.mixer_in)
    live.gate_z = projected[:, :DI]
    conv_in = projected[:, DI : DI + CONV_CH].astype(BF).astype(F32)
    dt_raw = projected[:, DI + CONV_CH : DI + CONV_CH + MHEADS]
    logs = jnp.sum(-jax.nn.softplus(dt_raw + head_params[0]) * jnp.exp(head_params[1]), axis=0)
    flag = jnp.max(resets).astype(F32)
    live.logs = jnp.concatenate([logs, flag[None]])
    not_reset = 1.0 - resets.astype(F32)
    keep_tail = jnp.concatenate(
        [jnp.cumprod(not_reset[patch_rows - CONV + 2 :][::-1])[::-1], jnp.ones((1,), F32)]
    )
    tail_sent = (conv_in[patch_rows - CONV + 1 :] * keep_tail[:, None]).astype(BF)
    halo_rows = passed_along(tail_sent, 1)
    flags_ext = jnp.concatenate([jnp.zeros((CONV - 1,), jnp.int32), resets])
    validity = tap_masks(flags_ext, patch_rows)
    conv_ext = jnp.concatenate([halo_rows.astype(F32), conv_in])
    conv_out, conv_back = jax.vjp(
        functools.partial(conv_apply, validity=validity, row_count=patch_rows),
        conv_ext,
        live.conv_weight,
        live.conv_bias,
    )
    state_parts, state_back = jax.vjp(
        functools.partial(block_state, starts=resets), conv_out, dt_raw, head_params
    )
    local_state, decay_total = state_parts
    live.state_in = pass_states(n, local_state, live.logs, False)
    live.fence()

    mixer_y, output_back = jax.vjp(
        functools.partial(block_output, starts=resets),
        conv_out,
        dt_raw,
        head_params,
        live.state_in.astype(F32).reshape(MHEADS, MHEAD_DIM, NSTATE),
    )
    gate_act = silu(live.gate_z)
    gated = mixer_y * gate_act
    live.gated_norm = rms_scale(gated, live.mixer_gain).astype(BF)
    branch = dot(live.gated_norm, live.mixer_out)
    live.hidden = (live.embedded + branch).astype(BF)
    live.early = early
    slots = flat_dot(live.hidden, live.early, 0, PATCH, F32)
    live.stream0 = byte_wide + slots.reshape(-1, D)
    live.normed0 = rms_scale(live.stream0, live.attn_gain).astype(BF)
    live.fence()

    rows = byte_wide.shape[0]
    live.triple = flat_dot(live.normed0, live.early, PATCH, 3, BF)
    live.mixed = attention(live.triple)
    live.stream1 = live.stream0 + flat_dot(live.mixed, live.early, PATCH + 3, 1, F32)
    live.normed1 = rms_scale(live.stream1, live.ffn_gain).astype(BF)
    live.gate, live.up, live.hid = feed_forward(live.normed1, live.early)
    small_slice = n == 32
    if small_slice:
        live.flat = down_grad(n, live.hid, out_grad)

    def lefts_of(*values):
        parts = []
        for value in values:
            cut = value.reshape(value.shape[0], n, -1, SUM_ROWS).transpose(2, 0, 1, 3)
            parts.append(cut.reshape(-1, value.shape[0], n * SUM_ROWS))
        return jnp.concatenate(parts, axis=0)

    if small_slice:
        place = jnp.arange(n * SUM_ROWS)
        source = jnp.repeat(order * SUM_ROWS, SUM_ROWS) + place % SUM_ROWS
        live.order = (place[None, :] == source[:, None]).astype(BF)
        live.last_lefts = lefts_of(live.normed, live.gated_norm)
        live.steps, live.marks = mixer_tables(dt_raw, head_params, resets)
        live.told = told_logs(live.logs)
    live.fence()

    layer_out, d_both, d_stream1, d_stream1_low, g_ffn_gain = feed_forward_back(
        out_grad, live.stream1, live.ffn_gain, live.gate, live.up, live.hid, live.early, late
    )
    if small_slice:
        block = down_weight.shape[0]
        flat = gate_up_grad(live.normed1, d_both, live.flat)
        found = lax.psum_scatter(flat, "seq", scatter_dimension=0, tiled=True)[0].astype(F32)
        g_down = found[:block]
        g_gate_up = found[block:].reshape(-1, SUM_ROWS, D).transpose(1, 0, 2)
        g_gate_up = g_gate_up.reshape(SUM_ROWS, -1)
    else:
        g_down = summed_grad(live.hid, out_grad)
        g_gate_up = summed_grad(live.normed1, jnp.concatenate([d_both[0], d_both[1]], axis=1))
    d_triple, d_stream0, g_attn_gain = attention_back(
        live.triple, d_stream1_low, d_stream1, live.stream0, live.attn_gain, live.early
    )
    live.d_stream0 = d_stream0.reshape(patch_rows, PATCH * D)

    d_slots = live.d_stream0.astype(BF)
    d_hidden = flat_dot_t(d_slots, live.early, 0, PATCH)
    d_branch = d_hidden.astype(BF)
    d_gated, g_mixer_gain = rms_back(gated, live.mixer_gain, dot_t(d_branch, live.mixer_out))
    d_gate_z = d_gated * mixer_y * silu_slope(live.gate_z)
    if small_slice:
        d_conv_out, d_dt, g_head, g_attn_out, g_qkv, g_unpatch = mixer_back(
            live.told,
            live.order,
            [live.mixed, live.normed0],
            [d_stream1_low, d_triple],
            live.hidden[None],
            d_slots,
            d_gated * gate_act,
            conv_out,
            live.state_in,
            live.steps,
            live.marks,
            head_params,
        )
        conv_cot = conv_back(d_conv_out)
        g_head = g_head[:3]
    else:
        output_grads = output_back(d_gated * gate_act)
        state_grad = pass_states(n, output_grads[3], live.logs, True).astype(F32)
        state_grad = state_grad.reshape(MHEADS, MHEAD_DIM, NSTATE)
        state_in = live.state_in.astype(F32).reshape(MHEADS, MHEAD_DIM, NSTATE)
        state_cot = state_back((state_grad, jnp.sum(state_grad * state_in, axis=(1, 2))))
        conv_cot = conv_back(output_grads[0] + state_cot[0])
        d_dt = output_grads[1] + state_cot[1]
        g_head = output_grads[2] + state_cot[2]
    returned = passed_along(conv_cot[0][: CONV - 1], -1)
    d_conv_in = conv_cot[0][CONV - 1 :] + jnp.concatenate(
        [jnp.zeros((patch_rows - CONV + 1, CONV_CH), F32), returned * keep_tail[:, None]]
    )
    d_projected = jnp.concatenate([d_gate_z, d_conv_in, d_dt], axis=1).astype(BF)
    d_projected = jnp.pad(d_projected, ((0, 0), (0, -d_projected.shape[1] % 128)))
    d_embedded, g_patch_gain = rms_back(
        live.embedded, live.patch_gain, dot_t(d_projected, live.mixer_in)
    )
    d_embedded = (d_hidden + d_embedded).astype(BF)

    g_conv_weight = conv_cot[1].reshape(CONV, n, -1).transpose(1, 0, 2).reshape(n, -1)
    g_head = jnp.broadcast_to(g_head.reshape(1, -1), (n, 3 * MHEADS))
    g_small = [g_patch_gain, g_conv_weight, conv_cot[2], g_mixer_gain, g_attn_gain, g_ffn_gain, g_head]
    g_small = jnp.concatenate([piece.reshape(n, -1) for piece in g_small], axis=1)
    small_width = g_small.shape[1]
    g_small = jnp.pad(g_small, ((0, 0), (0, LOG_ROWS * 128 - small_width)))
    g_small = g_small.reshape(n * LOG_ROWS, 128)
    if small_slice:
        d_projected = jnp.pad(d_projected, ((0, 0), (0, -d_projected.shape[1] % SUM_COLUMNS)))
        g_patch, g_small, g_mixer_in, g_mixer_out, input_grad = last_sums(
            n,
            d_embedded,
            live.parted,
            g_small,
            live.order,
            live.last_lefts,
            jnp.concatenate([d_projected, d_branch, d_branch], axis=1),
            live.d_stream0,
            patch_weight,
            mixer_in.shape[1],
        )
    else:
        g_attn_out = summed_grad(live.mixed, d_stream1_low)
        g_qkv = summed_grad(live.normed0, d_triple)
        known = lax.all_gather(d_embedded, "seq", axis=0, tiled=True)
        g_patch = dot(live.parted.T, known)
        d_parted = dot_t(known, patch_weight).astype(BF).reshape(n, patch_rows, -1)
        d_parted = lax.all_to_all(d_parted, "seq", 0, 0, tiled=True)
        d_parted = d_parted.transpose(1, 0, 2).reshape(patch_rows, -1).astype(F32)
        input_grad = (live.d_stream0 + d_parted).astype(BF)
        g_small = lax.psum_scatter(g_small, "seq", scatter_dimension=0, tiled=True)
        g_unpatch = summed_grad(live.hidden, d_slots)
        g_mixer_in = summed_grad(live.normed, d_projected)[:, : mixer_in.shape[1]]
        g_mixer_out = summed_grad(live.gated_norm, d_branch)
    g_small = g_small.reshape(-1)[:small_width]
    s = jnp.split(g_small, cuts)
    return (
        layer_out,
        input_grad.reshape(-1, D),
        g_patch,
        s[0],
        g_mixer_in,
        s[1].reshape(CONV, -1),
        s[2],
        s[6].reshape(3, MHEADS),
        s[3],
        g_mixer_out,
        g_unpatch,
        s[4],
        g_qkv,
        g_attn_out,
        s[5],
        g_gate_up,
        g_down,
    )


def solution(mesh):
    rows, vector = P("seq", None), P("seq")
    placed = (
        rows, vector, rows, rows, vector, rows, P(None, "seq"), vector, P(),
        vector, rows, rows, vector, rows, rows, vector, rows, rows,
    )
    returned = (
        rows, rows, rows, vector, rows, P(None, "seq"), vector, P(), vector,
        rows, rows, vector, rows, rows, vector, rows, rows,
    )
    return jax.shard_map(
        local, mesh=mesh, in_specs=placed, out_specs=returned, check_vma=False
    )
```

```python
import functools

import jax
import jax.numpy as jnp
import numpy as np
from jax import lax
from jax.experimental import pallas as pl
from jax.experimental.pallas import tpu as pltpu
from jax.sharding import PartitionSpec as P

D = 1024
PATCH = 8
MHEADS = 32
MHEAD_DIM = 64
DI = 2048
NSTATE = 128
CONV = 4
AHEADS = 16
AHEAD_DIM = 64
FF = 4096
CONV_CH = 2304

EPS = 1e-05
HIGH = lax.Precision.HIGHEST
BF = jnp.bfloat16
F32 = jnp.float32


class Ring:
    def __init__(self, n):
        self.n = n
        self.depth = n // 8
        coords = [(i // 8, (i // 4) % 2, (i // 2) % 2, i % 2) for i in range(n)]

        def index(z, y, x, c):
            return ((z * 2 + y) * 2 + x) * 2 + c

        def flip(z, y, x, c, along_x):
            return index(z, y, 1 - x, c) if along_x else index(z, 1 - y, x, c)

        self.core = [(index(*p), index(*p) ^ 1) for p in coords]
        self.first = [(index(*p), flip(*p, p[3] == 0)) for p in coords]
        self.second = [(index(*p), flip(*p, p[3] == 1)) for p in coords]
        self.bits = [1 << b for b in range(self.depth.bit_length() - 1)]
        self.along = {
            bit: [(index(*p), index(p[0] ^ bit, *p[1:])) for p in coords] for bit in self.bits
        }
        table = np.zeros((n, n), np.int32)
        for me, (z, y, x, c) in enumerate(coords):
            place = 0
            for rc in range(2):
                owner = c ^ rc
                for r2 in range(2):
                    for r1 in range(2):
                        rx, ry = (r1, r2) if owner == 0 else (r2, r1)
                        for rz in range(self.depth):
                            table[me, place] = index((z + rz) % self.depth, y ^ ry, x ^ rx, owner)
                            place += 1
        self.table = table

    def order(self):
        return jnp.asarray(self.table)[lax.axis_index("seq")]


def swap(block, route):
    return lax.ppermute(block, "seq", route)


def flat_kernel(*refs):
    out, first = refs[-1], 0
    for ref in refs[:-1]:
        rows = ref.shape[0]
        for column in range(0, ref.shape[1], D):
            out[pl.ds(first, rows)] = ref[:, pl.ds(column, D)]
            first += rows


def flat_rows(shards):
    total = sum(shard.shape[0] * shard.shape[1] // D for shard in shards)
    return pl.pallas_call(
        flat_kernel,
        out_shape=jax.ShapeDtypeStruct((total, D), BF),
        in_specs=[pl.BlockSpec(memory_space=pltpu.VMEM)] * len(shards),
        out_specs=pl.BlockSpec(memory_space=pltpu.VMEM),
    )(*shards)


def gather_flat(n, shards):
    return lax.all_gather(flat_rows(shards), "seq", axis=0)


def flat_block(n, rows, place):
    return pl.BlockSpec((n, rows, D), lambda i: (0, place(i), 0))


def whole_of(ref):
    return ref[...].reshape(-1, ref.shape[-1])


def flat_dot_kernel(values_ref, flat_ref, out_ref):
    out_ref[...] = dot(values_ref[...], whole_of(flat_ref)).astype(out_ref.dtype)


def flat_dot(values, flat, first, count, kind):
    n, rows = flat.shape[0], values.shape[0]
    return pl.pallas_call(
        flat_dot_kernel,
        grid=(count,),
        out_shape=jax.ShapeDtypeStruct((rows, count * D), kind),
        in_specs=[
            pl.BlockSpec((rows, D), lambda i: (0, 0)),
            flat_block(n, D // n, lambda i: first + i),
        ],
        out_specs=pl.BlockSpec((rows, D), lambda i: (0, i)),
        compiler_params=pltpu.CompilerParams(vmem_limit_bytes=56 * 2**20),
        cost_estimate=pl.CostEstimate(
            flops=2 * rows * D * D * count, bytes_accessed=2 * D * D * count, transcendentals=0
        ),
    )(values, flat)


def flat_dot_t_kernel(values_ref, flat_ref, out_ref, total):
    few = values_ref.shape[0] < 256
    step = pl.program_id(0)
    if few:
        found = dot_t(whole_of(flat_ref), values_ref[...])
    else:
        found = dot_t(values_ref[...], whole_of(flat_ref))

    @pl.when(step == 0)
    def _():
        total[...] = found

    @pl.when(step > 0)
    def _():
        total[...] += found

    @pl.when(step == pl.num_programs(0) - 1)
    def _():
        out_ref[...] = total[...].T if few else total[...]


def flat_dot_t(values, flat, first, count):
    n, rows = flat.shape[0], values.shape[0]
    return pl.pallas_call(
        flat_dot_t_kernel,
        grid=(count,),
        out_shape=jax.ShapeDtypeStruct((rows, D), F32),
        in_specs=[
            pl.BlockSpec((rows, D), lambda i: (0, i)),
            flat_block(n, D // n, lambda i: first + i),
        ],
        out_specs=pl.BlockSpec((rows, D), lambda i: (0, 0)),
        scratch_shapes=[pltpu.VMEM((D, rows) if rows < 256 else (rows, D), F32)],
        compiler_params=pltpu.CompilerParams(vmem_limit_bytes=56 * 2**20),
        cost_estimate=pl.CostEstimate(
            flops=2 * rows * D * D * count, bytes_accessed=2 * D * D * count, transcendentals=0
        ),
    )(values, flat)


class Live:
    def fence(self):
        vars(self).update(lax.optimization_barrier(dict(vars(self))))


def summed_grad(left, right):
    product = lax.dot_general(left, right, (((0,), (0,)), ((), ())), preferred_element_type=F32)
    summed = lax.psum_scatter(product.astype(BF), "seq", scatter_dimension=0, tiled=True)
    return summed.astype(F32)


def turned_product(left, right):
    found = lax.dot_general(left, right, (((0,), (0,)), ((), ())), preferred_element_type=F32)
    return found.astype(BF)


def down_grad_kernel(hid_ref, grad_ref, out_ref):
    devices, block = out_ref.shape[:2]
    few = 256 // block
    for first in range(0, devices, few):
        found = turned_product(hid_ref[:, pl.ds(first * block, 256)], grad_ref[...])
        out_ref[pl.ds(first, few)] = found.reshape(few, block, D)


def down_grad(n, hid, out_grad):
    rows, block, devices = hid.shape[0], hid.shape[1] // n, n // 4
    return pl.pallas_call(
        down_grad_kernel,
        grid=(4,),
        out_shape=jax.ShapeDtypeStruct((n, 3 * block, D), BF),
        in_specs=[
            pl.BlockSpec((rows, devices * block), lambda i: (0, i)),
            pl.BlockSpec((rows, D), lambda i: (0, 0)),
        ],
        out_specs=pl.BlockSpec((devices, block, D), lambda i: (i, 0, 0)),
        compiler_params=pltpu.CompilerParams(vmem_limit_bytes=56 * 2**20),
        cost_estimate=pl.CostEstimate(
            flops=2 * rows * FF * D, bytes_accessed=2**24, transcendentals=0
        ),
    )(hid, out_grad)


def gate_up_grad_kernel(normed_ref, both_ref, flat_ref, out_ref):
    del flat_ref
    devices, block = out_ref.shape[:2]
    for part in range(block // SUM_ROWS):
        found = turned_product(normed_ref[...], both_ref[0, :, pl.ds(part * D, D)])
        out_ref[:, pl.ds(part * SUM_ROWS, SUM_ROWS)] = found.reshape(devices, SUM_ROWS, D)


def gate_up_grad(normed, both, flat):
    n, rows, devices = flat.shape[0], normed.shape[0], flat.shape[0] // 4
    return pl.pallas_call(
        gate_up_grad_kernel,
        grid=(8,),
        out_shape=jax.ShapeDtypeStruct(flat.shape, BF),
        in_specs=[
            pl.BlockSpec((rows, devices * SUM_ROWS), lambda i: (0, i % 4)),
            pl.BlockSpec((1, rows, FF), lambda i: (i // 4, 0, 0)),
            pl.BlockSpec(memory_space=pltpu.HBM),
        ],
        out_specs=pl.BlockSpec((devices, flat.shape[1] // 3, D), lambda i: (i % 4, 1 + i // 4, 0)),
        input_output_aliases={2: 0},
        compiler_params=pltpu.CompilerParams(vmem_limit_bytes=56 * 2**20),
        cost_estimate=pl.CostEstimate(
            flops=4 * rows * FF * D, bytes_accessed=2**25, transcendentals=0
        ),
    )(normed, both, flat)


def dot(left, right):
    return jnp.dot(left, right, preferred_element_type=F32)


def dot_t(left, right):
    return lax.dot_general(left, right, (((1,), (1,)), ((), ())), preferred_element_type=F32)


def rms_scale(values, gain):
    return values * lax.rsqrt(jnp.mean(values * values, axis=-1, keepdims=True) + EPS) * gain


def rms_back(values, gain, grad):
    r = lax.rsqrt(jnp.mean(values * values, axis=-1, keepdims=True) + EPS)
    scaled = gain * grad
    inner = jnp.mean(values * scaled, axis=-1, keepdims=True)
    return r * scaled - values * (r * r * r) * inner, jnp.sum(values * r * grad, axis=0)


def silu(v):
    return v * jax.nn.sigmoid(v)


def silu_slope(v):
    s = jax.nn.sigmoid(v)
    return s * (1.0 + v * (1.0 - s))


def tap_masks(flags_ext, row_count):
    not_reset = 1.0 - flags_ext.astype(F32)
    validity = [jnp.ones((row_count,), F32)]
    for offset in range(1, CONV):
        validity.append(validity[-1] * not_reset[CONV - offset : CONV - offset + row_count])
    return validity


def conv_apply(conv_ext, conv_weight, conv_bias, validity, row_count):
    summed = conv_bias + conv_ext[CONV - 1 : CONV - 1 + row_count] * conv_weight[0]
    for offset in range(1, CONV):
        summed = (
            summed
            + validity[offset][:, None]
            * conv_ext[CONV - 1 - offset : CONV - 1 - offset + row_count]
            * conv_weight[offset]
        )
    return jax.nn.silu(summed)


def block_parts(conv_out, dt_raw, head_params, starts):
    row_count = conv_out.shape[0]
    values = conv_out[:, :DI].reshape(row_count, MHEADS, MHEAD_DIM)
    key_rows = conv_out[:, DI : DI + NSTATE]
    queries = conv_out[:, DI + NSTATE :]
    step_size = jax.nn.softplus(dt_raw + head_params[0])
    cumlog = jnp.cumsum(-step_size * jnp.exp(head_params[1]), axis=0)
    segment = jnp.cumsum(starts, axis=0, dtype=jnp.int32)
    return (values, key_rows, queries, step_size, cumlog, segment)


def block_state(conv_out, dt_raw, head_params, starts):
    values, key_rows, queries, step_size, cumlog, segment = block_parts(
        conv_out, dt_raw, head_params, starts
    )
    same_doc = (segment == segment[-1]).astype(F32)
    weighting = jnp.exp(cumlog[-1][None, :] - cumlog) * same_doc[:, None] * step_size
    state_out = jnp.einsum("rh,rhp,rn->hpn", weighting, values, key_rows, precision=HIGH)
    decay_total = jnp.exp(cumlog[-1]) * (segment[-1] == 0).astype(F32)
    return (state_out, decay_total)


def block_output(conv_out, dt_raw, head_params, state_in, starts):
    values, key_rows, queries, step_size, cumlog, segment = block_parts(
        conv_out, dt_raw, head_params, starts
    )
    position = jnp.arange(conv_out.shape[0])
    causal = (position[:, None] >= position[None, :]) & (segment[:, None] == segment[None, :])
    log_gaps = jnp.where(causal[:, :, None], cumlog[:, None, :] - cumlog[None, :, :], 0.0)
    decays = jnp.exp(log_gaps) * causal[:, :, None].astype(F32)
    scores = jnp.dot(queries, key_rows.T, precision=HIGH)
    mixing = scores[:, :, None] * decays * step_size[None, :, :]
    within = jnp.einsum("tsh,shp->thp", mixing, values, precision=HIGH)
    inflow = jnp.exp(cumlog) * (segment == 0).astype(F32)[:, None]
    carried = jnp.einsum("tn,hpn->thp", queries, state_in, precision=HIGH) * inflow[:, :, None]
    skipped = head_params[2][None, :, None] * values
    return (within + carried + skipped).reshape(conv_out.shape[0], DI)


MESH = pl.DeviceIdType.MESH


class Place:
    def __init__(self, n):
        self.n, self.depth = n, n // 8
        self.me = me = lax.axis_index("seq")
        self.z, self.y, self.x, self.c = me // 8, (me // 4) % 2, (me // 2) % 2, me % 2

    def flipped(self, rz, ry, rx, rc):
        z, bit = 0, 1
        while bit < self.depth:
            z = z + ((self.z // bit + rz // bit) % 2) * bit
            bit *= 2
        y, x, c = (self.y + ry) % 2, (self.x + rx) % 2, (self.c + rc) % 2
        return ((z * 2 + y) * 2 + x) * 2 + c

    def split(self, place):
        depth = self.depth
        rz, r1, r2 = place % depth, (place // depth) % 2, (place // (2 * depth)) % 2
        return rz, r1, r2, place // (4 * depth)

    def device(self, place):
        rz, r1, r2, rc = self.split(place)
        owner = (self.c + rc) % 2
        return self.flipped(rz, r2 + owner * (r1 - r2), r1 + owner * (r2 - r1), rc)

    def place_there(self, place):
        rz, r1, r2, rc = self.split(place)
        s1, s2 = r1 + rc * (r2 - r1), r2 + rc * (r1 - r2)
        return ((rc * 2 + s2) * 2 + s1) * self.depth + rz

    def sum_steps(self):
        steps = [(blocks, blocks, partner) for blocks, partner in self.halves()[:-4:-1]]
        above = self.me + ((self.z + 1) % self.depth - self.z) * 8
        return steps + [(block, 1, above) for block in range(self.depth - 1, 0, -1)]

    def halves(self):
        steps, bit = [], 1
        while bit < self.depth:
            steps.append((bit, self.flipped(bit, 0, 0, 0)))
            bit *= 2
        steps.append((self.depth, self.flipped(0, self.c, 1 - self.c, 0)))
        steps.append((2 * self.depth, self.flipped(0, 1 - self.c, self.c, 0)))
        steps.append((4 * self.depth, self.flipped(0, 0, 0, 1)))
        return steps


def greet(n):
    barrier = pltpu.get_barrier_semaphore()
    me = lax.axis_index("seq")

    @pl.loop(1, n)
    def _(hop):
        other = lax.rem(me + hop, n)
        pl.semaphore_signal(barrier, inc=1, device_id=(other,), device_id_type=MESH)

    pl.semaphore_wait(barrier, n - 1)


def remote(source, target, send_sem, recv_sem, device):
    return pltpu.make_async_remote_copy(
        src_ref=source,
        dst_ref=target,
        send_sem=send_sem,
        recv_sem=recv_sem,
        device_id=(device,),
        device_id_type=MESH,
    )


def landed(ref, sem):
    pltpu.make_async_copy(ref, ref, sem).wait()


def rows_of(place, count, rows):
    return pl.ds(pl.multiple_of(place * rows, rows), count * rows)


GATHER_TIMES = [0, 1, 2, 3, 5, 6]
EMBED_TIMES = [2, 4, 6, 8, 10, 11]


def gather_kernel(n, chunks, *refs):
    count = (len(refs) - 13) // 2
    shards, patches_ref, weight_ref = refs[:count], refs[count], refs[count + 1]
    wholes = refs[count + 2 : -11]
    embedded_ref, parted_ref, product, got, own_sem = refs[-11:-6]
    send_sem, recv_sem, part_send, part_recv, sum_send, sum_recv = refs[-6:]
    here = Place(n)
    greet(n)
    owns = []
    for index in range(count):
        rows = shards[index].shape[0]
        target = wholes[index].at[rows_of(here.me, 1, rows)]
        owns.append(pltpu.make_async_copy(shards[index], target, own_sem.at[index]))
        owns[-1].start()
    for own in owns:
        own.wait()
    steps = here.halves()

    def block(chunk, place):
        index, first, rows, column, columns = chunks[chunk]
        start = here.device(place) * shards[index].shape[0] + first
        return wholes[index].at[pl.ds(pl.multiple_of(start, 16), rows), pl.ds(column, columns)]

    def sending(chunk, step, place):
        blocks, partner = steps[step]
        there = blocks + place
        ref = block(chunk, place)
        return remote(ref, ref, send_sem.at[chunk, there], recv_sem.at[chunk, there], partner)

    def arrive(chunk, step):
        blocks = steps[step][0]

        @pl.loop(blocks, 2 * blocks)
        def _(place):
            landed(block(chunk, place), recv_sem.at[chunk, place])

    def send(chunk, step):
        @pl.loop(0, steps[step][0])
        def _(place):
            sending(chunk, step, place).start()

    rows, width = patches_ref.shape[0], patches_ref.shape[1] // n

    def part_of(place):
        start = pl.multiple_of(here.device(place) * width, 128)
        return patches_ref.at[:, pl.ds(start, width)]

    def parting(place):
        there = here.place_there(place)
        target = parted_ref.at[rows_of(there, 1, rows)]
        return remote(
            part_of(place), target, part_send.at[place], part_recv.at[there], here.device(place)
        )

    half = n // 2
    own_part = pltpu.make_async_copy(part_of(0), parted_ref.at[rows_of(0, 1, rows)], part_recv.at[0])
    own_part.start()

    @pl.loop(1, n)
    def _(hop):
        parting(n - hop).start()

    def multiply(first):
        @pl.loop(first, first + half)
        def _(place):
            landed(parted_ref.at[rows_of(place, 1, rows)], part_recv.at[place])

        @pl.loop(0, half // 4)
        def _(index):
            cut = rows_of(first // 4 + index, 1, 4 * rows)
            product[cut] = dot(parted_ref[cut], weight_ref[...])

    def summing(step):
        blocks, partner = steps[len(steps) - 1 - step]
        cut = pl.ds(blocks * rows, blocks * rows)
        return remote(product.at[cut], got.at[cut], sum_send.at[step], sum_recv.at[step], partner)

    def add(step):
        blocks = steps[len(steps) - 1 - step][0]
        summing(step).wait_recv()
        mine, cut = pl.ds(0, blocks * rows), pl.ds(blocks * rows, blocks * rows)
        product[mine] += got[cut]

    def embed(time):
        if time == EMBED_TIMES[0]:
            multiply(half)
            summing(0).start()
            multiply(0)
        for step in range(len(steps)):
            if time == EMBED_TIMES[step + 1]:
                add(step)
                if step + 1 < len(steps):
                    summing(step + 1).start()

    for time in range(max(len(chunks) + GATHER_TIMES[-1], EMBED_TIMES[-1] + 1)):
        for step in range(len(steps), -1, -1):
            chunk = time - GATHER_TIMES[step]
            if 0 <= chunk < len(chunks):
                if step > 0:
                    arrive(chunk, step - 1)
                if step < len(steps):
                    send(chunk, step)
        embed(time)
    embedded_ref[...] = product[pl.ds(0, rows)]

    @pl.loop(1, n)
    def _(place):
        parting(place).wait_send()

    for step in range(len(steps)):
        summing(step).wait_send()
    for chunk in range(len(chunks)):
        for step in range(len(steps)):

            @pl.loop(0, steps[step][0])
            def _(place):
                sending(chunk, step, place).wait_send()


def gather_weights(n, shards, cuts, patches, patch_weight):
    if n != 32 or any(shard.shape[0] % 16 for shard in shards):
        wholes = [lax.all_gather(shard, "seq", axis=0, tiled=True) for shard in shards]
        parted = patches.reshape(patches.shape[0], n, -1).transpose(1, 0, 2)
        parted = lax.all_to_all(parted, "seq", 0, 0, tiled=True)
        parted = parted.reshape(-1, parted.shape[-1])
        product = dot(parted, patch_weight)
        return wholes + [
            lax.psum_scatter(product, "seq", scatter_dimension=0, tiled=True),
            parted,
        ]
    rows, phases = patches.shape[0], n.bit_length() - 1
    chunks = [
        (index, first, rows, column, min(columns, shard.shape[1] - column))
        for index, (shard, (rows, columns)) in enumerate(zip(shards, cuts))
        for first in range(0, shard.shape[0], rows)
        for column in range(0, shard.shape[1], columns)
    ]
    sems = [pltpu.SemaphoreType.DMA((len(chunks), n))] * 2
    return pl.pallas_call(
        functools.partial(gather_kernel, n, chunks),
        out_shape=[
            jax.ShapeDtypeStruct((n * shard.shape[0], shard.shape[1]), shard.dtype) for shard in shards
        ]
        + [
            jax.ShapeDtypeStruct((rows, D), F32),
            jax.ShapeDtypeStruct((n * rows, patches.shape[1] // n), BF),
        ],
        in_specs=[pl.BlockSpec(memory_space=pltpu.VMEM)] * (len(shards) + 2),
        out_specs=[pl.BlockSpec(memory_space=pltpu.HBM)] * len(shards)
        + [pl.BlockSpec(memory_space=pltpu.VMEM)] * 2,
        scratch_shapes=[
            pltpu.VMEM((n * rows, D), F32),
            pltpu.VMEM((n * rows, D), F32),
            pltpu.SemaphoreType.DMA((len(shards),)),
        ]
        + sems
        + [pltpu.SemaphoreType.DMA((n,))] * 2
        + [pltpu.SemaphoreType.DMA((phases,))] * 2,
        compiler_params=pltpu.CompilerParams(
            collective_id=0, has_side_effects=True, vmem_limit_bytes=32 * 2**20
        ),
        cost_estimate=pl.CostEstimate(flops=0, bytes_accessed=2**25, transcendentals=0),
    )(*shards, patches, patch_weight)


SUM_ROWS, SUM_COLUMNS, SUM_SLOTS = 32, 512, 8
SUM_TIMES = [0, 1, 3, 4, 5, 6, 7]


def columns_of(chunk):
    return pl.ds(pl.multiple_of(chunk * SUM_COLUMNS, SUM_COLUMNS), SUM_COLUMNS)


class Sums:
    def __init__(self, here, sources, out, kept, sent, got, send_sem, recv_sem):
        self.here, self.sources, self.out = here, sources, out
        self.kept, self.sent, self.got = kept, sent, got
        self.send_sem, self.recv_sem = send_sem, recv_sem
        self.steps = here.sum_steps()
        self.chunks = got.shape[0]
        self.times = self.chunks + SUM_TIMES[-1]

    def copy(self, chunk, step):
        first, blocks, partner = self.steps[step]
        cut = pl.ds(first * SUM_ROWS, blocks * SUM_ROWS)
        return remote(
            self.sent.at[chunk % SUM_SLOTS, cut],
            self.got.at[chunk, cut],
            self.send_sem.at[chunk, step],
            self.recv_sem.at[chunk, step],
            partner,
        )

    def sent_all(self, chunk):
        for step in range(len(self.steps)):
            self.copy(chunk, step).wait_send()

    def begin(self, chunk):
        half = self.here.n // 2 * SUM_ROWS
        slot = chunk % SUM_SLOTS

        @pl.when(chunk >= SUM_SLOTS)
        def _():
            self.sent_all(chunk - SUM_SLOTS)

        for first, stop, find, left, right in self.sources:

            @pl.when((chunk >= first) & (chunk < stop))
            def _():
                which, column = find(chunk - first)

                def product(row):
                    return dot(left[which, pl.ds(row, half)], right[:, columns_of(column)])

                self.sent[slot, pl.ds(half, half)] = product(half).astype(BF)
                self.copy(chunk, 0).start()
                self.kept[slot] = product(0)

    def go_on(self, chunk, step):
        slot, (first, blocks, _) = chunk % SUM_SLOTS, self.steps[step - 1]
        self.copy(chunk, step - 1).wait_recv()
        got = self.got[chunk, pl.ds(first * SUM_ROWS, blocks * SUM_ROWS)].astype(F32)
        start = (first - blocks) * SUM_ROWS
        total = self.kept[slot, pl.ds(start, blocks * SUM_ROWS)] + got
        if step == len(self.steps):
            self.out(chunk, total)
            return
        next_first, next_blocks, _ = self.steps[step]
        sent = total[next_first * SUM_ROWS - start :][: next_blocks * SUM_ROWS]
        self.sent[slot, pl.ds(next_first * SUM_ROWS, next_blocks * SUM_ROWS)] = sent.astype(BF)
        self.copy(chunk, step).start()
        if blocks > 1:
            self.kept[slot, pl.ds(0, next_first * SUM_ROWS)] = total[: next_first * SUM_ROWS]

    def at(self, time):
        for step in range(len(self.steps), -1, -1):
            chunk = time - SUM_TIMES[step]

            @pl.when((chunk >= 0) & (chunk < self.chunks))
            def _():
                if step == 0:
                    self.begin(chunk)
                else:
                    self.go_on(chunk, step)

    def run(self, first, stop):
        pl.loop(first, stop)(self.at)

    def end(self):
        @pl.loop(max(0, self.chunks - SUM_SLOTS), self.chunks)
        def _(chunk):
            self.sent_all(chunk)


def turn(order_ref, left_ref, values_ref):
    for index in range(values_ref.shape[0]):
        left_ref[index] = dot_t(order_ref[...], values_ref[index]).astype(BF)


def lefts_scratch(n, lefts):
    return [pltpu.VMEM((lefts.shape[0], n * SUM_ROWS, lefts.shape[1]), BF)]


def sums_scratch(n, chunks):
    rows, phases = n * SUM_ROWS, n // 8 + 2
    return [
        pltpu.VMEM((SUM_SLOTS, rows // 2, SUM_COLUMNS), F32),
        pltpu.VMEM((SUM_SLOTS, rows, SUM_COLUMNS), BF),
        pltpu.VMEM((chunks, rows, SUM_COLUMNS), BF),
        pltpu.SemaphoreType.DMA((chunks, phases)),
        pltpu.SemaphoreType.DMA((chunks, phases)),
    ]


def last_find(chunk):
    return (chunk + 7) // 16 + (chunk + 5) // 16, chunk


def last_kernel(
    n, grad_ref, parted_ref, small_ref, order_ref, values_ref, right_ref, direct_ref, weight_ref,
    d_weight_ref, d_small_ref, d_in_ref, d_out_ref, input_ref,
    back, d_patches, b_send, b_recv, known, small_kept, small_got, g_send, g_recv, t_send, t_recv, left_ref, *scratch
):
    here = Place(n)
    rows = grad_ref.shape[0]
    greet(n)
    known[pl.ds(0, rows)] = grad_ref[...]

    @pl.loop(0, n)
    def _(place):
        device = here.device(place)
        small_kept[rows_of(place, 1, LOG_ROWS)] = small_ref[rows_of(device, 1, LOG_ROWS)]

    left_ref[0] = dot_t(order_ref[...], values_ref[0]).astype(BF)
    spare = d_in_ref.shape[1] % SUM_COLUMNS

    def store(chunk, total):
        @pl.when(chunk < 8)
        def _():
            d_in_ref[:, columns_of(chunk)] = total

        @pl.when(chunk == 8)
        def _():
            d_in_ref[:, pl.ds(8 * SUM_COLUMNS, spare)] = total[:, :spare]

        @pl.when(chunk >= 9)
        def _():
            part = (chunk - 9) // 2
            d_out_ref[rows_of(part, 1, SUM_ROWS), columns_of((chunk - 9) % 2)] = total

    sums = Sums(here, [(0, 13, last_find, left_ref, right_ref)], store, *scratch)
    steps = here.halves()
    copies = []
    for step in range(len(steps)):
        blocks, partner = steps[step]
        source, target = pl.ds(0, blocks * rows), pl.ds(blocks * rows, blocks * rows)
        gather = remote(known.at[source], known.at[target], g_send.at[step], g_recv.at[step], partner)
        gather.start()
        blocks, partner = steps[::-1][step]
        cut, mine = pl.ds(blocks * LOG_ROWS, blocks * LOG_ROWS), pl.ds(0, blocks * LOG_ROWS)
        told = remote(small_kept.at[cut], small_got.at[cut], t_send.at[step], t_recv.at[step], partner)
        told.start()
        copies += [gather, told]
        sums.run(2 * step, 2 * step + 2)
        if step == 0:
            for index in range(1, values_ref.shape[0]):
                left_ref[index] = dot_t(order_ref[...], values_ref[index]).astype(BF)
        gather.wait_recv()
        told.wait_recv()
        small_kept[mine] = small_kept[mine] + small_got[cut]
    width = weight_ref.shape[0]
    back[...] = dot_t(known[...], weight_ref[...]).astype(BF)
    mine = pl.ds(pl.multiple_of(here.me * width, 128), width)

    def returning(place):
        source, target = back.at[rows_of(place, 1, rows)], d_patches.at[:, mine]
        there = here.place_there(place)
        return remote(source, target, b_send.at[place], b_recv.at[there], here.device(place))

    @pl.loop(1, n)
    def _(place):
        returning(place).start()

    pltpu.make_async_copy(back.at[pl.ds(0, rows)], d_patches.at[:, mine], b_recv.at[0]).start()
    sums.run(2 * len(steps), 2 * len(steps) + 1)
    d_weight_ref[...] = lax.dot_general(
        parted_ref[...], known[...], (((0,), (0,)), ((), ())), preferred_element_type=F32
    )
    sums.run(2 * len(steps) + 1, sums.times)

    @pl.loop(0, n)
    def _(place):
        cut = pl.ds(pl.multiple_of(here.device(place) * width, 128), width)
        landed(d_patches.at[:, cut], b_recv.at[place])

    input_ref[...] = (direct_ref[...] + d_patches[...].astype(F32)).astype(BF)

    @pl.loop(1, n)
    def _(place):
        returning(place).wait_send()

    d_small_ref[...] = small_kept[pl.ds(0, LOG_ROWS)]
    for copy in copies:
        copy.wait_send()
    sums.end()


def last_sums(n, grad, parted, small, order, lefts, right, direct, weight, projections):
    rows, width = grad.shape[0], parted.shape[1]
    phases, chunks = n.bit_length() - 1, right.shape[1] // SUM_COLUMNS
    return pl.pallas_call(
        functools.partial(last_kernel, n),
        out_shape=[
            jax.ShapeDtypeStruct((width, D), F32),
            jax.ShapeDtypeStruct((LOG_ROWS, 128), F32),
            jax.ShapeDtypeStruct((SUM_ROWS, projections), F32),
            jax.ShapeDtypeStruct((2 * SUM_ROWS, D), F32),
            jax.ShapeDtypeStruct(direct.shape, BF),
        ],
        in_specs=[pl.BlockSpec(memory_space=pltpu.VMEM)] * 8,
        out_specs=[pl.BlockSpec(memory_space=pltpu.VMEM)] * 5,
        scratch_shapes=[
            pltpu.VMEM((n * rows, width), BF),
            pltpu.VMEM(direct.shape, BF),
            pltpu.SemaphoreType.DMA((n,)),
            pltpu.SemaphoreType.DMA((n,)),
            pltpu.VMEM((n * rows, D), BF),
            pltpu.VMEM(small.shape, F32),
            pltpu.VMEM(small.shape, F32),
        ]
        + [pltpu.SemaphoreType.DMA((phases,))] * 4
        + lefts_scratch(n, lefts)
        + sums_scratch(n, chunks),
        compiler_params=pltpu.CompilerParams(
            collective_id=1, has_side_effects=True, vmem_limit_bytes=62 * 2**20
        ),
        cost_estimate=pl.CostEstimate(flops=2**32, bytes_accessed=2**24, transcendentals=0),
    )(grad, parted, small, order, lefts, right, direct, weight)


LOG_ROWS = 8


class Exchange:
    def __init__(self, n, reverse, states, logs_in, out, spread, logs, summed, *sems):
        self.n, self.reverse = n, reverse
        self.me = lax.axis_index("seq")
        self.states, self.logs_in, self.out = states, logs_in, out
        self.spread, self.logs, self.summed = spread, logs, summed
        self.sems = sems
        self.rows = states.shape[0] // n

    def spreading(self, other):
        send, recv = self.sems[:2]
        source = self.states.at[rows_of(other, 1, self.rows)]
        target = self.spread.at[rows_of(self.me, 1, self.rows)]
        return remote(source, target, send.at[other], recv.at[self.me], other)

    def telling(self, other):
        send, recv = self.sems[2:4]
        target = self.logs.at[rows_of(self.me, 1, LOG_ROWS)]
        return remote(self.logs_in, target, send.at[other], recv.at[self.me], other)

    def returning(self, other):
        send, recv = self.sems[4:6]
        source = self.summed.at[rows_of(other, 1, self.rows)]
        target = self.out.at[rows_of(self.me, 1, self.rows)]
        return remote(source, target, send.at[other], recv.at[self.me], other)

    def tell(self):
        @pl.loop(1, self.n)
        def _(hop):
            self.telling(lax.rem(self.me + hop, self.n)).start()

        target = self.logs.at[rows_of(self.me, 1, LOG_ROWS)]
        pltpu.make_async_copy(self.logs_in, target, self.sems[3].at[self.me]).start()

    def start(self):
        @pl.loop(1, self.n)
        def _(hop):
            self.spreading(lax.rem(self.me + hop, self.n)).start()

        mine = rows_of(self.me, 1, self.rows)
        recv = self.sems[1].at[self.me]
        pltpu.make_async_copy(self.states.at[mine], self.spread.at[mine], recv).start()

    def join(self):
        n, rows, summed, spread = self.n, self.rows, self.summed, self.spread

        @pl.loop(0, n)
        def _(other):
            landed(spread.at[rows_of(other, 1, rows)], self.sems[1].at[other])
            landed(self.logs.at[rows_of(other, 1, LOG_ROWS)], self.sems[3].at[other])

        head = self.me * MHEADS // n
        lane = lax.broadcasted_iota(jnp.int32, (LOG_ROWS, 128), 1)
        row = lax.broadcasted_iota(jnp.int32, (LOG_ROWS, 128), 0)

        def step(count, total):
            place = n - 1 - count if self.reverse else count
            cut = rows_of(place, 1, rows)
            summed[cut] = total.astype(BF)
            told = self.logs[rows_of(place, 1, LOG_ROWS)]
            log = jnp.sum(jnp.where((lane == head) & (row == 0), told, 0.0), keepdims=True)
            flag = jnp.sum(jnp.where((lane == MHEADS) & (row == 0), told, 0.0), keepdims=True)
            decay = jnp.where(flag > 0.0, 0.0, jnp.exp(log))
            return decay * total + spread[cut].astype(F32)

        lax.fori_loop(0, n, step, jnp.zeros((rows, NSTATE), F32))

        @pl.loop(1, n)
        def _(hop):
            self.returning(lax.rem(self.me + hop, n)).start()

        mine = rows_of(self.me, 1, rows)
        recv = self.sems[5].at[self.me]
        pltpu.make_async_copy(summed.at[mine], self.out.at[mine], recv).start()

    def arrive(self):
        @pl.loop(0, self.n)
        def _(other):
            landed(self.out.at[rows_of(other, 1, self.rows)], self.sems[5].at[other])

    def end(self):
        @pl.loop(1, self.n)
        def _(hop):
            other = lax.rem(self.me + hop, self.n)
            self.spreading(other).wait_send()
            self.telling(other).wait_send()
            self.returning(other).wait_send()


def exchange_scratch(n):
    total = MHEADS * MHEAD_DIM
    return [
        pltpu.VMEM((total, NSTATE), BF),
        pltpu.VMEM((n * LOG_ROWS, 128), F32),
        pltpu.VMEM((total, NSTATE), BF),
    ] + [pltpu.SemaphoreType.DMA((n,))] * 6


def states_kernel(n, reverse, states_ref, logs_ref, out_ref, *scratch):
    greet(n)
    exchange = Exchange(n, reverse, states_ref, logs_ref, out_ref, *scratch)
    exchange.tell()
    exchange.start()
    exchange.join()
    exchange.arrive()
    exchange.end()


def told_logs(logs):
    return jnp.zeros((LOG_ROWS, 128), F32).at[0, : logs.shape[0]].set(logs)


def pass_states(n, states, logs, reverse):
    total = MHEADS * MHEAD_DIM
    return pl.pallas_call(
        functools.partial(states_kernel, n, reverse),
        out_shape=jax.ShapeDtypeStruct((total, NSTATE), BF),
        in_specs=[pl.BlockSpec(memory_space=pltpu.VMEM)] * 2,
        out_specs=pl.BlockSpec(memory_space=pltpu.VMEM),
        scratch_shapes=exchange_scratch(n),
        compiler_params=pltpu.CompilerParams(
            collective_id=3 if reverse else 2, has_side_effects=True, vmem_limit_bytes=16 * 2**20
        ),
        cost_estimate=pl.CostEstimate(flops=2**22, bytes_accessed=2**21, transcendentals=0),
    )(states.reshape(total, NSTATE).astype(BF), told_logs(logs))


NN, NT, TN = ((1,), (0,)), ((1,), (1,)), ((0,), (0,))


def in_parts(value, count):
    if value.dtype == BF:
        return [value]
    parts = []
    for _ in range(count):
        parts.append(value.astype(BF))
        value = value - parts[-1].astype(F32)
    return parts


def dot_fine(left, right, dims, count=2):
    total = None
    for i, a in enumerate(in_parts(left, count)):
        for j, b in enumerate(in_parts(right, count)):
            if i + j < count:
                found = lax.dot_general(a, b, (dims, ((), ())), preferred_element_type=F32)
                total = found if total is None else total + found
    return total


def mixer_back_kernel(
    n, logs_ref, order_ref, mixed_ref, normed_ref, out_right_ref, qkv_right_ref, hidden_ref, slots_ref,
    dy_ref, x_ref, keys_ref, queries_ref, state_ref, steps_ref, marks_ref, head_ref,
    dx_ref, d_dt_ref, d_head_ref, d_out_ref, d_qkv_ref, unpatch_ref, dkeys_ref, dqueries_ref,
    scores, d_scores, d_step, d_cum, d_turned, grads, back, left_ref, hidden_left, *scratch
):
    rows, width = x_ref.shape[0], 2 * MHEAD_DIM
    greet(n)
    exchange = Exchange(n, True, grads, logs_ref, back, *scratch[:9])

    def store(chunk, total):
        for (first, stop, *_), target in zip(sources, (unpatch_ref, d_out_ref, d_qkv_ref)):

            @pl.when((chunk >= first) & (chunk < stop))
            def _():
                target[:, columns_of(chunk - first)] = total

    def find(which):
        return lambda chunk: (which, chunk)

    sources = [
        (0, 16, find(0), hidden_left, slots_ref),
        (16, 18, find(0), left_ref, out_right_ref),
        (18, 24, find(1), left_ref, qkv_right_ref),
    ]
    sums = Sums(Place(n), sources, store, *scratch[9:])
    exchange.tell()
    turn(order_ref, hidden_left, hidden_ref)

    head_lane = lax.broadcasted_iota(jnp.int32, (1, MHEADS), 1)
    lanes = lax.broadcasted_iota(jnp.int32, (1, width), 1)
    halves = [lanes < MHEAD_DIM, lanes >= MHEAD_DIM]
    step, cum = steps_ref[0, :rows, :MHEADS], steps_ref[1, :rows, :MHEADS]
    turned_step, turned_cum = steps_ref.at[3], steps_ref.at[4]
    reach = marks_ref[0][:, :rows]
    from_before, to_after = marks_ref[1][:, 0:1], marks_ref[1][:, 1:2]
    last_cum = cum[rows - 1 : rows]
    to_end = jnp.exp(last_cum - cum) * to_after

    def column(values, head):
        return jnp.sum(jnp.where(head_lane == head, values, 0.0), axis=1, keepdims=True)

    def at_head(head, values):
        return jnp.where(head_lane == head, values, 0.0)

    def of_pair(pair, values):
        return jnp.where(halves[0], column(values, 2 * pair), column(values, 2 * pair + 1))

    def columns(pair):
        return pl.ds(pl.multiple_of(pair * width, width), width)

    scores[...] = dot_fine(queries_ref[...], keys_ref[...], NT)
    d_scores[...] = jnp.zeros_like(d_scores)
    d_step[...] = jnp.zeros_like(d_step)
    d_cum[...] = jnp.zeros_like(d_cum)
    d_turned[...] = jnp.zeros_like(d_turned)
    dqueries_ref[...] = jnp.zeros_like(dqueries_ref)
    d_head_ref[...] = jnp.zeros_like(d_head_ref)

    @pl.loop(0, MHEADS // 2)
    def _(pair):
        sums.at(pair)
        x, dy, state = x_ref[:, columns(pair)], dy_ref[:, columns(pair)], state_ref[columns(pair)]
        dx = of_pair(pair, head_ref[2:3]) * dy
        inflow = jnp.exp(of_pair(pair, cum)) * from_before
        dy_in = dy * inflow
        carried = dy_in * dot_fine(queries_ref[...], state, NT)
        dqueries_ref[...] += dot_fine(dy_in, state, NN)
        grads[columns(pair)] = dot_fine(dy_in, queries_ref[...], TN).astype(BF)
        for which, half in enumerate(halves):
            head = 2 * pair + which
            mine = pl.ds(head, 1)
            gap = column(cum, head) - turned_cum[mine, :rows]
            decay = jnp.exp(jnp.where(reach > 0.0, gap, 0.0)) * reach
            weighted = scores[...] * decay
            step_row = turned_step[mine, :rows]
            mixing = weighted * step_row
            d_mixing = dot_fine(dy, jnp.where(half, x, 0.0), NT)
            dx += dot_fine(mixing, jnp.where(half, dy, 0.0), TN)
            d_scores[...] += d_mixing * decay * step_row
            d_gap = d_mixing * mixing
            d_turned[0, mine, :rows] = jnp.sum(d_mixing * weighted, axis=0, keepdims=True)
            d_turned[1, mine, :rows] = -jnp.sum(d_gap, axis=0, keepdims=True)
            moved = jnp.sum(d_gap, axis=1, keepdims=True)
            moved += jnp.sum(jnp.where(half, carried, 0.0), axis=1, keepdims=True)
            d_cum[...] += at_head(head, moved)
            skipped = jnp.sum(jnp.where(half, dy * x, 0.0), keepdims=True)
            d_head_ref[2:3] += at_head(head, skipped)
        dx_ref[:, columns(pair)] = dx

    dkeys_ref[...] = dot_fine(d_scores[...], queries_ref[...], TN)
    dqueries_ref[...] += dot_fine(d_scores[...], keys_ref[...], NN)
    exchange.start()
    left_ref[0] = dot_t(order_ref[...], mixed_ref[...]).astype(BF)
    left_ref[1] = dot_t(order_ref[...], normed_ref[...]).astype(BF)
    sums.run(16, 20)
    exchange.join()
    sums.run(20, 24)
    exchange.arrive()

    @pl.loop(0, MHEADS // 2)
    def _(pair):
        @pl.when(pair < 7)
        def _():
            sums.at(24 + pair)

        x, state, grad = x_ref[:, columns(pair)], state_ref[columns(pair)], back[columns(pair)]
        weight = of_pair(pair, to_end * step)
        d_weighted = dot_fine(keys_ref[...], grad, NT)
        dkeys_ref[...] += dot_fine(x * weight, grad, NN)
        dx_ref[:, columns(pair)] += weight * d_weighted
        kept = grad.astype(F32) * state.astype(F32)
        for which, half in enumerate(halves):
            head = 2 * pair + which
            d_weight = jnp.sum(jnp.where(half, x * d_weighted, 0.0), axis=1, keepdims=True)
            d_step[...] += at_head(head, d_weight * column(to_end, head))
            moved = d_weight * column(to_end * step, head)
            d_cum[...] -= at_head(head, moved)
            d_decay = jnp.sum(kept[which * MHEAD_DIM : (which + 1) * MHEAD_DIM], keepdims=True)
            ended = jnp.sum(moved, keepdims=True)
            ended += d_decay * jnp.exp(column(last_cum, head)) * from_before[rows - 1 : rows]
            d_cum[rows - 1 : rows] += at_head(head, ended)

    d_steps = d_step[...] + d_turned[0].T[:rows, :MHEADS]
    d_cums = d_cum[...] + d_turned[1].T[:rows, :MHEADS]
    later = lax.broadcasted_iota(jnp.int32, (rows, rows), 0) <= lax.broadcasted_iota(
        jnp.int32, (rows, rows), 1
    )
    d_logs = dot_fine(later.astype(BF), d_cums, NN, 3)
    rate = jnp.exp(head_ref[1:2])
    d_raw = (d_steps - rate * d_logs) * steps_ref[2, :rows, :MHEADS]
    d_dt_ref[...] = d_raw
    d_head_ref[0:1] = jnp.sum(d_raw, axis=0, keepdims=True)
    d_head_ref[1:2] = -rate * jnp.sum(step * d_logs, axis=0, keepdims=True)
    dx_ref[:, pl.ds(DI, NSTATE)] = dkeys_ref[...]
    dx_ref[:, pl.ds(DI + NSTATE, NSTATE)] = dqueries_ref[...]
    sums.run(31, sums.times)
    sums.end()
    exchange.end()


def mixer_tables(dt_raw, head_params, starts):
    rows = dt_raw.shape[0]
    step = jax.nn.softplus(dt_raw + head_params[0])
    cum = jnp.cumsum(-step * jnp.exp(head_params[1]), axis=0)
    segment = jnp.cumsum(starts, axis=0, dtype=jnp.int32)
    slope = jax.nn.sigmoid(dt_raw + head_params[0])
    square = [jnp.pad(v, ((0, 128 - v.shape[0]), (0, 128 - v.shape[1]))) for v in (step.T, cum.T)]
    tall = [jnp.pad(v, ((0, 128 - rows), (0, 128 - MHEADS))) for v in (step, cum, slope)]
    position = jnp.arange(rows)
    reach = (position[:, None] >= position[None, :]) & (segment[:, None] == segment[None, :])
    ends = jnp.stack([segment == 0, segment == segment[-1]], axis=1)
    marks = [jnp.pad(v.astype(F32), ((0, 0), (0, 128 - v.shape[1]))) for v in (reach, ends)]
    return jnp.stack(tall + square), jnp.stack(marks)


def mixer_back(told, order, values, rights, hidden, slots, dy, conv_out, state_in, steps, marks, head_params):
    n, rows = lax.axis_size("seq"), conv_out.shape[0]
    x, keys, queries = jnp.split(conv_out, [DI, DI + NSTATE], axis=1)
    total = MHEADS * MHEAD_DIM
    wide = sum(right.shape[1] for right in rights)
    return pl.pallas_call(
        functools.partial(mixer_back_kernel, n),
        out_shape=[
            jax.ShapeDtypeStruct((rows, CONV_CH), F32),
            jax.ShapeDtypeStruct((rows, MHEADS), F32),
            jax.ShapeDtypeStruct((8, MHEADS), F32),
        ]
        + [jax.ShapeDtypeStruct((SUM_ROWS, right.shape[1]), F32) for right in rights]
        + [jax.ShapeDtypeStruct((SUM_ROWS, slots.shape[1]), F32)],
        in_specs=[pl.BlockSpec(memory_space=pltpu.VMEM)] * 16,
        out_specs=[pl.BlockSpec(memory_space=pltpu.VMEM)] * 6,
        scratch_shapes=[
            pltpu.VMEM((rows, NSTATE), F32),
            pltpu.VMEM((rows, NSTATE), F32),
            pltpu.VMEM((rows, rows), F32),
            pltpu.VMEM((rows, rows), F32),
            pltpu.VMEM((rows, MHEADS), F32),
            pltpu.VMEM((rows, MHEADS), F32),
            pltpu.VMEM((2, 128, 128), F32),
            pltpu.VMEM((total, NSTATE), BF),
            pltpu.VMEM((total, NSTATE), BF),
        ]
        + [pltpu.VMEM((2, n * SUM_ROWS, values[0].shape[0]), BF)]
        + lefts_scratch(n, hidden)
        + exchange_scratch(n)
        + sums_scratch(n, 24),
        compiler_params=pltpu.CompilerParams(
            collective_id=3, has_side_effects=True, vmem_limit_bytes=62 * 2**20
        ),
        cost_estimate=pl.CostEstimate(flops=2**32, bytes_accessed=2**24, transcendentals=2**20),
    )(
        told, order, *values, *rights, hidden, slots, dy, x, keys, queries,
        state_in, steps, marks, head_params,
    )


FF_TILE = D


def feed_forward_kernel(normed_ref, gate_w_ref, up_w_ref, gate_ref, up_ref, hid_ref):
    gate, up = dot(normed_ref[...], whole_of(gate_w_ref)), dot(normed_ref[...], whole_of(up_w_ref))
    gate_ref[...], up_ref[...] = gate.astype(BF), up.astype(BF)
    hid_ref[...] = (silu(gate) * up).astype(BF)


def feed_forward_blocks(n):
    tiles, first = FF // FF_TILE, PATCH + 4
    return [
        flat_block(n, D // n, lambda i: first + i),
        flat_block(n, D // n, lambda i: first + tiles + i),
        pl.BlockSpec((FF_TILE, D), lambda i: (i, 0)),
    ]


def feed_forward(normed, flat):
    rows = normed.shape[0]
    tile = pl.BlockSpec((rows, FF_TILE), lambda i: (0, i))
    return pl.pallas_call(
        feed_forward_kernel,
        grid=(FF // FF_TILE,),
        out_shape=[jax.ShapeDtypeStruct((rows, FF), BF)] * 3,
        in_specs=[pl.BlockSpec((rows, D), lambda i: (0, 0)), *feed_forward_blocks(flat.shape[0])[:2]],
        out_specs=[tile, tile, tile],
        compiler_params=pltpu.CompilerParams(vmem_limit_bytes=56 * 2**20),
        cost_estimate=pl.CostEstimate(
            flops=4 * rows * D * FF, bytes_accessed=2**25, transcendentals=rows * FF
        ),
    )(normed, flat, flat)


def feed_forward_back_kernel(
    grad_ref, stream_ref, gain_ref, gate_ref, up_ref, hid_ref, gate_w_ref, up_w_ref, down_ref,
    out_ref, both_ref, d_stream_ref, d_low_ref, d_gain_ref, layer, total,
):
    step = pl.program_id(0)
    added = dot(hid_ref[...], down_ref[...])

    @pl.when(step == 0)
    def _():
        layer[...] = stream_ref[...] + added

    @pl.when(step > 0)
    def _():
        layer[...] += added

    d_hid = dot_t(grad_ref[...], down_ref[...])
    gate, up = gate_ref[...].astype(F32), up_ref[...].astype(F32)
    s = jax.nn.sigmoid(gate)
    d_gate = (d_hid * up * (s * (1.0 + gate * (1.0 - s)))).astype(BF)
    d_up = (d_hid * (gate * s)).astype(BF)
    both_ref[0], both_ref[1] = d_gate, d_up
    found = dot_t(d_gate, whole_of(gate_w_ref)) + dot_t(d_up, whole_of(up_w_ref))

    @pl.when(step == 0)
    def _():
        total[...] = found

    @pl.when(step > 0)
    def _():
        total[...] += found

    @pl.when(step == pl.num_programs(0) - 1)
    def _():
        out_ref[...] = layer[...].astype(BF)
        stream, d_normed = stream_ref[...], total[...]
        r = lax.rsqrt(jnp.mean(stream * stream, axis=-1, keepdims=True) + EPS)
        scaled = gain_ref[...] * d_normed
        inner = jnp.mean(stream * scaled, axis=-1, keepdims=True)
        d_stream = grad_ref[...].astype(F32) + r * scaled - stream * (r * r * r) * inner
        d_stream_ref[...] = d_stream
        d_low_ref[...] = d_stream.astype(BF)
        d_gain_ref[...] = jnp.sum(stream * r * d_normed, axis=0, keepdims=True)


def feed_forward_back(grad, stream, gain, gate, up, hid, flat, down):
    rows, tiles = stream.shape[0], FF // FF_TILE
    wide = pl.BlockSpec((rows, D), lambda i: (0, 0))
    tile = pl.BlockSpec((rows, FF_TILE), lambda i: (0, i))
    narrow = pl.BlockSpec((1, D), lambda i: (0, 0))
    out, both, d_stream, d_low, d_gain = pl.pallas_call(
        feed_forward_back_kernel,
        grid=(tiles,),
        out_shape=[
            jax.ShapeDtypeStruct((rows, D), BF),
            jax.ShapeDtypeStruct((2, rows, FF), BF),
            jax.ShapeDtypeStruct((rows, D), F32),
            jax.ShapeDtypeStruct((rows, D), BF),
            jax.ShapeDtypeStruct((1, D), F32),
        ],
        in_specs=[
            wide,
            wide,
            narrow,
            tile,
            tile,
            tile,
            *feed_forward_blocks(flat.shape[0]),
        ],
        out_specs=[wide, pl.BlockSpec((2, rows, FF_TILE), lambda i: (0, 0, i)), wide, wide, narrow],
        scratch_shapes=[pltpu.VMEM((rows, D), F32)] * 2,
        compiler_params=pltpu.CompilerParams(vmem_limit_bytes=60 * 2**20),
        cost_estimate=pl.CostEstimate(
            flops=8 * rows * D * FF, bytes_accessed=2**25, transcendentals=rows * FF
        ),
    )(grad, stream, gain[None], gate, up, hid, flat, flat, down)
    return out, both, d_stream, d_low, d_gain[0]


ATTN_ROWS, BACK_ROWS = 128, 256


def tile_mask():
    row = lax.broadcasted_iota(jnp.int32, (ATTN_ROWS, 2 * ATTN_ROWS), 0)
    column = lax.broadcasted_iota(jnp.int32, (ATTN_ROWS, 2 * ATTN_ROWS), 1) % ATTN_ROWS
    return (row // PATCH == column // PATCH) & (row >= column)


def first_head():
    return lax.broadcasted_iota(jnp.int32, (1, 2 * AHEAD_DIM), 1) < AHEAD_DIM


def one_below_other(pair):
    lanes, zeros = first_head(), jnp.zeros_like(pair)
    return jnp.concatenate([jnp.where(lanes, pair, zeros), jnp.where(lanes, zeros, pair)], axis=0)


def by_head(values, reduce):
    first = reduce(values[:, :ATTN_ROWS], axis=-1, keepdims=True)
    second = reduce(values[:, ATTN_ROWS:], axis=-1, keepdims=True)
    shape = (values.shape[0], ATTN_ROWS)
    return jnp.concatenate(
        [jnp.broadcast_to(first, shape), jnp.broadcast_to(second, shape)], axis=1
    )


def pair_probs(queries, key_rows, mask):
    scores = jnp.where(mask, dot_t(queries, key_rows) * AHEAD_DIM ** (-0.5), -1e30)
    raised = jnp.exp(scores - by_head(scores, jnp.max))
    return raised / by_head(raised, jnp.sum)


def attention_kernel(triple_ref, out_ref):
    mask = tile_mask()
    width = 2 * AHEAD_DIM
    for pair in range(AHEADS // 2):
        queries, key_rows, value_rows = [
            triple_ref[:, part * D + pair * width : part * D + (pair + 1) * width] for part in range(3)
        ]
        probs = pair_probs(queries, one_below_other(key_rows), mask)
        mixed = dot(probs.astype(BF), one_below_other(value_rows))
        out_ref[:, pair * width : (pair + 1) * width] = mixed.astype(BF)


def attention(triple):
    rows = triple.shape[0]
    return pl.pallas_call(
        attention_kernel,
        grid=(rows // ATTN_ROWS,),
        out_shape=jax.ShapeDtypeStruct((rows, D), BF),
        in_specs=[pl.BlockSpec((ATTN_ROWS, 3 * D), lambda i: (i, 0))],
        out_specs=pl.BlockSpec((ATTN_ROWS, D), lambda i: (i, 0)),
    )(triple)


def attention_back_kernel(
    triple_ref, low_ref, d_stream_ref, stream_ref, gain_ref, out_w_ref, q_ref, k_ref, v_ref,
    out_ref, d_out_ref, d_gain_ref,
):
    mask = tile_mask()
    width = 2 * AHEAD_DIM
    scale = AHEAD_DIM ** (-0.5)

    def of_keys(left, right):
        found = lax.dot_general(left, right, (((0,), (0,)), ((), ())), preferred_element_type=F32)
        return jnp.where(first_head(), found[:ATTN_ROWS], found[ATTN_ROWS:])

    grads = dot_t(low_ref[...], whole_of(out_w_ref)).astype(BF)
    for first in range(0, BACK_ROWS, ATTN_ROWS):
        rows = slice(first, first + ATTN_ROWS)
        for pair in range(AHEADS // 2):
            lo, hi = pair * width, (pair + 1) * width
            queries, key_rows, value_rows = [
                triple_ref[rows, part * D + lo : part * D + hi] for part in range(3)
            ]
            grad = grads[rows, lo:hi]
            key_rows = one_below_other(key_rows)
            probs = pair_probs(queries, key_rows, mask)
            d_probs = dot_t(grad, one_below_other(value_rows))
            d_scores = (probs * (d_probs - by_head(probs * d_probs, jnp.sum))).astype(BF)
            out_ref[rows, lo:hi] = (scale * dot(d_scores, key_rows)).astype(BF)
            out_ref[rows, D + lo : D + hi] = (scale * of_keys(d_scores, queries)).astype(BF)
            d_values = of_keys(probs.astype(BF), grad)
            out_ref[rows, 2 * D + lo : 2 * D + hi] = d_values.astype(BF)

    d_normed = None
    for part, ref in enumerate((q_ref, k_ref, v_ref)):
        found = dot_t(out_ref[:, part * D : (part + 1) * D], whole_of(ref))
        d_normed = found if part == 0 else d_normed + found
    stream = stream_ref[...]
    r = lax.rsqrt(jnp.mean(stream * stream, axis=-1, keepdims=True) + EPS)
    scaled = gain_ref[...] * d_normed
    inner = jnp.mean(stream * scaled, axis=-1, keepdims=True)
    d_out_ref[...] = d_stream_ref[...] + r * scaled - stream * (r * r * r) * inner
    gained = jnp.sum(stream * r * d_normed, axis=0, keepdims=True)

    @pl.when(pl.program_id(0) == 0)
    def _():
        d_gain_ref[...] = gained

    @pl.when(pl.program_id(0) > 0)
    def _():
        d_gain_ref[...] += gained


def attention_back(triple, low, d_stream, stream, gain, flat):
    rows, n = triple.shape[0], flat.shape[0]
    wide = pl.BlockSpec((BACK_ROWS, 3 * D), lambda i: (i, 0))
    tile = pl.BlockSpec((BACK_ROWS, D), lambda i: (i, 0))
    narrow = pl.BlockSpec((1, D), lambda i: (0, 0))

    def block(place):
        return flat_block(n, D // n, lambda i: place)

    d_triple, d_out, d_gain = pl.pallas_call(
        attention_back_kernel,
        grid=(rows // BACK_ROWS,),
        out_shape=[
            jax.ShapeDtypeStruct((rows, 3 * D), BF),
            jax.ShapeDtypeStruct((rows, D), F32),
            jax.ShapeDtypeStruct((1, D), F32),
        ],
        in_specs=[wide, tile, tile, tile, narrow]
        + [block(PATCH + 3), block(PATCH), block(PATCH + 1), block(PATCH + 2)],
        out_specs=[wide, tile, narrow],
        compiler_params=pltpu.CompilerParams(vmem_limit_bytes=56 * 2**20),
        cost_estimate=pl.CostEstimate(
            flops=8 * rows * D * D, bytes_accessed=2**24, transcendentals=0
        ),
    )(triple, low, d_stream, stream, gain[None], flat, flat, flat, flat)
    return d_triple, d_out, d_gain[0]


def local(
    byte_acts,
    resets,
    out_grad,
    patch_weight,
    patch_gain,
    mixer_in,
    conv_weight,
    conv_bias,
    head_params,
    mixer_gain,
    mixer_out,
    unpatch_weight,
    attn_gain,
    qkv_weight,
    attn_out,
    ffn_gain,
    gate_up,
    down_weight,
):
    n = lax.axis_size("seq")
    me = lax.axis_index("seq")
    ring = Ring(n)

    def passed_along(block, distance):
        route = [(i - distance, i) for i in range(n) if 0 <= i - distance < n]
        return lax.ppermute(block, "seq", route)

    live = Live()
    order = ring.order()

    byte_wide = byte_acts.astype(F32)
    patches = byte_acts.reshape(-1, PATCH * D)
    patch_rows = patches.shape[0]
    early = gather_flat(n, [unpatch_weight, qkv_weight, attn_out, gate_up])
    late = lax.all_gather(down_weight, "seq", axis=0, tiled=True)
    small = [patch_gain, conv_weight.reshape(-1), conv_bias, mixer_gain, attn_gain, ffn_gain]
    cuts = list(np.cumsum([piece.shape[0] for piece in small]))
    small_shard = jnp.concatenate(small)
    small_shard = jnp.pad(small_shard, (0, -small_shard.shape[0] % 2048)).reshape(-1, 128)
    live.mixer_in, live.mixer_out, small_all, live.embedded, live.parted = gather_weights(
        n,
        [
            jnp.pad(mixer_in, ((0, 0), (0, -mixer_in.shape[1] % 128))),
            mixer_out,
            small_shard,
        ],
        [(16, 2304), (32, D), (16, 128)],
        patches,
        patch_weight,
    )
    small_all = small_all.reshape(n, -1)[:, : cuts[-1]].astype(F32)
    parts = jnp.split(small_all, cuts[:-1], axis=1)
    live.patch_gain = parts[0].reshape(-1)
    live.conv_weight = parts[1].reshape(n, CONV, -1).transpose(1, 0, 2).reshape(CONV, CONV_CH)
    live.conv_bias, live.mixer_gain, live.attn_gain, live.ffn_gain = [
        piece.reshape(-1) for piece in parts[2:]
    ]
    live.normed = rms_scale(live.embedded, live.patch_gain).astype(BF)
    projected = dot(live.normed, live.mixer_in)
    live.gate_z = projected[:, :DI]
    conv_in = projected[:, DI : DI + CONV_CH].astype(BF).astype(F32)
    dt_raw = projected[:, DI + CONV_CH : DI + CONV_CH + MHEADS]
    logs = jnp.sum(-jax.nn.softplus(dt_raw + head_params[0]) * jnp.exp(head_params[1]), axis=0)
    flag = jnp.max(resets).astype(F32)
    live.logs = jnp.concatenate([logs, flag[None]])
    not_reset = 1.0 - resets.astype(F32)
    keep_tail = jnp.concatenate(
        [jnp.cumprod(not_reset[patch_rows - CONV + 2 :][::-1])[::-1], jnp.ones((1,), F32)]
    )
    tail_sent = (conv_in[patch_rows - CONV + 1 :] * keep_tail[:, None]).astype(BF)
    halo_rows = passed_along(tail_sent, 1)
    flags_ext = jnp.concatenate([jnp.zeros((CONV - 1,), jnp.int32), resets])
    validity = tap_masks(flags_ext, patch_rows)
    conv_ext = jnp.concatenate([halo_rows.astype(F32), conv_in])
    conv_out, conv_back = jax.vjp(
        functools.partial(conv_apply, validity=validity, row_count=patch_rows),
        conv_ext,
        live.conv_weight,
        live.conv_bias,
    )
    state_parts, state_back = jax.vjp(
        functools.partial(block_state, starts=resets), conv_out, dt_raw, head_params
    )
    local_state, decay_total = state_parts
    live.state_in = pass_states(n, local_state, live.logs, False)
    live.fence()

    mixer_y, output_back = jax.vjp(
        functools.partial(block_output, starts=resets),
        conv_out,
        dt_raw,
        head_params,
        live.state_in.astype(F32).reshape(MHEADS, MHEAD_DIM, NSTATE),
    )
    gate_act = silu(live.gate_z)
    gated = mixer_y * gate_act
    live.gated_norm = rms_scale(gated, live.mixer_gain).astype(BF)
    branch = dot(live.gated_norm, live.mixer_out)
    live.hidden = (live.embedded + branch).astype(BF)
    live.early = early
    slots = flat_dot(live.hidden, live.early, 0, PATCH, F32)
    live.stream0 = byte_wide + slots.reshape(-1, D)
    live.normed0 = rms_scale(live.stream0, live.attn_gain).astype(BF)
    live.fence()

    rows = byte_wide.shape[0]
    live.triple = flat_dot(live.normed0, live.early, PATCH, 3, BF)
    live.mixed = attention(live.triple)
    live.stream1 = live.stream0 + flat_dot(live.mixed, live.early, PATCH + 3, 1, F32)
    live.normed1 = rms_scale(live.stream1, live.ffn_gain).astype(BF)
    live.gate, live.up, live.hid = feed_forward(live.normed1, live.early)
    small_slice = n == 32
    if small_slice:
        live.flat = down_grad(n, live.hid, out_grad)

    def lefts_of(*values):
        parts = []
        for value in values:
            cut = value.reshape(value.shape[0], n, -1, SUM_ROWS).transpose(2, 0, 1, 3)
            parts.append(cut.reshape(-1, value.shape[0], n * SUM_ROWS))
        return jnp.concatenate(parts, axis=0)

    if small_slice:
        place = jnp.arange(n * SUM_ROWS)
        source = jnp.repeat(order * SUM_ROWS, SUM_ROWS) + place % SUM_ROWS
        live.order = (place[None, :] == source[:, None]).astype(BF)
        live.last_lefts = lefts_of(live.normed, live.gated_norm)
        live.steps, live.marks = mixer_tables(dt_raw, head_params, resets)
        live.told = told_logs(live.logs)
    live.fence()

    layer_out, d_both, d_stream1, d_stream1_low, g_ffn_gain = feed_forward_back(
        out_grad, live.stream1, live.ffn_gain, live.gate, live.up, live.hid, live.early, late
    )
    if small_slice:
        block = down_weight.shape[0]
        flat = gate_up_grad(live.normed1, d_both, live.flat)
        found = lax.psum_scatter(flat, "seq", scatter_dimension=0, tiled=True)[0].astype(F32)
        g_down = found[:block]
        g_gate_up = found[block:].reshape(-1, SUM_ROWS, D).transpose(1, 0, 2)
        g_gate_up = g_gate_up.reshape(SUM_ROWS, -1)
    else:
        g_down = summed_grad(live.hid, out_grad)
        g_gate_up = summed_grad(live.normed1, jnp.concatenate([d_both[0], d_both[1]], axis=1))
    d_triple, d_stream0, g_attn_gain = attention_back(
        live.triple, d_stream1_low, d_stream1, live.stream0, live.attn_gain, live.early
    )
    live.d_stream0 = d_stream0.reshape(patch_rows, PATCH * D)

    d_slots = live.d_stream0.astype(BF)
    d_hidden = flat_dot_t(d_slots, live.early, 0, PATCH)
    d_branch = d_hidden.astype(BF)
    d_gated, g_mixer_gain = rms_back(gated, live.mixer_gain, dot_t(d_branch, live.mixer_out))
    d_gate_z = d_gated * mixer_y * silu_slope(live.gate_z)
    if small_slice:
        d_conv_out, d_dt, g_head, g_attn_out, g_qkv, g_unpatch = mixer_back(
            live.told,
            live.order,
            [live.mixed, live.normed0],
            [d_stream1_low, d_triple],
            live.hidden[None],
            d_slots,
            d_gated * gate_act,
            conv_out,
            live.state_in,
            live.steps,
            live.marks,
            head_params,
        )
        conv_cot = conv_back(d_conv_out)
        g_head = g_head[:3]
    else:
        output_grads = output_back(d_gated * gate_act)
        state_grad = pass_states(n, output_grads[3], live.logs, True).astype(F32)
        state_grad = state_grad.reshape(MHEADS, MHEAD_DIM, NSTATE)
        state_in = live.state_in.astype(F32).reshape(MHEADS, MHEAD_DIM, NSTATE)
        state_cot = state_back((state_grad, jnp.sum(state_grad * state_in, axis=(1, 2))))
        conv_cot = conv_back(output_grads[0] + state_cot[0])
        d_dt = output_grads[1] + state_cot[1]
        g_head = output_grads[2] + state_cot[2]
    returned = passed_along(conv_cot[0][: CONV - 1], -1)
    d_conv_in = conv_cot[0][CONV - 1 :] + jnp.concatenate(
        [jnp.zeros((patch_rows - CONV + 1, CONV_CH), F32), returned * keep_tail[:, None]]
    )
    d_projected = jnp.concatenate([d_gate_z, d_conv_in, d_dt], axis=1).astype(BF)
    d_projected = jnp.pad(d_projected, ((0, 0), (0, -d_projected.shape[1] % 128)))
    d_embedded, g_patch_gain = rms_back(
        live.embedded, live.patch_gain, dot_t(d_projected, live.mixer_in)
    )
    d_embedded = (d_hidden + d_embedded).astype(BF)

    g_conv_weight = conv_cot[1].reshape(CONV, n, -1).transpose(1, 0, 2).reshape(n, -1)
    g_head = jnp.broadcast_to(g_head.reshape(1, -1), (n, 3 * MHEADS))
    g_small = [g_patch_gain, g_conv_weight, conv_cot[2], g_mixer_gain, g_attn_gain, g_ffn_gain, g_head]
    g_small = jnp.concatenate([piece.reshape(n, -1) for piece in g_small], axis=1)
    small_width = g_small.shape[1]
    g_small = jnp.pad(g_small, ((0, 0), (0, LOG_ROWS * 128 - small_width)))
    g_small = g_small.reshape(n * LOG_ROWS, 128)
    if small_slice:
        d_projected = jnp.pad(d_projected, ((0, 0), (0, -d_projected.shape[1] % SUM_COLUMNS)))
        g_patch, g_small, g_mixer_in, g_mixer_out, input_grad = last_sums(
            n,
            d_embedded,
            live.parted,
            g_small,
            live.order,
            live.last_lefts,
            jnp.concatenate([d_projected, d_branch, d_branch], axis=1),
            live.d_stream0,
            patch_weight,
            mixer_in.shape[1],
        )
    else:
        g_attn_out = summed_grad(live.mixed, d_stream1_low)
        g_qkv = summed_grad(live.normed0, d_triple)
        known = lax.all_gather(d_embedded, "seq", axis=0, tiled=True)
        g_patch = dot(live.parted.T, known)
        d_parted = dot_t(known, patch_weight).astype(BF).reshape(n, patch_rows, -1)
        d_parted = lax.all_to_all(d_parted, "seq", 0, 0, tiled=True)
        d_parted = d_parted.transpose(1, 0, 2).reshape(patch_rows, -1).astype(F32)
        input_grad = (live.d_stream0 + d_parted).astype(BF)
        g_small = lax.psum_scatter(g_small, "seq", scatter_dimension=0, tiled=True)
        g_unpatch = summed_grad(live.hidden, d_slots)
        g_mixer_in = summed_grad(live.normed, d_projected)[:, : mixer_in.shape[1]]
        g_mixer_out = summed_grad(live.gated_norm, d_branch)
    g_small = g_small.reshape(-1)[:small_width]
    s = jnp.split(g_small, cuts)
    return (
        layer_out,
        input_grad.reshape(-1, D),
        g_patch,
        s[0],
        g_mixer_in,
        s[1].reshape(CONV, -1),
        s[2],
        s[6].reshape(3, MHEADS),
        s[3],
        g_mixer_out,
        g_unpatch,
        s[4],
        g_qkv,
        g_attn_out,
        s[5],
        g_gate_up,
        g_down,
    )


def solution(mesh):
    rows, vector = P("seq", None), P("seq")
    placed = (
        rows, vector, rows, rows, vector, rows, P(None, "seq"), vector, P(),
        vector, rows, rows, vector, rows, rows, vector, rows, rows,
    )
    returned = (
        rows, rows, rows, vector, rows, P(None, "seq"), vector, P(), vector,
        rows, rows, vector, rows, rows, vector, rows, rows,
    )
    return jax.shard_map(
        local, mesh=mesh, in_specs=placed, out_specs=returned, check_vma=False
    )
```
